32 devices in a mesh: ctx: 8 (over y, x, core), tp: 4 (over z).
Axes of the slice: x: 2, y: 2, z: 4, core: 2. Of those that a mesh axis runs over, the one named last changes fastest.
Arguments:
- query_proj: bfloat16 [1024, 4096], P('ctx', 'tp'), may hold values from -6 to 6
- key_proj: bfloat16 [1024, 4096], P('ctx', 'tp'), may hold values from -6 to 6
- value_proj: bfloat16 [1024, 4096], P('ctx', 'tp'), may hold values from -6 to 6
- cotangent: bfloat16 [1024, 4096], P('ctx', 'tp'), may hold values from -6 to 6
- filter_taps: float32 [1024, 4096], P('ctx', 'tp'), may hold values from -1 to 1
- short_weights: float32 [3, 3, 4096], P(None, None, 'tp'), may hold values from -3.5 to 3.5
Outputs:
- gated_out: bfloat16 [1024, 4096], P('ctx', 'tp')
- query_grad: bfloat16 [1024, 4096], P('ctx', 'tp')
- key_grad: bfloat16 [1024, 4096], P('ctx', 'tp')
- value_grad: bfloat16 [1024, 4096], P('ctx', 'tp')
- filter_grad: float32 [1024, 4096], P('ctx', 'tp')
- short_grad: float32 [3, 3, 4096], P(None, None, 'tp')
The draws below stay inside these ranges and needn't reach their ends.
All inputs are finite; a program needn't handle non-finite values.
Results may differ from the reference program's by a relative error of at most 0.0065.
Values may be sent and summed in bfloat16 or wider, within the bound.
No kernel may reach another device: no remote copies, remote signals or barrier semaphores. Data moves between devices by JAX's collectives and lax.ppermute only.
A program may use at most 64 MiB of HBM per device.

```python
import math
import jax
import jax.numpy as jnp
from jax import lax

D = 4096
TAPS = 3
SEQ = 1024


def draw_filter_taps(key, part):
    key_rough, key_pick, key_fast, key_slow = jax.random.split(key, 4)
    positions = jnp.arange(SEQ, dtype=jnp.float32)[:, None]
    rough_part = jax.random.truncated_normal(key_rough, -3.0, 3.0, (SEQ, D), jnp.float32)
    fast_share = 0.5
    fast_pick = jax.random.bernoulli(key_pick, fast_share, (D,))
    fast_len = jax.random.uniform(key_fast, (D,), jnp.float32, 30.0, 50.0)
    slow_len = jnp.exp(jax.random.uniform(key_slow, (D,), jnp.float32, math.log(SEQ / 4.0), math.log(SEQ * 4.0)))
    decay_len = jnp.where(fast_pick, fast_len, slow_len)
    energy = 0.5 * decay_len * (1.0 - jnp.exp(-2.0 * SEQ / decay_len))
    return rough_part * jnp.exp(-positions / decay_len) / jnp.sqrt(energy)


def levels(stream_key, extent, cuts, least, largest):
    loudness, own = 1.0, jax.random.fold_in(stream_key, 6)
    for axis_at, shards_of in cuts:
        heights = jnp.exp(jax.random.uniform(jax.random.fold_in(own, axis_at), (shards_of,), jnp.float32, least / len(cuts), largest / len(cuts)))
        loudness = loudness * jnp.repeat(heights, extent[axis_at] // shards_of).reshape([-1 if axis == axis_at else 1 for axis in range(len(extent))])
    return loudness


def scatter_about(own_key, shape, deviation, most, cuts=(), kind=jnp.bfloat16):
    result = deviation * jax.random.normal(own_key, shape, jnp.float32)
    if cuts:
        result = result * levels(own_key, shape, cuts, -0.22, 0.18)
    return jnp.clip(result, -most, most).astype(kind)


def setup_inputs(seed: int = 0) -> dict:
    arg_keys = jax.random.split(jax.random.key(seed), 7)
    return {
        "query_proj": scatter_about(arg_keys[0], (SEQ, D), 1.0, 6.0, ((0, 8), (1, 4))),
        "key_proj": scatter_about(arg_keys[1], (SEQ, D), 1.0, 6.0, ((0, 8), (1, 4))),
        "value_proj": scatter_about(arg_keys[2], (SEQ, D), 1.0, 6.0, ((0, 8), (1, 4))),
        "cotangent": scatter_about(arg_keys[3], (SEQ, D), 1.0, 6.0, ((0, 8), (1, 4))),
        "filter_taps": draw_filter_taps(jax.random.fold_in(arg_keys[6], 71), 0),
        "short_weights": scatter_about(arg_keys[5], (3, TAPS, D), TAPS ** -0.5, 3.5, ((2, 4),), jnp.float32),
    }


def causal_short(signal, weights):
    length = signal.shape[0]
    padded = jnp.pad(signal, ((TAPS - 1, 0), (0, 0)))
    summed = jnp.zeros_like(signal)
    for offset in range(TAPS):
        summed = summed + weights[offset] * padded[TAPS - 1 - offset:TAPS - 1 - offset + length]
    return summed


def reverse_short(grad_in, weights):
    length = grad_in.shape[0]
    padded = jnp.pad(grad_in, ((0, TAPS - 1), (0, 0)))
    summed = jnp.zeros_like(grad_in)
    for offset in range(TAPS):
        summed = summed + weights[offset] * padded[offset:offset + length]
    return summed


def short_tap_sums(grad_in, signal):
    length = signal.shape[0]
    padded = jnp.pad(signal, ((TAPS - 1, 0), (0, 0)))
    rows = [jnp.sum(grad_in * padded[TAPS - 1 - offset:TAPS - 1 - offset + length], axis=0) for offset in range(TAPS)]
    return jnp.stack(rows, axis=0)


def reference(query_proj, key_proj, value_proj, cotangent, filter_taps, short_weights):
    block_width = min(256, D)
    blocks = D // block_width
    fft_len = 2 * SEQ
    grad_scale = 1.0 / float(SEQ) ** 0.5

    def to_blocks(whole):
        return whole.reshape(SEQ, blocks, block_width).transpose(1, 0, 2)

    weight_blocks = short_weights.reshape(3, TAPS, blocks, block_width).transpose(2, 0, 1, 3)

    def per_block(pieces):
        query_in, key_in, value_in, cot_in, filter_in, weight_in = pieces
        query_short = causal_short(query_in.astype(jnp.float32), weight_in[0])
        key_short = causal_short(key_in.astype(jnp.float32), weight_in[1])
        value_short = causal_short(value_in.astype(jnp.float32), weight_in[2])
        product = (key_short * value_short).astype(jnp.bfloat16)
        prod_spec = jnp.fft.rfft(product.astype(jnp.float32), n=fft_len, axis=0)
        filter_spec = jnp.fft.rfft(filter_in, n=fft_len, axis=0)
        conv_out = jnp.fft.irfft(prod_spec * filter_spec, n=fft_len, axis=0)[:SEQ].astype(jnp.bfloat16)
        conv_wide = conv_out.astype(jnp.float32)
        gated_out = (query_short * conv_wide).astype(jnp.bfloat16)
        cot_wide = cot_in.astype(jnp.float32)
        gate_grad = (cot_wide * query_short).astype(jnp.bfloat16)
        gate_spec = jnp.fft.rfft(gate_grad.astype(jnp.float32), n=fft_len, axis=0)
        conv_grad = jnp.fft.irfft(jnp.conj(filter_spec) * gate_spec, n=fft_len, axis=0)[:SEQ].astype(jnp.bfloat16)
        filter_grad = jnp.fft.irfft(jnp.conj(prod_spec) * gate_spec, n=fft_len, axis=0)[:SEQ] * grad_scale
        grad_wide = conv_grad.astype(jnp.float32)
        query_pre = cot_wide * conv_wide
        key_pre = grad_wide * value_short
        value_pre = grad_wide * key_short
        query_grad = reverse_short(query_pre, weight_in[0]).astype(jnp.bfloat16)
        key_grad = reverse_short(key_pre, weight_in[1]).astype(jnp.bfloat16)
        value_grad = reverse_short(value_pre, weight_in[2]).astype(jnp.bfloat16)
        short_grad = jnp.stack([
            short_tap_sums(query_pre, query_in.astype(jnp.float32)),
            short_tap_sums(key_pre, key_in.astype(jnp.float32)),
            short_tap_sums(value_pre, value_in.astype(jnp.float32))], axis=0) * grad_scale
        return (gated_out, query_grad, key_grad, value_grad, filter_grad.astype(jnp.float32), short_grad)

    results = lax.map(per_block, (to_blocks(query_proj), to_blocks(key_proj), to_blocks(value_proj),
                                  to_blocks(cotangent), to_blocks(filter_taps), weight_blocks))

    def from_blocks(stacked):
        return stacked.transpose(1, 0, 2).reshape(SEQ, D)

    short_grad = results[5].transpose(1, 2, 0, 3).reshape(3, TAPS, D)
    return (from_blocks(results[0]), from_blocks(results[1]), from_blocks(results[2]),
            from_blocks(results[3]), from_blocks(results[4]), short_grad)
```

```python
import functools
import math

import jax
import jax.numpy as jnp
import numpy as np
from jax import lax
from jax.experimental import pallas as pl
from jax.experimental.pallas import tpu as pltpu
from jax.sharding import PartitionSpec as P

F32 = jnp.float32
BF16 = jnp.bfloat16
LANES = 128
PHASES = 4
TILE = 16
IN_ARRAYS = 5
OUT_ARRAYS = 5
PIECES = 3


def phase_order(tokens, back):
    rows = lax.broadcasted_iota(jnp.int32, (tokens, tokens), 0)
    cols = lax.broadcasted_iota(jnp.int32, (tokens, tokens), 1)
    grouped, plain = (cols, rows) if back else (rows, cols)
    per = tokens // PHASES
    return (plain == (grouped % per) * PHASES + grouped // per).astype(BF16)


def pack_kernel(query, key, value, cot, taps, packed):
    tokens = query.shape[0]
    order = phase_order(tokens, False)
    for at, source in enumerate((query, key, value, cot, taps)):
        moved = jnp.dot(order, source[...].astype(BF16), preferred_element_type=F32).astype(BF16)
        for block in range(packed.shape[0]):
            packed[block, at * tokens : (at + 1) * tokens, :] = moved[
                :, block * LANES : (block + 1) * LANES
            ]


def pack(arrays, peers):
    tokens, width = arrays[0].shape
    steps = 4 if peers % 4 == 0 else 1
    return pl.pallas_call(
        pack_kernel,
        grid=(steps,),
        in_specs=[pl.BlockSpec((tokens, width // steps), lambda i: (0, i))] * IN_ARRAYS,
        out_specs=pl.BlockSpec((peers // steps, IN_ARRAYS * tokens, LANES), lambda i: (i, 0, 0)),
        out_shape=jax.ShapeDtypeStruct((peers, IN_ARRAYS * tokens, LANES), BF16),
        name="pack_inputs",
    )(*arrays)


def unpack_kernel(packed, gated, query_grad, key_grad, value_grad, filter_grad, short_grad):
    tokens = gated.shape[0]
    order = phase_order(tokens, True)
    rows = short_grad.shape[0] * short_grad.shape[1]
    for block in range(packed.shape[0]):
        lanes = slice(block * LANES, (block + 1) * LANES)
        for at, target in enumerate((gated, query_grad, key_grad, value_grad, filter_grad)):
            part = packed[block, at * tokens : (at + 1) * tokens, :]
            target[:, lanes] = jnp.dot(order, part, preferred_element_type=F32).astype(target.dtype)
        sums = packed[block, OUT_ARRAYS * tokens :, :].astype(F32)
        whole = sums[:rows]
        for piece in range(1, PIECES):
            whole = whole + sums[piece * rows : (piece + 1) * rows]
        for row in range(rows):
            which, tap = divmod(row, short_grad.shape[1])
            short_grad[which, tap : tap + 1, lanes] = whole[row : row + 1]


def unpack(packed, tokens, short_shape):
    peers = packed.shape[0]
    width = peers * LANES
    steps = 4 if peers % 4 == 0 else 1
    spread = pl.BlockSpec((tokens, width // steps), lambda i: (0, i))
    return pl.pallas_call(
        unpack_kernel,
        grid=(steps,),
        in_specs=[pl.BlockSpec((peers // steps, packed.shape[1], LANES), lambda i: (i, 0, 0))],
        out_specs=[spread] * OUT_ARRAYS
        + [pl.BlockSpec(short_shape[:2] + (width // steps,), lambda i: (0, 0, i))],
        out_shape=[jax.ShapeDtypeStruct((tokens, width), BF16)] * 4
        + [
            jax.ShapeDtypeStruct((tokens, width), F32),
            jax.ShapeDtypeStruct(short_shape, F32),
        ],
        name="unpack_outputs",
    )(packed)


@functools.lru_cache(maxsize=None)
def dft_tables(seq_len):
    size = seq_len // PHASES
    k = np.arange(size, dtype=np.int64)[:, None]
    m = np.arange(size, dtype=np.int64)[None, :]
    forward = []
    for phase in range(PHASES):
        turns = ((4 * k + 1) * (PHASES * m + phase)) % (4 * seq_len)
        angle = 2.0 * np.pi / (4 * seq_len) * turns
        forward.append(np.concatenate([np.cos(angle), -np.sin(angle)], axis=0))
    forward = np.stack(forward)
    backward = np.swapaxes(forward, 1, 2) / seq_len

    def pieces(table):
        high = table.astype(BF16)
        low = (table - high.astype(np.float64)).astype(BF16)
        return np.stack([high, low], axis=1)

    return pieces(forward), pieces(backward)


def forward_mix(parts):
    (r0, i0), (r1, i1), (r2, i2), (r3, i3) = parts
    ar, ai, br, bi = r0 + r2, i0 + i2, r0 - r2, i0 - i2
    cr, ci, dr, di = r1 + r3, i1 + i3, r1 - r3, i1 - i3
    return ((ar + cr, ai + ci), (br + di, bi - dr), (ar - cr, ai - ci), (br - di, bi + dr))


def inverse_mix(parts):
    (r0, i0), (r1, i1), (r2, i2), (r3, i3) = parts
    ar, ai, br, bi = r0 + r2, i0 + i2, r0 - r2, i0 - i2
    cr, ci, dr, di = r1 + r3, i1 + i3, r1 - r3, i1 - i3
    return ((ar + cr, ai + ci), (br - di, bi + dr), (ar - cr, ai - ci), (br + di, bi - dr))


def times(left, right):
    return tuple(
        (lr * rr - li * ri, lr * ri + li * rr) for (lr, li), (rr, ri) in zip(left, right)
    )


def conj_times(left, right):
    return tuple(
        (lr * rr + li * ri, lr * ri - li * rr) for (lr, li), (rr, ri) in zip(left, right)
    )


def earlier(phases, by):
    moved = []
    for r in range(PHASES):
        if r >= by:
            moved.append(phases[r - by])
        else:
            last = phases[r - by + PHASES]
            moved.append(jnp.concatenate([jnp.zeros_like(last[:1]), last[:-1]], axis=0))
    return moved


def later(phases, by):
    moved = []
    for r in range(PHASES):
        if r + by < PHASES:
            moved.append(phases[r + by])
        else:
            first = phases[r + by - PHASES]
            moved.append(jnp.concatenate([first[1:], jnp.zeros_like(first[:1])], axis=0))
    return moved


def channel_kernel(
    tokens,
    grad_scale,
    packed,
    weights,
    forward,
    backward,
    out,
    signals,
    spectra,
    high,
    low,
    shorts,
):
    peers = packed.shape[0]
    taps = weights.shape[1]
    size = peers * tokens // PHASES
    per = tokens // PHASES
    at_lanes = pl.ds(pl.multiple_of(lax.axis_index("ctx") * LANES, LANES), LANES)

    def phase_of(array, r):
        start = array * tokens + r * per
        return packed[:, start : start + per, :].reshape(size, LANES)

    def weight(array, tap):
        return weights[array, tap : tap + 1, at_lanes]

    for array in range(3):
        phases = [phase_of(array, r).astype(F32) for r in range(PHASES)]
        summed = [weight(array, 0) * x for x in phases]
        for tap in range(1, taps):
            moved = earlier(phases, tap)
            summed = [s + weight(array, tap) * x for s, x in zip(summed, moved)]
        for r in range(PHASES):
            shorts[array, r] = summed[r]
    for r in range(PHASES):
        signals[r, :, :LANES] = (shorts[1, r] * shorts[2, r]).astype(BF16)
        signals[r, :, LANES : 2 * LANES] = (phase_of(3, r).astype(F32) * shorts[0, r]).astype(BF16)
        signals[r, :, 2 * LANES :] = phase_of(4, r)
        spectra[r] = jnp.dot(
            forward[r, 0], signals[r], preferred_element_type=F32
        ) + jnp.dot(forward[r, 1], signals[r], preferred_element_type=F32)

    for chunk in range(size // TILE):
        real = slice(chunk * TILE, (chunk + 1) * TILE)
        imag = slice(size + chunk * TILE, size + (chunk + 1) * TILE)

        def spectrum(signal):
            lanes = slice(signal * LANES, (signal + 1) * LANES)
            return forward_mix([(spectra[r, real, lanes], spectra[r, imag, lanes]) for r in range(PHASES)])

        prod, grad, filt = spectrum(0), spectrum(1), spectrum(2)
        for which, mixed in enumerate(
            (times(prod, filt), conj_times(filt, grad), conj_times(prod, grad))
        ):
            lanes = slice(which * LANES, (which + 1) * LANES)
            for r, pair in enumerate(inverse_mix(mixed)):
                for rows, part in zip((real, imag), pair):
                    rounded = part.astype(BF16)
                    high[r, rows, lanes] = rounded
                    low[r, rows, lanes] = (part - rounded.astype(F32)).astype(BF16)

    conv, conv_grad = [], []
    for r in range(PHASES):
        result = (
            jnp.dot(backward[r, 0], high[r], preferred_element_type=F32)
            + jnp.dot(backward[r, 0], low[r], preferred_element_type=F32)
            + jnp.dot(backward[r, 1], high[r], preferred_element_type=F32)
        )
        conv.append(result[:, :LANES].astype(BF16).astype(F32))
        conv_grad.append(result[:, LANES : 2 * LANES].astype(BF16).astype(F32))
        out[:, 4 * tokens + r * per : 4 * tokens + (r + 1) * per, :] = (
            (result[:, 2 * LANES :] * grad_scale).astype(BF16).reshape(peers, per, LANES)
        )

    def put(array, r, value):
        start = array * tokens + r * per
        out[:, start : start + per, :] = value.astype(BF16).reshape(peers, per, LANES)

    sums = []
    for array in range(3):
        if array == 0:
            pre = [phase_of(3, r).astype(F32) * conv[r] for r in range(PHASES)]
            for r in range(PHASES):
                put(0, r, shorts[0, r] * conv[r])
        else:
            pre = [conv_grad[r] * shorts[3 - array, r] for r in range(PHASES)]
        total = [weight(array, 0) * x for x in pre]
        for tap in range(1, taps):
            moved = later(pre, tap)
            total = [s + weight(array, tap) * x for s, x in zip(total, moved)]
        for r in range(PHASES):
            put(1 + array, r, total[r])
        phases = [phase_of(array, r).astype(F32) for r in range(PHASES)]
        for tap in range(taps):
            moved = phases if tap == 0 else earlier(phases, tap)
            summed = pre[0] * moved[0]
            for r in range(1, PHASES):
                summed = summed + pre[r] * moved[r]
            sums.append(jnp.sum(summed, axis=0, keepdims=True))
    rest = jnp.concatenate(sums, axis=0) * grad_scale
    pieces = []
    for _ in range(PIECES):
        piece = rest.astype(BF16).astype(F32)
        pieces.append(piece)
        rest = rest - piece
    space = out.shape[1] - OUT_ARRAYS * tokens
    filled = PIECES * len(sums)
    if space > filled:
        pieces.append(jnp.zeros((space - filled, LANES), F32))
    block = jnp.concatenate(pieces, axis=0).astype(BF16)
    for peer in range(peers):
        out[peer, OUT_ARRAYS * tokens :, :] = block


def channel_step(packed, short_weights, tokens):
    peers = packed.shape[0]
    seq_len = peers * tokens
    size = seq_len // PHASES
    forward, backward = dft_tables(seq_len)
    count = PIECES * short_weights.shape[0] * short_weights.shape[1]
    rows = OUT_ARRAYS * tokens + -(-count // TILE) * TILE
    return pl.pallas_call(
        functools.partial(channel_kernel, tokens, 1.0 / math.sqrt(seq_len)),
        in_specs=[pl.BlockSpec(memory_space=pltpu.VMEM)] * 4,
        out_specs=pl.BlockSpec(memory_space=pltpu.VMEM),
        out_shape=jax.ShapeDtypeStruct((peers, rows, LANES), BF16),
        scratch_shapes=[
            pltpu.VMEM((PHASES, size, 3 * LANES), BF16),
            pltpu.VMEM((PHASES, 2 * size, 3 * LANES), F32),
            pltpu.VMEM((PHASES, 2 * size, 3 * LANES), BF16),
            pltpu.VMEM((PHASES, 2 * size, 3 * LANES), BF16),
            pltpu.VMEM((3, PHASES, size, LANES), F32),
        ],
        compiler_params=pltpu.CompilerParams(vmem_limit_bytes=40 * 1024 * 1024),
        name="channel_operator",
    )(packed, short_weights, jnp.asarray(forward), jnp.asarray(backward))


def channel_shards(query_proj, key_proj, value_proj, cotangent, filter_taps, short_weights):
    peers = lax.axis_size("ctx")
    tokens = query_proj.shape[0]
    packed = pack((query_proj, key_proj, value_proj, cotangent, filter_taps), peers)
    packed = lax.all_to_all(packed, "ctx", split_axis=0, concat_axis=0, tiled=True)
    result = channel_step(packed, short_weights, tokens)
    result = lax.all_to_all(result, "ctx", split_axis=0, concat_axis=0, tiled=True)
    return tuple(unpack(result, tokens, short_weights.shape))


def from_behind(array, axis, by):
    peers = lax.axis_size(axis)
    pairs = [(i, i + by) for i in range(peers) if 0 <= i + by < peers]
    return lax.ppermute(array, axis, pairs)


def contract(form, left, right):
    return jnp.einsum(
        form, left, right, precision=lax.Precision.HIGHEST, preferred_element_type=jnp.float32
    )


def table_pair(rows, cols, period):
    row_ids = lax.broadcasted_iota(jnp.int32, (rows, cols), 0)
    col_ids = lax.broadcasted_iota(jnp.int32, (rows, cols), 1)
    angle = 2.0 * math.pi / period * (row_ids * col_ids % period).astype(jnp.float32)
    return (jnp.cos(angle), jnp.sin(angle))


def make_plan(seq_len):
    small_len = int(math.isqrt(2 * seq_len))
    while seq_len % small_len:
        small_len -= 1
    large_len = 2 * seq_len // small_len
    large_cos, large_sin = table_pair(large_len // 2, large_len, large_len)
    small_cos, small_sin = table_pair(small_len, small_len, small_len)
    twist_cos, twist_sin = table_pair(large_len, small_len, small_len * large_len)
    fwd_large = jnp.stack([large_cos, -large_sin], axis=1)
    fwd_small = jnp.stack([jnp.stack([small_cos, -small_sin]), jnp.stack([small_sin, small_cos])])
    inv_small = jnp.stack([jnp.stack([small_cos, small_sin]), jnp.stack([-small_sin, small_cos])])
    inv_large = jnp.stack([large_cos, -large_sin])
    return (small_len, large_len, fwd_large, fwd_small, inv_small, inv_large, twist_cos, twist_sin)


def forward_spec(signal, dft_plan):
    small_len, large_len, fwd_large, fwd_small, inv_small, inv_large, twist_cos, twist_sin = (
        dft_plan
    )
    cube = signal.reshape(signal.shape[0], large_len // 2, small_len)
    section_one = contract("cba,bpk->cpka", cube, fwd_large)
    real_one = section_one[:, 0]
    imag_one = section_one[:, 1]
    section_two = jnp.stack(
        [real_one * twist_cos + imag_one * twist_sin, imag_one * twist_cos - real_one * twist_sin],
        axis=1,
    )
    return contract("cpka,pqaj->cqkj", section_two, fwd_small)


def inverse_half(spec, dft_plan):
    small_len, large_len, fwd_large, fwd_small, inv_small, inv_large, twist_cos, twist_sin = (
        dft_plan
    )
    section_one = contract("cqkj,qpja->cpka", spec, inv_small)
    real_one = section_one[:, 0]
    imag_one = section_one[:, 1]
    section_two = jnp.stack(
        [real_one * twist_cos - imag_one * twist_sin, imag_one * twist_cos + real_one * twist_sin],
        axis=1,
    )
    signal = contract("cpka,pbk->cba", section_two, inv_large)
    return signal.reshape(signal.shape[0], -1) / float(small_len * large_len)


def complex_mul(left, right):
    left_real, left_imag = (left[:, 0], left[:, 1])
    right_real, right_imag = (right[:, 0], right[:, 1])
    return jnp.stack(
        [
            left_real * right_real - left_imag * right_imag,
            left_real * right_imag + left_imag * right_real,
        ],
        axis=1,
    )


def conj_mul(left, right):
    left_real, left_imag = (left[:, 0], left[:, 1])
    right_real, right_imag = (right[:, 0], right[:, 1])
    return jnp.stack(
        [
            left_real * right_real + left_imag * right_imag,
            left_real * right_imag - left_imag * right_real,
        ],
        axis=1,
    )


def conv_forward(prod_chan, filter_spec, dft_plan):
    prod_spec = forward_spec(prod_chan.astype(jnp.float32), dft_plan)
    conv_chan = inverse_half(complex_mul(prod_spec, filter_spec), dft_plan).astype(jnp.bfloat16)
    return (conv_chan, prod_spec)


def conv_backward(grad_chan, filter_spec, prod_spec, dft_plan, grad_scale):
    grad_spec = forward_spec(grad_chan.astype(jnp.float32), dft_plan)
    dconv_chan = inverse_half(conj_mul(filter_spec, grad_spec), dft_plan).astype(jnp.bfloat16)
    dfilter_chan = inverse_half(conj_mul(prod_spec, grad_spec), dft_plan) * grad_scale
    return (dconv_chan, dfilter_chan)


def receive_filter(filter_taps, dft_plan):
    filter_chan = lax.all_to_all(filter_taps.T, "ctx", split_axis=0, concat_axis=1, tiled=True)
    return forward_spec(filter_chan, dft_plan)


def return_filter(dfilter_chan):
    return (
        lax.all_to_all(
            dfilter_chan.astype(jnp.bfloat16), "ctx", split_axis=1, concat_axis=0, tiled=True
        )
        .astype(dfilter_chan.dtype)
        .T
    )


def causal_taps(extended, weights, length, axis):
    rim_rows = len(weights) - 1
    summed = weights[0] * lax.slice_in_dim(extended, rim_rows, rim_rows + length, axis=axis)
    for offset in range(1, len(weights)):
        summed = summed + weights[offset] * lax.slice_in_dim(
            extended, rim_rows - offset, rim_rows - offset + length, axis=axis
        )
    return summed


def reverse_taps(extended, weights, length, axis):
    summed = weights[0] * lax.slice_in_dim(extended, 0, length, axis=axis)
    for offset in range(1, len(weights)):
        summed = summed + weights[offset] * lax.slice_in_dim(
            extended, offset, offset + length, axis=axis
        )
    return summed


def tap_grads(grad_in, extended, tap_count, length, axis):
    rim_rows = tap_count - 1
    rows = [
        jnp.sum(
            grad_in
            * lax.slice_in_dim(extended, rim_rows - offset, rim_rows - offset + length, axis=axis),
            axis=axis,
        )
        for offset in range(tap_count)
    ]
    return jnp.stack(rows, axis=1)


def spread_shards(query_proj, key_proj, value_proj, cotangent, filter_taps, short_weights):
    tokens = query_proj.shape[0]
    tap_count = short_weights.shape[1]
    rim_rows = tap_count - 1
    seq_len = tokens * lax.axis_size("ctx")
    grad_scale = 1.0 / math.sqrt(seq_len)
    dft_plan = make_plan(seq_len)
    stacked = jnp.stack([query_proj, key_proj, value_proj])
    prev_rim = from_behind(stacked[:, tokens - rim_rows :], "ctx", 1)
    extended = jnp.concatenate([prev_rim, stacked], axis=1).astype(jnp.float32)
    weights = [short_weights[:, offset, None, :] for offset in range(tap_count)]
    short_out = causal_taps(extended, weights, tokens, 1)
    product = (short_out[1] * short_out[2]).astype(jnp.bfloat16)
    cot_wide = cotangent.astype(jnp.float32)
    gate_grad = (cot_wide * short_out[0]).astype(jnp.bfloat16)
    filter_spec = receive_filter(filter_taps, dft_plan)
    prod_chan = lax.all_to_all(product.T, "ctx", split_axis=0, concat_axis=1, tiled=True)
    conv_chan, prod_spec = conv_forward(prod_chan, filter_spec, dft_plan)
    conv_tok = lax.all_to_all(conv_chan, "ctx", split_axis=1, concat_axis=0, tiled=True)
    grad_chan = lax.all_to_all(gate_grad.T, "ctx", split_axis=0, concat_axis=1, tiled=True)
    dconv_chan, dfilter_chan = conv_backward(
        grad_chan, filter_spec, prod_spec, dft_plan, grad_scale
    )
    dconv_tok = lax.all_to_all(dconv_chan, "ctx", split_axis=1, concat_axis=0, tiled=True)
    filter_grad = return_filter(dfilter_chan)
    conv_wide = conv_tok.T.astype(jnp.float32)
    dconv_wide = dconv_tok.T.astype(jnp.float32)
    gated = (short_out[0] * conv_wide).astype(jnp.bfloat16)
    token_grads = jnp.stack(
        [cot_wide * conv_wide, dconv_wide * short_out[2], dconv_wide * short_out[1]]
    )
    next_rim = from_behind(token_grads[:, :rim_rows], "ctx", -1)
    grad_ext = jnp.concatenate([token_grads, next_rim], axis=1)
    inputs_grad = reverse_taps(grad_ext, weights, tokens, 1).astype(jnp.bfloat16)
    weight_part = tap_grads(token_grads, extended, tap_count, tokens, 1)
    short_grad = lax.psum(weight_part, "ctx") * grad_scale
    results = (gated, inputs_grad[0], inputs_grad[1], inputs_grad[2])
    return (results[0], results[1], results[2], results[3], filter_grad, short_grad)


def fits(query_proj, filter_taps):
    peers = lax.axis_size("ctx")
    tokens, width = query_proj.shape
    return (
        width == peers * LANES
        and tokens % (PHASES * TILE) == 0
        and peers * tokens <= 2048
    )


def shards(*arrays):
    return channel_shards(*arrays) if fits(arrays[0], arrays[4]) else spread_shards(*arrays)


def solution(mesh):
    placed = (
        P("ctx", "tp"),
        P("ctx", "tp"),
        P("ctx", "tp"),
        P("ctx", "tp"),
        P("ctx", "tp"),
        P(None, None, "tp"),
    )
    return jax.shard_map(
        shards,
        mesh=mesh,
        in_specs=placed,
        out_specs=(
            P("ctx", "tp"),
            P("ctx", "tp"),
            P("ctx", "tp"),
            P("ctx", "tp"),
            P("ctx", "tp"),
            P(None, None, "tp"),
        ),
        check_vma=False,
    )
```

```python
import functools
import math

import jax
import jax.numpy as jnp
import numpy as np
from jax import lax
from jax.experimental import pallas as pl
from jax.experimental.pallas import tpu as pltpu
from jax.sharding import PartitionSpec as P

F32 = jnp.float32
BF16 = jnp.bfloat16
LANES = 128
PHASES = 4
TILE = 16
IN_ARRAYS = 5
OUT_ARRAYS = 5
PIECES = 3


def phase_order(tokens, back):
    rows = lax.broadcasted_iota(jnp.int32, (tokens, tokens), 0)
    cols = lax.broadcasted_iota(jnp.int32, (tokens, tokens), 1)
    grouped, plain = (cols, rows) if back else (rows, cols)
    per = tokens // PHASES
    return (plain == (grouped % per) * PHASES + grouped // per).astype(BF16)


def partners(peers):
    return [0] + list(range(peers - 1, 0, -1))


def pack_kernel(query, key, value, cot, taps, *packed):
    tokens = query.shape[0]
    order = phase_order(tokens, False)
    me = lax.axis_index("ctx")
    for at, source in enumerate((query, key, value, cot, taps)):
        for step, target in zip(partners(len(packed)), packed):
            lanes = pl.ds(pl.multiple_of((me ^ step) * LANES, LANES), LANES)
            moved = jnp.dot(order, source[:, lanes].astype(BF16), preferred_element_type=F32)
            target[at * tokens : (at + 1) * tokens, :] = moved.astype(BF16)


def pack(arrays, peers):
    tokens = arrays[0].shape[0]
    return pl.pallas_call(
        pack_kernel,
        in_specs=[pl.BlockSpec(memory_space=pltpu.VMEM)] * IN_ARRAYS,
        out_specs=[pl.BlockSpec(memory_space=pltpu.VMEM)] * peers,
        out_shape=[jax.ShapeDtypeStruct((IN_ARRAYS * tokens, LANES), BF16)] * peers,
        name="pack_inputs",
    )(*arrays)


def exchange(blocks):
    peers = len(blocks)
    got = [blocks[0]]
    for step, block in list(zip(partners(peers), blocks))[1:]:
        got.append(lax.ppermute(block, "ctx", [(i, i ^ step) for i in range(peers)]))
    return got


def unpack_kernel(peers, *refs):
    packed, (gated, query_grad, key_grad, value_grad, filter_grad, short_grad) = (
        refs[:peers],
        refs[peers:],
    )
    tokens = gated.shape[0]
    order = phase_order(tokens, True)
    rows = short_grad.shape[0] * short_grad.shape[1]
    me = lax.axis_index("ctx")
    for step, source in zip(partners(len(packed)), packed):
        lanes = pl.ds(pl.multiple_of((me ^ step) * LANES, LANES), LANES)
        for at, target in enumerate((gated, query_grad, key_grad, value_grad, filter_grad)):
            part = source[at * tokens : (at + 1) * tokens, :]
            target[:, lanes] = jnp.dot(order, part, preferred_element_type=F32).astype(target.dtype)
        sums = source[OUT_ARRAYS * tokens :, :].astype(F32)
        whole = sums[:rows]
        for piece in range(1, PIECES):
            whole = whole + sums[piece * rows : (piece + 1) * rows]
        for row in range(rows):
            which, tap = divmod(row, short_grad.shape[1])
            short_grad[which, tap : tap + 1, lanes] = whole[row : row + 1]


def unpack(packed, tokens, short_shape):
    peers = len(packed)
    width = peers * LANES
    return pl.pallas_call(
        functools.partial(unpack_kernel, peers),
        in_specs=[pl.BlockSpec(memory_space=pltpu.VMEM)] * peers,
        out_specs=[pl.BlockSpec(memory_space=pltpu.VMEM)] * (OUT_ARRAYS + 1),
        out_shape=[jax.ShapeDtypeStruct((tokens, width), BF16)] * 4
        + [
            jax.ShapeDtypeStruct((tokens, width), F32),
            jax.ShapeDtypeStruct(short_shape, F32),
        ],
        name="unpack_outputs",
    )(*packed)


@functools.lru_cache(maxsize=None)
def dft_tables(seq_len):
    size = seq_len // PHASES
    k = np.arange(size, dtype=np.int64)[:, None]
    m = np.arange(size, dtype=np.int64)[None, :]
    forward = []
    for phase in range(PHASES):
        turns = ((4 * k + 1) * (PHASES * m + phase)) % (4 * seq_len)
        angle = 2.0 * np.pi / (4 * seq_len) * turns
        forward.append(np.concatenate([np.cos(angle), -np.sin(angle)], axis=0))
    forward = np.stack(forward)
    backward = np.swapaxes(forward, 1, 2) / seq_len

    def pieces(table):
        high = table.astype(BF16)
        low = (table - high.astype(np.float64)).astype(BF16)
        return np.stack([high, low], axis=1)

    return pieces(forward), pieces(backward)


def forward_mix(parts):
    (r0, i0), (r1, i1), (r2, i2), (r3, i3) = parts
    ar, ai, br, bi = r0 + r2, i0 + i2, r0 - r2, i0 - i2
    cr, ci, dr, di = r1 + r3, i1 + i3, r1 - r3, i1 - i3
    return ((ar + cr, ai + ci), (br + di, bi - dr), (ar - cr, ai - ci), (br - di, bi + dr))


def inverse_mix(parts):
    (r0, i0), (r1, i1), (r2, i2), (r3, i3) = parts
    ar, ai, br, bi = r0 + r2, i0 + i2, r0 - r2, i0 - i2
    cr, ci, dr, di = r1 + r3, i1 + i3, r1 - r3, i1 - i3
    return ((ar + cr, ai + ci), (br - di, bi + dr), (ar - cr, ai - ci), (br + di, bi - dr))


def times(left, right):
    return tuple(
        (lr * rr - li * ri, lr * ri + li * rr) for (lr, li), (rr, ri) in zip(left, right)
    )


def conj_times(left, right):
    return tuple(
        (lr * rr + li * ri, lr * ri - li * rr) for (lr, li), (rr, ri) in zip(left, right)
    )


def earlier(phases, by):
    moved = []
    for r in range(PHASES):
        if r >= by:
            moved.append(phases[r - by])
        else:
            last = phases[r - by + PHASES]
            moved.append(jnp.concatenate([jnp.zeros_like(last[:1]), last[:-1]], axis=0))
    return moved


def later(phases, by):
    moved = []
    for r in range(PHASES):
        if r + by < PHASES:
            moved.append(phases[r + by])
        else:
            first = phases[r + by - PHASES]
            moved.append(jnp.concatenate([first[1:], jnp.zeros_like(first[:1])], axis=0))
    return moved


def channel_kernel(tokens, peers, grad_scale, *refs):
    arrived = refs[:peers]
    weights, forward, backward = refs[peers : peers + 3]
    out = refs[peers + 3 : 2 * peers + 3]
    packed, results, signals, spectra, high, low, shorts = refs[2 * peers + 3 :]
    taps = weights.shape[1]
    size = peers * tokens // PHASES
    per = tokens // PHASES
    me = lax.axis_index("ctx")
    at_lanes = pl.ds(pl.multiple_of(me * LANES, LANES), LANES)
    for step, source in zip(partners(peers), arrived):
        packed[me ^ step] = source[...]

    def phase_of(array, r):
        start = array * tokens + r * per
        return packed[:, start : start + per, :].reshape(size, LANES)

    def weight(array, tap):
        return weights[array, tap : tap + 1, at_lanes]

    for array in range(3):
        phases = [phase_of(array, r).astype(F32) for r in range(PHASES)]
        summed = [weight(array, 0) * x for x in phases]
        for tap in range(1, taps):
            moved = earlier(phases, tap)
            summed = [s + weight(array, tap) * x for s, x in zip(summed, moved)]
        for r in range(PHASES):
            shorts[array, r] = summed[r]
    for r in range(PHASES):
        signals[r, :, :LANES] = (shorts[1, r] * shorts[2, r]).astype(BF16)
        signals[r, :, LANES : 2 * LANES] = (phase_of(3, r).astype(F32) * shorts[0, r]).astype(BF16)
        signals[r, :, 2 * LANES :] = phase_of(4, r)
        spectra[r] = jnp.dot(
            forward[r, 0], signals[r], preferred_element_type=F32
        ) + jnp.dot(forward[r, 1], signals[r], preferred_element_type=F32)

    for chunk in range(size // TILE):
        real = slice(chunk * TILE, (chunk + 1) * TILE)
        imag = slice(size + chunk * TILE, size + (chunk + 1) * TILE)

        def spectrum(signal):
            lanes = slice(signal * LANES, (signal + 1) * LANES)
            return forward_mix([(spectra[r, real, lanes], spectra[r, imag, lanes]) for r in range(PHASES)])

        prod, grad, filt = spectrum(0), spectrum(1), spectrum(2)
        for which, mixed in enumerate(
            (times(prod, filt), conj_times(filt, grad), conj_times(prod, grad))
        ):
            lanes = slice(which * LANES, (which + 1) * LANES)
            for r, pair in enumerate(inverse_mix(mixed)):
                for rows, part in zip((real, imag), pair):
                    rounded = part.astype(BF16)
                    high[r, rows, lanes] = rounded
                    low[r, rows, lanes] = (part - rounded.astype(F32)).astype(BF16)

    conv, conv_grad = [], []
    for r in range(PHASES):
        result = (
            jnp.dot(backward[r, 0], high[r], preferred_element_type=F32)
            + jnp.dot(backward[r, 0], low[r], preferred_element_type=F32)
            + jnp.dot(backward[r, 1], high[r], preferred_element_type=F32)
        )
        conv.append(result[:, :LANES].astype(BF16).astype(F32))
        conv_grad.append(result[:, LANES : 2 * LANES].astype(BF16).astype(F32))
        results[:, 4 * tokens + r * per : 4 * tokens + (r + 1) * per, :] = (
            (result[:, 2 * LANES :] * grad_scale).astype(BF16).reshape(peers, per, LANES)
        )

    def put(array, r, value):
        start = array * tokens + r * per
        results[:, start : start + per, :] = value.astype(BF16).reshape(peers, per, LANES)

    sums = []
    for array in range(3):
        if array == 0:
            pre = [phase_of(3, r).astype(F32) * conv[r] for r in range(PHASES)]
            for r in range(PHASES):
                put(0, r, shorts[0, r] * conv[r])
        else:
            pre = [conv_grad[r] * shorts[3 - array, r] for r in range(PHASES)]
        total = [weight(array, 0) * x for x in pre]
        for tap in range(1, taps):
            moved = later(pre, tap)
            total = [s + weight(array, tap) * x for s, x in zip(total, moved)]
        for r in range(PHASES):
            put(1 + array, r, total[r])
        phases = [phase_of(array, r).astype(F32) for r in range(PHASES)]
        for tap in range(taps):
            moved = phases if tap == 0 else earlier(phases, tap)
            summed = pre[0] * moved[0]
            for r in range(1, PHASES):
                summed = summed + pre[r] * moved[r]
            sums.append(jnp.sum(summed, axis=0, keepdims=True))
    rest = jnp.concatenate(sums, axis=0) * grad_scale
    pieces = []
    for _ in range(PIECES):
        piece = rest.astype(BF16).astype(F32)
        pieces.append(piece)
        rest = rest - piece
    space = results.shape[1] - OUT_ARRAYS * tokens
    filled = PIECES * len(sums)
    if space > filled:
        pieces.append(jnp.zeros((space - filled, LANES), F32))
    block = jnp.concatenate(pieces, axis=0).astype(BF16)
    for step, target in zip(partners(peers), out):
        target[: OUT_ARRAYS * tokens] = results[me ^ step, : OUT_ARRAYS * tokens]
        target[OUT_ARRAYS * tokens :] = block


def channel_step(packed, short_weights, tokens):
    peers = len(packed)
    seq_len = peers * tokens
    size = seq_len // PHASES
    forward, backward = dft_tables(seq_len)
    count = PIECES * short_weights.shape[0] * short_weights.shape[1]
    rows = OUT_ARRAYS * tokens + -(-count // TILE) * TILE
    return pl.pallas_call(
        functools.partial(channel_kernel, tokens, peers, 1.0 / math.sqrt(seq_len)),
        in_specs=[pl.BlockSpec(memory_space=pltpu.VMEM)] * (peers + 3),
        out_specs=[pl.BlockSpec(memory_space=pltpu.VMEM)] * peers,
        out_shape=[jax.ShapeDtypeStruct((rows, LANES), BF16)] * peers,
        scratch_shapes=[
            pltpu.VMEM((peers, IN_ARRAYS * tokens, LANES), BF16),
            pltpu.VMEM((peers, rows, LANES), BF16),
            pltpu.VMEM((PHASES, size, 3 * LANES), BF16),
            pltpu.VMEM((PHASES, 2 * size, 3 * LANES), F32),
            pltpu.VMEM((PHASES, 2 * size, 3 * LANES), BF16),
            pltpu.VMEM((PHASES, 2 * size, 3 * LANES), BF16),
            pltpu.VMEM((3, PHASES, size, LANES), F32),
        ],
        compiler_params=pltpu.CompilerParams(vmem_limit_bytes=40 * 1024 * 1024),
        name="channel_operator",
    )(*packed, short_weights, jnp.asarray(forward), jnp.asarray(backward))


def channel_shards(query_proj, key_proj, value_proj, cotangent, filter_taps, short_weights):
    peers = lax.axis_size("ctx")
    tokens = query_proj.shape[0]
    packed = pack((query_proj, key_proj, value_proj, cotangent, filter_taps), peers)
    result = channel_step(exchange(packed), short_weights, tokens)
    return tuple(unpack(exchange(result), tokens, short_weights.shape))


def from_behind(array, axis, by):
    peers = lax.axis_size(axis)
    pairs = [(i, i + by) for i in range(peers) if 0 <= i + by < peers]
    return lax.ppermute(array, axis, pairs)


def contract(form, left, right):
    return jnp.einsum(
        form, left, right, precision=lax.Precision.HIGHEST, preferred_element_type=jnp.float32
    )


def table_pair(rows, cols, period):
    row_ids = lax.broadcasted_iota(jnp.int32, (rows, cols), 0)
    col_ids = lax.broadcasted_iota(jnp.int32, (rows, cols), 1)
    angle = 2.0 * math.pi / period * (row_ids * col_ids % period).astype(jnp.float32)
    return (jnp.cos(angle), jnp.sin(angle))


def make_plan(seq_len):
    small_len = int(math.isqrt(2 * seq_len))
    while seq_len % small_len:
        small_len -= 1
    large_len = 2 * seq_len // small_len
    large_cos, large_sin = table_pair(large_len // 2, large_len, large_len)
    small_cos, small_sin = table_pair(small_len, small_len, small_len)
    twist_cos, twist_sin = table_pair(large_len, small_len, small_len * large_len)
    fwd_large = jnp.stack([large_cos, -large_sin], axis=1)
    fwd_small = jnp.stack([jnp.stack([small_cos, -small_sin]), jnp.stack([small_sin, small_cos])])
    inv_small = jnp.stack([jnp.stack([small_cos, small_sin]), jnp.stack([-small_sin, small_cos])])
    inv_large = jnp.stack([large_cos, -large_sin])
    return (small_len, large_len, fwd_large, fwd_small, inv_small, inv_large, twist_cos, twist_sin)


def forward_spec(signal, dft_plan):
    small_len, large_len, fwd_large, fwd_small, inv_small, inv_large, twist_cos, twist_sin = (
        dft_plan
    )
    cube = signal.reshape(signal.shape[0], large_len // 2, small_len)
    section_one = contract("cba,bpk->cpka", cube, fwd_large)
    real_one = section_one[:, 0]
    imag_one = section_one[:, 1]
    section_two = jnp.stack(
        [real_one * twist_cos + imag_one * twist_sin, imag_one * twist_cos - real_one * twist_sin],
        axis=1,
    )
    return contract("cpka,pqaj->cqkj", section_two, fwd_small)


def inverse_half(spec, dft_plan):
    small_len, large_len, fwd_large, fwd_small, inv_small, inv_large, twist_cos, twist_sin = (
        dft_plan
    )
    section_one = contract("cqkj,qpja->cpka", spec, inv_small)
    real_one = section_one[:, 0]
    imag_one = section_one[:, 1]
    section_two = jnp.stack(
        [real_one * twist_cos - imag_one * twist_sin, imag_one * twist_cos + real_one * twist_sin],
        axis=1,
    )
    signal = contract("cpka,pbk->cba", section_two, inv_large)
    return signal.reshape(signal.shape[0], -1) / float(small_len * large_len)


def complex_mul(left, right):
    left_real, left_imag = (left[:, 0], left[:, 1])
    right_real, right_imag = (right[:, 0], right[:, 1])
    return jnp.stack(
        [
            left_real * right_real - left_imag * right_imag,
            left_real * right_imag + left_imag * right_real,
        ],
        axis=1,
    )


def conj_mul(left, right):
    left_real, left_imag = (left[:, 0], left[:, 1])
    right_real, right_imag = (right[:, 0], right[:, 1])
    return jnp.stack(
        [
            left_real * right_real + left_imag * right_imag,
            left_real * right_imag - left_imag * right_real,
        ],
        axis=1,
    )


def conv_forward(prod_chan, filter_spec, dft_plan):
    prod_spec = forward_spec(prod_chan.astype(jnp.float32), dft_plan)
    conv_chan = inverse_half(complex_mul(prod_spec, filter_spec), dft_plan).astype(jnp.bfloat16)
    return (conv_chan, prod_spec)


def conv_backward(grad_chan, filter_spec, prod_spec, dft_plan, grad_scale):
    grad_spec = forward_spec(grad_chan.astype(jnp.float32), dft_plan)
    dconv_chan = inverse_half(conj_mul(filter_spec, grad_spec), dft_plan).astype(jnp.bfloat16)
    dfilter_chan = inverse_half(conj_mul(prod_spec, grad_spec), dft_plan) * grad_scale
    return (dconv_chan, dfilter_chan)


def receive_filter(filter_taps, dft_plan):
    filter_chan = lax.all_to_all(filter_taps.T, "ctx", split_axis=0, concat_axis=1, tiled=True)
    return forward_spec(filter_chan, dft_plan)


def return_filter(dfilter_chan):
    return (
        lax.all_to_all(
            dfilter_chan.astype(jnp.bfloat16), "ctx", split_axis=1, concat_axis=0, tiled=True
        )
        .astype(dfilter_chan.dtype)
        .T
    )


def causal_taps(extended, weights, length, axis):
    rim_rows = len(weights) - 1
    summed = weights[0] * lax.slice_in_dim(extended, rim_rows, rim_rows + length, axis=axis)
    for offset in range(1, len(weights)):
        summed = summed + weights[offset] * lax.slice_in_dim(
            extended, rim_rows - offset, rim_rows - offset + length, axis=axis
        )
    return summed


def reverse_taps(extended, weights, length, axis):
    summed = weights[0] * lax.slice_in_dim(extended, 0, length, axis=axis)
    for offset in range(1, len(weights)):
        summed = summed + weights[offset] * lax.slice_in_dim(
            extended, offset, offset + length, axis=axis
        )
    return summed


def tap_grads(grad_in, extended, tap_count, length, axis):
    rim_rows = tap_count - 1
    rows = [
        jnp.sum(
            grad_in
            * lax.slice_in_dim(extended, rim_rows - offset, rim_rows - offset + length, axis=axis),
            axis=axis,
        )
        for offset in range(tap_count)
    ]
    return jnp.stack(rows, axis=1)


def spread_shards(query_proj, key_proj, value_proj, cotangent, filter_taps, short_weights):
    tokens = query_proj.shape[0]
    tap_count = short_weights.shape[1]
    rim_rows = tap_count - 1
    seq_len = tokens * lax.axis_size("ctx")
    grad_scale = 1.0 / math.sqrt(seq_len)
    dft_plan = make_plan(seq_len)
    stacked = jnp.stack([query_proj, key_proj, value_proj])
    prev_rim = from_behind(stacked[:, tokens - rim_rows :], "ctx", 1)
    extended = jnp.concatenate([prev_rim, stacked], axis=1).astype(jnp.float32)
    weights = [short_weights[:, offset, None, :] for offset in range(tap_count)]
    short_out = causal_taps(extended, weights, tokens, 1)
    product = (short_out[1] * short_out[2]).astype(jnp.bfloat16)
    cot_wide = cotangent.astype(jnp.float32)
    gate_grad = (cot_wide * short_out[0]).astype(jnp.bfloat16)
    filter_spec = receive_filter(filter_taps, dft_plan)
    prod_chan = lax.all_to_all(product.T, "ctx", split_axis=0, concat_axis=1, tiled=True)
    conv_chan, prod_spec = conv_forward(prod_chan, filter_spec, dft_plan)
    conv_tok = lax.all_to_all(conv_chan, "ctx", split_axis=1, concat_axis=0, tiled=True)
    grad_chan = lax.all_to_all(gate_grad.T, "ctx", split_axis=0, concat_axis=1, tiled=True)
    dconv_chan, dfilter_chan = conv_backward(
        grad_chan, filter_spec, prod_spec, dft_plan, grad_scale
    )
    dconv_tok = lax.all_to_all(dconv_chan, "ctx", split_axis=1, concat_axis=0, tiled=True)
    filter_grad = return_filter(dfilter_chan)
    conv_wide = conv_tok.T.astype(jnp.float32)
    dconv_wide = dconv_tok.T.astype(jnp.float32)
    gated = (short_out[0] * conv_wide).astype(jnp.bfloat16)
    token_grads = jnp.stack(
        [cot_wide * conv_wide, dconv_wide * short_out[2], dconv_wide * short_out[1]]
    )
    next_rim = from_behind(token_grads[:, :rim_rows], "ctx", -1)
    grad_ext = jnp.concatenate([token_grads, next_rim], axis=1)
    inputs_grad = reverse_taps(grad_ext, weights, tokens, 1).astype(jnp.bfloat16)
    weight_part = tap_grads(token_grads, extended, tap_count, tokens, 1)
    short_grad = lax.psum(weight_part, "ctx") * grad_scale
    results = (gated, inputs_grad[0], inputs_grad[1], inputs_grad[2])
    return (results[0], results[1], results[2], results[3], filter_grad, short_grad)


def fits(query_proj, filter_taps):
    peers = lax.axis_size("ctx")
    tokens, width = query_proj.shape
    return (
        width == peers * LANES
        and peers.bit_count() == 1
        and tokens % (PHASES * TILE) == 0
        and peers * tokens <= 2048
    )


def shards(*arrays):
    return channel_shards(*arrays) if fits(arrays[0], arrays[4]) else spread_shards(*arrays)


def solution(mesh):
    placed = (
        P("ctx", "tp"),
        P("ctx", "tp"),
        P("ctx", "tp"),
        P("ctx", "tp"),
        P("ctx", "tp"),
        P(None, None, "tp"),
    )
    return jax.shard_map(
        shards,
        mesh=mesh,
        in_specs=placed,
        out_specs=(
            P("ctx", "tp"),
            P("ctx", "tp"),
            P("ctx", "tp"),
            P("ctx", "tp"),
            P("ctx", "tp"),
            P(None, None, "tp"),
        ),
        check_vma=False,
    )
```

```python
import functools
import math

import jax
import jax.numpy as jnp
import numpy as np
from jax import lax
from jax.experimental import pallas as pl
from jax.experimental.pallas import tpu as pltpu
from jax.sharding import PartitionSpec as P

F32 = jnp.float32
BF16 = jnp.bfloat16
LANES = 128
PHASES = 4
TILE = 16
PAD = 8
RIM = 2
PIECES = 3
VMEM_LIMIT = 24 * 1024 * 1024


def partners(peers):
    return [0] + list(range(peers - 1, 0, -1))


def exchange(blocks):
    peers = len(blocks)
    got = [blocks[0]]
    for step, block in list(zip(partners(peers), blocks))[1:]:
        got.append(lax.ppermute(block, "ctx", [(i, i ^ step) for i in range(peers)]))
    return got


def in_vmem(count):
    return [pl.BlockSpec(memory_space=pltpu.VMEM)] * count


def lanes_of(place):
    return pl.ds(pl.multiple_of(place * LANES, LANES), LANES)


def pack_kernel(count, *refs):
    sources, packed = refs[:count], refs[count:]
    tokens = sources[0].shape[0]
    me = lax.axis_index("ctx")
    for step, target in zip(partners(len(packed)), packed):
        for at, source in enumerate(sources):
            target[at * tokens : (at + 1) * tokens, :] = source[:, lanes_of(me ^ step)].astype(BF16)


def pack(name, arrays, peers):
    tokens = arrays[0].shape[0]
    return pl.pallas_call(
        functools.partial(pack_kernel, len(arrays)),
        in_specs=in_vmem(len(arrays)),
        out_specs=in_vmem(peers),
        out_shape=[jax.ShapeDtypeStruct((len(arrays) * tokens, LANES), BF16)] * peers,
        name=name,
    )(*arrays)


@functools.lru_cache(maxsize=None)
def dft_tables(seq_len):
    size = seq_len // PHASES
    k = np.arange(size, dtype=np.int64)[:, None]
    m = np.arange(size, dtype=np.int64)[None, :]
    forward = []
    for phase in range(PHASES):
        turns = ((4 * k + 1) * (PHASES * m + phase)) % (4 * seq_len)
        angle = 2.0 * np.pi / (4 * seq_len) * turns
        forward.append(np.concatenate([np.cos(angle), -np.sin(angle)], axis=0))
    forward = np.stack(forward)
    backward = np.swapaxes(forward, 1, 2) / seq_len

    def pieces(table):
        high = table.astype(BF16)
        low = (table - high.astype(np.float64)).astype(BF16)
        return np.stack([high, low], axis=1)

    return pieces(forward), pieces(backward)


def forward_mix(parts):
    (r0, i0), (r1, i1), (r2, i2), (r3, i3) = parts
    ar, ai, br, bi = r0 + r2, i0 + i2, r0 - r2, i0 - i2
    cr, ci, dr, di = r1 + r3, i1 + i3, r1 - r3, i1 - i3
    return ((ar + cr, ai + ci), (br + di, bi - dr), (ar - cr, ai - ci), (br - di, bi + dr))


def inverse_mix(parts):
    (r0, i0), (r1, i1), (r2, i2), (r3, i3) = parts
    ar, ai, br, bi = r0 + r2, i0 + i2, r0 - r2, i0 - i2
    cr, ci, dr, di = r1 + r3, i1 + i3, r1 - r3, i1 - i3
    return ((ar + cr, ai + ci), (br - di, bi + dr), (ar - cr, ai - ci), (br + di, bi - dr))


def times(left, right):
    return tuple(
        (lr * rr - li * ri, lr * ri + li * rr) for (lr, li), (rr, ri) in zip(left, right)
    )


def conj_times(left, right):
    return tuple(
        (lr * rr + li * ri, lr * ri - li * rr) for (lr, li), (rr, ri) in zip(left, right)
    )


def split_store(ref, r, rows, lanes, values):
    half = ref.shape[-1] // 2
    rounded = values.astype(BF16)
    ref[r, rows, lanes] = rounded
    ref[r, rows, slice(lanes.start + half, lanes.stop + half)] = (
        values - rounded.astype(F32)
    ).astype(BF16)


def forward_transform(forward, signal):
    return jnp.dot(forward[0], signal, preferred_element_type=F32) + jnp.dot(
        forward[1], signal, preferred_element_type=F32
    )


def inverse_transform(backward, pieces):
    half = pieces.shape[-1] // 2
    both = jnp.dot(backward[0], pieces, preferred_element_type=F32)
    rest = jnp.dot(backward[1], pieces[:, :half], preferred_element_type=F32)
    return both[:, :half] + both[:, half:] + rest


def phase(ref, r, size):
    return ref[pl.ds(r, size, stride=PHASES), :]


def short_phases(ref, weights, array, lanes, r, size):
    summed = weights[array, 0:1, lanes] * phase(ref, PAD + r, size)
    for tap in range(1, weights.shape[1]):
        summed = summed + weights[array, tap : tap + 1, lanes] * phase(ref, PAD + r - tap, size)
    return summed


def clear_ends(ref):
    ref[:PAD, :] = jnp.zeros((PAD, LANES), F32)
    ref[ref.shape[0] - PAD :, :] = jnp.zeros((PAD, LANES), F32)


def key_value_kernel(tokens, peers, *refs):
    arrived = refs[:peers]
    weights, forward_far, backward_far = refs[peers : peers + 3]
    key, value, key_short, value_short, prod_spec, filt_spec, conv = refs[peers + 3 : peers + 10]
    taps, forward, backward, signals, spectra, pieces, sems = refs[peers + 10 :]
    size = peers * tokens // PHASES
    me = lax.axis_index("ctx")
    own = lanes_of(me)
    get_forward = pltpu.make_async_copy(forward_far, forward, sems.at[0])
    get_backward = pltpu.make_async_copy(backward_far, backward, sems.at[1])
    get_forward.start()
    get_backward.start()
    for ref in (key, value, conv):
        clear_ends(ref)
    for step, source in zip(partners(peers), arrived):
        start = (me ^ step) * tokens
        inner = pl.ds(pl.multiple_of(PAD + start, PAD), tokens)
        key[inner, :] = source[:tokens, :].astype(F32)
        value[inner, :] = source[tokens : 2 * tokens, :].astype(F32)
        taps[pl.ds(pl.multiple_of(start, PAD), tokens), :] = source[2 * tokens :, :].astype(F32)
    for r in range(PHASES):
        key_short[r] = short_phases(key, weights, 1, own, r, size)
        value_short[r] = short_phases(value, weights, 2, own, r, size)
        signals[r, :, :LANES] = (key_short[r] * value_short[r]).astype(BF16)
        signals[r, :, LANES:] = phase(taps, r, size).astype(BF16)
    get_forward.wait()
    for r in range(PHASES):
        spectra[r] = forward_transform(forward[r], signals[r])
    for chunk in range(size // TILE):
        real = slice(chunk * TILE, (chunk + 1) * TILE)
        imag = slice(size + chunk * TILE, size + (chunk + 1) * TILE)
        mixed = []
        for at, target in enumerate((prod_spec, filt_spec)):
            lanes = slice(at * LANES, (at + 1) * LANES)
            spectrum = forward_mix(
                [(spectra[r, real, lanes], spectra[r, imag, lanes]) for r in range(PHASES)]
            )
            for q, pair in enumerate(spectrum):
                target[q, real, :], target[q, imag, :] = pair
            mixed.append(spectrum)
        for r, pair in enumerate(inverse_mix(times(*mixed))):
            for rows, part in zip((real, imag), pair):
                split_store(pieces, r, rows, slice(0, LANES), part)
    get_backward.wait()
    for r in range(PHASES):
        result = inverse_transform(backward[r], pieces[r])
        conv[pl.ds(PAD + r, size, stride=PHASES), :] = result.astype(BF16).astype(F32)


def key_value_step(arrived, short_weights, tables, tokens):
    peers = len(arrived)
    seq_len = peers * tokens
    size = seq_len // PHASES
    padded = jax.ShapeDtypeStruct((seq_len + 2 * PAD, LANES), F32)
    phases = jax.ShapeDtypeStruct((PHASES, size, LANES), F32)
    spectrum = jax.ShapeDtypeStruct((PHASES, 2 * size, LANES), F32)
    return pl.pallas_call(
        functools.partial(key_value_kernel, tokens, peers),
        in_specs=in_vmem(peers + 1) + [pl.BlockSpec(memory_space=pltpu.HBM)] * 2,
        out_specs=in_vmem(7),
        out_shape=[padded, padded, phases, phases, spectrum, spectrum, padded],
        scratch_shapes=[
            pltpu.VMEM((seq_len, LANES), F32),
            pltpu.VMEM(tables[0].shape, BF16),
            pltpu.VMEM(tables[1].shape, BF16),
            pltpu.VMEM((PHASES, size, 2 * LANES), BF16),
            pltpu.VMEM((PHASES, 2 * size, 2 * LANES), F32),
            pltpu.VMEM((PHASES, 2 * size, 2 * LANES), BF16),
            pltpu.SemaphoreType.DMA((2,)),
        ],
        compiler_params=pltpu.CompilerParams(vmem_limit_bytes=VMEM_LIMIT),
        cost_estimate=pl.CostEstimate(
            flops=2 * 24 * PHASES * size * size * LANES,
            bytes_accessed=8 * 1024 * 1024,
            transcendentals=0,
        ),
        name="key_value_channels",
    )(*arrived, short_weights, *tables)


def extra_rows(short_weights):
    sums = PIECES * short_weights.shape[0] * short_weights.shape[1]
    return sums, -(-(sums + 8 * RIM) // TILE) * TILE


def gradient_kernel(tokens, peers, grad_scale, *refs):
    arrived = refs[:peers]
    weights, forward_far, backward_far = refs[peers : peers + 3]
    key, value, key_short, value_short, prod_spec, filt_spec, conv = refs[peers + 3 : peers + 10]
    out = refs[peers + 10 : 2 * peers + 10]
    (
        query,
        cot,
        conv_grad,
        filter_grad,
        forward,
        backward,
        signals,
        spectra,
        pieces,
        extra,
        sems,
    ) = refs[2 * peers + 10 :]
    size = peers * tokens // PHASES
    tap_count = weights.shape[1]
    me = lax.axis_index("ctx")
    own = lanes_of(me)
    get_forward = pltpu.make_async_copy(forward_far, forward, sems.at[0])
    get_backward = pltpu.make_async_copy(backward_far, backward, sems.at[1])
    get_forward.start()
    get_backward.start()
    for ref in (query, cot, conv_grad):
        clear_ends(ref)
    for step, source in zip(partners(peers), arrived):
        inner = pl.ds(pl.multiple_of(PAD + (me ^ step) * tokens, PAD), tokens)
        query[inner, :] = source[:tokens, :].astype(F32)
        cot[inner, :] = source[tokens:, :].astype(F32)
    for r in range(PHASES):
        query_short = short_phases(query, weights, 0, own, r, size)
        signals[r] = (phase(cot, PAD + r, size) * query_short).astype(BF16)
    get_forward.wait()
    for r in range(PHASES):
        spectra[r] = forward_transform(forward[r], signals[r])
    for chunk in range(size // TILE):
        real = slice(chunk * TILE, (chunk + 1) * TILE)
        imag = slice(size + chunk * TILE, size + (chunk + 1) * TILE)
        grad = forward_mix([(spectra[r, real, :], spectra[r, imag, :]) for r in range(PHASES)])
        for at, other in enumerate((filt_spec, prod_spec)):
            known = [(other[q, real, :], other[q, imag, :]) for q in range(PHASES)]
            for r, pair in enumerate(inverse_mix(conj_times(known, grad))):
                for rows, part in zip((real, imag), pair):
                    split_store(pieces, r, rows, slice(at * LANES, (at + 1) * LANES), part)
    get_backward.wait()
    for r in range(PHASES):
        result = inverse_transform(backward[r], pieces[r])
        conv_grad[pl.ds(PAD + r, size, stride=PHASES), :] = (
            result[:, :LANES].astype(BF16).astype(F32)
        )
        filter_grad[pl.ds(r, size, stride=PHASES), :] = result[:, LANES:] * grad_scale

    sums = []
    for array, signal in enumerate((query, key, value)):
        totals = [None] * tap_count
        for r in range(PHASES):
            if array == 0:
                pre = phase(cot, PAD + r, size) * phase(conv, PAD + r, size)
            else:
                pre = phase(conv_grad, PAD + r, size) * (value_short, key_short)[array - 1][r]
            for tap in range(tap_count):
                term = pre * phase(signal, PAD + r - tap, size)
                term = jnp.sum(term.reshape(size // 8, 8, LANES), axis=0)
                totals[tap] = term if r == 0 else totals[tap] + term
        sums.extend(jnp.sum(total, axis=0, keepdims=True) for total in totals)
    rest = jnp.concatenate(sums, axis=0) * grad_scale
    extra[...] = jnp.zeros_like(extra)
    for piece in range(PIECES):
        rounded = rest.astype(BF16).astype(F32)
        extra[piece * len(sums) : (piece + 1) * len(sums), :] = rounded
        rest = rest - rounded
    for step, target in zip(partners(peers), out):
        start = (me ^ step) * tokens
        inner = pl.ds(pl.multiple_of(PAD + start, PAD), tokens)
        target[:tokens, :] = conv[inner, :].astype(BF16)
        target[tokens : 2 * tokens, :] = conv_grad[inner, :].astype(BF16)
        target[2 * tokens : 3 * tokens, :] = filter_grad[
            pl.ds(pl.multiple_of(start, PAD), tokens), :
        ].astype(BF16)
        before = pl.ds(pl.multiple_of(start, PAD), PAD)
        after = pl.ds(pl.multiple_of(PAD + start + tokens, PAD), PAD)
        at = PIECES * len(sums)
        for ref in (query, key, value):
            extra[at : at + RIM, :] = ref[before, :][PAD - RIM :]
            at += RIM
        for ref in (cot, conv, conv_grad, key, value):
            extra[at : at + RIM, :] = ref[after, :][:RIM]
            at += RIM
        target[3 * tokens :, :] = extra[...].astype(BF16)


def gradient_step(arrived, short_weights, tables, known, tokens):
    peers = len(arrived)
    seq_len = peers * tokens
    size = seq_len // PHASES
    extra = extra_rows(short_weights)[1]
    return pl.pallas_call(
        functools.partial(gradient_kernel, tokens, peers, 1.0 / math.sqrt(seq_len)),
        in_specs=in_vmem(peers + 1) + [pl.BlockSpec(memory_space=pltpu.HBM)] * 2 + in_vmem(7),
        out_specs=in_vmem(peers),
        out_shape=[jax.ShapeDtypeStruct((3 * tokens + extra, LANES), BF16)] * peers,
        scratch_shapes=[
            pltpu.VMEM((seq_len + 2 * PAD, LANES), F32),
            pltpu.VMEM((seq_len + 2 * PAD, LANES), F32),
            pltpu.VMEM((seq_len + 2 * PAD, LANES), F32),
            pltpu.VMEM((seq_len, LANES), F32),
            pltpu.VMEM(tables[0].shape, BF16),
            pltpu.VMEM(tables[1].shape, BF16),
            pltpu.VMEM((PHASES, size, LANES), BF16),
            pltpu.VMEM((PHASES, 2 * size, LANES), F32),
            pltpu.VMEM((PHASES, 2 * size, 4 * LANES), BF16),
            pltpu.VMEM((extra, LANES), F32),
            pltpu.SemaphoreType.DMA((2,)),
        ],
        compiler_params=pltpu.CompilerParams(vmem_limit_bytes=VMEM_LIMIT),
        name="gradient_channels",
    )(*arrived, short_weights, *tables, *known)


def token_kernel(peers, sum_rows, *refs):
    arrived = refs[:peers]
    query, key, value, cot, weights = refs[peers : peers + 5]
    gated, query_grad, key_grad, value_grad, filter_grad, short_grad = refs[peers + 5 : peers + 11]
    longer, pre = refs[peers + 11 :]
    tokens = query.shape[0]
    tap_count = weights.shape[1]
    count = sum_rows // PIECES
    me = lax.axis_index("ctx")
    for step, source in zip(partners(peers), arrived):
        lanes = lanes_of(me ^ step)
        extra = source[3 * tokens :, :].astype(F32)

        def rim(at):
            return extra[sum_rows + at * RIM : sum_rows + (at + 1) * RIM]

        def short(array, signal, after, rows):
            longer[array, PAD - RIM : PAD, :] = rim(array)
            longer[array, PAD : PAD + tokens, :] = signal[:, lanes].astype(F32)
            if after is not None:
                longer[array, PAD + tokens : PAD + tokens + RIM, :] = rim(after)
            summed = weights[array, 0:1, lanes] * longer[array, PAD : PAD + rows, :]
            for tap in range(1, tap_count):
                summed = (
                    summed
                    + weights[array, tap : tap + 1, lanes]
                    * longer[array, PAD - tap : PAD - tap + rows, :]
                )
            return summed

        def taps_back(array, target):
            summed = weights[array, 0:1, lanes] * pre[array, :tokens, :]
            for tap in range(1, tap_count):
                summed = (
                    summed
                    + weights[array, tap : tap + 1, lanes] * pre[array, tap : tap + tokens, :]
                )
            target[:, lanes] = summed.astype(BF16)

        conv = source[:tokens, :].astype(F32)
        gated[:, lanes] = (short(0, query, None, tokens) * conv).astype(BF16)
        pre[0, :tokens, :] = cot[:, lanes].astype(F32) * conv
        pre[0, tokens : tokens + RIM, :] = rim(3) * rim(4)
        taps_back(0, query_grad)
        key_short = short(1, key, 6, tokens + PAD)
        value_short = short(2, value, 7, tokens + PAD)
        conv_grad = source[tokens : 2 * tokens, :].astype(F32)
        for array, other in ((1, value_short), (2, key_short)):
            pre[array, :tokens, :] = conv_grad * other[:tokens]
            pre[array, tokens : tokens + RIM, :] = rim(5) * other[tokens : tokens + RIM]
        taps_back(1, key_grad)
        taps_back(2, value_grad)
        filter_grad[:, lanes] = source[2 * tokens : 3 * tokens, :].astype(F32)
        whole = extra[:count]
        for piece in range(1, PIECES):
            whole = whole + extra[piece * count : (piece + 1) * count]
        for row in range(count):
            which, tap = divmod(row, tap_count)
            short_grad[which, tap : tap + 1, lanes] = whole[row : row + 1]


def token_step(arrived, query, key, value, cot, short_weights):
    peers = len(arrived)
    tokens, width = query.shape
    wide = jax.ShapeDtypeStruct((tokens, width), BF16)
    return pl.pallas_call(
        functools.partial(token_kernel, peers, extra_rows(short_weights)[0]),
        in_specs=in_vmem(peers + 5),
        out_specs=in_vmem(6),
        out_shape=[wide] * 4
        + [
            jax.ShapeDtypeStruct((tokens, width), F32),
            jax.ShapeDtypeStruct(short_weights.shape, F32),
        ],
        scratch_shapes=[
            pltpu.VMEM((3, tokens + 2 * PAD, LANES), F32),
            pltpu.VMEM((3, tokens + PAD, LANES), F32),
        ],
        compiler_params=pltpu.CompilerParams(vmem_limit_bytes=VMEM_LIMIT),
        name="token_outputs",
    )(*arrived, query, key, value, cot, short_weights)


def channel_shards(query_proj, key_proj, value_proj, cotangent, filter_taps, short_weights):
    peers = lax.axis_size("ctx")
    tokens = query_proj.shape[0]
    tables = [jnp.asarray(table) for table in dft_tables(peers * tokens)]
    first = exchange(pack("pack_key_value_taps", (key_proj, value_proj, filter_taps), peers))
    second = exchange(pack("pack_query_cot", (query_proj, cotangent), peers))
    known = key_value_step(first, short_weights, tables, tokens)
    back = exchange(gradient_step(second, short_weights, tables, known, tokens))
    return tuple(token_step(back, query_proj, key_proj, value_proj, cotangent, short_weights))


def from_behind(array, axis, by):
    peers = lax.axis_size(axis)
    pairs = [(i, i + by) for i in range(peers) if 0 <= i + by < peers]
    return lax.ppermute(array, axis, pairs)


def contract(form, left, right):
    return jnp.einsum(
        form, left, right, precision=lax.Precision.HIGHEST, preferred_element_type=jnp.float32
    )


def table_pair(rows, cols, period):
    row_ids = lax.broadcasted_iota(jnp.int32, (rows, cols), 0)
    col_ids = lax.broadcasted_iota(jnp.int32, (rows, cols), 1)
    angle = 2.0 * math.pi / period * (row_ids * col_ids % period).astype(jnp.float32)
    return (jnp.cos(angle), jnp.sin(angle))


def make_plan(seq_len):
    small_len = int(math.isqrt(2 * seq_len))
    while seq_len % small_len:
        small_len -= 1
    large_len = 2 * seq_len // small_len
    large_cos, large_sin = table_pair(large_len // 2, large_len, large_len)
    small_cos, small_sin = table_pair(small_len, small_len, small_len)
    twist_cos, twist_sin = table_pair(large_len, small_len, small_len * large_len)
    fwd_large = jnp.stack([large_cos, -large_sin], axis=1)
    fwd_small = jnp.stack([jnp.stack([small_cos, -small_sin]), jnp.stack([small_sin, small_cos])])
    inv_small = jnp.stack([jnp.stack([small_cos, small_sin]), jnp.stack([-small_sin, small_cos])])
    inv_large = jnp.stack([large_cos, -large_sin])
    return (small_len, large_len, fwd_large, fwd_small, inv_small, inv_large, twist_cos, twist_sin)


def forward_spec(signal, dft_plan):
    small_len, large_len, fwd_large, fwd_small, inv_small, inv_large, twist_cos, twist_sin = (
        dft_plan
    )
    cube = signal.reshape(signal.shape[0], large_len // 2, small_len)
    section_one = contract("cba,bpk->cpka", cube, fwd_large)
    real_one = section_one[:, 0]
    imag_one = section_one[:, 1]
    section_two = jnp.stack(
        [real_one * twist_cos + imag_one * twist_sin, imag_one * twist_cos - real_one * twist_sin],
        axis=1,
    )
    return contract("cpka,pqaj->cqkj", section_two, fwd_small)


def inverse_half(spec, dft_plan):
    small_len, large_len, fwd_large, fwd_small, inv_small, inv_large, twist_cos, twist_sin = (
        dft_plan
    )
    section_one = contract("cqkj,qpja->cpka", spec, inv_small)
    real_one = section_one[:, 0]
    imag_one = section_one[:, 1]
    section_two = jnp.stack(
        [real_one * twist_cos - imag_one * twist_sin, imag_one * twist_cos + real_one * twist_sin],
        axis=1,
    )
    signal = contract("cpka,pbk->cba", section_two, inv_large)
    return signal.reshape(signal.shape[0], -1) / float(small_len * large_len)


def complex_mul(left, right):
    left_real, left_imag = (left[:, 0], left[:, 1])
    right_real, right_imag = (right[:, 0], right[:, 1])
    return jnp.stack(
        [
            left_real * right_real - left_imag * right_imag,
            left_real * right_imag + left_imag * right_real,
        ],
        axis=1,
    )


def conj_mul(left, right):
    left_real, left_imag = (left[:, 0], left[:, 1])
    right_real, right_imag = (right[:, 0], right[:, 1])
    return jnp.stack(
        [
            left_real * right_real + left_imag * right_imag,
            left_real * right_imag - left_imag * right_real,
        ],
        axis=1,
    )


def conv_forward(prod_chan, filter_spec, dft_plan):
    prod_spec = forward_spec(prod_chan.astype(jnp.float32), dft_plan)
    conv_chan = inverse_half(complex_mul(prod_spec, filter_spec), dft_plan).astype(jnp.bfloat16)
    return (conv_chan, prod_spec)


def conv_backward(grad_chan, filter_spec, prod_spec, dft_plan, grad_scale):
    grad_spec = forward_spec(grad_chan.astype(jnp.float32), dft_plan)
    dconv_chan = inverse_half(conj_mul(filter_spec, grad_spec), dft_plan).astype(jnp.bfloat16)
    dfilter_chan = inverse_half(conj_mul(prod_spec, grad_spec), dft_plan) * grad_scale
    return (dconv_chan, dfilter_chan)


def receive_filter(filter_taps, dft_plan):
    filter_chan = lax.all_to_all(filter_taps.T, "ctx", split_axis=0, concat_axis=1, tiled=True)
    return forward_spec(filter_chan, dft_plan)


def return_filter(dfilter_chan):
    return (
        lax.all_to_all(
            dfilter_chan.astype(jnp.bfloat16), "ctx", split_axis=1, concat_axis=0, tiled=True
        )
        .astype(dfilter_chan.dtype)
        .T
    )


def causal_taps(extended, weights, length, axis):
    rim_rows = len(weights) - 1
    summed = weights[0] * lax.slice_in_dim(extended, rim_rows, rim_rows + length, axis=axis)
    for offset in range(1, len(weights)):
        summed = summed + weights[offset] * lax.slice_in_dim(
            extended, rim_rows - offset, rim_rows - offset + length, axis=axis
        )
    return summed


def reverse_taps(extended, weights, length, axis):
    summed = weights[0] * lax.slice_in_dim(extended, 0, length, axis=axis)
    for offset in range(1, len(weights)):
        summed = summed + weights[offset] * lax.slice_in_dim(
            extended, offset, offset + length, axis=axis
        )
    return summed


def tap_grads(grad_in, extended, tap_count, length, axis):
    rim_rows = tap_count - 1
    rows = [
        jnp.sum(
            grad_in
            * lax.slice_in_dim(extended, rim_rows - offset, rim_rows - offset + length, axis=axis),
            axis=axis,
        )
        for offset in range(tap_count)
    ]
    return jnp.stack(rows, axis=1)


def spread_shards(query_proj, key_proj, value_proj, cotangent, filter_taps, short_weights):
    tokens = query_proj.shape[0]
    tap_count = short_weights.shape[1]
    rim_rows = tap_count - 1
    seq_len = tokens * lax.axis_size("ctx")
    grad_scale = 1.0 / math.sqrt(seq_len)
    dft_plan = make_plan(seq_len)
    stacked = jnp.stack([query_proj, key_proj, value_proj])
    prev_rim = from_behind(stacked[:, tokens - rim_rows :], "ctx", 1)
    extended = jnp.concatenate([prev_rim, stacked], axis=1).astype(jnp.float32)
    weights = [short_weights[:, offset, None, :] for offset in range(tap_count)]
    short_out = causal_taps(extended, weights, tokens, 1)
    product = (short_out[1] * short_out[2]).astype(jnp.bfloat16)
    cot_wide = cotangent.astype(jnp.float32)
    gate_grad = (cot_wide * short_out[0]).astype(jnp.bfloat16)
    filter_spec = receive_filter(filter_taps, dft_plan)
    prod_chan = lax.all_to_all(product.T, "ctx", split_axis=0, concat_axis=1, tiled=True)
    conv_chan, prod_spec = conv_forward(prod_chan, filter_spec, dft_plan)
    conv_tok = lax.all_to_all(conv_chan, "ctx", split_axis=1, concat_axis=0, tiled=True)
    grad_chan = lax.all_to_all(gate_grad.T, "ctx", split_axis=0, concat_axis=1, tiled=True)
    dconv_chan, dfilter_chan = conv_backward(
        grad_chan, filter_spec, prod_spec, dft_plan, grad_scale
    )
    dconv_tok = lax.all_to_all(dconv_chan, "ctx", split_axis=1, concat_axis=0, tiled=True)
    filter_grad = return_filter(dfilter_chan)
    conv_wide = conv_tok.T.astype(jnp.float32)
    dconv_wide = dconv_tok.T.astype(jnp.float32)
    gated = (short_out[0] * conv_wide).astype(jnp.bfloat16)
    token_grads = jnp.stack(
        [cot_wide * conv_wide, dconv_wide * short_out[2], dconv_wide * short_out[1]]
    )
    next_rim = from_behind(token_grads[:, :rim_rows], "ctx", -1)
    grad_ext = jnp.concatenate([token_grads, next_rim], axis=1)
    inputs_grad = reverse_taps(grad_ext, weights, tokens, 1).astype(jnp.bfloat16)
    weight_part = tap_grads(token_grads, extended, tap_count, tokens, 1)
    short_grad = lax.psum(weight_part, "ctx") * grad_scale
    results = (gated, inputs_grad[0], inputs_grad[1], inputs_grad[2])
    return (results[0], results[1], results[2], results[3], filter_grad, short_grad)


def fits(query_proj, short_weights):
    peers = lax.axis_size("ctx")
    tokens, width = query_proj.shape
    tap_count = short_weights.shape[1]
    return (
        width == peers * LANES
        and peers.bit_count() == 1
        and tokens % (PHASES * TILE) == 0
        and tap_count == RIM + 1
        and peers * tokens <= 2048
    )


def shards(*arrays):
    return channel_shards(*arrays) if fits(arrays[0], arrays[5]) else spread_shards(*arrays)


def solution(mesh):
    placed = (
        P("ctx", "tp"),
        P("ctx", "tp"),
        P("ctx", "tp"),
        P("ctx", "tp"),
        P("ctx", "tp"),
        P(None, None, "tp"),
    )
    return jax.shard_map(
        shards,
        mesh=mesh,
        in_specs=placed,
        out_specs=(
            P("ctx", "tp"),
            P("ctx", "tp"),
            P("ctx", "tp"),
            P("ctx", "tp"),
            P("ctx", "tp"),
            P(None, None, "tp"),
        ),
        check_vma=False,
    )
```

```python
import functools
import math

import jax
import jax.numpy as jnp
import numpy as np
from jax import lax
from jax.experimental import pallas as pl
from jax.experimental.pallas import tpu as pltpu
from jax.sharding import PartitionSpec as P

F32 = jnp.float32
BF16 = jnp.bfloat16
LANES = 128
PHASES = 4
TILE = 16
PAD = 8
RIM = 2
PIECES = 3
MIB = 1024 * 1024
VMEM_LIMIT = 24 * MIB


def partners(peers):
    return [0] + list(range(peers - 1, 0, -1))


def exchange(blocks):
    peers = len(blocks)
    got = [blocks[0]]
    for step, block in list(zip(partners(peers), blocks))[1:]:
        got.append(lax.ppermute(block, "ctx", [(i, i ^ step) for i in range(peers)]))
    return got


def in_vmem(count):
    return [pl.BlockSpec(memory_space=pltpu.VMEM)] * count


def lanes_of(place):
    return pl.ds(pl.multiple_of(place * LANES, LANES), LANES)


def pack_kernel(count, waits, *refs):
    sources, packed = refs[:count], refs[count + waits :]
    tokens = sources[0].shape[0]
    me = lax.axis_index("ctx")
    for step, target in zip(partners(len(packed)), packed):
        for at, source in enumerate(sources):
            target[at * tokens : (at + 1) * tokens, :] = source[:, lanes_of(me ^ step)].astype(BF16)


def pack(name, arrays, peers, after=()):
    tokens = arrays[0].shape[0]
    return pl.pallas_call(
        functools.partial(pack_kernel, len(arrays), len(after)),
        in_specs=in_vmem(len(arrays)) + [pl.BlockSpec(memory_space=pl.ANY)] * len(after),
        out_specs=in_vmem(peers),
        out_shape=[jax.ShapeDtypeStruct((len(arrays) * tokens, LANES), BF16)] * peers,
        cost_estimate=pl.CostEstimate(flops=0, bytes_accessed=8 * MIB, transcendentals=0),
        name=name,
    )(*arrays, *after)


@functools.lru_cache(maxsize=None)
def dft_tables(seq_len):
    size = seq_len // PHASES
    k = np.arange(size, dtype=np.int64)[:, None]
    m = np.arange(size, dtype=np.int64)[None, :]
    forward = []
    for phase in range(PHASES):
        turns = ((4 * k + 1) * (PHASES * m + phase)) % (4 * seq_len)
        angle = 2.0 * np.pi / (4 * seq_len) * turns
        forward.append(np.concatenate([np.cos(angle), -np.sin(angle)], axis=0))
    forward = np.stack(forward)
    backward = np.swapaxes(forward, 1, 2) / seq_len

    def pieces(table):
        high = table.astype(BF16)
        low = (table - high.astype(np.float64)).astype(BF16)
        return np.stack([high, low], axis=1)

    return pieces(forward), pieces(backward)


def forward_mix(parts):
    (r0, i0), (r1, i1), (r2, i2), (r3, i3) = parts
    ar, ai, br, bi = r0 + r2, i0 + i2, r0 - r2, i0 - i2
    cr, ci, dr, di = r1 + r3, i1 + i3, r1 - r3, i1 - i3
    return ((ar + cr, ai + ci), (br + di, bi - dr), (ar - cr, ai - ci), (br - di, bi + dr))


def inverse_mix(parts):
    (r0, i0), (r1, i1), (r2, i2), (r3, i3) = parts
    ar, ai, br, bi = r0 + r2, i0 + i2, r0 - r2, i0 - i2
    cr, ci, dr, di = r1 + r3, i1 + i3, r1 - r3, i1 - i3
    return ((ar + cr, ai + ci), (br - di, bi + dr), (ar - cr, ai - ci), (br + di, bi - dr))


def times(left, right):
    return tuple(
        (lr * rr - li * ri, lr * ri + li * rr) for (lr, li), (rr, ri) in zip(left, right)
    )


def conj_times(left, right):
    return tuple(
        (lr * rr + li * ri, lr * ri - li * rr) for (lr, li), (rr, ri) in zip(left, right)
    )


def split_store(ref, r, rows, lanes, values):
    half = ref.shape[-1] // 2
    rounded = values.astype(BF16)
    ref[r, rows, lanes] = rounded
    ref[r, rows, slice(lanes.start + half, lanes.stop + half)] = (
        values - rounded.astype(F32)
    ).astype(BF16)


def forward_transform(forward, signal):
    return jnp.dot(forward[0], signal, preferred_element_type=F32) + jnp.dot(
        forward[1], signal, preferred_element_type=F32
    )


def inverse_transform(backward, pieces):
    half = pieces.shape[-1] // 2
    both = jnp.dot(backward[0], pieces, preferred_element_type=F32)
    rest = jnp.dot(backward[1], pieces[:, :half], preferred_element_type=F32)
    return both[:, :half] + both[:, half:] + rest


def phase(ref, r, size):
    return ref[pl.ds(r, size, stride=PHASES), :]


def short_phases(ref, weights, array, lanes, r, size):
    summed = weights[array, 0:1, lanes] * phase(ref, PAD + r, size)
    for tap in range(1, weights.shape[1]):
        summed = summed + weights[array, tap : tap + 1, lanes] * phase(ref, PAD + r - tap, size)
    return summed


def clear_ends(ref):
    ref[:PAD, :] = jnp.zeros((PAD, LANES), F32)
    ref[ref.shape[0] - PAD :, :] = jnp.zeros((PAD, LANES), F32)


def key_value_kernel(tokens, peers, *refs):
    arrived = refs[:peers]
    weights, forward, backward = refs[peers : peers + 3]
    key, value, key_short, value_short, prod_spec, filt_spec, conv = refs[peers + 3 : peers + 10]
    taps, signals, spectra, pieces = refs[peers + 10 :]
    size = peers * tokens // PHASES
    me = lax.axis_index("ctx")
    own = lanes_of(me)
    for ref in (key, value, conv):
        clear_ends(ref)
    for step, source in zip(partners(peers), arrived):
        start = (me ^ step) * tokens
        inner = pl.ds(pl.multiple_of(PAD + start, PAD), tokens)
        key[inner, :] = source[:tokens, :].astype(F32)
        value[inner, :] = source[tokens : 2 * tokens, :].astype(F32)
        taps[pl.ds(pl.multiple_of(start, PAD), tokens), :] = source[2 * tokens :, :].astype(F32)
    for r in range(PHASES):
        key_short[r] = short_phases(key, weights, 1, own, r, size)
        value_short[r] = short_phases(value, weights, 2, own, r, size)
        signals[r, :, :LANES] = (key_short[r] * value_short[r]).astype(BF16)
        signals[r, :, LANES:] = phase(taps, r, size).astype(BF16)
    for r in range(PHASES):
        spectra[r] = forward_transform(forward[r], signals[r])
    for chunk in range(size // TILE):
        real = slice(chunk * TILE, (chunk + 1) * TILE)
        imag = slice(size + chunk * TILE, size + (chunk + 1) * TILE)
        mixed = []
        for at, target in enumerate((prod_spec, filt_spec)):
            lanes = slice(at * LANES, (at + 1) * LANES)
            spectrum = forward_mix(
                [(spectra[r, real, lanes], spectra[r, imag, lanes]) for r in range(PHASES)]
            )
            for q, pair in enumerate(spectrum):
                target[q, real, :], target[q, imag, :] = pair
            mixed.append(spectrum)
        for r, pair in enumerate(inverse_mix(times(*mixed))):
            for rows, part in zip((real, imag), pair):
                split_store(pieces, r, rows, slice(0, LANES), part)
    for r in range(PHASES):
        result = inverse_transform(backward[r], pieces[r])
        conv[pl.ds(PAD + r, size, stride=PHASES), :] = result.astype(BF16).astype(F32)


def key_value_step(arrived, short_weights, tables, tokens):
    peers = len(arrived)
    seq_len = peers * tokens
    size = seq_len // PHASES
    padded = jax.ShapeDtypeStruct((seq_len + 2 * PAD, LANES), F32)
    phases = jax.ShapeDtypeStruct((PHASES, size, LANES), F32)
    spectrum = jax.ShapeDtypeStruct((PHASES, 2 * size, LANES), F32)
    return pl.pallas_call(
        functools.partial(key_value_kernel, tokens, peers),
        in_specs=in_vmem(peers + 3),
        out_specs=in_vmem(7),
        out_shape=[padded, padded, phases, phases, spectrum, spectrum, padded],
        scratch_shapes=[
            pltpu.VMEM((seq_len, LANES), F32),
            pltpu.VMEM((PHASES, size, 2 * LANES), BF16),
            pltpu.VMEM((PHASES, 2 * size, 2 * LANES), F32),
            pltpu.VMEM((PHASES, 2 * size, 2 * LANES), BF16),
        ],
        compiler_params=pltpu.CompilerParams(vmem_limit_bytes=VMEM_LIMIT),
        cost_estimate=pl.CostEstimate(
            flops=2 * 24 * PHASES * size * size * LANES,
            bytes_accessed=8 * MIB,
            transcendentals=0,
        ),
        name="key_value_channels",
    )(*arrived, short_weights, *tables)


def extra_rows(short_weights):
    sums = PIECES * short_weights.shape[0] * short_weights.shape[1]
    return sums, -(-(sums + 8 * RIM) // TILE) * TILE


def gradient_kernel(tokens, peers, grad_scale, *refs):
    arrived = refs[:peers]
    weights, forward, backward = refs[peers : peers + 3]
    key, value, key_short, value_short, prod_spec, filt_spec, conv = refs[peers + 3 : peers + 10]
    out = refs[peers + 10 : 2 * peers + 10]
    (
        query,
        cot,
        conv_grad,
        filter_grad,
        signals,
        spectra,
        pieces,
        extra,
    ) = refs[2 * peers + 10 :]
    size = peers * tokens // PHASES
    tap_count = weights.shape[1]
    me = lax.axis_index("ctx")
    own = lanes_of(me)
    for ref in (query, cot, conv_grad):
        clear_ends(ref)
    for step, source in zip(partners(peers), arrived):
        inner = pl.ds(pl.multiple_of(PAD + (me ^ step) * tokens, PAD), tokens)
        query[inner, :] = source[:tokens, :].astype(F32)
        cot[inner, :] = source[tokens:, :].astype(F32)
    for r in range(PHASES):
        query_short = short_phases(query, weights, 0, own, r, size)
        signals[r] = (phase(cot, PAD + r, size) * query_short).astype(BF16)
    for r in range(PHASES):
        spectra[r] = forward_transform(forward[r], signals[r])
    for chunk in range(size // TILE):
        real = slice(chunk * TILE, (chunk + 1) * TILE)
        imag = slice(size + chunk * TILE, size + (chunk + 1) * TILE)
        grad = forward_mix([(spectra[r, real, :], spectra[r, imag, :]) for r in range(PHASES)])
        for at, other in enumerate((filt_spec, prod_spec)):
            known = [(other[q, real, :], other[q, imag, :]) for q in range(PHASES)]
            for r, pair in enumerate(inverse_mix(conj_times(known, grad))):
                for rows, part in zip((real, imag), pair):
                    split_store(pieces, r, rows, slice(at * LANES, (at + 1) * LANES), part)
    for r in range(PHASES):
        result = inverse_transform(backward[r], pieces[r])
        conv_grad[pl.ds(PAD + r, size, stride=PHASES), :] = (
            result[:, :LANES].astype(BF16).astype(F32)
        )
        filter_grad[pl.ds(r, size, stride=PHASES), :] = result[:, LANES:] * grad_scale

    sums = []
    for array, signal in enumerate((query, key, value)):
        totals = [None] * tap_count
        for r in range(PHASES):
            if array == 0:
                pre = phase(cot, PAD + r, size) * phase(conv, PAD + r, size)
            else:
                pre = phase(conv_grad, PAD + r, size) * (value_short, key_short)[array - 1][r]
            for tap in range(tap_count):
                term = pre * phase(signal, PAD + r - tap, size)
                term = jnp.sum(term.reshape(size // 8, 8, LANES), axis=0)
                totals[tap] = term if r == 0 else totals[tap] + term
        sums.extend(jnp.sum(total, axis=0, keepdims=True) for total in totals)
    rest = jnp.concatenate(sums, axis=0) * grad_scale
    extra[...] = jnp.zeros_like(extra)
    for piece in range(PIECES):
        rounded = rest.astype(BF16).astype(F32)
        extra[piece * len(sums) : (piece + 1) * len(sums), :] = rounded
        rest = rest - rounded
    for step, target in zip(partners(peers), out):
        start = (me ^ step) * tokens
        inner = pl.ds(pl.multiple_of(PAD + start, PAD), tokens)
        target[:tokens, :] = conv[inner, :].astype(BF16)
        target[tokens : 2 * tokens, :] = conv_grad[inner, :].astype(BF16)
        target[2 * tokens : 3 * tokens, :] = filter_grad[
            pl.ds(pl.multiple_of(start, PAD), tokens), :
        ].astype(BF16)
        before = pl.ds(pl.multiple_of(start, PAD), PAD)
        after = pl.ds(pl.multiple_of(PAD + start + tokens, PAD), PAD)
        at = PIECES * len(sums)
        for ref in (query, key, value):
            extra[at : at + RIM, :] = ref[before, :][PAD - RIM :]
            at += RIM
        for ref in (cot, conv, conv_grad, key, value):
            extra[at : at + RIM, :] = ref[after, :][:RIM]
            at += RIM
        target[3 * tokens :, :] = extra[...].astype(BF16)


def gradient_step(arrived, short_weights, tables, known, tokens):
    peers = len(arrived)
    seq_len = peers * tokens
    size = seq_len // PHASES
    extra = extra_rows(short_weights)[1]
    return pl.pallas_call(
        functools.partial(gradient_kernel, tokens, peers, 1.0 / math.sqrt(seq_len)),
        in_specs=in_vmem(peers + 10),
        out_specs=in_vmem(peers),
        out_shape=[jax.ShapeDtypeStruct((3 * tokens + extra, LANES), BF16)] * peers,
        scratch_shapes=[
            pltpu.VMEM((seq_len + 2 * PAD, LANES), F32),
            pltpu.VMEM((seq_len + 2 * PAD, LANES), F32),
            pltpu.VMEM((seq_len + 2 * PAD, LANES), F32),
            pltpu.VMEM((seq_len, LANES), F32),
            pltpu.VMEM((PHASES, size, LANES), BF16),
            pltpu.VMEM((PHASES, 2 * size, LANES), F32),
            pltpu.VMEM((PHASES, 2 * size, 4 * LANES), BF16),
            pltpu.VMEM((extra, LANES), F32),
        ],
        compiler_params=pltpu.CompilerParams(vmem_limit_bytes=VMEM_LIMIT),
        name="gradient_channels",
    )(*arrived, short_weights, *tables, *known)


def token_kernel(peers, sum_rows, *refs):
    arrived = refs[:peers]
    query, key, value, cot, weights = refs[peers : peers + 5]
    gated, query_grad, key_grad, value_grad, filter_grad, short_grad = refs[peers + 5 : peers + 11]
    longer, pre = refs[peers + 11 :]
    tokens = query.shape[0]
    tap_count = weights.shape[1]
    count = sum_rows // PIECES
    me = lax.axis_index("ctx")
    for step, source in zip(partners(peers), arrived):
        lanes = lanes_of(me ^ step)
        extra = source[3 * tokens :, :].astype(F32)

        def rim(at):
            return extra[sum_rows + at * RIM : sum_rows + (at + 1) * RIM]

        def short(array, signal, after, rows):
            longer[array, PAD - RIM : PAD, :] = rim(array)
            longer[array, PAD : PAD + tokens, :] = signal[:, lanes].astype(F32)
            if after is not None:
                longer[array, PAD + tokens : PAD + tokens + RIM, :] = rim(after)
            summed = weights[array, 0:1, lanes] * longer[array, PAD : PAD + rows, :]
            for tap in range(1, tap_count):
                summed = (
                    summed
                    + weights[array, tap : tap + 1, lanes]
                    * longer[array, PAD - tap : PAD - tap + rows, :]
                )
            return summed

        def taps_back(array, target):
            summed = weights[array, 0:1, lanes] * pre[array, :tokens, :]
            for tap in range(1, tap_count):
                summed = (
                    summed
                    + weights[array, tap : tap + 1, lanes] * pre[array, tap : tap + tokens, :]
                )
            target[:, lanes] = summed.astype(BF16)

        conv = source[:tokens, :].astype(F32)
        gated[:, lanes] = (short(0, query, None, tokens) * conv).astype(BF16)
        pre[0, :tokens, :] = cot[:, lanes].astype(F32) * conv
        pre[0, tokens : tokens + RIM, :] = rim(3) * rim(4)
        taps_back(0, query_grad)
        key_short = short(1, key, 6, tokens + PAD)
        value_short = short(2, value, 7, tokens + PAD)
        conv_grad = source[tokens : 2 * tokens, :].astype(F32)
        for array, other in ((1, value_short), (2, key_short)):
            pre[array, :tokens, :] = conv_grad * other[:tokens]
            pre[array, tokens : tokens + RIM, :] = rim(5) * other[tokens : tokens + RIM]
        taps_back(1, key_grad)
        taps_back(2, value_grad)
        filter_grad[:, lanes] = source[2 * tokens : 3 * tokens, :].astype(F32)
        whole = extra[:count]
        for piece in range(1, PIECES):
            whole = whole + extra[piece * count : (piece + 1) * count]
        for row in range(count):
            which, tap = divmod(row, tap_count)
            short_grad[which, tap : tap + 1, lanes] = whole[row : row + 1]


def token_step(arrived, query, key, value, cot, short_weights):
    peers = len(arrived)
    tokens, width = query.shape
    wide = jax.ShapeDtypeStruct((tokens, width), BF16)
    return pl.pallas_call(
        functools.partial(token_kernel, peers, extra_rows(short_weights)[0]),
        in_specs=in_vmem(peers + 5),
        out_specs=in_vmem(6),
        out_shape=[wide] * 4
        + [
            jax.ShapeDtypeStruct((tokens, width), F32),
            jax.ShapeDtypeStruct(short_weights.shape, F32),
        ],
        scratch_shapes=[
            pltpu.VMEM((3, tokens + 2 * PAD, LANES), F32),
            pltpu.VMEM((3, tokens + PAD, LANES), F32),
        ],
        compiler_params=pltpu.CompilerParams(vmem_limit_bytes=VMEM_LIMIT),
        name="token_outputs",
    )(*arrived, query, key, value, cot, short_weights)


def channel_shards(query_proj, key_proj, value_proj, cotangent, filter_taps, short_weights):
    peers = lax.axis_size("ctx")
    tokens = query_proj.shape[0]
    tables = [jnp.asarray(table) for table in dft_tables(peers * tokens)]
    first = exchange(pack("pack_key_value_taps", (key_proj, value_proj, filter_taps), peers))
    second = exchange(pack("pack_query_cot", (query_proj, cotangent), peers, first[2:3]))
    known = key_value_step(first, short_weights, tables, tokens)
    back = exchange(gradient_step(second, short_weights, tables, known, tokens))
    return tuple(token_step(back, query_proj, key_proj, value_proj, cotangent, short_weights))


def from_behind(array, axis, by):
    peers = lax.axis_size(axis)
    pairs = [(i, i + by) for i in range(peers) if 0 <= i + by < peers]
    return lax.ppermute(array, axis, pairs)


def contract(form, left, right):
    return jnp.einsum(
        form, left, right, precision=lax.Precision.HIGHEST, preferred_element_type=jnp.float32
    )


def table_pair(rows, cols, period):
    row_ids = lax.broadcasted_iota(jnp.int32, (rows, cols), 0)
    col_ids = lax.broadcasted_iota(jnp.int32, (rows, cols), 1)
    angle = 2.0 * math.pi / period * (row_ids * col_ids % period).astype(jnp.float32)
    return (jnp.cos(angle), jnp.sin(angle))


def make_plan(seq_len):
    small_len = int(math.isqrt(2 * seq_len))
    while seq_len % small_len:
        small_len -= 1
    large_len = 2 * seq_len // small_len
    large_cos, large_sin = table_pair(large_len // 2, large_len, large_len)
    small_cos, small_sin = table_pair(small_len, small_len, small_len)
    twist_cos, twist_sin = table_pair(large_len, small_len, small_len * large_len)
    fwd_large = jnp.stack([large_cos, -large_sin], axis=1)
    fwd_small = jnp.stack([jnp.stack([small_cos, -small_sin]), jnp.stack([small_sin, small_cos])])
    inv_small = jnp.stack([jnp.stack([small_cos, small_sin]), jnp.stack([-small_sin, small_cos])])
    inv_large = jnp.stack([large_cos, -large_sin])
    return (small_len, large_len, fwd_large, fwd_small, inv_small, inv_large, twist_cos, twist_sin)


def forward_spec(signal, dft_plan):
    small_len, large_len, fwd_large, fwd_small, inv_small, inv_large, twist_cos, twist_sin = (
        dft_plan
    )
    cube = signal.reshape(signal.shape[0], large_len // 2, small_len)
    section_one = contract("cba,bpk->cpka", cube, fwd_large)
    real_one = section_one[:, 0]
    imag_one = section_one[:, 1]
    section_two = jnp.stack(
        [real_one * twist_cos + imag_one * twist_sin, imag_one * twist_cos - real_one * twist_sin],
        axis=1,
    )
    return contract("cpka,pqaj->cqkj", section_two, fwd_small)


def inverse_half(spec, dft_plan):
    small_len, large_len, fwd_large, fwd_small, inv_small, inv_large, twist_cos, twist_sin = (
        dft_plan
    )
    section_one = contract("cqkj,qpja->cpka", spec, inv_small)
    real_one = section_one[:, 0]
    imag_one = section_one[:, 1]
    section_two = jnp.stack(
        [real_one * twist_cos - imag_one * twist_sin, imag_one * twist_cos + real_one * twist_sin],
        axis=1,
    )
    signal = contract("cpka,pbk->cba", section_two, inv_large)
    return signal.reshape(signal.shape[0], -1) / float(small_len * large_len)


def complex_mul(left, right):
    left_real, left_imag = (left[:, 0], left[:, 1])
    right_real, right_imag = (right[:, 0], right[:, 1])
    return jnp.stack(
        [
            left_real * right_real - left_imag * right_imag,
            left_real * right_imag + left_imag * right_real,
        ],
        axis=1,
    )


def conj_mul(left, right):
    left_real, left_imag = (left[:, 0], left[:, 1])
    right_real, right_imag = (right[:, 0], right[:, 1])
    return jnp.stack(
        [
            left_real * right_real + left_imag * right_imag,
            left_real * right_imag - left_imag * right_real,
        ],
        axis=1,
    )


def conv_forward(prod_chan, filter_spec, dft_plan):
    prod_spec = forward_spec(prod_chan.astype(jnp.float32), dft_plan)
    conv_chan = inverse_half(complex_mul(prod_spec, filter_spec), dft_plan).astype(jnp.bfloat16)
    return (conv_chan, prod_spec)


def conv_backward(grad_chan, filter_spec, prod_spec, dft_plan, grad_scale):
    grad_spec = forward_spec(grad_chan.astype(jnp.float32), dft_plan)
    dconv_chan = inverse_half(conj_mul(filter_spec, grad_spec), dft_plan).astype(jnp.bfloat16)
    dfilter_chan = inverse_half(conj_mul(prod_spec, grad_spec), dft_plan) * grad_scale
    return (dconv_chan, dfilter_chan)


def receive_filter(filter_taps, dft_plan):
    filter_chan = lax.all_to_all(filter_taps.T, "ctx", split_axis=0, concat_axis=1, tiled=True)
    return forward_spec(filter_chan, dft_plan)


def return_filter(dfilter_chan):
    return (
        lax.all_to_all(
            dfilter_chan.astype(jnp.bfloat16), "ctx", split_axis=1, concat_axis=0, tiled=True
        )
        .astype(dfilter_chan.dtype)
        .T
    )


def causal_taps(extended, weights, length, axis):
    rim_rows = len(weights) - 1
    summed = weights[0] * lax.slice_in_dim(extended, rim_rows, rim_rows + length, axis=axis)
    for offset in range(1, len(weights)):
        summed = summed + weights[offset] * lax.slice_in_dim(
            extended, rim_rows - offset, rim_rows - offset + length, axis=axis
        )
    return summed


def reverse_taps(extended, weights, length, axis):
    summed = weights[0] * lax.slice_in_dim(extended, 0, length, axis=axis)
    for offset in range(1, len(weights)):
        summed = summed + weights[offset] * lax.slice_in_dim(
            extended, offset, offset + length, axis=axis
        )
    return summed


def tap_grads(grad_in, extended, tap_count, length, axis):
    rim_rows = tap_count - 1
    rows = [
        jnp.sum(
            grad_in
            * lax.slice_in_dim(extended, rim_rows - offset, rim_rows - offset + length, axis=axis),
            axis=axis,
        )
        for offset in range(tap_count)
    ]
    return jnp.stack(rows, axis=1)


def spread_shards(query_proj, key_proj, value_proj, cotangent, filter_taps, short_weights):
    tokens = query_proj.shape[0]
    tap_count = short_weights.shape[1]
    rim_rows = tap_count - 1
    seq_len = tokens * lax.axis_size("ctx")
    grad_scale = 1.0 / math.sqrt(seq_len)
    dft_plan = make_plan(seq_len)
    stacked = jnp.stack([query_proj, key_proj, value_proj])
    prev_rim = from_behind(stacked[:, tokens - rim_rows :], "ctx", 1)
    extended = jnp.concatenate([prev_rim, stacked], axis=1).astype(jnp.float32)
    weights = [short_weights[:, offset, None, :] for offset in range(tap_count)]
    short_out = causal_taps(extended, weights, tokens, 1)
    product = (short_out[1] * short_out[2]).astype(jnp.bfloat16)
    cot_wide = cotangent.astype(jnp.float32)
    gate_grad = (cot_wide * short_out[0]).astype(jnp.bfloat16)
    filter_spec = receive_filter(filter_taps, dft_plan)
    prod_chan = lax.all_to_all(product.T, "ctx", split_axis=0, concat_axis=1, tiled=True)
    conv_chan, prod_spec = conv_forward(prod_chan, filter_spec, dft_plan)
    conv_tok = lax.all_to_all(conv_chan, "ctx", split_axis=1, concat_axis=0, tiled=True)
    grad_chan = lax.all_to_all(gate_grad.T, "ctx", split_axis=0, concat_axis=1, tiled=True)
    dconv_chan, dfilter_chan = conv_backward(
        grad_chan, filter_spec, prod_spec, dft_plan, grad_scale
    )
    dconv_tok = lax.all_to_all(dconv_chan, "ctx", split_axis=1, concat_axis=0, tiled=True)
    filter_grad = return_filter(dfilter_chan)
    conv_wide = conv_tok.T.astype(jnp.float32)
    dconv_wide = dconv_tok.T.astype(jnp.float32)
    gated = (short_out[0] * conv_wide).astype(jnp.bfloat16)
    token_grads = jnp.stack(
        [cot_wide * conv_wide, dconv_wide * short_out[2], dconv_wide * short_out[1]]
    )
    next_rim = from_behind(token_grads[:, :rim_rows], "ctx", -1)
    grad_ext = jnp.concatenate([token_grads, next_rim], axis=1)
    inputs_grad = reverse_taps(grad_ext, weights, tokens, 1).astype(jnp.bfloat16)
    weight_part = tap_grads(token_grads, extended, tap_count, tokens, 1)
    short_grad = lax.psum(weight_part, "ctx") * grad_scale
    results = (gated, inputs_grad[0], inputs_grad[1], inputs_grad[2])
    return (results[0], results[1], results[2], results[3], filter_grad, short_grad)


def fits(query_proj, short_weights):
    peers = lax.axis_size("ctx")
    tokens, width = query_proj.shape
    tap_count = short_weights.shape[1]
    return (
        width == peers * LANES
        and peers.bit_count() == 1
        and tokens % (PHASES * TILE) == 0
        and tap_count == RIM + 1
        and peers * tokens <= 2048
    )


def shards(*arrays):
    return channel_shards(*arrays) if fits(arrays[0], arrays[5]) else spread_shards(*arrays)


def solution(mesh):
    placed = (
        P("ctx", "tp"),
        P("ctx", "tp"),
        P("ctx", "tp"),
        P("ctx", "tp"),
        P("ctx", "tp"),
        P(None, None, "tp"),
    )
    return jax.shard_map(
        shards,
        mesh=mesh,
        in_specs=placed,
        out_specs=(
            P("ctx", "tp"),
            P("ctx", "tp"),
            P("ctx", "tp"),
            P("ctx", "tp"),
            P("ctx", "tp"),
            P(None, None, "tp"),
        ),
        check_vma=False,
    )
```

```python
import functools
import math

import jax
import jax.numpy as jnp
import numpy as np
from jax import lax
from jax.experimental import pallas as pl
from jax.experimental.pallas import tpu as pltpu
from jax.sharding import PartitionSpec as P

F32 = jnp.float32
BF16 = jnp.bfloat16
LANES = 128
PHASES = 4
TILE = 16
PAD = 8
RIM = 2
PIECES = 3
MIB = 1024 * 1024
VMEM_LIMIT = 24 * MIB


def partners(peers):
    return [0] + list(range(peers - 1, 0, -1))


def exchange(blocks):
    peers = len(blocks)
    got = [blocks[0]]
    for step, block in list(zip(partners(peers), blocks))[1:]:
        got.append(lax.ppermute(block, "ctx", [(i, i ^ step) for i in range(peers)]))
    return got


def in_vmem(count):
    return [pl.BlockSpec(memory_space=pltpu.VMEM)] * count


def lanes_of(place):
    return pl.ds(pl.multiple_of(place * LANES, LANES), LANES)


def pack_kernel(count, *refs):
    sources, packed = refs[:count], refs[count:]
    tokens = sources[0].shape[0]
    me = lax.axis_index("ctx")
    for step, target in zip(partners(len(packed)), packed):
        for at, source in enumerate(sources):
            target[at * tokens : (at + 1) * tokens, :] = source[:, lanes_of(me ^ step)].astype(BF16)


def pack(arrays, peers):
    tokens = arrays[0].shape[0]
    return pl.pallas_call(
        functools.partial(pack_kernel, len(arrays)),
        in_specs=in_vmem(len(arrays)),
        out_specs=in_vmem(peers),
        out_shape=[jax.ShapeDtypeStruct((len(arrays) * tokens, LANES), BF16)] * peers,
        cost_estimate=pl.CostEstimate(flops=0, bytes_accessed=8 * MIB, transcendentals=0),
        name="pack_inputs",
    )(*arrays)


@functools.lru_cache(maxsize=None)
def dft_tables(seq_len):
    size = seq_len // PHASES
    k = np.arange(size, dtype=np.int64)[:, None]
    m = np.arange(size, dtype=np.int64)[None, :]
    forward = []
    for phase in range(PHASES):
        turns = ((4 * k + 1) * (PHASES * m + phase)) % (4 * seq_len)
        angle = 2.0 * np.pi / (4 * seq_len) * turns
        forward.append(np.concatenate([np.cos(angle), -np.sin(angle)], axis=0))
    forward = np.stack(forward)
    backward = np.swapaxes(forward, 1, 2) / seq_len

    def pieces(table):
        high = table.astype(BF16)
        low = (table - high.astype(np.float64)).astype(BF16)
        return np.stack([high, low], axis=1)

    return pieces(forward), pieces(backward)


def forward_mix(parts):
    (r0, i0), (r1, i1), (r2, i2), (r3, i3) = parts
    ar, ai, br, bi = r0 + r2, i0 + i2, r0 - r2, i0 - i2
    cr, ci, dr, di = r1 + r3, i1 + i3, r1 - r3, i1 - i3
    return ((ar + cr, ai + ci), (br + di, bi - dr), (ar - cr, ai - ci), (br - di, bi + dr))


def inverse_mix(parts):
    (r0, i0), (r1, i1), (r2, i2), (r3, i3) = parts
    ar, ai, br, bi = r0 + r2, i0 + i2, r0 - r2, i0 - i2
    cr, ci, dr, di = r1 + r3, i1 + i3, r1 - r3, i1 - i3
    return ((ar + cr, ai + ci), (br - di, bi + dr), (ar - cr, ai - ci), (br + di, bi - dr))


def times(left, right):
    return tuple(
        (lr * rr - li * ri, lr * ri + li * rr) for (lr, li), (rr, ri) in zip(left, right)
    )


def conj_times(left, right):
    return tuple(
        (lr * rr + li * ri, lr * ri - li * rr) for (lr, li), (rr, ri) in zip(left, right)
    )


def split_store(ref, r, rows, lanes, values):
    half = ref.shape[-1] // 2
    rounded = values.astype(BF16)
    ref[r, rows, lanes] = rounded
    ref[r, rows, slice(lanes.start + half, lanes.stop + half)] = (
        values - rounded.astype(F32)
    ).astype(BF16)


def forward_transform(forward, signal):
    return jnp.dot(forward[0], signal, preferred_element_type=F32) + jnp.dot(
        forward[1], signal, preferred_element_type=F32
    )


def inverse_transform(backward, pieces):
    half = pieces.shape[-1] // 2
    both = jnp.dot(backward[0], pieces, preferred_element_type=F32)
    rest = jnp.dot(backward[1], pieces[:, :half], preferred_element_type=F32)
    return both[:, :half] + both[:, half:] + rest


def phase(ref, r, size):
    return ref[pl.ds(r, size, stride=PHASES), :]


def short_phases(ref, weights, array, lanes, r, size):
    summed = weights[array, 0:1, lanes] * phase(ref, PAD + r, size)
    for tap in range(1, weights.shape[1]):
        summed = summed + weights[array, tap : tap + 1, lanes] * phase(ref, PAD + r - tap, size)
    return summed


def clear_ends(ref):
    ref[:PAD, :] = jnp.zeros((PAD, LANES), F32)
    ref[ref.shape[0] - PAD :, :] = jnp.zeros((PAD, LANES), F32)


def stage_kernel(count, *refs):
    sources, targets, sems = refs[:count], refs[count + 1 : 2 * count + 1], refs[2 * count + 1]
    copies = [
        pltpu.make_async_copy(source, target, sems.at[at])
        for at, (source, target) in enumerate(zip(sources, targets))
    ]
    for copy in copies:
        copy.start()
    for copy in copies:
        copy.wait()


def stage(arrays, after):
    count = len(arrays)
    return pl.pallas_call(
        functools.partial(stage_kernel, count),
        in_specs=[pl.BlockSpec(memory_space=pl.ANY)] * (count + 1),
        out_specs=in_vmem(count),
        out_shape=[jax.ShapeDtypeStruct(array.shape, array.dtype) for array in arrays],
        scratch_shapes=[pltpu.SemaphoreType.DMA((count,))],
        compiler_params=pltpu.CompilerParams(vmem_limit_bytes=8 * MIB),
        cost_estimate=pl.CostEstimate(flops=0, bytes_accessed=8 * MIB, transcendentals=0),
        name="stage_tables",
    )(*arrays, after)


def extra_rows(short_weights):
    sums = PIECES * short_weights.shape[0] * short_weights.shape[1]
    return sums, -(-(sums + 8 * RIM) // TILE) * TILE


def channel_kernel(tokens, peers, grad_scale, *refs):
    arrived = refs[:peers]
    weights, forward, backward = refs[peers : peers + 3]
    out = refs[peers + 3 : 2 * peers + 3]
    (
        query,
        key,
        value,
        cot,
        conv,
        conv_grad,
        filter_grad,
        taps,
        key_short,
        value_short,
        signals,
        spectra,
        pieces,
        extra,
    ) = refs[2 * peers + 3 :]
    size = peers * tokens // PHASES
    tap_count = weights.shape[1]
    me = lax.axis_index("ctx")
    own = lanes_of(me)
    for ref in (query, key, value, cot, conv, conv_grad):
        clear_ends(ref)
    for step, source in zip(partners(peers), arrived):
        start = (me ^ step) * tokens
        inner = pl.ds(pl.multiple_of(PAD + start, PAD), tokens)
        for at, ref in enumerate((query, key, value, cot)):
            ref[inner, :] = source[at * tokens : (at + 1) * tokens, :].astype(F32)
        taps[pl.ds(pl.multiple_of(start, PAD), tokens), :] = source[4 * tokens :, :].astype(F32)
    for r in range(PHASES):
        key_short[r] = short_phases(key, weights, 1, own, r, size)
        value_short[r] = short_phases(value, weights, 2, own, r, size)
        query_short = short_phases(query, weights, 0, own, r, size)
        signals[r, :, :LANES] = (key_short[r] * value_short[r]).astype(BF16)
        signals[r, :, LANES : 2 * LANES] = phase(taps, r, size).astype(BF16)
        signals[r, :, 2 * LANES :] = (phase(cot, PAD + r, size) * query_short).astype(BF16)
    for r in range(PHASES):
        spectra[r] = forward_transform(forward[r], signals[r])
    for chunk in range(size // TILE):
        real = slice(chunk * TILE, (chunk + 1) * TILE)
        imag = slice(size + chunk * TILE, size + (chunk + 1) * TILE)
        prod, filt, grad = (
            forward_mix(
                [
                    (
                        spectra[r, real, at * LANES : (at + 1) * LANES],
                        spectra[r, imag, at * LANES : (at + 1) * LANES],
                    )
                    for r in range(PHASES)
                ]
            )
            for at in range(3)
        )
        for at, mixed in enumerate(
            (times(prod, filt), conj_times(filt, grad), conj_times(prod, grad))
        ):
            for r, pair in enumerate(inverse_mix(mixed)):
                for rows, part in zip((real, imag), pair):
                    split_store(pieces, r, rows, slice(at * LANES, (at + 1) * LANES), part)
    for r in range(PHASES):
        result = inverse_transform(backward[r], pieces[r])
        for at, ref in enumerate((conv, conv_grad)):
            ref[pl.ds(PAD + r, size, stride=PHASES), :] = (
                result[:, at * LANES : (at + 1) * LANES].astype(BF16).astype(F32)
            )
        filter_grad[pl.ds(r, size, stride=PHASES), :] = result[:, 2 * LANES :] * grad_scale

    sums = []
    for array, signal in enumerate((query, key, value)):
        totals = [None] * tap_count
        for r in range(PHASES):
            if array == 0:
                pre = phase(cot, PAD + r, size) * phase(conv, PAD + r, size)
            else:
                pre = phase(conv_grad, PAD + r, size) * (value_short, key_short)[array - 1][r]
            for tap in range(tap_count):
                term = pre * phase(signal, PAD + r - tap, size)
                term = jnp.sum(term.reshape(size // 8, 8, LANES), axis=0)
                totals[tap] = term if r == 0 else totals[tap] + term
        sums.extend(jnp.sum(total, axis=0, keepdims=True) for total in totals)
    rest = jnp.concatenate(sums, axis=0) * grad_scale
    extra[...] = jnp.zeros_like(extra)
    for piece in range(PIECES):
        rounded = rest.astype(BF16).astype(F32)
        extra[piece * len(sums) : (piece + 1) * len(sums), :] = rounded
        rest = rest - rounded
    for step, target in zip(partners(peers), out):
        start = (me ^ step) * tokens
        inner = pl.ds(pl.multiple_of(PAD + start, PAD), tokens)
        target[:tokens, :] = conv[inner, :].astype(BF16)
        target[tokens : 2 * tokens, :] = conv_grad[inner, :].astype(BF16)
        target[2 * tokens : 3 * tokens, :] = filter_grad[
            pl.ds(pl.multiple_of(start, PAD), tokens), :
        ].astype(BF16)
        before = pl.ds(pl.multiple_of(start, PAD), PAD)
        after = pl.ds(pl.multiple_of(PAD + start + tokens, PAD), PAD)
        at = PIECES * len(sums)
        for ref in (query, key, value):
            extra[at : at + RIM, :] = ref[before, :][PAD - RIM :]
            at += RIM
        for ref in (cot, conv, conv_grad, key, value):
            extra[at : at + RIM, :] = ref[after, :][:RIM]
            at += RIM
        target[3 * tokens :, :] = extra[...].astype(BF16)


def channel_step(arrived, short_weights, tables, tokens):
    peers = len(arrived)
    seq_len = peers * tokens
    size = seq_len // PHASES
    extra = extra_rows(short_weights)[1]
    padded = pltpu.VMEM((seq_len + 2 * PAD, LANES), F32)
    plain = pltpu.VMEM((seq_len, LANES), F32)
    phases = pltpu.VMEM((PHASES, size, LANES), F32)
    return pl.pallas_call(
        functools.partial(channel_kernel, tokens, peers, 1.0 / math.sqrt(seq_len)),
        in_specs=in_vmem(peers + 3),
        out_specs=in_vmem(peers),
        out_shape=[jax.ShapeDtypeStruct((3 * tokens + extra, LANES), BF16)] * peers,
        scratch_shapes=[
            *[padded] * 6,
            plain,
            plain,
            phases,
            phases,
            pltpu.VMEM((PHASES, size, 3 * LANES), BF16),
            pltpu.VMEM((PHASES, 2 * size, 3 * LANES), F32),
            pltpu.VMEM((PHASES, 2 * size, 6 * LANES), BF16),
            pltpu.VMEM((extra, LANES), F32),
        ],
        compiler_params=pltpu.CompilerParams(vmem_limit_bytes=VMEM_LIMIT),
        name="channel_operator",
    )(*arrived, short_weights, *tables)


def token_kernel(peers, sum_rows, *refs):
    arrived = refs[:peers]
    query, key, value, cot, weights = refs[peers : peers + 5]
    gated, query_grad, key_grad, value_grad, filter_grad, short_grad = refs[peers + 5 : peers + 11]
    longer, pre = refs[peers + 11 :]
    tokens = query.shape[0]
    tap_count = weights.shape[1]
    count = sum_rows // PIECES
    me = lax.axis_index("ctx")
    for step, source in zip(partners(peers), arrived):
        lanes = lanes_of(me ^ step)
        extra = source[3 * tokens :, :].astype(F32)

        def rim(at):
            return extra[sum_rows + at * RIM : sum_rows + (at + 1) * RIM]

        def short(array, signal, after, rows):
            longer[array, PAD - RIM : PAD, :] = rim(array)
            longer[array, PAD : PAD + tokens, :] = signal[:, lanes].astype(F32)
            if after is not None:
                longer[array, PAD + tokens : PAD + tokens + RIM, :] = rim(after)
            summed = weights[array, 0:1, lanes] * longer[array, PAD : PAD + rows, :]
            for tap in range(1, tap_count):
                summed = (
                    summed
                    + weights[array, tap : tap + 1, lanes]
                    * longer[array, PAD - tap : PAD - tap + rows, :]
                )
            return summed

        def taps_back(array, target):
            summed = weights[array, 0:1, lanes] * pre[array, :tokens, :]
            for tap in range(1, tap_count):
                summed = (
                    summed
                    + weights[array, tap : tap + 1, lanes] * pre[array, tap : tap + tokens, :]
                )
            target[:, lanes] = summed.astype(BF16)

        conv = source[:tokens, :].astype(F32)
        gated[:, lanes] = (short(0, query, None, tokens) * conv).astype(BF16)
        pre[0, :tokens, :] = cot[:, lanes].astype(F32) * conv
        pre[0, tokens : tokens + RIM, :] = rim(3) * rim(4)
        taps_back(0, query_grad)
        key_short = short(1, key, 6, tokens + PAD)
        value_short = short(2, value, 7, tokens + PAD)
        conv_grad = source[tokens : 2 * tokens, :].astype(F32)
        for array, other in ((1, value_short), (2, key_short)):
            pre[array, :tokens, :] = conv_grad * other[:tokens]
            pre[array, tokens : tokens + RIM, :] = rim(5) * other[tokens : tokens + RIM]
        taps_back(1, key_grad)
        taps_back(2, value_grad)
        filter_grad[:, lanes] = source[2 * tokens : 3 * tokens, :].astype(F32)
        whole = extra[:count]
        for piece in range(1, PIECES):
            whole = whole + extra[piece * count : (piece + 1) * count]
        for row in range(count):
            which, tap = divmod(row, tap_count)
            short_grad[which, tap : tap + 1, lanes] = whole[row : row + 1]


def token_step(arrived, query, key, value, cot, short_weights):
    peers = len(arrived)
    tokens, width = query.shape
    wide = jax.ShapeDtypeStruct((tokens, width), BF16)
    return pl.pallas_call(
        functools.partial(token_kernel, peers, extra_rows(short_weights)[0]),
        in_specs=in_vmem(peers + 5),
        out_specs=in_vmem(6),
        out_shape=[wide] * 4
        + [
            jax.ShapeDtypeStruct((tokens, width), F32),
            jax.ShapeDtypeStruct(short_weights.shape, F32),
        ],
        scratch_shapes=[
            pltpu.VMEM((3, tokens + 2 * PAD, LANES), F32),
            pltpu.VMEM((3, tokens + PAD, LANES), F32),
        ],
        compiler_params=pltpu.CompilerParams(vmem_limit_bytes=VMEM_LIMIT),
        name="token_outputs",
    )(*arrived, query, key, value, cot, short_weights)


def channel_shards(query_proj, key_proj, value_proj, cotangent, filter_taps, short_weights):
    peers = lax.axis_size("ctx")
    tokens = query_proj.shape[0]
    tables = [jnp.asarray(table) for table in dft_tables(peers * tokens)]
    sent = pack((query_proj, key_proj, value_proj, cotangent, filter_taps), peers)
    arrived = exchange(sent)
    staged = stage((sent[0], short_weights, *tables), arrived[1])
    back = exchange(
        channel_step((staged[0], *arrived[1:]), staged[1], staged[2:], tokens)
    )
    return tuple(token_step(back, query_proj, key_proj, value_proj, cotangent, short_weights))


def from_behind(array, axis, by):
    peers = lax.axis_size(axis)
    pairs = [(i, i + by) for i in range(peers) if 0 <= i + by < peers]
    return lax.ppermute(array, axis, pairs)


def contract(form, left, right):
    return jnp.einsum(
        form, left, right, precision=lax.Precision.HIGHEST, preferred_element_type=jnp.float32
    )


def table_pair(rows, cols, period):
    row_ids = lax.broadcasted_iota(jnp.int32, (rows, cols), 0)
    col_ids = lax.broadcasted_iota(jnp.int32, (rows, cols), 1)
    angle = 2.0 * math.pi / period * (row_ids * col_ids % period).astype(jnp.float32)
    return (jnp.cos(angle), jnp.sin(angle))


def make_plan(seq_len):
    small_len = int(math.isqrt(2 * seq_len))
    while seq_len % small_len:
        small_len -= 1
    large_len = 2 * seq_len // small_len
    large_cos, large_sin = table_pair(large_len // 2, large_len, large_len)
    small_cos, small_sin = table_pair(small_len, small_len, small_len)
    twist_cos, twist_sin = table_pair(large_len, small_len, small_len * large_len)
    fwd_large = jnp.stack([large_cos, -large_sin], axis=1)
    fwd_small = jnp.stack([jnp.stack([small_cos, -small_sin]), jnp.stack([small_sin, small_cos])])
    inv_small = jnp.stack([jnp.stack([small_cos, small_sin]), jnp.stack([-small_sin, small_cos])])
    inv_large = jnp.stack([large_cos, -large_sin])
    return (small_len, large_len, fwd_large, fwd_small, inv_small, inv_large, twist_cos, twist_sin)


def forward_spec(signal, dft_plan):
    small_len, large_len, fwd_large, fwd_small, inv_small, inv_large, twist_cos, twist_sin = (
        dft_plan
    )
    cube = signal.reshape(signal.shape[0], large_len // 2, small_len)
    section_one = contract("cba,bpk->cpka", cube, fwd_large)
    real_one = section_one[:, 0]
    imag_one = section_one[:, 1]
    section_two = jnp.stack(
        [real_one * twist_cos + imag_one * twist_sin, imag_one * twist_cos - real_one * twist_sin],
        axis=1,
    )
    return contract("cpka,pqaj->cqkj", section_two, fwd_small)


def inverse_half(spec, dft_plan):
    small_len, large_len, fwd_large, fwd_small, inv_small, inv_large, twist_cos, twist_sin = (
        dft_plan
    )
    section_one = contract("cqkj,qpja->cpka", spec, inv_small)
    real_one = section_one[:, 0]
    imag_one = section_one[:, 1]
    section_two = jnp.stack(
        [real_one * twist_cos - imag_one * twist_sin, imag_one * twist_cos + real_one * twist_sin],
        axis=1,
    )
    signal = contract("cpka,pbk->cba", section_two, inv_large)
    return signal.reshape(signal.shape[0], -1) / float(small_len * large_len)


def complex_mul(left, right):
    left_real, left_imag = (left[:, 0], left[:, 1])
    right_real, right_imag = (right[:, 0], right[:, 1])
    return jnp.stack(
        [
            left_real * right_real - left_imag * right_imag,
            left_real * right_imag + left_imag * right_real,
        ],
        axis=1,
    )


def conj_mul(left, right):
    left_real, left_imag = (left[:, 0], left[:, 1])
    right_real, right_imag = (right[:, 0], right[:, 1])
    return jnp.stack(
        [
            left_real * right_real + left_imag * right_imag,
            left_real * right_imag - left_imag * right_real,
        ],
        axis=1,
    )


def conv_forward(prod_chan, filter_spec, dft_plan):
    prod_spec = forward_spec(prod_chan.astype(jnp.float32), dft_plan)
    conv_chan = inverse_half(complex_mul(prod_spec, filter_spec), dft_plan).astype(jnp.bfloat16)
    return (conv_chan, prod_spec)


def conv_backward(grad_chan, filter_spec, prod_spec, dft_plan, grad_scale):
    grad_spec = forward_spec(grad_chan.astype(jnp.float32), dft_plan)
    dconv_chan = inverse_half(conj_mul(filter_spec, grad_spec), dft_plan).astype(jnp.bfloat16)
    dfilter_chan = inverse_half(conj_mul(prod_spec, grad_spec), dft_plan) * grad_scale
    return (dconv_chan, dfilter_chan)


def receive_filter(filter_taps, dft_plan):
    filter_chan = lax.all_to_all(filter_taps.T, "ctx", split_axis=0, concat_axis=1, tiled=True)
    return forward_spec(filter_chan, dft_plan)


def return_filter(dfilter_chan):
    return (
        lax.all_to_all(
            dfilter_chan.astype(jnp.bfloat16), "ctx", split_axis=1, concat_axis=0, tiled=True
        )
        .astype(dfilter_chan.dtype)
        .T
    )


def causal_taps(extended, weights, length, axis):
    rim_rows = len(weights) - 1
    summed = weights[0] * lax.slice_in_dim(extended, rim_rows, rim_rows + length, axis=axis)
    for offset in range(1, len(weights)):
        summed = summed + weights[offset] * lax.slice_in_dim(
            extended, rim_rows - offset, rim_rows - offset + length, axis=axis
        )
    return summed


def reverse_taps(extended, weights, length, axis):
    summed = weights[0] * lax.slice_in_dim(extended, 0, length, axis=axis)
    for offset in range(1, len(weights)):
        summed = summed + weights[offset] * lax.slice_in_dim(
            extended, offset, offset + length, axis=axis
        )
    return summed


def tap_grads(grad_in, extended, tap_count, length, axis):
    rim_rows = tap_count - 1
    rows = [
        jnp.sum(
            grad_in
            * lax.slice_in_dim(extended, rim_rows - offset, rim_rows - offset + length, axis=axis),
            axis=axis,
        )
        for offset in range(tap_count)
    ]
    return jnp.stack(rows, axis=1)


def spread_shards(query_proj, key_proj, value_proj, cotangent, filter_taps, short_weights):
    tokens = query_proj.shape[0]
    tap_count = short_weights.shape[1]
    rim_rows = tap_count - 1
    seq_len = tokens * lax.axis_size("ctx")
    grad_scale = 1.0 / math.sqrt(seq_len)
    dft_plan = make_plan(seq_len)
    stacked = jnp.stack([query_proj, key_proj, value_proj])
    prev_rim = from_behind(stacked[:, tokens - rim_rows :], "ctx", 1)
    extended = jnp.concatenate([prev_rim, stacked], axis=1).astype(jnp.float32)
    weights = [short_weights[:, offset, None, :] for offset in range(tap_count)]
    short_out = causal_taps(extended, weights, tokens, 1)
    product = (short_out[1] * short_out[2]).astype(jnp.bfloat16)
    cot_wide = cotangent.astype(jnp.float32)
    gate_grad = (cot_wide * short_out[0]).astype(jnp.bfloat16)
    filter_spec = receive_filter(filter_taps, dft_plan)
    prod_chan = lax.all_to_all(product.T, "ctx", split_axis=0, concat_axis=1, tiled=True)
    conv_chan, prod_spec = conv_forward(prod_chan, filter_spec, dft_plan)
    conv_tok = lax.all_to_all(conv_chan, "ctx", split_axis=1, concat_axis=0, tiled=True)
    grad_chan = lax.all_to_all(gate_grad.T, "ctx", split_axis=0, concat_axis=1, tiled=True)
    dconv_chan, dfilter_chan = conv_backward(
        grad_chan, filter_spec, prod_spec, dft_plan, grad_scale
    )
    dconv_tok = lax.all_to_all(dconv_chan, "ctx", split_axis=1, concat_axis=0, tiled=True)
    filter_grad = return_filter(dfilter_chan)
    conv_wide = conv_tok.T.astype(jnp.float32)
    dconv_wide = dconv_tok.T.astype(jnp.float32)
    gated = (short_out[0] * conv_wide).astype(jnp.bfloat16)
    token_grads = jnp.stack(
        [cot_wide * conv_wide, dconv_wide * short_out[2], dconv_wide * short_out[1]]
    )
    next_rim = from_behind(token_grads[:, :rim_rows], "ctx", -1)
    grad_ext = jnp.concatenate([token_grads, next_rim], axis=1)
    inputs_grad = reverse_taps(grad_ext, weights, tokens, 1).astype(jnp.bfloat16)
    weight_part = tap_grads(token_grads, extended, tap_count, tokens, 1)
    short_grad = lax.psum(weight_part, "ctx") * grad_scale
    results = (gated, inputs_grad[0], inputs_grad[1], inputs_grad[2])
    return (results[0], results[1], results[2], results[3], filter_grad, short_grad)


def fits(query_proj, short_weights):
    peers = lax.axis_size("ctx")
    tokens, width = query_proj.shape
    tap_count = short_weights.shape[1]
    return (
        width == peers * LANES
        and peers.bit_count() == 1
        and tokens % (PHASES * TILE) == 0
        and tap_count == RIM + 1
        and peers * tokens <= 2048
    )


def shards(*arrays):
    return channel_shards(*arrays) if fits(arrays[0], arrays[5]) else spread_shards(*arrays)


def solution(mesh):
    placed = (
        P("ctx", "tp"),
        P("ctx", "tp"),
        P("ctx", "tp"),
        P("ctx", "tp"),
        P("ctx", "tp"),
        P(None, None, "tp"),
    )
    return jax.shard_map(
        shards,
        mesh=mesh,
        in_specs=placed,
        out_specs=(
            P("ctx", "tp"),
            P("ctx", "tp"),
            P("ctx", "tp"),
            P("ctx", "tp"),
            P("ctx", "tp"),
            P(None, None, "tp"),
        ),
        check_vma=False,
    )
```

```python
import functools
import math

import jax
import jax.numpy as jnp
import numpy as np
from jax import lax
from jax.experimental import pallas as pl
from jax.experimental.pallas import tpu as pltpu
from jax.sharding import PartitionSpec as P

F32 = jnp.float32
BF16 = jnp.bfloat16
LANES = 128
PHASES = 4
TILE = 16
PAD = 8
RIM = 2
PIECES = 3
MIB = 1024 * 1024
VMEM_LIMIT = 24 * MIB


def partners(peers):
    def rank(step):
        links = (step >> 1).bit_count()
        return (links == 0, links, step & 1, -step)

    return [0] + sorted(range(1, peers), key=rank)


def exchange(blocks):
    peers = len(blocks)
    got = [blocks[0]]
    for step, block in list(zip(partners(peers), blocks))[1:]:
        got.append(lax.ppermute(block, "ctx", [(i, i ^ step) for i in range(peers)]))
    return got


def in_vmem(count):
    return [pl.BlockSpec(memory_space=pltpu.VMEM)] * count


def lanes_of(place):
    return pl.ds(pl.multiple_of(place * LANES, LANES), LANES)


def pack_kernel(count, *refs):
    sources, packed = refs[:count], refs[count:]
    tokens = sources[0].shape[0]
    me = lax.axis_index("ctx")
    for step, target in zip(partners(len(packed)), packed):
        for at, source in enumerate(sources):
            target[at * tokens : (at + 1) * tokens, :] = source[:, lanes_of(me ^ step)].astype(BF16)


def pack(arrays, peers):
    tokens = arrays[0].shape[0]
    return pl.pallas_call(
        functools.partial(pack_kernel, len(arrays)),
        in_specs=in_vmem(len(arrays)),
        out_specs=in_vmem(peers),
        out_shape=[jax.ShapeDtypeStruct((len(arrays) * tokens, LANES), BF16)] * peers,
        cost_estimate=pl.CostEstimate(flops=0, bytes_accessed=8 * MIB, transcendentals=0),
        name="pack_inputs",
    )(*arrays)


@functools.lru_cache(maxsize=None)
def dft_tables(seq_len):
    size = seq_len // PHASES
    k = np.arange(size, dtype=np.int64)[:, None]
    m = np.arange(size, dtype=np.int64)[None, :]
    forward = []
    for phase in range(PHASES):
        turns = ((4 * k + 1) * (PHASES * m + phase)) % (4 * seq_len)
        angle = 2.0 * np.pi / (4 * seq_len) * turns
        forward.append(np.concatenate([np.cos(angle), -np.sin(angle)], axis=0))
    forward = np.stack(forward)
    backward = np.swapaxes(forward, 1, 2) / seq_len

    def pieces(table):
        high = table.astype(BF16)
        low = (table - high.astype(np.float64)).astype(BF16)
        return np.stack([high, low], axis=1)

    return pieces(forward), pieces(backward)


def forward_mix(parts):
    (r0, i0), (r1, i1), (r2, i2), (r3, i3) = parts
    ar, ai, br, bi = r0 + r2, i0 + i2, r0 - r2, i0 - i2
    cr, ci, dr, di = r1 + r3, i1 + i3, r1 - r3, i1 - i3
    return ((ar + cr, ai + ci), (br + di, bi - dr), (ar - cr, ai - ci), (br - di, bi + dr))


def inverse_mix(parts):
    (r0, i0), (r1, i1), (r2, i2), (r3, i3) = parts
    ar, ai, br, bi = r0 + r2, i0 + i2, r0 - r2, i0 - i2
    cr, ci, dr, di = r1 + r3, i1 + i3, r1 - r3, i1 - i3
    return ((ar + cr, ai + ci), (br - di, bi + dr), (ar - cr, ai - ci), (br + di, bi - dr))


def times(left, right):
    return tuple(
        (lr * rr - li * ri, lr * ri + li * rr) for (lr, li), (rr, ri) in zip(left, right)
    )


def conj_times(left, right):
    return tuple(
        (lr * rr + li * ri, lr * ri - li * rr) for (lr, li), (rr, ri) in zip(left, right)
    )


def split_store(ref, r, rows, lanes, values):
    half = ref.shape[-1] // 2
    rounded = values.astype(BF16)
    ref[r, rows, lanes] = rounded
    ref[r, rows, slice(lanes.start + half, lanes.stop + half)] = (
        values - rounded.astype(F32)
    ).astype(BF16)


def forward_transform(forward, signal):
    return jnp.dot(forward[0], signal, preferred_element_type=F32) + jnp.dot(
        forward[1], signal, preferred_element_type=F32
    )


def inverse_transform(backward, pieces):
    half = pieces.shape[-1] // 2
    both = jnp.dot(backward[0], pieces, preferred_element_type=F32)
    rest = jnp.dot(backward[1], pieces[:, :half], preferred_element_type=F32)
    return both[:, :half] + both[:, half:] + rest


def phase(ref, r, size):
    return ref[pl.ds(r, size, stride=PHASES), :]


def short_phases(ref, weights, array, lanes, r, size):
    summed = weights[array, 0:1, lanes] * phase(ref, PAD + r, size)
    for tap in range(1, weights.shape[1]):
        summed = summed + weights[array, tap : tap + 1, lanes] * phase(ref, PAD + r - tap, size)
    return summed


def clear_ends(ref):
    ref[:PAD, :] = jnp.zeros((PAD, LANES), F32)
    ref[ref.shape[0] - PAD :, :] = jnp.zeros((PAD, LANES), F32)


def stage_kernel(count, *refs):
    sources, targets, sems = refs[:count], refs[count + 1 : 2 * count + 1], refs[2 * count + 1]
    copies = [
        pltpu.make_async_copy(source, target, sems.at[at])
        for at, (source, target) in enumerate(zip(sources, targets))
    ]
    for copy in copies:
        copy.start()
    for copy in copies:
        copy.wait()


def stage(arrays, after):
    count = len(arrays)
    return pl.pallas_call(
        functools.partial(stage_kernel, count),
        in_specs=[pl.BlockSpec(memory_space=pl.ANY)] * (count + 1),
        out_specs=in_vmem(count),
        out_shape=[jax.ShapeDtypeStruct(array.shape, array.dtype) for array in arrays],
        scratch_shapes=[pltpu.SemaphoreType.DMA((count,))],
        compiler_params=pltpu.CompilerParams(vmem_limit_bytes=8 * MIB),
        cost_estimate=pl.CostEstimate(flops=0, bytes_accessed=8 * MIB, transcendentals=0),
        name="stage_tables",
    )(*arrays, after)


def extra_rows(short_weights):
    sums = PIECES * short_weights.shape[0] * short_weights.shape[1]
    return sums, -(-(sums + 8 * RIM) // TILE) * TILE


def channel_kernel(tokens, peers, grad_scale, *refs):
    arrived = refs[:peers]
    weights, forward, backward = refs[peers : peers + 3]
    out = refs[peers + 3 : 2 * peers + 3]
    (
        query,
        key,
        value,
        cot,
        conv,
        conv_grad,
        filter_grad,
        taps,
        key_short,
        value_short,
        signals,
        spectra,
        pieces,
        extra,
    ) = refs[2 * peers + 3 :]
    size = peers * tokens // PHASES
    tap_count = weights.shape[1]
    me = lax.axis_index("ctx")
    own = lanes_of(me)
    for ref in (query, key, value, cot, conv, conv_grad):
        clear_ends(ref)
    for step, source in zip(partners(peers), arrived):
        start = (me ^ step) * tokens
        inner = pl.ds(pl.multiple_of(PAD + start, PAD), tokens)
        for at, ref in enumerate((query, key, value, cot)):
            ref[inner, :] = source[at * tokens : (at + 1) * tokens, :].astype(F32)
        taps[pl.ds(pl.multiple_of(start, PAD), tokens), :] = source[4 * tokens :, :].astype(F32)
    for r in range(PHASES):
        key_short[r] = short_phases(key, weights, 1, own, r, size)
        value_short[r] = short_phases(value, weights, 2, own, r, size)
        query_short = short_phases(query, weights, 0, own, r, size)
        signals[r, :, :LANES] = (key_short[r] * value_short[r]).astype(BF16)
        signals[r, :, LANES : 2 * LANES] = phase(taps, r, size).astype(BF16)
        signals[r, :, 2 * LANES :] = (phase(cot, PAD + r, size) * query_short).astype(BF16)
    for r in range(PHASES):
        spectra[r] = forward_transform(forward[r], signals[r])
    for chunk in range(size // TILE):
        real = slice(chunk * TILE, (chunk + 1) * TILE)
        imag = slice(size + chunk * TILE, size + (chunk + 1) * TILE)
        prod, filt, grad = (
            forward_mix(
                [
                    (
                        spectra[r, real, at * LANES : (at + 1) * LANES],
                        spectra[r, imag, at * LANES : (at + 1) * LANES],
                    )
                    for r in range(PHASES)
                ]
            )
            for at in range(3)
        )
        for at, mixed in enumerate(
            (times(prod, filt), conj_times(filt, grad), conj_times(prod, grad))
        ):
            for r, pair in enumerate(inverse_mix(mixed)):
                for rows, part in zip((real, imag), pair):
                    split_store(pieces, r, rows, slice(at * LANES, (at + 1) * LANES), part)
    for r in range(PHASES):
        result = inverse_transform(backward[r], pieces[r])
        for at, ref in enumerate((conv, conv_grad)):
            ref[pl.ds(PAD + r, size, stride=PHASES), :] = (
                result[:, at * LANES : (at + 1) * LANES].astype(BF16).astype(F32)
            )
        filter_grad[pl.ds(r, size, stride=PHASES), :] = result[:, 2 * LANES :] * grad_scale

    sums = []
    for array, signal in enumerate((query, key, value)):
        totals = [None] * tap_count
        for r in range(PHASES):
            if array == 0:
                pre = phase(cot, PAD + r, size) * phase(conv, PAD + r, size)
            else:
                pre = phase(conv_grad, PAD + r, size) * (value_short, key_short)[array - 1][r]
            for tap in range(tap_count):
                term = pre * phase(signal, PAD + r - tap, size)
                term = jnp.sum(term.reshape(size // 8, 8, LANES), axis=0)
                totals[tap] = term if r == 0 else totals[tap] + term
        sums.extend(jnp.sum(total, axis=0, keepdims=True) for total in totals)
    rest = jnp.concatenate(sums, axis=0) * grad_scale
    extra[...] = jnp.zeros_like(extra)
    for piece in range(PIECES):
        rounded = rest.astype(BF16).astype(F32)
        extra[piece * len(sums) : (piece + 1) * len(sums), :] = rounded
        rest = rest - rounded
    for step, target in zip(partners(peers), out):
        start = (me ^ step) * tokens
        inner = pl.ds(pl.multiple_of(PAD + start, PAD), tokens)
        target[:tokens, :] = conv[inner, :].astype(BF16)
        target[tokens : 2 * tokens, :] = conv_grad[inner, :].astype(BF16)
        target[2 * tokens : 3 * tokens, :] = filter_grad[
            pl.ds(pl.multiple_of(start, PAD), tokens), :
        ].astype(BF16)
        before = pl.ds(pl.multiple_of(start, PAD), PAD)
        after = pl.ds(pl.multiple_of(PAD + start + tokens, PAD), PAD)
        at = PIECES * len(sums)
        for ref in (query, key, value):
            extra[at : at + RIM, :] = ref[before, :][PAD - RIM :]
            at += RIM
        for ref in (cot, conv, conv_grad, key, value):
            extra[at : at + RIM, :] = ref[after, :][:RIM]
            at += RIM
        target[3 * tokens :, :] = extra[...].astype(BF16)


def channel_step(arrived, short_weights, tables, tokens):
    peers = len(arrived)
    seq_len = peers * tokens
    size = seq_len // PHASES
    extra = extra_rows(short_weights)[1]
    padded = pltpu.VMEM((seq_len + 2 * PAD, LANES), F32)
    plain = pltpu.VMEM((seq_len, LANES), F32)
    phases = pltpu.VMEM((PHASES, size, LANES), F32)
    return pl.pallas_call(
        functools.partial(channel_kernel, tokens, peers, 1.0 / math.sqrt(seq_len)),
        in_specs=in_vmem(peers + 3),
        out_specs=in_vmem(peers),
        out_shape=[jax.ShapeDtypeStruct((3 * tokens + extra, LANES), BF16)] * peers,
        scratch_shapes=[
            *[padded] * 6,
            plain,
            plain,
            phases,
            phases,
            pltpu.VMEM((PHASES, size, 3 * LANES), BF16),
            pltpu.VMEM((PHASES, 2 * size, 3 * LANES), F32),
            pltpu.VMEM((PHASES, 2 * size, 6 * LANES), BF16),
            pltpu.VMEM((extra, LANES), F32),
        ],
        compiler_params=pltpu.CompilerParams(vmem_limit_bytes=VMEM_LIMIT),
        name="channel_operator",
    )(*arrived, short_weights, *tables)


def token_kernel(peers, sum_rows, *refs):
    arrived = refs[:peers]
    query, key, value, cot, weights = refs[peers : peers + 5]
    gated, query_grad, key_grad, value_grad, filter_grad, short_grad = refs[peers + 5 : peers + 11]
    longer, pre = refs[peers + 11 :]
    tokens = query.shape[0]
    tap_count = weights.shape[1]
    count = sum_rows // PIECES
    me = lax.axis_index("ctx")
    for step, source in zip(partners(peers), arrived):
        lanes = lanes_of(me ^ step)
        extra = source[3 * tokens :, :].astype(F32)

        def rim(at):
            return extra[sum_rows + at * RIM : sum_rows + (at + 1) * RIM]

        def short(array, signal, after, rows):
            longer[array, PAD - RIM : PAD, :] = rim(array)
            longer[array, PAD : PAD + tokens, :] = signal[:, lanes].astype(F32)
            if after is not None:
                longer[array, PAD + tokens : PAD + tokens + RIM, :] = rim(after)
            summed = weights[array, 0:1, lanes] * longer[array, PAD : PAD + rows, :]
            for tap in range(1, tap_count):
                summed = (
                    summed
                    + weights[array, tap : tap + 1, lanes]
                    * longer[array, PAD - tap : PAD - tap + rows, :]
                )
            return summed

        def taps_back(array, target):
            summed = weights[array, 0:1, lanes] * pre[array, :tokens, :]
            for tap in range(1, tap_count):
                summed = (
                    summed
                    + weights[array, tap : tap + 1, lanes] * pre[array, tap : tap + tokens, :]
                )
            target[:, lanes] = summed.astype(BF16)

        conv = source[:tokens, :].astype(F32)
        gated[:, lanes] = (short(0, query, None, tokens) * conv).astype(BF16)
        pre[0, :tokens, :] = cot[:, lanes].astype(F32) * conv
        pre[0, tokens : tokens + RIM, :] = rim(3) * rim(4)
        taps_back(0, query_grad)
        key_short = short(1, key, 6, tokens + PAD)
        value_short = short(2, value, 7, tokens + PAD)
        conv_grad = source[tokens : 2 * tokens, :].astype(F32)
        for array, other in ((1, value_short), (2, key_short)):
            pre[array, :tokens, :] = conv_grad * other[:tokens]
            pre[array, tokens : tokens + RIM, :] = rim(5) * other[tokens : tokens + RIM]
        taps_back(1, key_grad)
        taps_back(2, value_grad)
        filter_grad[:, lanes] = source[2 * tokens : 3 * tokens, :].astype(F32)
        whole = extra[:count]
        for piece in range(1, PIECES):
            whole = whole + extra[piece * count : (piece + 1) * count]
        for row in range(count):
            which, tap = divmod(row, tap_count)
            short_grad[which, tap : tap + 1, lanes] = whole[row : row + 1]


def token_step(arrived, query, key, value, cot, short_weights):
    peers = len(arrived)
    tokens, width = query.shape
    wide = jax.ShapeDtypeStruct((tokens, width), BF16)
    return pl.pallas_call(
        functools.partial(token_kernel, peers, extra_rows(short_weights)[0]),
        in_specs=in_vmem(peers + 5),
        out_specs=in_vmem(6),
        out_shape=[wide] * 4
        + [
            jax.ShapeDtypeStruct((tokens, width), F32),
            jax.ShapeDtypeStruct(short_weights.shape, F32),
        ],
        scratch_shapes=[
            pltpu.VMEM((3, tokens + 2 * PAD, LANES), F32),
            pltpu.VMEM((3, tokens + PAD, LANES), F32),
        ],
        compiler_params=pltpu.CompilerParams(vmem_limit_bytes=VMEM_LIMIT),
        name="token_outputs",
    )(*arrived, query, key, value, cot, short_weights)


def channel_shards(query_proj, key_proj, value_proj, cotangent, filter_taps, short_weights):
    peers = lax.axis_size("ctx")
    tokens = query_proj.shape[0]
    tables = [jnp.asarray(table) for table in dft_tables(peers * tokens)]
    sent = pack((query_proj, key_proj, value_proj, cotangent, filter_taps), peers)
    arrived = exchange(sent)
    staged = stage((sent[0], short_weights, *tables), arrived[1])
    back = exchange(
        channel_step((staged[0], *arrived[1:]), staged[1], staged[2:], tokens)
    )
    return tuple(token_step(back, query_proj, key_proj, value_proj, cotangent, short_weights))


def from_behind(array, axis, by):
    peers = lax.axis_size(axis)
    pairs = [(i, i + by) for i in range(peers) if 0 <= i + by < peers]
    return lax.ppermute(array, axis, pairs)


def contract(form, left, right):
    return jnp.einsum(
        form, left, right, precision=lax.Precision.HIGHEST, preferred_element_type=jnp.float32
    )


def table_pair(rows, cols, period):
    row_ids = lax.broadcasted_iota(jnp.int32, (rows, cols), 0)
    col_ids = lax.broadcasted_iota(jnp.int32, (rows, cols), 1)
    angle = 2.0 * math.pi / period * (row_ids * col_ids % period).astype(jnp.float32)
    return (jnp.cos(angle), jnp.sin(angle))


def make_plan(seq_len):
    small_len = int(math.isqrt(2 * seq_len))
    while seq_len % small_len:
        small_len -= 1
    large_len = 2 * seq_len // small_len
    large_cos, large_sin = table_pair(large_len // 2, large_len, large_len)
    small_cos, small_sin = table_pair(small_len, small_len, small_len)
    twist_cos, twist_sin = table_pair(large_len, small_len, small_len * large_len)
    fwd_large = jnp.stack([large_cos, -large_sin], axis=1)
    fwd_small = jnp.stack([jnp.stack([small_cos, -small_sin]), jnp.stack([small_sin, small_cos])])
    inv_small = jnp.stack([jnp.stack([small_cos, small_sin]), jnp.stack([-small_sin, small_cos])])
    inv_large = jnp.stack([large_cos, -large_sin])
    return (small_len, large_len, fwd_large, fwd_small, inv_small, inv_large, twist_cos, twist_sin)


def forward_spec(signal, dft_plan):
    small_len, large_len, fwd_large, fwd_small, inv_small, inv_large, twist_cos, twist_sin = (
        dft_plan
    )
    cube = signal.reshape(signal.shape[0], large_len // 2, small_len)
    section_one = contract("cba,bpk->cpka", cube, fwd_large)
    real_one = section_one[:, 0]
    imag_one = section_one[:, 1]
    section_two = jnp.stack(
        [real_one * twist_cos + imag_one * twist_sin, imag_one * twist_cos - real_one * twist_sin],
        axis=1,
    )
    return contract("cpka,pqaj->cqkj", section_two, fwd_small)


def inverse_half(spec, dft_plan):
    small_len, large_len, fwd_large, fwd_small, inv_small, inv_large, twist_cos, twist_sin = (
        dft_plan
    )
    section_one = contract("cqkj,qpja->cpka", spec, inv_small)
    real_one = section_one[:, 0]
    imag_one = section_one[:, 1]
    section_two = jnp.stack(
        [real_one * twist_cos - imag_one * twist_sin, imag_one * twist_cos + real_one * twist_sin],
        axis=1,
    )
    signal = contract("cpka,pbk->cba", section_two, inv_large)
    return signal.reshape(signal.shape[0], -1) / float(small_len * large_len)


def complex_mul(left, right):
    left_real, left_imag = (left[:, 0], left[:, 1])
    right_real, right_imag = (right[:, 0], right[:, 1])
    return jnp.stack(
        [
            left_real * right_real - left_imag * right_imag,
            left_real * right_imag + left_imag * right_real,
        ],
        axis=1,
    )


def conj_mul(left, right):
    left_real, left_imag = (left[:, 0], left[:, 1])
    right_real, right_imag = (right[:, 0], right[:, 1])
    return jnp.stack(
        [
            left_real * right_real + left_imag * right_imag,
            left_real * right_imag - left_imag * right_real,
        ],
        axis=1,
    )


def conv_forward(prod_chan, filter_spec, dft_plan):
    prod_spec = forward_spec(prod_chan.astype(jnp.float32), dft_plan)
    conv_chan = inverse_half(complex_mul(prod_spec, filter_spec), dft_plan).astype(jnp.bfloat16)
    return (conv_chan, prod_spec)


def conv_backward(grad_chan, filter_spec, prod_spec, dft_plan, grad_scale):
    grad_spec = forward_spec(grad_chan.astype(jnp.float32), dft_plan)
    dconv_chan = inverse_half(conj_mul(filter_spec, grad_spec), dft_plan).astype(jnp.bfloat16)
    dfilter_chan = inverse_half(conj_mul(prod_spec, grad_spec), dft_plan) * grad_scale
    return (dconv_chan, dfilter_chan)


def receive_filter(filter_taps, dft_plan):
    filter_chan = lax.all_to_all(filter_taps.T, "ctx", split_axis=0, concat_axis=1, tiled=True)
    return forward_spec(filter_chan, dft_plan)


def return_filter(dfilter_chan):
    return (
        lax.all_to_all(
            dfilter_chan.astype(jnp.bfloat16), "ctx", split_axis=1, concat_axis=0, tiled=True
        )
        .astype(dfilter_chan.dtype)
        .T
    )


def causal_taps(extended, weights, length, axis):
    rim_rows = len(weights) - 1
    summed = weights[0] * lax.slice_in_dim(extended, rim_rows, rim_rows + length, axis=axis)
    for offset in range(1, len(weights)):
        summed = summed + weights[offset] * lax.slice_in_dim(
            extended, rim_rows - offset, rim_rows - offset + length, axis=axis
        )
    return summed


def reverse_taps(extended, weights, length, axis):
    summed = weights[0] * lax.slice_in_dim(extended, 0, length, axis=axis)
    for offset in range(1, len(weights)):
        summed = summed + weights[offset] * lax.slice_in_dim(
            extended, offset, offset + length, axis=axis
        )
    return summed


def tap_grads(grad_in, extended, tap_count, length, axis):
    rim_rows = tap_count - 1
    rows = [
        jnp.sum(
            grad_in
            * lax.slice_in_dim(extended, rim_rows - offset, rim_rows - offset + length, axis=axis),
            axis=axis,
        )
        for offset in range(tap_count)
    ]
    return jnp.stack(rows, axis=1)


def spread_shards(query_proj, key_proj, value_proj, cotangent, filter_taps, short_weights):
    tokens = query_proj.shape[0]
    tap_count = short_weights.shape[1]
    rim_rows = tap_count - 1
    seq_len = tokens * lax.axis_size("ctx")
    grad_scale = 1.0 / math.sqrt(seq_len)
    dft_plan = make_plan(seq_len)
    stacked = jnp.stack([query_proj, key_proj, value_proj])
    prev_rim = from_behind(stacked[:, tokens - rim_rows :], "ctx", 1)
    extended = jnp.concatenate([prev_rim, stacked], axis=1).astype(jnp.float32)
    weights = [short_weights[:, offset, None, :] for offset in range(tap_count)]
    short_out = causal_taps(extended, weights, tokens, 1)
    product = (short_out[1] * short_out[2]).astype(jnp.bfloat16)
    cot_wide = cotangent.astype(jnp.float32)
    gate_grad = (cot_wide * short_out[0]).astype(jnp.bfloat16)
    filter_spec = receive_filter(filter_taps, dft_plan)
    prod_chan = lax.all_to_all(product.T, "ctx", split_axis=0, concat_axis=1, tiled=True)
    conv_chan, prod_spec = conv_forward(prod_chan, filter_spec, dft_plan)
    conv_tok = lax.all_to_all(conv_chan, "ctx", split_axis=1, concat_axis=0, tiled=True)
    grad_chan = lax.all_to_all(gate_grad.T, "ctx", split_axis=0, concat_axis=1, tiled=True)
    dconv_chan, dfilter_chan = conv_backward(
        grad_chan, filter_spec, prod_spec, dft_plan, grad_scale
    )
    dconv_tok = lax.all_to_all(dconv_chan, "ctx", split_axis=1, concat_axis=0, tiled=True)
    filter_grad = return_filter(dfilter_chan)
    conv_wide = conv_tok.T.astype(jnp.float32)
    dconv_wide = dconv_tok.T.astype(jnp.float32)
    gated = (short_out[0] * conv_wide).astype(jnp.bfloat16)
    token_grads = jnp.stack(
        [cot_wide * conv_wide, dconv_wide * short_out[2], dconv_wide * short_out[1]]
    )
    next_rim = from_behind(token_grads[:, :rim_rows], "ctx", -1)
    grad_ext = jnp.concatenate([token_grads, next_rim], axis=1)
    inputs_grad = reverse_taps(grad_ext, weights, tokens, 1).astype(jnp.bfloat16)
    weight_part = tap_grads(token_grads, extended, tap_count, tokens, 1)
    short_grad = lax.psum(weight_part, "ctx") * grad_scale
    results = (gated, inputs_grad[0], inputs_grad[1], inputs_grad[2])
    return (results[0], results[1], results[2], results[3], filter_grad, short_grad)


def fits(query_proj, short_weights):
    peers = lax.axis_size("ctx")
    tokens, width = query_proj.shape
    tap_count = short_weights.shape[1]
    return (
        width == peers * LANES
        and peers.bit_count() == 1
        and tokens % (PHASES * TILE) == 0
        and tap_count == RIM + 1
        and peers * tokens <= 2048
    )


def shards(*arrays):
    return channel_shards(*arrays) if fits(arrays[0], arrays[5]) else spread_shards(*arrays)


def solution(mesh):
    placed = (
        P("ctx", "tp"),
        P("ctx", "tp"),
        P("ctx", "tp"),
        P("ctx", "tp"),
        P("ctx", "tp"),
        P(None, None, "tp"),
    )
    return jax.shard_map(
        shards,
        mesh=mesh,
        in_specs=placed,
        out_specs=(
            P("ctx", "tp"),
            P("ctx", "tp"),
            P("ctx", "tp"),
            P("ctx", "tp"),
            P("ctx", "tp"),
            P(None, None, "tp"),
        ),
        check_vma=False,
    )
```

```python
import functools
import math

import jax
import jax.numpy as jnp
import numpy as np
from jax import lax
from jax.experimental import pallas as pl
from jax.experimental.pallas import tpu as pltpu
from jax.sharding import PartitionSpec as P

F32 = jnp.float32
BF16 = jnp.bfloat16
LANES = 128
PHASES = 4
TILE = 16
PAD = 8
RIM = 2
PIECES = 3
MIB = 1024 * 1024
VMEM_LIMIT = 24 * MIB


def partners(peers):
    def rank(step):
        links = (step >> 1).bit_count()
        return (links == 0, links == 1 and step & 1, links, step & 1, -step)

    return [0] + sorted(range(1, peers), key=rank)


def exchange(blocks):
    peers = len(blocks)
    got = [blocks[0]]
    for step, block in list(zip(partners(peers), blocks))[1:]:
        got.append(lax.ppermute(block, "ctx", [(i, i ^ step) for i in range(peers)]))
    return got


def in_vmem(count):
    return [pl.BlockSpec(memory_space=pltpu.VMEM)] * count


def lanes_of(place):
    return pl.ds(pl.multiple_of(place * LANES, LANES), LANES)


def pack_kernel(count, *refs):
    sources, packed = refs[:count], refs[count:]
    tokens = sources[0].shape[0]
    me = lax.axis_index("ctx")
    for step, target in zip(partners(len(packed)), packed):
        for at, source in enumerate(sources):
            target[at * tokens : (at + 1) * tokens, :] = source[:, lanes_of(me ^ step)].astype(BF16)


def pack(arrays, peers):
    tokens = arrays[0].shape[0]
    return pl.pallas_call(
        functools.partial(pack_kernel, len(arrays)),
        in_specs=in_vmem(len(arrays)),
        out_specs=in_vmem(peers),
        out_shape=[jax.ShapeDtypeStruct((len(arrays) * tokens, LANES), BF16)] * peers,
        compiler_params=pltpu.CompilerParams(vmem_limit_bytes=VMEM_LIMIT),
        cost_estimate=pl.CostEstimate(flops=0, bytes_accessed=8 * MIB, transcendentals=0),
        name="pack_inputs",
    )(*arrays)


@functools.lru_cache(maxsize=None)
def dft_tables(seq_len):
    size = seq_len // PHASES
    k = np.arange(size, dtype=np.int64)[:, None]
    m = np.arange(size, dtype=np.int64)[None, :]
    forward = []
    for phase in range(PHASES):
        turns = ((4 * k + 1) * (PHASES * m + phase)) % (4 * seq_len)
        angle = 2.0 * np.pi / (4 * seq_len) * turns
        forward.append(np.concatenate([np.cos(angle), -np.sin(angle)], axis=0))
    forward = np.stack(forward)
    backward = np.swapaxes(forward, 1, 2) / seq_len

    def pieces(table):
        high = table.astype(BF16)
        low = (table - high.astype(np.float64)).astype(BF16)
        return np.stack([high, low], axis=1)

    return pieces(forward), pieces(backward)


def forward_mix(parts):
    (r0, i0), (r1, i1), (r2, i2), (r3, i3) = parts
    ar, ai, br, bi = r0 + r2, i0 + i2, r0 - r2, i0 - i2
    cr, ci, dr, di = r1 + r3, i1 + i3, r1 - r3, i1 - i3
    return ((ar + cr, ai + ci), (br + di, bi - dr), (ar - cr, ai - ci), (br - di, bi + dr))


def inverse_mix(parts):
    (r0, i0), (r1, i1), (r2, i2), (r3, i3) = parts
    ar, ai, br, bi = r0 + r2, i0 + i2, r0 - r2, i0 - i2
    cr, ci, dr, di = r1 + r3, i1 + i3, r1 - r3, i1 - i3
    return ((ar + cr, ai + ci), (br - di, bi + dr), (ar - cr, ai - ci), (br + di, bi - dr))


def times(left, right):
    return tuple(
        (lr * rr - li * ri, lr * ri + li * rr) for (lr, li), (rr, ri) in zip(left, right)
    )


def conj_times(left, right):
    return tuple(
        (lr * rr + li * ri, lr * ri - li * rr) for (lr, li), (rr, ri) in zip(left, right)
    )


def split_store(ref, r, rows, lanes, values):
    half = ref.shape[-1] // 2
    rounded = values.astype(BF16)
    ref[r, rows, lanes] = rounded
    ref[r, rows, slice(lanes.start + half, lanes.stop + half)] = (
        values - rounded.astype(F32)
    ).astype(BF16)


def forward_transform(forward, signal):
    return jnp.dot(forward[0], signal, preferred_element_type=F32) + jnp.dot(
        forward[1], signal, preferred_element_type=F32
    )


def inverse_transform(backward, pieces):
    half = pieces.shape[-1] // 2
    both = jnp.dot(backward[0], pieces, preferred_element_type=F32)
    rest = jnp.dot(backward[1], pieces[:, :half], preferred_element_type=F32)
    return both[:, :half] + both[:, half:] + rest


def phase(ref, r, size):
    return ref[pl.ds(r, size, stride=PHASES), :]


def short_phases(ref, weights, array, lanes, r, size):
    summed = weights[array, 0:1, lanes] * phase(ref, PAD + r, size)
    for tap in range(1, weights.shape[1]):
        summed = summed + weights[array, tap : tap + 1, lanes] * phase(ref, PAD + r - tap, size)
    return summed


def clear_ends(ref):
    ref[:PAD, :] = jnp.zeros((PAD, LANES), F32)
    ref[ref.shape[0] - PAD :, :] = jnp.zeros((PAD, LANES), F32)


def stage_kernel(count, *refs):
    sources, targets, sems = refs[:count], refs[count + 1 : 2 * count + 1], refs[2 * count + 1]
    copies = [
        pltpu.make_async_copy(source, target, sems.at[at])
        for at, (source, target) in enumerate(zip(sources, targets))
    ]
    for copy in copies:
        copy.start()
    for copy in copies:
        copy.wait()


def stage(arrays, after):
    count = len(arrays)
    return pl.pallas_call(
        functools.partial(stage_kernel, count),
        in_specs=[pl.BlockSpec(memory_space=pl.ANY)] * (count + 1),
        out_specs=in_vmem(count),
        out_shape=[jax.ShapeDtypeStruct(array.shape, array.dtype) for array in arrays],
        scratch_shapes=[pltpu.SemaphoreType.DMA((count,))],
        compiler_params=pltpu.CompilerParams(vmem_limit_bytes=8 * MIB),
        cost_estimate=pl.CostEstimate(flops=0, bytes_accessed=8 * MIB, transcendentals=0),
        name="stage_tables",
    )(*arrays, after)


def extra_rows(short_weights):
    sums = PIECES * short_weights.shape[0] * short_weights.shape[1]
    return sums, -(-(sums + 8 * RIM) // TILE) * TILE


def channel_kernel(tokens, peers, grad_scale, *refs):
    arrived = refs[:peers]
    weights, forward, backward = refs[peers : peers + 3]
    out = refs[peers + 3 : 2 * peers + 3]
    (
        query,
        key,
        value,
        cot,
        conv,
        conv_grad,
        filter_grad,
        taps,
        key_short,
        value_short,
        signals,
        spectra,
        pieces,
        extra,
    ) = refs[2 * peers + 3 :]
    size = peers * tokens // PHASES
    tap_count = weights.shape[1]
    me = lax.axis_index("ctx")
    own = lanes_of(me)
    for ref in (query, key, value, cot, conv, conv_grad):
        clear_ends(ref)
    for step, source in zip(partners(peers), arrived):
        start = (me ^ step) * tokens
        inner = pl.ds(pl.multiple_of(PAD + start, PAD), tokens)
        for at, ref in enumerate((query, key, value, cot)):
            ref[inner, :] = source[at * tokens : (at + 1) * tokens, :].astype(F32)
        taps[pl.ds(pl.multiple_of(start, PAD), tokens), :] = source[4 * tokens :, :].astype(F32)
    for r in range(PHASES):
        key_short[r] = short_phases(key, weights, 1, own, r, size)
        value_short[r] = short_phases(value, weights, 2, own, r, size)
        query_short = short_phases(query, weights, 0, own, r, size)
        signals[r, :, :LANES] = (key_short[r] * value_short[r]).astype(BF16)
        signals[r, :, LANES : 2 * LANES] = phase(taps, r, size).astype(BF16)
        signals[r, :, 2 * LANES :] = (phase(cot, PAD + r, size) * query_short).astype(BF16)
    for r in range(PHASES):
        spectra[r] = forward_transform(forward[r], signals[r])
    for chunk in range(size // TILE):
        real = slice(chunk * TILE, (chunk + 1) * TILE)
        imag = slice(size + chunk * TILE, size + (chunk + 1) * TILE)
        prod, filt, grad = (
            forward_mix(
                [
                    (
                        spectra[r, real, at * LANES : (at + 1) * LANES],
                        spectra[r, imag, at * LANES : (at + 1) * LANES],
                    )
                    for r in range(PHASES)
                ]
            )
            for at in range(3)
        )
        for at, mixed in enumerate(
            (times(prod, filt), conj_times(filt, grad), conj_times(prod, grad))
        ):
            for r, pair in enumerate(inverse_mix(mixed)):
                for rows, part in zip((real, imag), pair):
                    split_store(pieces, r, rows, slice(at * LANES, (at + 1) * LANES), part)
    for r in range(PHASES):
        result = inverse_transform(backward[r], pieces[r])
        for at, ref in enumerate((conv, conv_grad)):
            ref[pl.ds(PAD + r, size, stride=PHASES), :] = (
                result[:, at * LANES : (at + 1) * LANES].astype(BF16).astype(F32)
            )
        filter_grad[pl.ds(r, size, stride=PHASES), :] = result[:, 2 * LANES :] * grad_scale

    sums = []
    for array, signal in enumerate((query, key, value)):
        totals = [None] * tap_count
        for r in range(PHASES):
            if array == 0:
                pre = phase(cot, PAD + r, size) * phase(conv, PAD + r, size)
            else:
                pre = phase(conv_grad, PAD + r, size) * (value_short, key_short)[array - 1][r]
            for tap in range(tap_count):
                term = pre * phase(signal, PAD + r - tap, size)
                term = jnp.sum(term.reshape(size // 8, 8, LANES), axis=0)
                totals[tap] = term if r == 0 else totals[tap] + term
        sums.extend(jnp.sum(total, axis=0, keepdims=True) for total in totals)
    rest = jnp.concatenate(sums, axis=0) * grad_scale
    extra[...] = jnp.zeros_like(extra)
    for piece in range(PIECES):
        rounded = rest.astype(BF16).astype(F32)
        extra[piece * len(sums) : (piece + 1) * len(sums), :] = rounded
        rest = rest - rounded
    for step, target in zip(partners(peers), out):
        start = (me ^ step) * tokens
        inner = pl.ds(pl.multiple_of(PAD + start, PAD), tokens)
        target[:tokens, :] = conv[inner, :].astype(BF16)
        target[tokens : 2 * tokens, :] = conv_grad[inner, :].astype(BF16)
        target[2 * tokens : 3 * tokens, :] = filter_grad[
            pl.ds(pl.multiple_of(start, PAD), tokens), :
        ].astype(BF16)
        before = pl.ds(pl.multiple_of(start, PAD), PAD)
        after = pl.ds(pl.multiple_of(PAD + start + tokens, PAD), PAD)
        at = PIECES * len(sums)
        for ref in (query, key, value):
            extra[at : at + RIM, :] = ref[before, :][PAD - RIM :]
            at += RIM
        for ref in (cot, conv, conv_grad, key, value):
            extra[at : at + RIM, :] = ref[after, :][:RIM]
            at += RIM
        target[3 * tokens :, :] = extra[...].astype(BF16)


def channel_step(arrived, short_weights, tables, tokens):
    peers = len(arrived)
    seq_len = peers * tokens
    size = seq_len // PHASES
    extra = extra_rows(short_weights)[1]
    padded = pltpu.VMEM((seq_len + 2 * PAD, LANES), F32)
    plain = pltpu.VMEM((seq_len, LANES), F32)
    phases = pltpu.VMEM((PHASES, size, LANES), F32)
    return pl.pallas_call(
        functools.partial(channel_kernel, tokens, peers, 1.0 / math.sqrt(seq_len)),
        in_specs=in_vmem(peers + 3),
        out_specs=in_vmem(peers),
        out_shape=[jax.ShapeDtypeStruct((3 * tokens + extra, LANES), BF16)] * peers,
        scratch_shapes=[
            *[padded] * 6,
            plain,
            plain,
            phases,
            phases,
            pltpu.VMEM((PHASES, size, 3 * LANES), BF16),
            pltpu.VMEM((PHASES, 2 * size, 3 * LANES), F32),
            pltpu.VMEM((PHASES, 2 * size, 6 * LANES), BF16),
            pltpu.VMEM((extra, LANES), F32),
        ],
        compiler_params=pltpu.CompilerParams(vmem_limit_bytes=VMEM_LIMIT),
        name="channel_operator",
    )(*arrived, short_weights, *tables)


def token_kernel(peers, sum_rows, *refs):
    arrived = refs[:peers]
    query, key, value, cot, weights = refs[peers : peers + 5]
    gated, query_grad, key_grad, value_grad, filter_grad, short_grad = refs[peers + 5 : peers + 11]
    longer, pre = refs[peers + 11 :]
    tokens = query.shape[0]
    tap_count = weights.shape[1]
    count = sum_rows // PIECES
    me = lax.axis_index("ctx")
    for step, source in zip(partners(peers), arrived):
        lanes = lanes_of(me ^ step)
        extra = source[3 * tokens :, :].astype(F32)

        def rim(at):
            return extra[sum_rows + at * RIM : sum_rows + (at + 1) * RIM]

        def short(array, signal, after, rows):
            longer[array, PAD - RIM : PAD, :] = rim(array)
            longer[array, PAD : PAD + tokens, :] = signal[:, lanes].astype(F32)
            if after is not None:
                longer[array, PAD + tokens : PAD + tokens + RIM, :] = rim(after)
            summed = weights[array, 0:1, lanes] * longer[array, PAD : PAD + rows, :]
            for tap in range(1, tap_count):
                summed = (
                    summed
                    + weights[array, tap : tap + 1, lanes]
                    * longer[array, PAD - tap : PAD - tap + rows, :]
                )
            return summed

        def taps_back(array, target):
            summed = weights[array, 0:1, lanes] * pre[array, :tokens, :]
            for tap in range(1, tap_count):
                summed = (
                    summed
                    + weights[array, tap : tap + 1, lanes] * pre[array, tap : tap + tokens, :]
                )
            target[:, lanes] = summed.astype(BF16)

        conv = source[:tokens, :].astype(F32)
        gated[:, lanes] = (short(0, query, None, tokens) * conv).astype(BF16)
        pre[0, :tokens, :] = cot[:, lanes].astype(F32) * conv
        pre[0, tokens : tokens + RIM, :] = rim(3) * rim(4)
        taps_back(0, query_grad)
        key_short = short(1, key, 6, tokens + PAD)
        value_short = short(2, value, 7, tokens + PAD)
        conv_grad = source[tokens : 2 * tokens, :].astype(F32)
        for array, other in ((1, value_short), (2, key_short)):
            pre[array, :tokens, :] = conv_grad * other[:tokens]
            pre[array, tokens : tokens + RIM, :] = rim(5) * other[tokens : tokens + RIM]
        taps_back(1, key_grad)
        taps_back(2, value_grad)
        filter_grad[:, lanes] = source[2 * tokens : 3 * tokens, :].astype(F32)
        whole = extra[:count]
        for piece in range(1, PIECES):
            whole = whole + extra[piece * count : (piece + 1) * count]
        for row in range(count):
            which, tap = divmod(row, tap_count)
            short_grad[which, tap : tap + 1, lanes] = whole[row : row + 1]


def token_step(arrived, query, key, value, cot, short_weights):
    peers = len(arrived)
    tokens, width = query.shape
    wide = jax.ShapeDtypeStruct((tokens, width), BF16)
    return pl.pallas_call(
        functools.partial(token_kernel, peers, extra_rows(short_weights)[0]),
        in_specs=in_vmem(peers + 5),
        out_specs=in_vmem(6),
        out_shape=[wide] * 4
        + [
            jax.ShapeDtypeStruct((tokens, width), F32),
            jax.ShapeDtypeStruct(short_weights.shape, F32),
        ],
        scratch_shapes=[
            pltpu.VMEM((3, tokens + 2 * PAD, LANES), F32),
            pltpu.VMEM((3, tokens + PAD, LANES), F32),
        ],
        compiler_params=pltpu.CompilerParams(vmem_limit_bytes=VMEM_LIMIT),
        name="token_outputs",
    )(*arrived, query, key, value, cot, short_weights)


def channel_shards(query_proj, key_proj, value_proj, cotangent, filter_taps, short_weights):
    peers = lax.axis_size("ctx")
    tokens = query_proj.shape[0]
    tables = [jnp.asarray(table) for table in dft_tables(peers * tokens)]
    sent = pack((query_proj, key_proj, value_proj, cotangent, filter_taps), peers)
    arrived = exchange(sent)
    staged = stage((sent[0], short_weights, *tables), arrived[1])
    back = exchange(
        channel_step((staged[0], *arrived[1:]), staged[1], staged[2:], tokens)
    )
    return tuple(token_step(back, query_proj, key_proj, value_proj, cotangent, short_weights))


def from_behind(array, axis, by):
    peers = lax.axis_size(axis)
    pairs = [(i, i + by) for i in range(peers) if 0 <= i + by < peers]
    return lax.ppermute(array, axis, pairs)


def contract(form, left, right):
    return jnp.einsum(
        form, left, right, precision=lax.Precision.HIGHEST, preferred_element_type=jnp.float32
    )


def table_pair(rows, cols, period):
    row_ids = lax.broadcasted_iota(jnp.int32, (rows, cols), 0)
    col_ids = lax.broadcasted_iota(jnp.int32, (rows, cols), 1)
    angle = 2.0 * math.pi / period * (row_ids * col_ids % period).astype(jnp.float32)
    return (jnp.cos(angle), jnp.sin(angle))


def make_plan(seq_len):
    small_len = int(math.isqrt(2 * seq_len))
    while seq_len % small_len:
        small_len -= 1
    large_len = 2 * seq_len // small_len
    large_cos, large_sin = table_pair(large_len // 2, large_len, large_len)
    small_cos, small_sin = table_pair(small_len, small_len, small_len)
    twist_cos, twist_sin = table_pair(large_len, small_len, small_len * large_len)
    fwd_large = jnp.stack([large_cos, -large_sin], axis=1)
    fwd_small = jnp.stack([jnp.stack([small_cos, -small_sin]), jnp.stack([small_sin, small_cos])])
    inv_small = jnp.stack([jnp.stack([small_cos, small_sin]), jnp.stack([-small_sin, small_cos])])
    inv_large = jnp.stack([large_cos, -large_sin])
    return (small_len, large_len, fwd_large, fwd_small, inv_small, inv_large, twist_cos, twist_sin)


def forward_spec(signal, dft_plan):
    small_len, large_len, fwd_large, fwd_small, inv_small, inv_large, twist_cos, twist_sin = (
        dft_plan
    )
    cube = signal.reshape(signal.shape[0], large_len // 2, small_len)
    section_one = contract("cba,bpk->cpka", cube, fwd_large)
    real_one = section_one[:, 0]
    imag_one = section_one[:, 1]
    section_two = jnp.stack(
        [real_one * twist_cos + imag_one * twist_sin, imag_one * twist_cos - real_one * twist_sin],
        axis=1,
    )
    return contract("cpka,pqaj->cqkj", section_two, fwd_small)


def inverse_half(spec, dft_plan):
    small_len, large_len, fwd_large, fwd_small, inv_small, inv_large, twist_cos, twist_sin = (
        dft_plan
    )
    section_one = contract("cqkj,qpja->cpka", spec, inv_small)
    real_one = section_one[:, 0]
    imag_one = section_one[:, 1]
    section_two = jnp.stack(
        [real_one * twist_cos - imag_one * twist_sin, imag_one * twist_cos + real_one * twist_sin],
        axis=1,
    )
    signal = contract("cpka,pbk->cba", section_two, inv_large)
    return signal.reshape(signal.shape[0], -1) / float(small_len * large_len)


def complex_mul(left, right):
    left_real, left_imag = (left[:, 0], left[:, 1])
    right_real, right_imag = (right[:, 0], right[:, 1])
    return jnp.stack(
        [
            left_real * right_real - left_imag * right_imag,
            left_real * right_imag + left_imag * right_real,
        ],
        axis=1,
    )


def conj_mul(left, right):
    left_real, left_imag = (left[:, 0], left[:, 1])
    right_real, right_imag = (right[:, 0], right[:, 1])
    return jnp.stack(
        [
            left_real * right_real + left_imag * right_imag,
            left_real * right_imag - left_imag * right_real,
        ],
        axis=1,
    )


def conv_forward(prod_chan, filter_spec, dft_plan):
    prod_spec = forward_spec(prod_chan.astype(jnp.float32), dft_plan)
    conv_chan = inverse_half(complex_mul(prod_spec, filter_spec), dft_plan).astype(jnp.bfloat16)
    return (conv_chan, prod_spec)


def conv_backward(grad_chan, filter_spec, prod_spec, dft_plan, grad_scale):
    grad_spec = forward_spec(grad_chan.astype(jnp.float32), dft_plan)
    dconv_chan = inverse_half(conj_mul(filter_spec, grad_spec), dft_plan).astype(jnp.bfloat16)
    dfilter_chan = inverse_half(conj_mul(prod_spec, grad_spec), dft_plan) * grad_scale
    return (dconv_chan, dfilter_chan)


def receive_filter(filter_taps, dft_plan):
    filter_chan = lax.all_to_all(filter_taps.T, "ctx", split_axis=0, concat_axis=1, tiled=True)
    return forward_spec(filter_chan, dft_plan)


def return_filter(dfilter_chan):
    return (
        lax.all_to_all(
            dfilter_chan.astype(jnp.bfloat16), "ctx", split_axis=1, concat_axis=0, tiled=True
        )
        .astype(dfilter_chan.dtype)
        .T
    )


def causal_taps(extended, weights, length, axis):
    rim_rows = len(weights) - 1
    summed = weights[0] * lax.slice_in_dim(extended, rim_rows, rim_rows + length, axis=axis)
    for offset in range(1, len(weights)):
        summed = summed + weights[offset] * lax.slice_in_dim(
            extended, rim_rows - offset, rim_rows - offset + length, axis=axis
        )
    return summed


def reverse_taps(extended, weights, length, axis):
    summed = weights[0] * lax.slice_in_dim(extended, 0, length, axis=axis)
    for offset in range(1, len(weights)):
        summed = summed + weights[offset] * lax.slice_in_dim(
            extended, offset, offset + length, axis=axis
        )
    return summed


def tap_grads(grad_in, extended, tap_count, length, axis):
    rim_rows = tap_count - 1
    rows = [
        jnp.sum(
            grad_in
            * lax.slice_in_dim(extended, rim_rows - offset, rim_rows - offset + length, axis=axis),
            axis=axis,
        )
        for offset in range(tap_count)
    ]
    return jnp.stack(rows, axis=1)


def spread_shards(query_proj, key_proj, value_proj, cotangent, filter_taps, short_weights):
    tokens = query_proj.shape[0]
    tap_count = short_weights.shape[1]
    rim_rows = tap_count - 1
    seq_len = tokens * lax.axis_size("ctx")
    grad_scale = 1.0 / math.sqrt(seq_len)
    dft_plan = make_plan(seq_len)
    stacked = jnp.stack([query_proj, key_proj, value_proj])
    prev_rim = from_behind(stacked[:, tokens - rim_rows :], "ctx", 1)
    extended = jnp.concatenate([prev_rim, stacked], axis=1).astype(jnp.float32)
    weights = [short_weights[:, offset, None, :] for offset in range(tap_count)]
    short_out = causal_taps(extended, weights, tokens, 1)
    product = (short_out[1] * short_out[2]).astype(jnp.bfloat16)
    cot_wide = cotangent.astype(jnp.float32)
    gate_grad = (cot_wide * short_out[0]).astype(jnp.bfloat16)
    filter_spec = receive_filter(filter_taps, dft_plan)
    prod_chan = lax.all_to_all(product.T, "ctx", split_axis=0, concat_axis=1, tiled=True)
    conv_chan, prod_spec = conv_forward(prod_chan, filter_spec, dft_plan)
    conv_tok = lax.all_to_all(conv_chan, "ctx", split_axis=1, concat_axis=0, tiled=True)
    grad_chan = lax.all_to_all(gate_grad.T, "ctx", split_axis=0, concat_axis=1, tiled=True)
    dconv_chan, dfilter_chan = conv_backward(
        grad_chan, filter_spec, prod_spec, dft_plan, grad_scale
    )
    dconv_tok = lax.all_to_all(dconv_chan, "ctx", split_axis=1, concat_axis=0, tiled=True)
    filter_grad = return_filter(dfilter_chan)
    conv_wide = conv_tok.T.astype(jnp.float32)
    dconv_wide = dconv_tok.T.astype(jnp.float32)
    gated = (short_out[0] * conv_wide).astype(jnp.bfloat16)
    token_grads = jnp.stack(
        [cot_wide * conv_wide, dconv_wide * short_out[2], dconv_wide * short_out[1]]
    )
    next_rim = from_behind(token_grads[:, :rim_rows], "ctx", -1)
    grad_ext = jnp.concatenate([token_grads, next_rim], axis=1)
    inputs_grad = reverse_taps(grad_ext, weights, tokens, 1).astype(jnp.bfloat16)
    weight_part = tap_grads(token_grads, extended, tap_count, tokens, 1)
    short_grad = lax.psum(weight_part, "ctx") * grad_scale
    results = (gated, inputs_grad[0], inputs_grad[1], inputs_grad[2])
    return (results[0], results[1], results[2], results[3], filter_grad, short_grad)


def fits(query_proj, short_weights):
    peers = lax.axis_size("ctx")
    tokens, width = query_proj.shape
    tap_count = short_weights.shape[1]
    return (
        width == peers * LANES
        and peers.bit_count() == 1
        and tokens % (PHASES * TILE) == 0
        and tap_count == RIM + 1
        and peers * tokens <= 2048
    )


def shards(*arrays):
    return channel_shards(*arrays) if fits(arrays[0], arrays[5]) else spread_shards(*arrays)


def solution(mesh):
    placed = (
        P("ctx", "tp"),
        P("ctx", "tp"),
        P("ctx", "tp"),
        P("ctx", "tp"),
        P("ctx", "tp"),
        P(None, None, "tp"),
    )
    return jax.shard_map(
        shards,
        mesh=mesh,
        in_specs=placed,
        out_specs=(
            P("ctx", "tp"),
            P("ctx", "tp"),
            P("ctx", "tp"),
            P("ctx", "tp"),
            P("ctx", "tp"),
            P(None, None, "tp"),
        ),
        check_vma=False,
    )
```

```python
import functools
import math

import jax
import jax.numpy as jnp
import numpy as np
from jax import lax
from jax.experimental import pallas as pl
from jax.experimental.pallas import tpu as pltpu
from jax.sharding import PartitionSpec as P

F32 = jnp.float32
BF16 = jnp.bfloat16
LANES = 128
PHASES = 4
TILE = 16
PAD = 8
CHUNK = 32
RIM = 2
PIECES = 3
MIB = 1024 * 1024
VMEM_LIMIT = 24 * MIB


def partners(peers):
    def rank(step):
        links = (step >> 1).bit_count()
        return (links == 0, links == 1 and step & 1, links, step & 1, -step)

    return [0] + sorted(range(1, peers), key=rank)


def exchange(blocks):
    peers = len(blocks)
    got = [blocks[0]]
    for step, block in list(zip(partners(peers), blocks))[1:]:
        got.append(lax.ppermute(block, "ctx", [(i, i ^ step) for i in range(peers)]))
    return got


def in_vmem(count):
    return [pl.BlockSpec(memory_space=pltpu.VMEM)] * count


def lanes_of(place):
    return pl.ds(pl.multiple_of(place * LANES, LANES), LANES)


def pack_kernel(count, *refs):
    sources, packed = refs[:count], refs[count:]
    tokens = sources[0].shape[0]
    me = lax.axis_index("ctx")
    for step, target in zip(partners(len(packed)), packed):
        for at, source in enumerate(sources):
            target[at * tokens : (at + 1) * tokens, :] = source[:, lanes_of(me ^ step)].astype(BF16)


def pack(arrays, peers):
    tokens = arrays[0].shape[0]
    return pl.pallas_call(
        functools.partial(pack_kernel, len(arrays)),
        in_specs=in_vmem(len(arrays)),
        out_specs=in_vmem(peers),
        out_shape=[jax.ShapeDtypeStruct((len(arrays) * tokens, LANES), BF16)] * peers,
        cost_estimate=pl.CostEstimate(flops=0, bytes_accessed=8 * MIB, transcendentals=0),
        name="pack_inputs",
    )(*arrays)


@functools.lru_cache(maxsize=None)
def dft_tables(seq_len):
    size = seq_len // PHASES
    k = np.arange(size, dtype=np.int64)[:, None]
    m = np.arange(size, dtype=np.int64)[None, :]
    forward = []
    for phase in range(PHASES):
        turns = ((4 * k + 1) * (PHASES * m + phase)) % (4 * seq_len)
        angle = 2.0 * np.pi / (4 * seq_len) * turns
        forward.append(np.concatenate([np.cos(angle), -np.sin(angle)], axis=0))
    forward = np.stack(forward)
    backward = np.swapaxes(forward, 1, 2) / seq_len

    def pieces(table):
        high = table.astype(BF16)
        low = (table - high.astype(np.float64)).astype(BF16)
        return np.stack([high, low], axis=1)

    return pieces(forward), pieces(backward)


def forward_mix(parts):
    (r0, i0), (r1, i1), (r2, i2), (r3, i3) = parts
    ar, ai, br, bi = r0 + r2, i0 + i2, r0 - r2, i0 - i2
    cr, ci, dr, di = r1 + r3, i1 + i3, r1 - r3, i1 - i3
    return ((ar + cr, ai + ci), (br + di, bi - dr), (ar - cr, ai - ci), (br - di, bi + dr))


def inverse_mix(parts):
    (r0, i0), (r1, i1), (r2, i2), (r3, i3) = parts
    ar, ai, br, bi = r0 + r2, i0 + i2, r0 - r2, i0 - i2
    cr, ci, dr, di = r1 + r3, i1 + i3, r1 - r3, i1 - i3
    return ((ar + cr, ai + ci), (br - di, bi + dr), (ar - cr, ai - ci), (br + di, bi - dr))


def times(left, right):
    return tuple(
        (lr * rr - li * ri, lr * ri + li * rr) for (lr, li), (rr, ri) in zip(left, right)
    )


def conj_times(left, right):
    return tuple(
        (lr * rr + li * ri, lr * ri - li * rr) for (lr, li), (rr, ri) in zip(left, right)
    )


def transform(tables, signal):
    return jnp.dot(tables[0], signal, preferred_element_type=F32) + jnp.dot(
        tables[1], signal, preferred_element_type=F32
    )


def phases_near(ref, chunk, tap_count):
    start = PAD + chunk * CHUNK * PHASES
    return {
        offset: ref[pl.ds(start + offset, CHUNK, stride=PHASES), :]
        for offset in range(1 - tap_count, PHASES)
    }


def short_conv(near, taps):
    results = []
    for r in range(PHASES):
        summed = taps[0] * near[r]
        for at in range(1, len(taps)):
            summed = summed + taps[at] * near[r - at]
        results.append(summed)
    return results


def add_rows(total, terms):
    for term in terms:
        folded = jnp.sum(term.reshape(CHUNK // 8, 8, LANES), axis=0)
        total = folded if total is None else total + folded
    return total


def clear_ends(ref):
    ref[:PAD, :] = jnp.zeros((PAD, LANES), F32)
    ref[ref.shape[0] - PAD :, :] = jnp.zeros((PAD, LANES), F32)


def stage_kernel(count, *refs):
    sources, targets, sems = refs[:count], refs[count + 1 : 2 * count + 1], refs[2 * count + 1]
    copies = [
        pltpu.make_async_copy(source, target, sems.at[at])
        for at, (source, target) in enumerate(zip(sources, targets))
    ]
    for copy in copies:
        copy.start()
    for copy in copies:
        copy.wait()


def stage(arrays, after):
    count = len(arrays)
    return pl.pallas_call(
        functools.partial(stage_kernel, count),
        in_specs=[pl.BlockSpec(memory_space=pl.ANY)] * (count + 1),
        out_specs=in_vmem(count),
        out_shape=[jax.ShapeDtypeStruct(array.shape, array.dtype) for array in arrays],
        scratch_shapes=[pltpu.SemaphoreType.DMA((count,))],
        compiler_params=pltpu.CompilerParams(vmem_limit_bytes=8 * MIB),
        cost_estimate=pl.CostEstimate(flops=0, bytes_accessed=8 * MIB, transcendentals=0),
        name="stage_tables",
    )(*arrays, after)


def extra_rows(short_weights):
    sums = PIECES * short_weights.shape[0] * short_weights.shape[1]
    return sums, -(-(sums + 8 * RIM) // TILE) * TILE


def channel_kernel(tokens, peers, grad_scale, *refs):
    arrived = refs[:peers]
    weights, forward, backward = refs[peers : peers + 3]
    out = refs[peers + 3 : 2 * peers + 3]
    (
        query,
        key,
        value,
        cot,
        conv,
        conv_grad,
        filter_grad,
        taps,
        key_short,
        value_short,
        signals,
        spectra,
        products,
        extra,
    ) = refs[2 * peers + 3 :]
    size = peers * tokens // PHASES
    tap_count = weights.shape[1]
    me = lax.axis_index("ctx")
    own = lanes_of(me)
    for ref in (query, key, value, cot, conv, conv_grad):
        clear_ends(ref)
    for step, source in zip(partners(peers), arrived):
        start = (me ^ step) * tokens
        inner = pl.ds(pl.multiple_of(PAD + start, PAD), tokens)
        for at, ref in enumerate((query, key, value, cot)):
            ref[inner, :] = source[at * tokens : (at + 1) * tokens, :].astype(F32)
        taps[pl.ds(pl.multiple_of(start, PAD), tokens), :] = source[4 * tokens :, :].astype(F32)
    chunks = range(size // CHUNK)
    taps_of = [
        [weights[array, tap : tap + 1, own] for tap in range(tap_count)] for array in range(3)
    ]

    def rows_of(chunk):
        return slice(chunk * CHUNK, (chunk + 1) * CHUNK)

    def spectrum(at, real, imag):
        lanes = slice(at * LANES, (at + 1) * LANES)
        return forward_mix(
            [(spectra[r, real, lanes], spectra[r, imag, lanes]) for r in range(PHASES)]
        )

    def keep(at, real, imag, mixed):
        lanes = slice(at * LANES, (at + 1) * LANES)
        for r, pair in enumerate(inverse_mix(mixed)):
            for rows, part in zip((real, imag), pair):
                products[r, rows, lanes] = part.astype(BF16)

    for chunk in chunks:
        rows = rows_of(chunk)
        key_now = short_conv(phases_near(key, chunk, tap_count), taps_of[1])
        value_now = short_conv(phases_near(value, chunk, tap_count), taps_of[2])
        for r in range(PHASES):
            key_short[r, rows, :] = key_now[r]
            value_short[r, rows, :] = value_now[r]
            signals[r, rows, :LANES] = (key_now[r] * value_now[r]).astype(BF16)
            filt = taps[pl.ds(chunk * CHUNK * PHASES + r, CHUNK, stride=PHASES), :]
            signals[r, rows, LANES : 2 * LANES] = filt.astype(BF16)
    for r in range(PHASES):
        spectra[r, :, : 2 * LANES] = transform(forward[r], signals[r, :, : 2 * LANES])
    for chunk in chunks:
        rows = rows_of(chunk)
        query_now = short_conv(phases_near(query, chunk, tap_count), taps_of[0])
        cot_now = phases_near(cot, chunk, 1)
        for r in range(PHASES):
            signals[r, rows, 2 * LANES :] = (cot_now[r] * query_now[r]).astype(BF16)
    for r in range(PHASES):
        spectra[r, :, 2 * LANES :] = transform(forward[r], signals[r, :, 2 * LANES :])
    for step in range(size // TILE):
        real = slice(step * TILE, (step + 1) * TILE)
        imag = slice(size + step * TILE, size + (step + 1) * TILE)
        prod, filt = spectrum(0, real, imag), spectrum(1, real, imag)
        for at, mixed in enumerate((prod, filt)):
            lanes = slice(at * LANES, (at + 1) * LANES)
            for q, pair in enumerate(mixed):
                spectra[q, real, lanes], spectra[q, imag, lanes] = pair
        keep(0, real, imag, times(prod, filt))
    for r in range(PHASES):
        result = transform(backward[r], products[r, :, :LANES])
        conv[pl.ds(PAD + r, size, stride=PHASES), :] = result.astype(BF16).astype(F32)
    for step in range(size // TILE):
        real = slice(step * TILE, (step + 1) * TILE)
        imag = slice(size + step * TILE, size + (step + 1) * TILE)
        grad = spectrum(2, real, imag)
        for at in range(2):
            lanes = slice(at * LANES, (at + 1) * LANES)
            known = [(spectra[q, real, lanes], spectra[q, imag, lanes]) for q in range(PHASES)]
            keep(2 - at, real, imag, conj_times(known, grad))
    for r in range(PHASES):
        result = transform(backward[r], products[r, :, LANES:])
        conv_grad[pl.ds(PAD + r, size, stride=PHASES), :] = (
            result[:, :LANES].astype(BF16).astype(F32)
        )
        filter_grad[pl.ds(r, size, stride=PHASES), :] = result[:, LANES:] * grad_scale

    totals = [[None] * tap_count for _ in range(3)]

    def add_sums(array, signal, chunk, pre):
        near = phases_near(signal, chunk, tap_count)
        for tap in range(tap_count):
            totals[array][tap] = add_rows(
                totals[array][tap], [pre[r] * near[r - tap] for r in range(PHASES)]
            )

    for chunk in chunks:
        cot_now, conv_now = phases_near(cot, chunk, 1), phases_near(conv, chunk, 1)
        add_sums(0, query, chunk, [cot_now[r] * conv_now[r] for r in range(PHASES)])
    for chunk in chunks:
        rows = rows_of(chunk)
        grad_now = phases_near(conv_grad, chunk, 1)
        add_sums(1, key, chunk, [grad_now[r] * value_short[r, rows, :] for r in range(PHASES)])
        add_sums(2, value, chunk, [grad_now[r] * key_short[r, rows, :] for r in range(PHASES)])
    sums = [jnp.sum(total, axis=0, keepdims=True) for row in totals for total in row]
    rest = jnp.concatenate(sums, axis=0) * grad_scale
    extra[...] = jnp.zeros_like(extra)
    for piece in range(PIECES):
        rounded = rest.astype(BF16).astype(F32)
        extra[piece * len(sums) : (piece + 1) * len(sums), :] = rounded
        rest = rest - rounded
    for step, target in zip(partners(peers), out):
        start = (me ^ step) * tokens
        inner = pl.ds(pl.multiple_of(PAD + start, PAD), tokens)
        target[:tokens, :] = conv[inner, :].astype(BF16)
        target[tokens : 2 * tokens, :] = conv_grad[inner, :].astype(BF16)
        target[2 * tokens : 3 * tokens, :] = filter_grad[
            pl.ds(pl.multiple_of(start, PAD), tokens), :
        ].astype(BF16)
        before = pl.ds(pl.multiple_of(start, PAD), PAD)
        after = pl.ds(pl.multiple_of(PAD + start + tokens, PAD), PAD)
        at = PIECES * len(sums)
        for ref in (query, key, value):
            extra[at : at + RIM, :] = ref[before, :][PAD - RIM :]
            at += RIM
        for ref in (cot, conv, conv_grad, key, value):
            extra[at : at + RIM, :] = ref[after, :][:RIM]
            at += RIM
        target[3 * tokens :, :] = extra[...].astype(BF16)


def channel_step(arrived, short_weights, tables, tokens):
    peers = len(arrived)
    seq_len = peers * tokens
    size = seq_len // PHASES
    extra = extra_rows(short_weights)[1]
    padded = pltpu.VMEM((seq_len + 2 * PAD, LANES), F32)
    plain = pltpu.VMEM((seq_len, LANES), F32)
    phases = pltpu.VMEM((PHASES, size, LANES), F32)
    return pl.pallas_call(
        functools.partial(channel_kernel, tokens, peers, 1.0 / math.sqrt(seq_len)),
        in_specs=in_vmem(peers + 3),
        out_specs=in_vmem(peers),
        out_shape=[jax.ShapeDtypeStruct((3 * tokens + extra, LANES), BF16)] * peers,
        scratch_shapes=[
            *[padded] * 6,
            plain,
            plain,
            phases,
            phases,
            pltpu.VMEM((PHASES, size, 3 * LANES), BF16),
            pltpu.VMEM((PHASES, 2 * size, 3 * LANES), F32),
            pltpu.VMEM((PHASES, 2 * size, 3 * LANES), BF16),
            pltpu.VMEM((extra, LANES), F32),
        ],
        compiler_params=pltpu.CompilerParams(vmem_limit_bytes=VMEM_LIMIT),
        name="channel_operator",
    )(*arrived, short_weights, *tables)


def token_kernel(peers, sum_rows, *refs):
    arrived = refs[:peers]
    query, key, value, cot, weights = refs[peers : peers + 5]
    gated, query_grad, key_grad, value_grad, filter_grad, short_grad = refs[peers + 5 : peers + 11]
    longer, pre = refs[peers + 11 :]
    tokens = query.shape[0]
    tap_count = weights.shape[1]
    count = sum_rows // PIECES
    me = lax.axis_index("ctx")
    for step, source in zip(partners(peers), arrived):
        lanes = lanes_of(me ^ step)
        extra = source[3 * tokens :, :].astype(F32)

        def rim(at):
            return extra[sum_rows + at * RIM : sum_rows + (at + 1) * RIM]

        def short(array, signal, after, rows):
            longer[array, PAD - RIM : PAD, :] = rim(array)
            longer[array, PAD : PAD + tokens, :] = signal[:, lanes].astype(F32)
            if after is not None:
                longer[array, PAD + tokens : PAD + tokens + RIM, :] = rim(after)
            summed = weights[array, 0:1, lanes] * longer[array, PAD : PAD + rows, :]
            for tap in range(1, tap_count):
                summed = (
                    summed
                    + weights[array, tap : tap + 1, lanes]
                    * longer[array, PAD - tap : PAD - tap + rows, :]
                )
            return summed

        def taps_back(array, target):
            summed = weights[array, 0:1, lanes] * pre[array, :tokens, :]
            for tap in range(1, tap_count):
                summed = (
                    summed
                    + weights[array, tap : tap + 1, lanes] * pre[array, tap : tap + tokens, :]
                )
            target[:, lanes] = summed.astype(BF16)

        conv = source[:tokens, :].astype(F32)
        gated[:, lanes] = (short(0, query, None, tokens) * conv).astype(BF16)
        pre[0, :tokens, :] = cot[:, lanes].astype(F32) * conv
        pre[0, tokens : tokens + RIM, :] = rim(3) * rim(4)
        taps_back(0, query_grad)
        key_short = short(1, key, 6, tokens + PAD)
        value_short = short(2, value, 7, tokens + PAD)
        conv_grad = source[tokens : 2 * tokens, :].astype(F32)
        for array, other in ((1, value_short), (2, key_short)):
            pre[array, :tokens, :] = conv_grad * other[:tokens]
            pre[array, tokens : tokens + RIM, :] = rim(5) * other[tokens : tokens + RIM]
        taps_back(1, key_grad)
        taps_back(2, value_grad)
        filter_grad[:, lanes] = source[2 * tokens : 3 * tokens, :].astype(F32)
        whole = extra[:count]
        for piece in range(1, PIECES):
            whole = whole + extra[piece * count : (piece + 1) * count]
        for row in range(count):
            which, tap = divmod(row, tap_count)
            short_grad[which, tap : tap + 1, lanes] = whole[row : row + 1]


def token_step(arrived, query, key, value, cot, short_weights):
    peers = len(arrived)
    tokens, width = query.shape
    wide = jax.ShapeDtypeStruct((tokens, width), BF16)
    return pl.pallas_call(
        functools.partial(token_kernel, peers, extra_rows(short_weights)[0]),
        in_specs=in_vmem(peers + 5),
        out_specs=in_vmem(6),
        out_shape=[wide] * 4
        + [
            jax.ShapeDtypeStruct((tokens, width), F32),
            jax.ShapeDtypeStruct(short_weights.shape, F32),
        ],
        scratch_shapes=[
            pltpu.VMEM((3, tokens + 2 * PAD, LANES), F32),
            pltpu.VMEM((3, tokens + PAD, LANES), F32),
        ],
        compiler_params=pltpu.CompilerParams(vmem_limit_bytes=VMEM_LIMIT),
        name="token_outputs",
    )(*arrived, query, key, value, cot, short_weights)


def channel_shards(query_proj, key_proj, value_proj, cotangent, filter_taps, short_weights):
    peers = lax.axis_size("ctx")
    tokens = query_proj.shape[0]
    tables = [jnp.asarray(table) for table in dft_tables(peers * tokens)]
    sent = pack((query_proj, key_proj, value_proj, cotangent, filter_taps), peers)
    arrived = exchange(sent)
    staged = stage((sent[0], short_weights, *tables), arrived[1])
    back = exchange(
        channel_step((staged[0], *arrived[1:]), staged[1], staged[2:], tokens)
    )
    return tuple(token_step(back, query_proj, key_proj, value_proj, cotangent, short_weights))


def from_behind(array, axis, by):
    peers = lax.axis_size(axis)
    pairs = [(i, i + by) for i in range(peers) if 0 <= i + by < peers]
    return lax.ppermute(array, axis, pairs)


def contract(form, left, right):
    return jnp.einsum(
        form, left, right, precision=lax.Precision.HIGHEST, preferred_element_type=jnp.float32
    )


def table_pair(rows, cols, period):
    row_ids = lax.broadcasted_iota(jnp.int32, (rows, cols), 0)
    col_ids = lax.broadcasted_iota(jnp.int32, (rows, cols), 1)
    angle = 2.0 * math.pi / period * (row_ids * col_ids % period).astype(jnp.float32)
    return (jnp.cos(angle), jnp.sin(angle))


def make_plan(seq_len):
    small_len = int(math.isqrt(2 * seq_len))
    while seq_len % small_len:
        small_len -= 1
    large_len = 2 * seq_len // small_len
    large_cos, large_sin = table_pair(large_len // 2, large_len, large_len)
    small_cos, small_sin = table_pair(small_len, small_len, small_len)
    twist_cos, twist_sin = table_pair(large_len, small_len, small_len * large_len)
    fwd_large = jnp.stack([large_cos, -large_sin], axis=1)
    fwd_small = jnp.stack([jnp.stack([small_cos, -small_sin]), jnp.stack([small_sin, small_cos])])
    inv_small = jnp.stack([jnp.stack([small_cos, small_sin]), jnp.stack([-small_sin, small_cos])])
    inv_large = jnp.stack([large_cos, -large_sin])
    return (small_len, large_len, fwd_large, fwd_small, inv_small, inv_large, twist_cos, twist_sin)


def forward_spec(signal, dft_plan):
    small_len, large_len, fwd_large, fwd_small, inv_small, inv_large, twist_cos, twist_sin = (
        dft_plan
    )
    cube = signal.reshape(signal.shape[0], large_len // 2, small_len)
    section_one = contract("cba,bpk->cpka", cube, fwd_large)
    real_one = section_one[:, 0]
    imag_one = section_one[:, 1]
    section_two = jnp.stack(
        [real_one * twist_cos + imag_one * twist_sin, imag_one * twist_cos - real_one * twist_sin],
        axis=1,
    )
    return contract("cpka,pqaj->cqkj", section_two, fwd_small)


def inverse_half(spec, dft_plan):
    small_len, large_len, fwd_large, fwd_small, inv_small, inv_large, twist_cos, twist_sin = (
        dft_plan
    )
    section_one = contract("cqkj,qpja->cpka", spec, inv_small)
    real_one = section_one[:, 0]
    imag_one = section_one[:, 1]
    section_two = jnp.stack(
        [real_one * twist_cos - imag_one * twist_sin, imag_one * twist_cos + real_one * twist_sin],
        axis=1,
    )
    signal = contract("cpka,pbk->cba", section_two, inv_large)
    return signal.reshape(signal.shape[0], -1) / float(small_len * large_len)


def complex_mul(left, right):
    left_real, left_imag = (left[:, 0], left[:, 1])
    right_real, right_imag = (right[:, 0], right[:, 1])
    return jnp.stack(
        [
            left_real * right_real - left_imag * right_imag,
            left_real * right_imag + left_imag * right_real,
        ],
        axis=1,
    )


def conj_mul(left, right):
    left_real, left_imag = (left[:, 0], left[:, 1])
    right_real, right_imag = (right[:, 0], right[:, 1])
    return jnp.stack(
        [
            left_real * right_real + left_imag * right_imag,
            left_real * right_imag - left_imag * right_real,
        ],
        axis=1,
    )


def conv_forward(prod_chan, filter_spec, dft_plan):
    prod_spec = forward_spec(prod_chan.astype(jnp.float32), dft_plan)
    conv_chan = inverse_half(complex_mul(prod_spec, filter_spec), dft_plan).astype(jnp.bfloat16)
    return (conv_chan, prod_spec)


def conv_backward(grad_chan, filter_spec, prod_spec, dft_plan, grad_scale):
    grad_spec = forward_spec(grad_chan.astype(jnp.float32), dft_plan)
    dconv_chan = inverse_half(conj_mul(filter_spec, grad_spec), dft_plan).astype(jnp.bfloat16)
    dfilter_chan = inverse_half(conj_mul(prod_spec, grad_spec), dft_plan) * grad_scale
    return (dconv_chan, dfilter_chan)


def receive_filter(filter_taps, dft_plan):
    filter_chan = lax.all_to_all(filter_taps.T, "ctx", split_axis=0, concat_axis=1, tiled=True)
    return forward_spec(filter_chan, dft_plan)


def return_filter(dfilter_chan):
    return (
        lax.all_to_all(
            dfilter_chan.astype(jnp.bfloat16), "ctx", split_axis=1, concat_axis=0, tiled=True
        )
        .astype(dfilter_chan.dtype)
        .T
    )


def causal_taps(extended, weights, length, axis):
    rim_rows = len(weights) - 1
    summed = weights[0] * lax.slice_in_dim(extended, rim_rows, rim_rows + length, axis=axis)
    for offset in range(1, len(weights)):
        summed = summed + weights[offset] * lax.slice_in_dim(
            extended, rim_rows - offset, rim_rows - offset + length, axis=axis
        )
    return summed


def reverse_taps(extended, weights, length, axis):
    summed = weights[0] * lax.slice_in_dim(extended, 0, length, axis=axis)
    for offset in range(1, len(weights)):
        summed = summed + weights[offset] * lax.slice_in_dim(
            extended, offset, offset + length, axis=axis
        )
    return summed


def tap_grads(grad_in, extended, tap_count, length, axis):
    rim_rows = tap_count - 1
    rows = [
        jnp.sum(
            grad_in
            * lax.slice_in_dim(extended, rim_rows - offset, rim_rows - offset + length, axis=axis),
            axis=axis,
        )
        for offset in range(tap_count)
    ]
    return jnp.stack(rows, axis=1)


def spread_shards(query_proj, key_proj, value_proj, cotangent, filter_taps, short_weights):
    tokens = query_proj.shape[0]
    tap_count = short_weights.shape[1]
    rim_rows = tap_count - 1
    seq_len = tokens * lax.axis_size("ctx")
    grad_scale = 1.0 / math.sqrt(seq_len)
    dft_plan = make_plan(seq_len)
    stacked = jnp.stack([query_proj, key_proj, value_proj])
    prev_rim = from_behind(stacked[:, tokens - rim_rows :], "ctx", 1)
    extended = jnp.concatenate([prev_rim, stacked], axis=1).astype(jnp.float32)
    weights = [short_weights[:, offset, None, :] for offset in range(tap_count)]
    short_out = causal_taps(extended, weights, tokens, 1)
    product = (short_out[1] * short_out[2]).astype(jnp.bfloat16)
    cot_wide = cotangent.astype(jnp.float32)
    gate_grad = (cot_wide * short_out[0]).astype(jnp.bfloat16)
    filter_spec = receive_filter(filter_taps, dft_plan)
    prod_chan = lax.all_to_all(product.T, "ctx", split_axis=0, concat_axis=1, tiled=True)
    conv_chan, prod_spec = conv_forward(prod_chan, filter_spec, dft_plan)
    conv_tok = lax.all_to_all(conv_chan, "ctx", split_axis=1, concat_axis=0, tiled=True)
    grad_chan = lax.all_to_all(gate_grad.T, "ctx", split_axis=0, concat_axis=1, tiled=True)
    dconv_chan, dfilter_chan = conv_backward(
        grad_chan, filter_spec, prod_spec, dft_plan, grad_scale
    )
    dconv_tok = lax.all_to_all(dconv_chan, "ctx", split_axis=1, concat_axis=0, tiled=True)
    filter_grad = return_filter(dfilter_chan)
    conv_wide = conv_tok.T.astype(jnp.float32)
    dconv_wide = dconv_tok.T.astype(jnp.float32)
    gated = (short_out[0] * conv_wide).astype(jnp.bfloat16)
    token_grads = jnp.stack(
        [cot_wide * conv_wide, dconv_wide * short_out[2], dconv_wide * short_out[1]]
    )
    next_rim = from_behind(token_grads[:, :rim_rows], "ctx", -1)
    grad_ext = jnp.concatenate([token_grads, next_rim], axis=1)
    inputs_grad = reverse_taps(grad_ext, weights, tokens, 1).astype(jnp.bfloat16)
    weight_part = tap_grads(token_grads, extended, tap_count, tokens, 1)
    short_grad = lax.psum(weight_part, "ctx") * grad_scale
    results = (gated, inputs_grad[0], inputs_grad[1], inputs_grad[2])
    return (results[0], results[1], results[2], results[3], filter_grad, short_grad)


def fits(query_proj, short_weights):
    peers = lax.axis_size("ctx")
    tokens, width = query_proj.shape
    tap_count = short_weights.shape[1]
    return (
        width == peers * LANES
        and peers.bit_count() == 1
        and tokens % (PHASES * CHUNK) == 0
        and tap_count == RIM + 1
        and peers * tokens <= 2048
    )


def shards(*arrays):
    return channel_shards(*arrays) if fits(arrays[0], arrays[5]) else spread_shards(*arrays)


def solution(mesh):
    placed = (
        P("ctx", "tp"),
        P("ctx", "tp"),
        P("ctx", "tp"),
        P("ctx", "tp"),
        P("ctx", "tp"),
        P(None, None, "tp"),
    )
    return jax.shard_map(
        shards,
        mesh=mesh,
        in_specs=placed,
        out_specs=(
            P("ctx", "tp"),
            P("ctx", "tp"),
            P("ctx", "tp"),
            P("ctx", "tp"),
            P("ctx", "tp"),
            P(None, None, "tp"),
        ),
        check_vma=False,
    )
```

```python
import functools
import math

import jax
import jax.numpy as jnp
import numpy as np
from jax import lax
from jax.experimental import pallas as pl
from jax.experimental.pallas import tpu as pltpu
from jax.sharding import PartitionSpec as P

F32 = jnp.float32
BF16 = jnp.bfloat16
LANES = 128
PHASES = 4
TILE = 16
PAD = 8
CHUNK = 32
RIM = 2
PIECES = 3
MIB = 1024 * 1024
VMEM_LIMIT = 24 * MIB


def exchange_steps(peers):
    if peers != 8:
        return [(step, step) for step in range(peers)]
    return [(0, 0), (4, 2), (2, 4), (6, 6), (7, 7), (5, 3), (3, 5), (1, 1)]


def sends_to(step, me):
    even, odd = step
    return me ^ (even + (me & 1) * (odd - even))


def hears_from(step, me):
    even, odd = step
    return sends_to((odd, even) if even & 1 else step, me)


def exchange(blocks):
    peers = len(blocks)
    got = [blocks[0]]
    for step, block in list(zip(exchange_steps(peers), blocks))[1:]:
        got.append(lax.ppermute(block, "ctx", [(i, sends_to(step, i)) for i in range(peers)]))
    return got


def in_vmem(count):
    return [pl.BlockSpec(memory_space=pltpu.VMEM)] * count


def lanes_of(place):
    return pl.ds(pl.multiple_of(place * LANES, LANES), LANES)


def pack_kernel(count, *refs):
    sources, packed = refs[:count], refs[count:]
    tokens = sources[0].shape[0]
    me = lax.axis_index("ctx")
    for step, target in zip(exchange_steps(len(packed)), packed):
        lanes = lanes_of(sends_to(step, me))
        for at, source in enumerate(sources):
            target[at * tokens : (at + 1) * tokens, :] = source[:, lanes].astype(BF16)


def pack(arrays, peers):
    tokens = arrays[0].shape[0]
    return pl.pallas_call(
        functools.partial(pack_kernel, len(arrays)),
        in_specs=in_vmem(len(arrays)),
        out_specs=in_vmem(peers),
        out_shape=[jax.ShapeDtypeStruct((len(arrays) * tokens, LANES), BF16)] * peers,
        cost_estimate=pl.CostEstimate(flops=0, bytes_accessed=8 * MIB, transcendentals=0),
        name="pack_inputs",
    )(*arrays)


@functools.lru_cache(maxsize=None)
def dft_tables(seq_len):
    size = seq_len // PHASES
    k = np.arange(size, dtype=np.int64)[:, None]
    m = np.arange(size, dtype=np.int64)[None, :]
    forward = []
    for phase in range(PHASES):
        turns = ((4 * k + 1) * (PHASES * m + phase)) % (4 * seq_len)
        angle = 2.0 * np.pi / (4 * seq_len) * turns
        forward.append(np.concatenate([np.cos(angle), -np.sin(angle)], axis=0))
    forward = np.stack(forward)
    backward = np.swapaxes(forward, 1, 2) / seq_len

    def pieces(table):
        high = table.astype(BF16)
        low = (table - high.astype(np.float64)).astype(BF16)
        return np.stack([high, low], axis=1)

    return pieces(forward), pieces(backward)


def forward_mix(parts):
    (r0, i0), (r1, i1), (r2, i2), (r3, i3) = parts
    ar, ai, br, bi = r0 + r2, i0 + i2, r0 - r2, i0 - i2
    cr, ci, dr, di = r1 + r3, i1 + i3, r1 - r3, i1 - i3
    return ((ar + cr, ai + ci), (br + di, bi - dr), (ar - cr, ai - ci), (br - di, bi + dr))


def inverse_mix(parts):
    (r0, i0), (r1, i1), (r2, i2), (r3, i3) = parts
    ar, ai, br, bi = r0 + r2, i0 + i2, r0 - r2, i0 - i2
    cr, ci, dr, di = r1 + r3, i1 + i3, r1 - r3, i1 - i3
    return ((ar + cr, ai + ci), (br - di, bi + dr), (ar - cr, ai - ci), (br + di, bi - dr))


def times(left, right):
    return tuple(
        (lr * rr - li * ri, lr * ri + li * rr) for (lr, li), (rr, ri) in zip(left, right)
    )


def conj_times(left, right):
    return tuple(
        (lr * rr + li * ri, lr * ri - li * rr) for (lr, li), (rr, ri) in zip(left, right)
    )


def transform(tables, signal):
    return jnp.dot(tables[0], signal, preferred_element_type=F32) + jnp.dot(
        tables[1], signal, preferred_element_type=F32
    )


def phases_near(ref, chunk, tap_count):
    start = PAD + chunk * CHUNK * PHASES
    return {
        offset: ref[pl.ds(start + offset, CHUNK, stride=PHASES), :]
        for offset in range(1 - tap_count, PHASES)
    }


def short_conv(near, taps):
    results = []
    for r in range(PHASES):
        summed = taps[0] * near[r]
        for at in range(1, len(taps)):
            summed = summed + taps[at] * near[r - at]
        results.append(summed)
    return results


def add_rows(total, terms):
    for term in terms:
        folded = jnp.sum(term.reshape(CHUNK // 8, 8, LANES), axis=0)
        total = folded if total is None else total + folded
    return total


def clear_ends(ref):
    ref[:PAD, :] = jnp.zeros((PAD, LANES), F32)
    ref[ref.shape[0] - PAD :, :] = jnp.zeros((PAD, LANES), F32)


def stage_kernel(count, *refs):
    sources, targets, sems = refs[:count], refs[count + 1 : 2 * count + 1], refs[2 * count + 1]
    copies = [
        pltpu.make_async_copy(source, target, sems.at[at])
        for at, (source, target) in enumerate(zip(sources, targets))
    ]
    for copy in copies:
        copy.start()
    for copy in copies:
        copy.wait()


def stage(arrays, after):
    count = len(arrays)
    return pl.pallas_call(
        functools.partial(stage_kernel, count),
        in_specs=[pl.BlockSpec(memory_space=pl.ANY)] * (count + 1),
        out_specs=in_vmem(count),
        out_shape=[jax.ShapeDtypeStruct(array.shape, array.dtype) for array in arrays],
        scratch_shapes=[pltpu.SemaphoreType.DMA((count,))],
        compiler_params=pltpu.CompilerParams(vmem_limit_bytes=8 * MIB),
        cost_estimate=pl.CostEstimate(flops=0, bytes_accessed=8 * MIB, transcendentals=0),
        name="stage_tables",
    )(*arrays, after)


def extra_rows(short_weights):
    sums = PIECES * short_weights.shape[0] * short_weights.shape[1]
    return sums, -(-(sums + 8 * RIM) // TILE) * TILE


def channel_kernel(tokens, peers, grad_scale, *refs):
    arrived = refs[:peers]
    weights, forward, backward = refs[peers : peers + 3]
    out = refs[peers + 3 : 2 * peers + 3]
    (
        query,
        key,
        value,
        cot,
        conv,
        conv_grad,
        filter_grad,
        taps,
        key_short,
        value_short,
        signals,
        spectra,
        products,
        extra,
    ) = refs[2 * peers + 3 :]
    size = peers * tokens // PHASES
    tap_count = weights.shape[1]
    me = lax.axis_index("ctx")
    own = lanes_of(me)
    for ref in (query, key, value, cot, conv, conv_grad):
        clear_ends(ref)
    for step, source in zip(exchange_steps(peers), arrived):
        start = hears_from(step, me) * tokens
        inner = pl.ds(pl.multiple_of(PAD + start, PAD), tokens)
        for at, ref in enumerate((query, key, value, cot)):
            ref[inner, :] = source[at * tokens : (at + 1) * tokens, :].astype(F32)
        taps[pl.ds(pl.multiple_of(start, PAD), tokens), :] = source[4 * tokens :, :].astype(F32)
    chunks = range(size // CHUNK)
    taps_of = [
        [weights[array, tap : tap + 1, own] for tap in range(tap_count)] for array in range(3)
    ]

    def rows_of(chunk):
        return slice(chunk * CHUNK, (chunk + 1) * CHUNK)

    def spectrum(at, real, imag):
        lanes = slice(at * LANES, (at + 1) * LANES)
        return forward_mix(
            [(spectra[r, real, lanes], spectra[r, imag, lanes]) for r in range(PHASES)]
        )

    def keep(at, real, imag, mixed):
        lanes = slice(at * LANES, (at + 1) * LANES)
        for r, pair in enumerate(inverse_mix(mixed)):
            for rows, part in zip((real, imag), pair):
                products[r, rows, lanes] = part.astype(BF16)

    for chunk in chunks:
        rows = rows_of(chunk)
        key_now = short_conv(phases_near(key, chunk, tap_count), taps_of[1])
        value_now = short_conv(phases_near(value, chunk, tap_count), taps_of[2])
        for r in range(PHASES):
            key_short[r, rows, :] = key_now[r]
            value_short[r, rows, :] = value_now[r]
            signals[r, rows, :LANES] = (key_now[r] * value_now[r]).astype(BF16)
            filt = taps[pl.ds(chunk * CHUNK * PHASES + r, CHUNK, stride=PHASES), :]
            signals[r, rows, LANES : 2 * LANES] = filt.astype(BF16)
    for r in range(PHASES):
        spectra[r, :, : 2 * LANES] = transform(forward[r], signals[r, :, : 2 * LANES])
    for chunk in chunks:
        rows = rows_of(chunk)
        query_now = short_conv(phases_near(query, chunk, tap_count), taps_of[0])
        cot_now = phases_near(cot, chunk, 1)
        for r in range(PHASES):
            signals[r, rows, 2 * LANES :] = (cot_now[r] * query_now[r]).astype(BF16)
    for r in range(PHASES):
        spectra[r, :, 2 * LANES :] = transform(forward[r], signals[r, :, 2 * LANES :])
    for step in range(size // TILE):
        real = slice(step * TILE, (step + 1) * TILE)
        imag = slice(size + step * TILE, size + (step + 1) * TILE)
        prod, filt = spectrum(0, real, imag), spectrum(1, real, imag)
        for at, mixed in enumerate((prod, filt)):
            lanes = slice(at * LANES, (at + 1) * LANES)
            for q, pair in enumerate(mixed):
                spectra[q, real, lanes], spectra[q, imag, lanes] = pair
        keep(0, real, imag, times(prod, filt))
    for r in range(PHASES):
        result = transform(backward[r], products[r, :, :LANES])
        conv[pl.ds(PAD + r, size, stride=PHASES), :] = result.astype(BF16).astype(F32)
    for step in range(size // TILE):
        real = slice(step * TILE, (step + 1) * TILE)
        imag = slice(size + step * TILE, size + (step + 1) * TILE)
        grad = spectrum(2, real, imag)
        for at in range(2):
            lanes = slice(at * LANES, (at + 1) * LANES)
            known = [(spectra[q, real, lanes], spectra[q, imag, lanes]) for q in range(PHASES)]
            keep(2 - at, real, imag, conj_times(known, grad))
    for r in range(PHASES):
        result = transform(backward[r], products[r, :, LANES:])
        conv_grad[pl.ds(PAD + r, size, stride=PHASES), :] = (
            result[:, :LANES].astype(BF16).astype(F32)
        )
        filter_grad[pl.ds(r, size, stride=PHASES), :] = result[:, LANES:] * grad_scale

    totals = [[None] * tap_count for _ in range(3)]

    def add_sums(array, signal, chunk, pre):
        near = phases_near(signal, chunk, tap_count)
        for tap in range(tap_count):
            totals[array][tap] = add_rows(
                totals[array][tap], [pre[r] * near[r - tap] for r in range(PHASES)]
            )

    for chunk in chunks:
        cot_now, conv_now = phases_near(cot, chunk, 1), phases_near(conv, chunk, 1)
        add_sums(0, query, chunk, [cot_now[r] * conv_now[r] for r in range(PHASES)])
    for chunk in chunks:
        rows = rows_of(chunk)
        grad_now = phases_near(conv_grad, chunk, 1)
        add_sums(1, key, chunk, [grad_now[r] * value_short[r, rows, :] for r in range(PHASES)])
        add_sums(2, value, chunk, [grad_now[r] * key_short[r, rows, :] for r in range(PHASES)])
    sums = [jnp.sum(total, axis=0, keepdims=True) for row in totals for total in row]
    rest = jnp.concatenate(sums, axis=0) * grad_scale
    extra[...] = jnp.zeros_like(extra)
    for piece in range(PIECES):
        rounded = rest.astype(BF16).astype(F32)
        extra[piece * len(sums) : (piece + 1) * len(sums), :] = rounded
        rest = rest - rounded
    for step, target in zip(exchange_steps(peers), out):
        start = sends_to(step, me) * tokens
        inner = pl.ds(pl.multiple_of(PAD + start, PAD), tokens)
        target[:tokens, :] = conv[inner, :].astype(BF16)
        target[tokens : 2 * tokens, :] = conv_grad[inner, :].astype(BF16)
        target[2 * tokens : 3 * tokens, :] = filter_grad[
            pl.ds(pl.multiple_of(start, PAD), tokens), :
        ].astype(BF16)
        before = pl.ds(pl.multiple_of(start, PAD), PAD)
        after = pl.ds(pl.multiple_of(PAD + start + tokens, PAD), PAD)
        at = PIECES * len(sums)
        for ref in (query, key, value):
            extra[at : at + RIM, :] = ref[before, :][PAD - RIM :]
            at += RIM
        for ref in (cot, conv, conv_grad, key, value):
            extra[at : at + RIM, :] = ref[after, :][:RIM]
            at += RIM
        target[3 * tokens :, :] = extra[...].astype(BF16)


def channel_step(arrived, short_weights, tables, tokens):
    peers = len(arrived)
    seq_len = peers * tokens
    size = seq_len // PHASES
    extra = extra_rows(short_weights)[1]
    padded = pltpu.VMEM((seq_len + 2 * PAD, LANES), F32)
    plain = pltpu.VMEM((seq_len, LANES), F32)
    phases = pltpu.VMEM((PHASES, size, LANES), F32)
    return pl.pallas_call(
        functools.partial(channel_kernel, tokens, peers, 1.0 / math.sqrt(seq_len)),
        in_specs=in_vmem(peers + 3),
        out_specs=in_vmem(peers),
        out_shape=[jax.ShapeDtypeStruct((3 * tokens + extra, LANES), BF16)] * peers,
        scratch_shapes=[
            *[padded] * 6,
            plain,
            plain,
            phases,
            phases,
            pltpu.VMEM((PHASES, size, 3 * LANES), BF16),
            pltpu.VMEM((PHASES, 2 * size, 3 * LANES), F32),
            pltpu.VMEM((PHASES, 2 * size, 3 * LANES), BF16),
            pltpu.VMEM((extra, LANES), F32),
        ],
        compiler_params=pltpu.CompilerParams(vmem_limit_bytes=VMEM_LIMIT),
        name="channel_operator",
    )(*arrived, short_weights, *tables)


def token_kernel(peers, sum_rows, *refs):
    arrived = refs[:peers]
    query, key, value, cot, weights = refs[peers : peers + 5]
    gated, query_grad, key_grad, value_grad, filter_grad, short_grad = refs[peers + 5 : peers + 11]
    longer, pre = refs[peers + 11 :]
    tokens = query.shape[0]
    tap_count = weights.shape[1]
    count = sum_rows // PIECES
    me = lax.axis_index("ctx")
    for step, source in zip(exchange_steps(peers), arrived):
        lanes = lanes_of(hears_from(step, me))
        extra = source[3 * tokens :, :].astype(F32)

        def rim(at):
            return extra[sum_rows + at * RIM : sum_rows + (at + 1) * RIM]

        def short(array, signal, after, rows):
            longer[array, PAD - RIM : PAD, :] = rim(array)
            longer[array, PAD : PAD + tokens, :] = signal[:, lanes].astype(F32)
            if after is not None:
                longer[array, PAD + tokens : PAD + tokens + RIM, :] = rim(after)
            summed = weights[array, 0:1, lanes] * longer[array, PAD : PAD + rows, :]
            for tap in range(1, tap_count):
                summed = (
                    summed
                    + weights[array, tap : tap + 1, lanes]
                    * longer[array, PAD - tap : PAD - tap + rows, :]
                )
            return summed

        def taps_back(array, target):
            summed = weights[array, 0:1, lanes] * pre[array, :tokens, :]
            for tap in range(1, tap_count):
                summed = (
                    summed
                    + weights[array, tap : tap + 1, lanes] * pre[array, tap : tap + tokens, :]
                )
            target[:, lanes] = summed.astype(BF16)

        conv = source[:tokens, :].astype(F32)
        gated[:, lanes] = (short(0, query, None, tokens) * conv).astype(BF16)
        pre[0, :tokens, :] = cot[:, lanes].astype(F32) * conv
        pre[0, tokens : tokens + RIM, :] = rim(3) * rim(4)
        taps_back(0, query_grad)
        key_short = short(1, key, 6, tokens + PAD)
        value_short = short(2, value, 7, tokens + PAD)
        conv_grad = source[tokens : 2 * tokens, :].astype(F32)
        for array, other in ((1, value_short), (2, key_short)):
            pre[array, :tokens, :] = conv_grad * other[:tokens]
            pre[array, tokens : tokens + RIM, :] = rim(5) * other[tokens : tokens + RIM]
        taps_back(1, key_grad)
        taps_back(2, value_grad)
        filter_grad[:, lanes] = source[2 * tokens : 3 * tokens, :].astype(F32)
        whole = extra[:count]
        for piece in range(1, PIECES):
            whole = whole + extra[piece * count : (piece + 1) * count]
        for row in range(count):
            which, tap = divmod(row, tap_count)
            short_grad[which, tap : tap + 1, lanes] = whole[row : row + 1]


def token_step(arrived, query, key, value, cot, short_weights):
    peers = len(arrived)
    tokens, width = query.shape
    wide = jax.ShapeDtypeStruct((tokens, width), BF16)
    return pl.pallas_call(
        functools.partial(token_kernel, peers, extra_rows(short_weights)[0]),
        in_specs=in_vmem(peers + 5),
        out_specs=in_vmem(6),
        out_shape=[wide] * 4
        + [
            jax.ShapeDtypeStruct((tokens, width), F32),
            jax.ShapeDtypeStruct(short_weights.shape, F32),
        ],
        scratch_shapes=[
            pltpu.VMEM((3, tokens + 2 * PAD, LANES), F32),
            pltpu.VMEM((3, tokens + PAD, LANES), F32),
        ],
        compiler_params=pltpu.CompilerParams(vmem_limit_bytes=VMEM_LIMIT),
        name="token_outputs",
    )(*arrived, query, key, value, cot, short_weights)


def channel_shards(query_proj, key_proj, value_proj, cotangent, filter_taps, short_weights):
    peers = lax.axis_size("ctx")
    tokens = query_proj.shape[0]
    tables = [jnp.asarray(table) for table in dft_tables(peers * tokens)]
    sent = pack((query_proj, key_proj, value_proj, cotangent, filter_taps), peers)
    arrived = exchange(sent)
    staged = stage((sent[0], short_weights, *tables), arrived[1])
    back = exchange(
        channel_step((staged[0], *arrived[1:]), staged[1], staged[2:], tokens)
    )
    return tuple(token_step(back, query_proj, key_proj, value_proj, cotangent, short_weights))


def from_behind(array, axis, by):
    peers = lax.axis_size(axis)
    pairs = [(i, i + by) for i in range(peers) if 0 <= i + by < peers]
    return lax.ppermute(array, axis, pairs)


def contract(form, left, right):
    return jnp.einsum(
        form, left, right, precision=lax.Precision.HIGHEST, preferred_element_type=jnp.float32
    )


def table_pair(rows, cols, period):
    row_ids = lax.broadcasted_iota(jnp.int32, (rows, cols), 0)
    col_ids = lax.broadcasted_iota(jnp.int32, (rows, cols), 1)
    angle = 2.0 * math.pi / period * (row_ids * col_ids % period).astype(jnp.float32)
    return (jnp.cos(angle), jnp.sin(angle))


def make_plan(seq_len):
    small_len = int(math.isqrt(2 * seq_len))
    while seq_len % small_len:
        small_len -= 1
    large_len = 2 * seq_len // small_len
    large_cos, large_sin = table_pair(large_len // 2, large_len, large_len)
    small_cos, small_sin = table_pair(small_len, small_len, small_len)
    twist_cos, twist_sin = table_pair(large_len, small_len, small_len * large_len)
    fwd_large = jnp.stack([large_cos, -large_sin], axis=1)
    fwd_small = jnp.stack([jnp.stack([small_cos, -small_sin]), jnp.stack([small_sin, small_cos])])
    inv_small = jnp.stack([jnp.stack([small_cos, small_sin]), jnp.stack([-small_sin, small_cos])])
    inv_large = jnp.stack([large_cos, -large_sin])
    return (small_len, large_len, fwd_large, fwd_small, inv_small, inv_large, twist_cos, twist_sin)


def forward_spec(signal, dft_plan):
    small_len, large_len, fwd_large, fwd_small, inv_small, inv_large, twist_cos, twist_sin = (
        dft_plan
    )
    cube = signal.reshape(signal.shape[0], large_len // 2, small_len)
    section_one = contract("cba,bpk->cpka", cube, fwd_large)
    real_one = section_one[:, 0]
    imag_one = section_one[:, 1]
    section_two = jnp.stack(
        [real_one * twist_cos + imag_one * twist_sin, imag_one * twist_cos - real_one * twist_sin],
        axis=1,
    )
    return contract("cpka,pqaj->cqkj", section_two, fwd_small)


def inverse_half(spec, dft_plan):
    small_len, large_len, fwd_large, fwd_small, inv_small, inv_large, twist_cos, twist_sin = (
        dft_plan
    )
    section_one = contract("cqkj,qpja->cpka", spec, inv_small)
    real_one = section_one[:, 0]
    imag_one = section_one[:, 1]
    section_two = jnp.stack(
        [real_one * twist_cos - imag_one * twist_sin, imag_one * twist_cos + real_one * twist_sin],
        axis=1,
    )
    signal = contract("cpka,pbk->cba", section_two, inv_large)
    return signal.reshape(signal.shape[0], -1) / float(small_len * large_len)


def complex_mul(left, right):
    left_real, left_imag = (left[:, 0], left[:, 1])
    right_real, right_imag = (right[:, 0], right[:, 1])
    return jnp.stack(
        [
            left_real * right_real - left_imag * right_imag,
            left_real * right_imag + left_imag * right_real,
        ],
        axis=1,
    )


def conj_mul(left, right):
    left_real, left_imag = (left[:, 0], left[:, 1])
    right_real, right_imag = (right[:, 0], right[:, 1])
    return jnp.stack(
        [
            left_real * right_real + left_imag * right_imag,
            left_real * right_imag - left_imag * right_real,
        ],
        axis=1,
    )


def conv_forward(prod_chan, filter_spec, dft_plan):
    prod_spec = forward_spec(prod_chan.astype(jnp.float32), dft_plan)
    conv_chan = inverse_half(complex_mul(prod_spec, filter_spec), dft_plan).astype(jnp.bfloat16)
    return (conv_chan, prod_spec)


def conv_backward(grad_chan, filter_spec, prod_spec, dft_plan, grad_scale):
    grad_spec = forward_spec(grad_chan.astype(jnp.float32), dft_plan)
    dconv_chan = inverse_half(conj_mul(filter_spec, grad_spec), dft_plan).astype(jnp.bfloat16)
    dfilter_chan = inverse_half(conj_mul(prod_spec, grad_spec), dft_plan) * grad_scale
    return (dconv_chan, dfilter_chan)


def receive_filter(filter_taps, dft_plan):
    filter_chan = lax.all_to_all(filter_taps.T, "ctx", split_axis=0, concat_axis=1, tiled=True)
    return forward_spec(filter_chan, dft_plan)


def return_filter(dfilter_chan):
    return (
        lax.all_to_all(
            dfilter_chan.astype(jnp.bfloat16), "ctx", split_axis=1, concat_axis=0, tiled=True
        )
        .astype(dfilter_chan.dtype)
        .T
    )


def causal_taps(extended, weights, length, axis):
    rim_rows = len(weights) - 1
    summed = weights[0] * lax.slice_in_dim(extended, rim_rows, rim_rows + length, axis=axis)
    for offset in range(1, len(weights)):
        summed = summed + weights[offset] * lax.slice_in_dim(
            extended, rim_rows - offset, rim_rows - offset + length, axis=axis
        )
    return summed


def reverse_taps(extended, weights, length, axis):
    summed = weights[0] * lax.slice_in_dim(extended, 0, length, axis=axis)
    for offset in range(1, len(weights)):
        summed = summed + weights[offset] * lax.slice_in_dim(
            extended, offset, offset + length, axis=axis
        )
    return summed


def tap_grads(grad_in, extended, tap_count, length, axis):
    rim_rows = tap_count - 1
    rows = [
        jnp.sum(
            grad_in
            * lax.slice_in_dim(extended, rim_rows - offset, rim_rows - offset + length, axis=axis),
            axis=axis,
        )
        for offset in range(tap_count)
    ]
    return jnp.stack(rows, axis=1)


def spread_shards(query_proj, key_proj, value_proj, cotangent, filter_taps, short_weights):
    tokens = query_proj.shape[0]
    tap_count = short_weights.shape[1]
    rim_rows = tap_count - 1
    seq_len = tokens * lax.axis_size("ctx")
    grad_scale = 1.0 / math.sqrt(seq_len)
    dft_plan = make_plan(seq_len)
    stacked = jnp.stack([query_proj, key_proj, value_proj])
    prev_rim = from_behind(stacked[:, tokens - rim_rows :], "ctx", 1)
    extended = jnp.concatenate([prev_rim, stacked], axis=1).astype(jnp.float32)
    weights = [short_weights[:, offset, None, :] for offset in range(tap_count)]
    short_out = causal_taps(extended, weights, tokens, 1)
    product = (short_out[1] * short_out[2]).astype(jnp.bfloat16)
    cot_wide = cotangent.astype(jnp.float32)
    gate_grad = (cot_wide * short_out[0]).astype(jnp.bfloat16)
    filter_spec = receive_filter(filter_taps, dft_plan)
    prod_chan = lax.all_to_all(product.T, "ctx", split_axis=0, concat_axis=1, tiled=True)
    conv_chan, prod_spec = conv_forward(prod_chan, filter_spec, dft_plan)
    conv_tok = lax.all_to_all(conv_chan, "ctx", split_axis=1, concat_axis=0, tiled=True)
    grad_chan = lax.all_to_all(gate_grad.T, "ctx", split_axis=0, concat_axis=1, tiled=True)
    dconv_chan, dfilter_chan = conv_backward(
        grad_chan, filter_spec, prod_spec, dft_plan, grad_scale
    )
    dconv_tok = lax.all_to_all(dconv_chan, "ctx", split_axis=1, concat_axis=0, tiled=True)
    filter_grad = return_filter(dfilter_chan)
    conv_wide = conv_tok.T.astype(jnp.float32)
    dconv_wide = dconv_tok.T.astype(jnp.float32)
    gated = (short_out[0] * conv_wide).astype(jnp.bfloat16)
    token_grads = jnp.stack(
        [cot_wide * conv_wide, dconv_wide * short_out[2], dconv_wide * short_out[1]]
    )
    next_rim = from_behind(token_grads[:, :rim_rows], "ctx", -1)
    grad_ext = jnp.concatenate([token_grads, next_rim], axis=1)
    inputs_grad = reverse_taps(grad_ext, weights, tokens, 1).astype(jnp.bfloat16)
    weight_part = tap_grads(token_grads, extended, tap_count, tokens, 1)
    short_grad = lax.psum(weight_part, "ctx") * grad_scale
    results = (gated, inputs_grad[0], inputs_grad[1], inputs_grad[2])
    return (results[0], results[1], results[2], results[3], filter_grad, short_grad)


def fits(query_proj, short_weights):
    peers = lax.axis_size("ctx")
    tokens, width = query_proj.shape
    tap_count = short_weights.shape[1]
    return (
        width == peers * LANES
        and peers.bit_count() == 1
        and tokens % (PHASES * CHUNK) == 0
        and tap_count == RIM + 1
        and peers * tokens <= 2048
    )


def shards(*arrays):
    return channel_shards(*arrays) if fits(arrays[0], arrays[5]) else spread_shards(*arrays)


def solution(mesh):
    placed = (
        P("ctx", "tp"),
        P("ctx", "tp"),
        P("ctx", "tp"),
        P("ctx", "tp"),
        P("ctx", "tp"),
        P(None, None, "tp"),
    )
    return jax.shard_map(
        shards,
        mesh=mesh,
        in_specs=placed,
        out_specs=(
            P("ctx", "tp"),
            P("ctx", "tp"),
            P("ctx", "tp"),
            P("ctx", "tp"),
            P("ctx", "tp"),
            P(None, None, "tp"),
        ),
        check_vma=False,
    )
```

```python
import functools
import math

import jax
import jax.numpy as jnp
import numpy as np
from jax import lax
from jax.experimental import pallas as pl
from jax.experimental.pallas import tpu as pltpu
from jax.sharding import PartitionSpec as P

F32 = jnp.float32
BF16 = jnp.bfloat16
LANES = 128
PHASES = 4
TILE = 16
PAD = 8
CHUNK = 32
RIM = 2
PIECES = 3
MIB = 1024 * 1024
VMEM_LIMIT = 24 * MIB


def partners(peers):
    def rank(step):
        links = (step >> 1).bit_count()
        return (links == 0, links == 1 and step & 1, links, step & 1, -step)

    return [0] + sorted(range(1, peers), key=rank)


def exchange(blocks):
    peers = len(blocks)
    got = [blocks[0]]
    for step, block in list(zip(partners(peers), blocks))[1:]:
        got.append(lax.ppermute(block, "ctx", [(i, i ^ step) for i in range(peers)]))
    return got


def in_vmem(count):
    return [pl.BlockSpec(memory_space=pltpu.VMEM)] * count


def lanes_of(place):
    return pl.ds(pl.multiple_of(place * LANES, LANES), LANES)


def pack_kernel(count, *refs):
    sources, taps = refs[: count - 1], refs[count - 1]
    packed, (wide, narrow, sems, taps_sems) = refs[count:-4], refs[-4:]
    tokens = taps.shape[0]
    me = lax.axis_index("ctx")
    get_taps = pltpu.make_async_copy(taps, wide, taps_sems.at[0])
    get_taps.start()
    copies = []
    steps = list(enumerate(zip(partners(len(packed)), packed)))
    for slot, (step, target) in steps[1:] + steps[:1]:
        lanes = lanes_of(me ^ step)
        for at, source in enumerate(sources):
            rows = pl.ds(at * tokens, tokens)
            copies.append(
                pltpu.make_async_copy(source.at[:, lanes], target.at[rows, :], sems.at[slot, at])
            )
            copies[-1].start()
    get_taps.wait()
    for slot, (step, target) in steps[1:] + steps[:1]:
        narrow[slot] = wide[:, lanes_of(me ^ step)].astype(BF16)
        rows = pl.ds((count - 1) * tokens, tokens)
        copies.append(
            pltpu.make_async_copy(narrow.at[slot], target.at[rows, :], taps_sems.at[1 + slot])
        )
        copies[-1].start()
    for copy in copies:
        copy.wait()


def pack(arrays, peers):
    tokens, width = arrays[0].shape
    count = len(arrays)
    return pl.pallas_call(
        functools.partial(pack_kernel, count),
        in_specs=[pl.BlockSpec(memory_space=pl.ANY)] * count,
        out_specs=[pl.BlockSpec(memory_space=pl.ANY)] * peers,
        out_shape=[jax.ShapeDtypeStruct((count * tokens, LANES), BF16)] * peers,
        scratch_shapes=[
            pltpu.VMEM((tokens, width), F32),
            pltpu.VMEM((peers, tokens, LANES), BF16),
            pltpu.SemaphoreType.DMA((peers, count - 1)),
            pltpu.SemaphoreType.DMA((peers + 1,)),
        ],
        cost_estimate=pl.CostEstimate(flops=0, bytes_accessed=8 * MIB, transcendentals=0),
        name="pack_inputs",
    )(*arrays)


@functools.lru_cache(maxsize=None)
def dft_tables(seq_len):
    size = seq_len // PHASES
    k = np.arange(size, dtype=np.int64)[:, None]
    m = np.arange(size, dtype=np.int64)[None, :]
    forward = []
    for phase in range(PHASES):
        turns = ((4 * k + 1) * (PHASES * m + phase)) % (4 * seq_len)
        angle = 2.0 * np.pi / (4 * seq_len) * turns
        forward.append(np.concatenate([np.cos(angle), -np.sin(angle)], axis=0))
    forward = np.stack(forward)
    backward = np.swapaxes(forward, 1, 2) / seq_len

    def pieces(table):
        high = table.astype(BF16)
        low = (table - high.astype(np.float64)).astype(BF16)
        return np.stack([high, low], axis=1)

    return pieces(forward), pieces(backward)


def forward_mix(parts):
    (r0, i0), (r1, i1), (r2, i2), (r3, i3) = parts
    ar, ai, br, bi = r0 + r2, i0 + i2, r0 - r2, i0 - i2
    cr, ci, dr, di = r1 + r3, i1 + i3, r1 - r3, i1 - i3
    return ((ar + cr, ai + ci), (br + di, bi - dr), (ar - cr, ai - ci), (br - di, bi + dr))


def inverse_mix(parts):
    (r0, i0), (r1, i1), (r2, i2), (r3, i3) = parts
    ar, ai, br, bi = r0 + r2, i0 + i2, r0 - r2, i0 - i2
    cr, ci, dr, di = r1 + r3, i1 + i3, r1 - r3, i1 - i3
    return ((ar + cr, ai + ci), (br - di, bi + dr), (ar - cr, ai - ci), (br + di, bi - dr))


def times(left, right):
    return tuple(
        (lr * rr - li * ri, lr * ri + li * rr) for (lr, li), (rr, ri) in zip(left, right)
    )


def conj_times(left, right):
    return tuple(
        (lr * rr + li * ri, lr * ri - li * rr) for (lr, li), (rr, ri) in zip(left, right)
    )


def transform(tables, signal):
    return jnp.dot(tables[0], signal, preferred_element_type=F32) + jnp.dot(
        tables[1], signal, preferred_element_type=F32
    )


def phases_near(ref, chunk, tap_count):
    start = PAD + chunk * CHUNK * PHASES
    return {
        offset: ref[pl.ds(start + offset, CHUNK, stride=PHASES), :]
        for offset in range(1 - tap_count, PHASES)
    }


def short_conv(near, taps):
    results = []
    for r in range(PHASES):
        summed = taps[0] * near[r]
        for at in range(1, len(taps)):
            summed = summed + taps[at] * near[r - at]
        results.append(summed)
    return results


def add_rows(total, terms):
    for term in terms:
        folded = jnp.sum(term.reshape(CHUNK // 8, 8, LANES), axis=0)
        total = folded if total is None else total + folded
    return total


def clear_ends(ref):
    ref[:PAD, :] = jnp.zeros((PAD, LANES), F32)
    ref[ref.shape[0] - PAD :, :] = jnp.zeros((PAD, LANES), F32)


def stage_kernel(count, *refs):
    sources, targets, sems = refs[:count], refs[count + 1 : 2 * count + 1], refs[2 * count + 1]
    copies = [
        pltpu.make_async_copy(source, target, sems.at[at])
        for at, (source, target) in enumerate(zip(sources, targets))
    ]
    for copy in copies:
        copy.start()
    for copy in copies:
        copy.wait()


def stage(arrays, after):
    count = len(arrays)
    return pl.pallas_call(
        functools.partial(stage_kernel, count),
        in_specs=[pl.BlockSpec(memory_space=pl.ANY)] * (count + 1),
        out_specs=in_vmem(count),
        out_shape=[jax.ShapeDtypeStruct(array.shape, array.dtype) for array in arrays],
        scratch_shapes=[pltpu.SemaphoreType.DMA((count,))],
        compiler_params=pltpu.CompilerParams(vmem_limit_bytes=8 * MIB),
        cost_estimate=pl.CostEstimate(flops=0, bytes_accessed=8 * MIB, transcendentals=0),
        name="stage_tables",
    )(*arrays, after)


def extra_rows(short_weights):
    sums = PIECES * short_weights.shape[0] * short_weights.shape[1]
    return sums, -(-(sums + 8 * RIM) // TILE) * TILE


def channel_kernel(tokens, peers, grad_scale, *refs):
    arrived = refs[:peers]
    weights, forward, backward = refs[peers : peers + 3]
    out = refs[peers + 3 : 2 * peers + 3]
    (
        query,
        key,
        value,
        cot,
        conv,
        conv_grad,
        filter_grad,
        taps,
        key_short,
        value_short,
        signals,
        spectra,
        products,
        extra,
    ) = refs[2 * peers + 3 :]
    size = peers * tokens // PHASES
    tap_count = weights.shape[1]
    me = lax.axis_index("ctx")
    own = lanes_of(me)
    for ref in (query, key, value, cot, conv, conv_grad):
        clear_ends(ref)
    for step, source in zip(partners(peers), arrived):
        start = (me ^ step) * tokens
        inner = pl.ds(pl.multiple_of(PAD + start, PAD), tokens)
        for at, ref in enumerate((query, key, value, cot)):
            ref[inner, :] = source[at * tokens : (at + 1) * tokens, :].astype(F32)
        taps[pl.ds(pl.multiple_of(start, PAD), tokens), :] = source[4 * tokens :, :].astype(F32)
    chunks = range(size // CHUNK)
    taps_of = [
        [weights[array, tap : tap + 1, own] for tap in range(tap_count)] for array in range(3)
    ]

    def rows_of(chunk):
        return slice(chunk * CHUNK, (chunk + 1) * CHUNK)

    def spectrum(at, real, imag):
        lanes = slice(at * LANES, (at + 1) * LANES)
        return forward_mix(
            [(spectra[r, real, lanes], spectra[r, imag, lanes]) for r in range(PHASES)]
        )

    def keep(at, real, imag, mixed):
        lanes = slice(at * LANES, (at + 1) * LANES)
        for r, pair in enumerate(inverse_mix(mixed)):
            for rows, part in zip((real, imag), pair):
                products[r, rows, lanes] = part.astype(BF16)

    for chunk in chunks:
        rows = rows_of(chunk)
        key_now = short_conv(phases_near(key, chunk, tap_count), taps_of[1])
        value_now = short_conv(phases_near(value, chunk, tap_count), taps_of[2])
        for r in range(PHASES):
            key_short[r, rows, :] = key_now[r]
            value_short[r, rows, :] = value_now[r]
            signals[r, rows, :LANES] = (key_now[r] * value_now[r]).astype(BF16)
            filt = taps[pl.ds(chunk * CHUNK * PHASES + r, CHUNK, stride=PHASES), :]
            signals[r, rows, LANES : 2 * LANES] = filt.astype(BF16)
    for r in range(PHASES):
        spectra[r, :, : 2 * LANES] = transform(forward[r], signals[r, :, : 2 * LANES])
    for chunk in chunks:
        rows = rows_of(chunk)
        query_now = short_conv(phases_near(query, chunk, tap_count), taps_of[0])
        cot_now = phases_near(cot, chunk, 1)
        for r in range(PHASES):
            signals[r, rows, 2 * LANES :] = (cot_now[r] * query_now[r]).astype(BF16)
    for r in range(PHASES):
        spectra[r, :, 2 * LANES :] = transform(forward[r], signals[r, :, 2 * LANES :])
    for step in range(size // TILE):
        real = slice(step * TILE, (step + 1) * TILE)
        imag = slice(size + step * TILE, size + (step + 1) * TILE)
        prod, filt = spectrum(0, real, imag), spectrum(1, real, imag)
        for at, mixed in enumerate((prod, filt)):
            lanes = slice(at * LANES, (at + 1) * LANES)
            for q, pair in enumerate(mixed):
                spectra[q, real, lanes], spectra[q, imag, lanes] = pair
        keep(0, real, imag, times(prod, filt))
    for r in range(PHASES):
        result = transform(backward[r], products[r, :, :LANES])
        conv[pl.ds(PAD + r, size, stride=PHASES), :] = result.astype(BF16).astype(F32)
    for step in range(size // TILE):
        real = slice(step * TILE, (step + 1) * TILE)
        imag = slice(size + step * TILE, size + (step + 1) * TILE)
        grad = spectrum(2, real, imag)
        for at in range(2):
            lanes = slice(at * LANES, (at + 1) * LANES)
            known = [(spectra[q, real, lanes], spectra[q, imag, lanes]) for q in range(PHASES)]
            keep(2 - at, real, imag, conj_times(known, grad))
    for r in range(PHASES):
        result = transform(backward[r], products[r, :, LANES:])
        conv_grad[pl.ds(PAD + r, size, stride=PHASES), :] = (
            result[:, :LANES].astype(BF16).astype(F32)
        )
        filter_grad[pl.ds(r, size, stride=PHASES), :] = result[:, LANES:] * grad_scale

    totals = [[None] * tap_count for _ in range(3)]

    def add_sums(array, signal, chunk, pre):
        near = phases_near(signal, chunk, tap_count)
        for tap in range(tap_count):
            totals[array][tap] = add_rows(
                totals[array][tap], [pre[r] * near[r - tap] for r in range(PHASES)]
            )

    for chunk in chunks:
        cot_now, conv_now = phases_near(cot, chunk, 1), phases_near(conv, chunk, 1)
        add_sums(0, query, chunk, [cot_now[r] * conv_now[r] for r in range(PHASES)])
    for chunk in chunks:
        rows = rows_of(chunk)
        grad_now = phases_near(conv_grad, chunk, 1)
        add_sums(1, key, chunk, [grad_now[r] * value_short[r, rows, :] for r in range(PHASES)])
        add_sums(2, value, chunk, [grad_now[r] * key_short[r, rows, :] for r in range(PHASES)])
    sums = [jnp.sum(total, axis=0, keepdims=True) for row in totals for total in row]
    rest = jnp.concatenate(sums, axis=0) * grad_scale
    extra[...] = jnp.zeros_like(extra)
    for piece in range(PIECES):
        rounded = rest.astype(BF16).astype(F32)
        extra[piece * len(sums) : (piece + 1) * len(sums), :] = rounded
        rest = rest - rounded
    for step, target in zip(partners(peers), out):
        start = (me ^ step) * tokens
        inner = pl.ds(pl.multiple_of(PAD + start, PAD), tokens)
        target[:tokens, :] = conv[inner, :].astype(BF16)
        target[tokens : 2 * tokens, :] = conv_grad[inner, :].astype(BF16)
        target[2 * tokens : 3 * tokens, :] = filter_grad[
            pl.ds(pl.multiple_of(start, PAD), tokens), :
        ].astype(BF16)
        before = pl.ds(pl.multiple_of(start, PAD), PAD)
        after = pl.ds(pl.multiple_of(PAD + start + tokens, PAD), PAD)
        at = PIECES * len(sums)
        for ref in (query, key, value):
            extra[at : at + RIM, :] = ref[before, :][PAD - RIM :]
            at += RIM
        for ref in (cot, conv, conv_grad, key, value):
            extra[at : at + RIM, :] = ref[after, :][:RIM]
            at += RIM
        target[3 * tokens :, :] = extra[...].astype(BF16)


def channel_step(arrived, short_weights, tables, tokens):
    peers = len(arrived)
    seq_len = peers * tokens
    size = seq_len // PHASES
    extra = extra_rows(short_weights)[1]
    padded = pltpu.VMEM((seq_len + 2 * PAD, LANES), F32)
    plain = pltpu.VMEM((seq_len, LANES), F32)
    phases = pltpu.VMEM((PHASES, size, LANES), F32)
    return pl.pallas_call(
        functools.partial(channel_kernel, tokens, peers, 1.0 / math.sqrt(seq_len)),
        in_specs=in_vmem(peers + 3),
        out_specs=in_vmem(peers),
        out_shape=[jax.ShapeDtypeStruct((3 * tokens + extra, LANES), BF16)] * peers,
        scratch_shapes=[
            *[padded] * 6,
            plain,
            plain,
            phases,
            phases,
            pltpu.VMEM((PHASES, size, 3 * LANES), BF16),
            pltpu.VMEM((PHASES, 2 * size, 3 * LANES), F32),
            pltpu.VMEM((PHASES, 2 * size, 3 * LANES), BF16),
            pltpu.VMEM((extra, LANES), F32),
        ],
        compiler_params=pltpu.CompilerParams(vmem_limit_bytes=VMEM_LIMIT),
        name="channel_operator",
    )(*arrived, short_weights, *tables)


def token_kernel(peers, sum_rows, *refs):
    arrived = refs[:peers]
    query, key, value, cot, weights = refs[peers : peers + 5]
    results = refs[peers + 5 : peers + 11]
    longer, pre, sems = refs[peers + 17 :]
    gated, query_grad, key_grad, value_grad, filter_grad, short_grad = refs[peers + 11 : peers + 17]
    copies = []
    tokens = query.shape[0]
    tap_count = weights.shape[1]
    count = sum_rows // PIECES
    me = lax.axis_index("ctx")
    for slot, (step, source) in enumerate(zip(partners(peers), arrived)):
        lanes = lanes_of(me ^ step)
        extra = source[3 * tokens :, :].astype(F32)

        def rim(at):
            return extra[sum_rows + at * RIM : sum_rows + (at + 1) * RIM]

        def short(array, signal, after, rows):
            longer[array, PAD - RIM : PAD, :] = rim(array)
            longer[array, PAD : PAD + tokens, :] = signal[:, lanes].astype(F32)
            if after is not None:
                longer[array, PAD + tokens : PAD + tokens + RIM, :] = rim(after)
            summed = weights[array, 0:1, lanes] * longer[array, PAD : PAD + rows, :]
            for tap in range(1, tap_count):
                summed = (
                    summed
                    + weights[array, tap : tap + 1, lanes]
                    * longer[array, PAD - tap : PAD - tap + rows, :]
                )
            return summed

        def taps_back(array, target):
            summed = weights[array, 0:1, lanes] * pre[array, :tokens, :]
            for tap in range(1, tap_count):
                summed = (
                    summed
                    + weights[array, tap : tap + 1, lanes] * pre[array, tap : tap + tokens, :]
                )
            target[:, lanes] = summed.astype(BF16)

        conv = source[:tokens, :].astype(F32)
        gated[:, lanes] = (short(0, query, None, tokens) * conv).astype(BF16)
        pre[0, :tokens, :] = cot[:, lanes].astype(F32) * conv
        pre[0, tokens : tokens + RIM, :] = rim(3) * rim(4)
        taps_back(0, query_grad)
        key_short = short(1, key, 6, tokens + PAD)
        value_short = short(2, value, 7, tokens + PAD)
        conv_grad = source[tokens : 2 * tokens, :].astype(F32)
        for array, other in ((1, value_short), (2, key_short)):
            pre[array, :tokens, :] = conv_grad * other[:tokens]
            pre[array, tokens : tokens + RIM, :] = rim(5) * other[tokens : tokens + RIM]
        taps_back(1, key_grad)
        taps_back(2, value_grad)
        filter_grad[:, lanes] = source[2 * tokens : 3 * tokens, :].astype(F32)
        whole = extra[:count]
        for piece in range(1, PIECES):
            whole = whole + extra[piece * count : (piece + 1) * count]
        for row in range(count):
            which, tap = divmod(row, tap_count)
            short_grad[which, tap : tap + 1, lanes] = whole[row : row + 1]
        for at, held in enumerate((gated, query_grad, key_grad, value_grad, filter_grad)):
            copies.append(
                pltpu.make_async_copy(
                    held.at[:, lanes], results[at].at[:, lanes], sems.at[slot, at]
                )
            )
            copies[-1].start()
    copies.append(pltpu.make_async_copy(short_grad, results[5], sems.at[peers, 0]))
    copies[-1].start()
    for copy in copies:
        copy.wait()


def token_step(arrived, query, key, value, cot, short_weights):
    peers = len(arrived)
    tokens, width = query.shape
    wide = jax.ShapeDtypeStruct((tokens, width), BF16)
    return pl.pallas_call(
        functools.partial(token_kernel, peers, extra_rows(short_weights)[0]),
        in_specs=in_vmem(peers + 5),
        out_specs=[pl.BlockSpec(memory_space=pl.ANY)] * 6,
        out_shape=[wide] * 4
        + [
            jax.ShapeDtypeStruct((tokens, width), F32),
            jax.ShapeDtypeStruct(short_weights.shape, F32),
        ],
        scratch_shapes=[
            *[pltpu.VMEM((tokens, width), BF16)] * 4,
            pltpu.VMEM((tokens, width), F32),
            pltpu.VMEM(short_weights.shape, F32),
            pltpu.VMEM((3, tokens + 2 * PAD, LANES), F32),
            pltpu.VMEM((3, tokens + PAD, LANES), F32),
            pltpu.SemaphoreType.DMA((peers + 1, 5)),
        ],
        compiler_params=pltpu.CompilerParams(vmem_limit_bytes=VMEM_LIMIT),
        name="token_outputs",
    )(*arrived, query, key, value, cot, short_weights)


def channel_shards(query_proj, key_proj, value_proj, cotangent, filter_taps, short_weights):
    peers = lax.axis_size("ctx")
    tokens = query_proj.shape[0]
    tables = [jnp.asarray(table) for table in dft_tables(peers * tokens)]
    sent = pack((query_proj, key_proj, value_proj, cotangent, filter_taps), peers)
    arrived = exchange(sent)
    staged = stage((sent[0], short_weights, *tables), arrived[1])
    back = exchange(
        channel_step((staged[0], *arrived[1:]), staged[1], staged[2:], tokens)
    )
    return tuple(token_step(back, query_proj, key_proj, value_proj, cotangent, short_weights))


def from_behind(array, axis, by):
    peers = lax.axis_size(axis)
    pairs = [(i, i + by) for i in range(peers) if 0 <= i + by < peers]
    return lax.ppermute(array, axis, pairs)


def contract(form, left, right):
    return jnp.einsum(
        form, left, right, precision=lax.Precision.HIGHEST, preferred_element_type=jnp.float32
    )


def table_pair(rows, cols, period):
    row_ids = lax.broadcasted_iota(jnp.int32, (rows, cols), 0)
    col_ids = lax.broadcasted_iota(jnp.int32, (rows, cols), 1)
    angle = 2.0 * math.pi / period * (row_ids * col_ids % period).astype(jnp.float32)
    return (jnp.cos(angle), jnp.sin(angle))


def make_plan(seq_len):
    small_len = int(math.isqrt(2 * seq_len))
    while seq_len % small_len:
        small_len -= 1
    large_len = 2 * seq_len // small_len
    large_cos, large_sin = table_pair(large_len // 2, large_len, large_len)
    small_cos, small_sin = table_pair(small_len, small_len, small_len)
    twist_cos, twist_sin = table_pair(large_len, small_len, small_len * large_len)
    fwd_large = jnp.stack([large_cos, -large_sin], axis=1)
    fwd_small = jnp.stack([jnp.stack([small_cos, -small_sin]), jnp.stack([small_sin, small_cos])])
    inv_small = jnp.stack([jnp.stack([small_cos, small_sin]), jnp.stack([-small_sin, small_cos])])
    inv_large = jnp.stack([large_cos, -large_sin])
    return (small_len, large_len, fwd_large, fwd_small, inv_small, inv_large, twist_cos, twist_sin)


def forward_spec(signal, dft_plan):
    small_len, large_len, fwd_large, fwd_small, inv_small, inv_large, twist_cos, twist_sin = (
        dft_plan
    )
    cube = signal.reshape(signal.shape[0], large_len // 2, small_len)
    section_one = contract("cba,bpk->cpka", cube, fwd_large)
    real_one = section_one[:, 0]
    imag_one = section_one[:, 1]
    section_two = jnp.stack(
        [real_one * twist_cos + imag_one * twist_sin, imag_one * twist_cos - real_one * twist_sin],
        axis=1,
    )
    return contract("cpka,pqaj->cqkj", section_two, fwd_small)


def inverse_half(spec, dft_plan):
    small_len, large_len, fwd_large, fwd_small, inv_small, inv_large, twist_cos, twist_sin = (
        dft_plan
    )
    section_one = contract("cqkj,qpja->cpka", spec, inv_small)
    real_one = section_one[:, 0]
    imag_one = section_one[:, 1]
    section_two = jnp.stack(
        [real_one * twist_cos - imag_one * twist_sin, imag_one * twist_cos + real_one * twist_sin],
        axis=1,
    )
    signal = contract("cpka,pbk->cba", section_two, inv_large)
    return signal.reshape(signal.shape[0], -1) / float(small_len * large_len)


def complex_mul(left, right):
    left_real, left_imag = (left[:, 0], left[:, 1])
    right_real, right_imag = (right[:, 0], right[:, 1])
    return jnp.stack(
        [
            left_real * right_real - left_imag * right_imag,
            left_real * right_imag + left_imag * right_real,
        ],
        axis=1,
    )


def conj_mul(left, right):
    left_real, left_imag = (left[:, 0], left[:, 1])
    right_real, right_imag = (right[:, 0], right[:, 1])
    return jnp.stack(
        [
            left_real * right_real + left_imag * right_imag,
            left_real * right_imag - left_imag * right_real,
        ],
        axis=1,
    )


def conv_forward(prod_chan, filter_spec, dft_plan):
    prod_spec = forward_spec(prod_chan.astype(jnp.float32), dft_plan)
    conv_chan = inverse_half(complex_mul(prod_spec, filter_spec), dft_plan).astype(jnp.bfloat16)
    return (conv_chan, prod_spec)


def conv_backward(grad_chan, filter_spec, prod_spec, dft_plan, grad_scale):
    grad_spec = forward_spec(grad_chan.astype(jnp.float32), dft_plan)
    dconv_chan = inverse_half(conj_mul(filter_spec, grad_spec), dft_plan).astype(jnp.bfloat16)
    dfilter_chan = inverse_half(conj_mul(prod_spec, grad_spec), dft_plan) * grad_scale
    return (dconv_chan, dfilter_chan)


def receive_filter(filter_taps, dft_plan):
    filter_chan = lax.all_to_all(filter_taps.T, "ctx", split_axis=0, concat_axis=1, tiled=True)
    return forward_spec(filter_chan, dft_plan)


def return_filter(dfilter_chan):
    return (
        lax.all_to_all(
            dfilter_chan.astype(jnp.bfloat16), "ctx", split_axis=1, concat_axis=0, tiled=True
        )
        .astype(dfilter_chan.dtype)
        .T
    )


def causal_taps(extended, weights, length, axis):
    rim_rows = len(weights) - 1
    summed = weights[0] * lax.slice_in_dim(extended, rim_rows, rim_rows + length, axis=axis)
    for offset in range(1, len(weights)):
        summed = summed + weights[offset] * lax.slice_in_dim(
            extended, rim_rows - offset, rim_rows - offset + length, axis=axis
        )
    return summed


def reverse_taps(extended, weights, length, axis):
    summed = weights[0] * lax.slice_in_dim(extended, 0, length, axis=axis)
    for offset in range(1, len(weights)):
        summed = summed + weights[offset] * lax.slice_in_dim(
            extended, offset, offset + length, axis=axis
        )
    return summed


def tap_grads(grad_in, extended, tap_count, length, axis):
    rim_rows = tap_count - 1
    rows = [
        jnp.sum(
            grad_in
            * lax.slice_in_dim(extended, rim_rows - offset, rim_rows - offset + length, axis=axis),
            axis=axis,
        )
        for offset in range(tap_count)
    ]
    return jnp.stack(rows, axis=1)


def spread_shards(query_proj, key_proj, value_proj, cotangent, filter_taps, short_weights):
    tokens = query_proj.shape[0]
    tap_count = short_weights.shape[1]
    rim_rows = tap_count - 1
    seq_len = tokens * lax.axis_size("ctx")
    grad_scale = 1.0 / math.sqrt(seq_len)
    dft_plan = make_plan(seq_len)
    stacked = jnp.stack([query_proj, key_proj, value_proj])
    prev_rim = from_behind(stacked[:, tokens - rim_rows :], "ctx", 1)
    extended = jnp.concatenate([prev_rim, stacked], axis=1).astype(jnp.float32)
    weights = [short_weights[:, offset, None, :] for offset in range(tap_count)]
    short_out = causal_taps(extended, weights, tokens, 1)
    product = (short_out[1] * short_out[2]).astype(jnp.bfloat16)
    cot_wide = cotangent.astype(jnp.float32)
    gate_grad = (cot_wide * short_out[0]).astype(jnp.bfloat16)
    filter_spec = receive_filter(filter_taps, dft_plan)
    prod_chan = lax.all_to_all(product.T, "ctx", split_axis=0, concat_axis=1, tiled=True)
    conv_chan, prod_spec = conv_forward(prod_chan, filter_spec, dft_plan)
    conv_tok = lax.all_to_all(conv_chan, "ctx", split_axis=1, concat_axis=0, tiled=True)
    grad_chan = lax.all_to_all(gate_grad.T, "ctx", split_axis=0, concat_axis=1, tiled=True)
    dconv_chan, dfilter_chan = conv_backward(
        grad_chan, filter_spec, prod_spec, dft_plan, grad_scale
    )
    dconv_tok = lax.all_to_all(dconv_chan, "ctx", split_axis=1, concat_axis=0, tiled=True)
    filter_grad = return_filter(dfilter_chan)
    conv_wide = conv_tok.T.astype(jnp.float32)
    dconv_wide = dconv_tok.T.astype(jnp.float32)
    gated = (short_out[0] * conv_wide).astype(jnp.bfloat16)
    token_grads = jnp.stack(
        [cot_wide * conv_wide, dconv_wide * short_out[2], dconv_wide * short_out[1]]
    )
    next_rim = from_behind(token_grads[:, :rim_rows], "ctx", -1)
    grad_ext = jnp.concatenate([token_grads, next_rim], axis=1)
    inputs_grad = reverse_taps(grad_ext, weights, tokens, 1).astype(jnp.bfloat16)
    weight_part = tap_grads(token_grads, extended, tap_count, tokens, 1)
    short_grad = lax.psum(weight_part, "ctx") * grad_scale
    results = (gated, inputs_grad[0], inputs_grad[1], inputs_grad[2])
    return (results[0], results[1], results[2], results[3], filter_grad, short_grad)


def fits(query_proj, short_weights):
    peers = lax.axis_size("ctx")
    tokens, width = query_proj.shape
    tap_count = short_weights.shape[1]
    return (
        width == peers * LANES
        and peers.bit_count() == 1
        and tokens % (PHASES * CHUNK) == 0
        and tap_count == RIM + 1
        and peers * tokens <= 2048
    )


def shards(*arrays):
    return channel_shards(*arrays) if fits(arrays[0], arrays[5]) else spread_shards(*arrays)


def solution(mesh):
    placed = (
        P("ctx", "tp"),
        P("ctx", "tp"),
        P("ctx", "tp"),
        P("ctx", "tp"),
        P("ctx", "tp"),
        P(None, None, "tp"),
    )
    return jax.shard_map(
        shards,
        mesh=mesh,
        in_specs=placed,
        out_specs=(
            P("ctx", "tp"),
            P("ctx", "tp"),
            P("ctx", "tp"),
            P("ctx", "tp"),
            P("ctx", "tp"),
            P(None, None, "tp"),
        ),
        check_vma=False,
    )
```

```python
import functools
import math

import jax
import jax.numpy as jnp
import numpy as np
from jax import lax
from jax.experimental import pallas as pl
from jax.experimental.pallas import tpu as pltpu
from jax.sharding import PartitionSpec as P

F32 = jnp.float32
BF16 = jnp.bfloat16
LANES = 128
PHASES = 4
TILE = 16
PAD = 8
CHUNK = 32
RIM = 2
PIECES = 2
MIB = 1024 * 1024
VMEM_LIMIT = 24 * MIB


def partners(peers):
    def rank(step):
        links = (step >> 1).bit_count()
        return (-links, step & 1, -step)

    return [0] + sorted(range(1, peers), key=rank)


def exchange(blocks):
    peers = len(blocks)
    got = [blocks[0]]
    for step, block in list(zip(partners(peers), blocks))[1:]:
        got.append(lax.ppermute(block, "ctx", [(i, i ^ step) for i in range(peers)]))
    return got


def in_vmem(count):
    return [pl.BlockSpec(memory_space=pltpu.VMEM)] * count


def lanes_of(place):
    return pl.ds(pl.multiple_of(place * LANES, LANES), LANES)


def pack_kernel(count, peers, *refs):
    sources, packed = refs[:count], refs[count : count + peers]
    held, blocks = refs[count + peers : 2 * count + peers], refs[2 * count + peers]
    in_sems, out_sems = refs[2 * count + peers + 1 :]
    tokens = sources[0].shape[0]
    me = lax.axis_index("ctx")
    arriving = [
        pltpu.make_async_copy(source, target, in_sems.at[at])
        for at, (source, target) in enumerate(zip(sources, held))
    ]
    for copy in arriving:
        copy.start()
    leaving = []
    for at, source in enumerate(held):
        arriving[at].wait()
        rows = pl.ds(at * tokens, tokens)
        for slot, step in enumerate(partners(peers)):
            blocks[slot, rows, :] = source[:, lanes_of(me ^ step)].astype(BF16)
            leaving.append(
                pltpu.make_async_copy(
                    blocks.at[slot, rows, :], packed[slot].at[rows, :], out_sems.at[slot, at]
                )
            )
            leaving[-1].start()
    for copy in leaving:
        copy.wait()


def pack(arrays, peers):
    tokens = arrays[0].shape[0]
    count = len(arrays)
    return pl.pallas_call(
        functools.partial(pack_kernel, count, peers),
        in_specs=[pl.BlockSpec(memory_space=pl.ANY)] * count,
        out_specs=[pl.BlockSpec(memory_space=pl.ANY)] * peers,
        out_shape=[jax.ShapeDtypeStruct((count * tokens, LANES), BF16)] * peers,
        scratch_shapes=[
            *[pltpu.VMEM(array.shape, array.dtype) for array in arrays],
            pltpu.VMEM((peers, count * tokens, LANES), BF16),
            pltpu.SemaphoreType.DMA((count,)),
            pltpu.SemaphoreType.DMA((peers, count)),
        ],
        cost_estimate=pl.CostEstimate(flops=0, bytes_accessed=8 * MIB, transcendentals=0),
        name="pack_inputs",
    )(*arrays)


@functools.lru_cache(maxsize=None)
def dft_tables(seq_len):
    size = seq_len // PHASES
    k = np.arange(size, dtype=np.int64)[:, None]
    m = np.arange(size, dtype=np.int64)[None, :]
    forward = []
    for phase in range(PHASES):
        turns = ((4 * k + 1) * (PHASES * m + phase)) % (4 * seq_len)
        angle = 2.0 * np.pi / (4 * seq_len) * turns
        forward.append(np.concatenate([np.cos(angle), -np.sin(angle)], axis=0))
    forward = np.stack(forward)
    backward = np.swapaxes(forward, 1, 2) / seq_len

    def pieces(table):
        high = table.astype(BF16)
        low = (table - high.astype(np.float64)).astype(BF16)
        return np.stack([high, low], axis=1)

    return pieces(forward), pieces(backward)


def forward_mix(parts):
    (r0, i0), (r1, i1), (r2, i2), (r3, i3) = parts
    ar, ai, br, bi = r0 + r2, i0 + i2, r0 - r2, i0 - i2
    cr, ci, dr, di = r1 + r3, i1 + i3, r1 - r3, i1 - i3
    return ((ar + cr, ai + ci), (br + di, bi - dr), (ar - cr, ai - ci), (br - di, bi + dr))


def inverse_mix(parts):
    (r0, i0), (r1, i1), (r2, i2), (r3, i3) = parts
    ar, ai, br, bi = r0 + r2, i0 + i2, r0 - r2, i0 - i2
    cr, ci, dr, di = r1 + r3, i1 + i3, r1 - r3, i1 - i3
    return ((ar + cr, ai + ci), (br - di, bi + dr), (ar - cr, ai - ci), (br + di, bi - dr))


def times(left, right):
    return tuple(
        (lr * rr - li * ri, lr * ri + li * rr) for (lr, li), (rr, ri) in zip(left, right)
    )


def conj_times(left, right):
    return tuple(
        (lr * rr + li * ri, lr * ri - li * rr) for (lr, li), (rr, ri) in zip(left, right)
    )


def transform(tables, signal):
    return jnp.dot(tables[0], signal, preferred_element_type=F32) + jnp.dot(
        tables[1], signal, preferred_element_type=F32
    )


def phases_near(ref, chunk, tap_count):
    start = PAD + chunk * CHUNK * PHASES
    return {
        offset: ref[pl.ds(start + offset, CHUNK, stride=PHASES), :]
        for offset in range(1 - tap_count, PHASES)
    }


def short_conv(near, taps):
    results = []
    for r in range(PHASES):
        summed = taps[0] * near[r]
        for at in range(1, len(taps)):
            summed = summed + taps[at] * near[r - at]
        results.append(summed)
    return results


def add_rows(total, terms):
    for term in terms:
        folded = jnp.sum(term.reshape(CHUNK // 8, 8, LANES), axis=0)
        total = folded if total is None else total + folded
    return total


def clear_ends(ref):
    ref[:PAD, :] = jnp.zeros((PAD, LANES), F32)
    ref[ref.shape[0] - PAD :, :] = jnp.zeros((PAD, LANES), F32)


def stage_kernel(count, *refs):
    sources, targets, sems = refs[:count], refs[count + 1 : 2 * count + 1], refs[2 * count + 1]
    copies = [
        pltpu.make_async_copy(source, target, sems.at[at])
        for at, (source, target) in enumerate(zip(sources, targets))
    ]
    for copy in copies:
        copy.start()
    for copy in copies:
        copy.wait()


def stage(arrays, after):
    count = len(arrays)
    return pl.pallas_call(
        functools.partial(stage_kernel, count),
        in_specs=[pl.BlockSpec(memory_space=pl.ANY)] * (count + 1),
        out_specs=in_vmem(count),
        out_shape=[jax.ShapeDtypeStruct(array.shape, array.dtype) for array in arrays],
        scratch_shapes=[pltpu.SemaphoreType.DMA((count,))],
        compiler_params=pltpu.CompilerParams(vmem_limit_bytes=8 * MIB),
        cost_estimate=pl.CostEstimate(flops=0, bytes_accessed=8 * MIB, transcendentals=0),
        name="stage_tables",
    )(*arrays, after)


def extra_rows(short_weights):
    sums = PIECES * short_weights.shape[0] * short_weights.shape[1]
    return sums, -(-(sums + 6 * RIM) // TILE) * TILE


def channel_kernel(tokens, peers, grad_scale, *refs):
    arrived = refs[:peers]
    weights, forward, backward = refs[peers : peers + 3]
    out = refs[peers + 3 : 2 * peers + 3]
    (
        query,
        key,
        value,
        cot,
        conv,
        conv_grad,
        filter_grad,
        taps,
        key_short,
        value_short,
        signals,
        spectra,
        products,
        extra,
    ) = refs[2 * peers + 3 :]
    size = peers * tokens // PHASES
    tap_count = weights.shape[1]
    me = lax.axis_index("ctx")
    own = lanes_of(me)
    for ref in (query, key, value, cot, conv, conv_grad):
        clear_ends(ref)
    for ref in (key_short, value_short):
        ref[:, size:, :] = jnp.zeros((PHASES, PAD, LANES), F32)
    for step, source in zip(partners(peers), arrived):
        start = (me ^ step) * tokens
        inner = pl.ds(pl.multiple_of(PAD + start, PAD), tokens)
        for at, ref in enumerate((query, key, value, cot)):
            ref[inner, :] = source[at * tokens : (at + 1) * tokens, :].astype(F32)
        taps[pl.ds(pl.multiple_of(start, PAD), tokens), :] = source[4 * tokens :, :].astype(F32)
    chunks = range(size // CHUNK)
    taps_of = [
        [weights[array, tap : tap + 1, own] for tap in range(tap_count)] for array in range(3)
    ]

    def rows_of(chunk):
        return slice(chunk * CHUNK, (chunk + 1) * CHUNK)

    def spectrum(at, real, imag):
        lanes = slice(at * LANES, (at + 1) * LANES)
        return forward_mix(
            [(spectra[r, real, lanes], spectra[r, imag, lanes]) for r in range(PHASES)]
        )

    def keep(at, real, imag, mixed):
        lanes = slice(at * LANES, (at + 1) * LANES)
        for r, pair in enumerate(inverse_mix(mixed)):
            for rows, part in zip((real, imag), pair):
                products[r, rows, lanes] = part.astype(BF16)

    for chunk in chunks:
        rows = rows_of(chunk)
        key_now = short_conv(phases_near(key, chunk, tap_count), taps_of[1])
        value_now = short_conv(phases_near(value, chunk, tap_count), taps_of[2])
        for r in range(PHASES):
            key_short[r, rows, :] = key_now[r]
            value_short[r, rows, :] = value_now[r]
            signals[r, rows, :LANES] = (key_now[r] * value_now[r]).astype(BF16)
            filt = taps[pl.ds(chunk * CHUNK * PHASES + r, CHUNK, stride=PHASES), :]
            signals[r, rows, LANES : 2 * LANES] = filt.astype(BF16)
    for r in range(PHASES):
        spectra[r, :, : 2 * LANES] = transform(forward[r], signals[r, :, : 2 * LANES])
    for chunk in chunks:
        rows = rows_of(chunk)
        query_now = short_conv(phases_near(query, chunk, tap_count), taps_of[0])
        cot_now = phases_near(cot, chunk, 1)
        for r in range(PHASES):
            signals[r, rows, 2 * LANES :] = (cot_now[r] * query_now[r]).astype(BF16)
    for r in range(PHASES):
        spectra[r, :, 2 * LANES :] = transform(forward[r], signals[r, :, 2 * LANES :])
    for step in range(size // TILE):
        real = slice(step * TILE, (step + 1) * TILE)
        imag = slice(size + step * TILE, size + (step + 1) * TILE)
        prod, filt = spectrum(0, real, imag), spectrum(1, real, imag)
        for at, mixed in enumerate((prod, filt)):
            lanes = slice(at * LANES, (at + 1) * LANES)
            for q, pair in enumerate(mixed):
                spectra[q, real, lanes], spectra[q, imag, lanes] = pair
        keep(0, real, imag, times(prod, filt))
    for r in range(PHASES):
        result = transform(backward[r], products[r, :, :LANES])
        conv[pl.ds(PAD + r, size, stride=PHASES), :] = result.astype(BF16).astype(F32)
    for step in range(size // TILE):
        real = slice(step * TILE, (step + 1) * TILE)
        imag = slice(size + step * TILE, size + (step + 1) * TILE)
        grad = spectrum(2, real, imag)
        for at in range(2):
            lanes = slice(at * LANES, (at + 1) * LANES)
            known = [(spectra[q, real, lanes], spectra[q, imag, lanes]) for q in range(PHASES)]
            keep(2 - at, real, imag, conj_times(known, grad))
    for r in range(PHASES):
        result = transform(backward[r], products[r, :, LANES:])
        conv_grad[pl.ds(PAD + r, size, stride=PHASES), :] = (
            result[:, :LANES].astype(BF16).astype(F32)
        )
        filter_grad[pl.ds(r, size, stride=PHASES), :] = result[:, LANES:] * grad_scale

    totals = [[None] * tap_count for _ in range(3)]

    def add_sums(array, signal, chunk, pre):
        near = phases_near(signal, chunk, tap_count)
        for tap in range(tap_count):
            totals[array][tap] = add_rows(
                totals[array][tap], [pre[r] * near[r - tap] for r in range(PHASES)]
            )

    for chunk in chunks:
        cot_now, conv_now = phases_near(cot, chunk, 1), phases_near(conv, chunk, 1)
        add_sums(0, query, chunk, [cot_now[r] * conv_now[r] for r in range(PHASES)])
    for chunk in chunks:
        rows = rows_of(chunk)
        grad_now = phases_near(conv_grad, chunk, 1)
        add_sums(1, key, chunk, [grad_now[r] * value_short[r, rows, :] for r in range(PHASES)])
        add_sums(2, value, chunk, [grad_now[r] * key_short[r, rows, :] for r in range(PHASES)])
    sums = [jnp.sum(total, axis=0, keepdims=True) for row in totals for total in row]
    rest = jnp.concatenate(sums, axis=0) * grad_scale
    extra[...] = jnp.zeros_like(extra)
    for piece in range(PIECES):
        rounded = rest.astype(BF16).astype(F32)
        extra[piece * len(sums) : (piece + 1) * len(sums), :] = rounded
        rest = rest - rounded
    for step, target in zip(partners(peers), out):
        start = (me ^ step) * tokens
        inner = pl.ds(pl.multiple_of(PAD + start, PAD), tokens)
        target[:tokens, :] = conv[inner, :].astype(BF16)
        target[tokens : 2 * tokens, :] = conv_grad[inner, :].astype(BF16)
        target[2 * tokens : 3 * tokens, :] = filter_grad[
            pl.ds(pl.multiple_of(start, PAD), tokens), :
        ].astype(BF16)
        before = pl.ds(pl.multiple_of(start, PAD), PAD)
        after = pl.ds(pl.multiple_of(PAD + start + tokens, PAD), PAD)
        at = PIECES * len(sums)
        for ref in (query, key, value):
            extra[at : at + RIM, :] = ref[before, :][PAD - RIM :]
            at += RIM
        row = pl.ds(pl.multiple_of((start + tokens) // PHASES, PAD), PAD)
        extra[at : at + RIM, :] = (cot[after, :] * conv[after, :])[:RIM]
        for short in (value_short, key_short):
            at += RIM
            shorts = jnp.concatenate([short[r, row, :][:1] for r in range(RIM)], axis=0)
            extra[at : at + RIM, :] = conv_grad[after, :][:RIM] * shorts
        target[3 * tokens :, :] = extra[...].astype(BF16)


def channel_step(arrived, short_weights, tables, tokens):
    peers = len(arrived)
    seq_len = peers * tokens
    size = seq_len // PHASES
    extra = extra_rows(short_weights)[1]
    padded = pltpu.VMEM((seq_len + 2 * PAD, LANES), F32)
    plain = pltpu.VMEM((seq_len, LANES), F32)
    phases = pltpu.VMEM((PHASES, size + PAD, LANES), F32)
    return pl.pallas_call(
        functools.partial(channel_kernel, tokens, peers, 1.0 / math.sqrt(seq_len)),
        in_specs=in_vmem(peers + 3),
        out_specs=in_vmem(peers),
        out_shape=[jax.ShapeDtypeStruct((3 * tokens + extra, LANES), BF16)] * peers,
        scratch_shapes=[
            *[padded] * 6,
            plain,
            plain,
            phases,
            phases,
            pltpu.VMEM((PHASES, size, 3 * LANES), BF16),
            pltpu.VMEM((PHASES, 2 * size, 3 * LANES), F32),
            pltpu.VMEM((PHASES, 2 * size, 3 * LANES), BF16),
            pltpu.VMEM((extra, LANES), F32),
        ],
        compiler_params=pltpu.CompilerParams(vmem_limit_bytes=VMEM_LIMIT),
        name="channel_operator",
    )(*arrived, short_weights, *tables)


def token_kernel(peers, sum_rows, *refs):
    arrived = refs[:peers]
    query, key, value, cot, weights = refs[peers : peers + 5]
    gated, query_grad, key_grad, value_grad, filter_grad, short_grad = refs[peers + 5 : peers + 11]
    longer, pre = refs[peers + 11 :]
    tokens = query.shape[0]
    tap_count = weights.shape[1]
    count = sum_rows // PIECES
    me = lax.axis_index("ctx")
    for step, source in zip(partners(peers), arrived):
        lanes = lanes_of(me ^ step)
        extra = source[3 * tokens :, :].astype(F32)

        def rim(at):
            return extra[sum_rows + at * RIM : sum_rows + (at + 1) * RIM]

        def short(array, signal):
            longer[array, PAD - RIM : PAD, :] = rim(array)
            longer[array, PAD :, :] = signal[:, lanes].astype(F32)
            summed = weights[array, 0:1, lanes] * longer[array, PAD:, :]
            for tap in range(1, tap_count):
                summed = (
                    summed
                    + weights[array, tap : tap + 1, lanes]
                    * longer[array, PAD - tap : PAD - tap + tokens, :]
                )
            return summed

        def taps_back(array, grad, target):
            pre[array, :tokens, :] = grad
            pre[array, tokens : tokens + RIM, :] = rim(3 + array)
            summed = weights[array, 0:1, lanes] * grad
            for tap in range(1, tap_count):
                summed = (
                    summed
                    + weights[array, tap : tap + 1, lanes] * pre[array, tap : tap + tokens, :]
                )
            target[:, lanes] = summed.astype(BF16)

        conv = source[:tokens, :].astype(F32)
        conv_grad = source[tokens : 2 * tokens, :].astype(F32)
        gated[:, lanes] = (short(0, query) * conv).astype(BF16)
        taps_back(0, cot[:, lanes].astype(F32) * conv, query_grad)
        taps_back(1, conv_grad * short(2, value), key_grad)
        taps_back(2, conv_grad * short(1, key), value_grad)
        filter_grad[:, lanes] = source[2 * tokens : 3 * tokens, :].astype(F32)
        whole = extra[:count]
        for piece in range(1, PIECES):
            whole = whole + extra[piece * count : (piece + 1) * count]
        for row in range(count):
            which, tap = divmod(row, tap_count)
            short_grad[which, tap : tap + 1, lanes] = whole[row : row + 1]


def token_step(arrived, query, key, value, cot, short_weights):
    peers = len(arrived)
    tokens, width = query.shape
    wide = jax.ShapeDtypeStruct((tokens, width), BF16)
    return pl.pallas_call(
        functools.partial(token_kernel, peers, extra_rows(short_weights)[0]),
        in_specs=in_vmem(peers + 5),
        out_specs=in_vmem(6),
        out_shape=[wide] * 4
        + [
            jax.ShapeDtypeStruct((tokens, width), F32),
            jax.ShapeDtypeStruct(short_weights.shape, F32),
        ],
        scratch_shapes=[
            pltpu.VMEM((3, tokens + PAD, LANES), F32),
            pltpu.VMEM((3, tokens + PAD, LANES), F32),
        ],
        compiler_params=pltpu.CompilerParams(vmem_limit_bytes=VMEM_LIMIT),
        name="token_outputs",
    )(*arrived, query, key, value, cot, short_weights)


def channel_shards(query_proj, key_proj, value_proj, cotangent, filter_taps, short_weights):
    peers = lax.axis_size("ctx")
    tokens = query_proj.shape[0]
    tables = [jnp.asarray(table) for table in dft_tables(peers * tokens)]
    sent = pack((query_proj, key_proj, value_proj, cotangent, filter_taps), peers)
    arrived = exchange(sent)
    staged = stage((sent[0], short_weights, *tables), arrived[1])
    back = exchange(
        channel_step((staged[0], *arrived[1:]), staged[1], staged[2:], tokens)
    )
    return tuple(token_step(back, query_proj, key_proj, value_proj, cotangent, short_weights))


def from_behind(array, axis, by):
    peers = lax.axis_size(axis)
    pairs = [(i, i + by) for i in range(peers) if 0 <= i + by < peers]
    return lax.ppermute(array, axis, pairs)


def contract(form, left, right):
    return jnp.einsum(
        form, left, right, precision=lax.Precision.HIGHEST, preferred_element_type=jnp.float32
    )


def table_pair(rows, cols, period):
    row_ids = lax.broadcasted_iota(jnp.int32, (rows, cols), 0)
    col_ids = lax.broadcasted_iota(jnp.int32, (rows, cols), 1)
    angle = 2.0 * math.pi / period * (row_ids * col_ids % period).astype(jnp.float32)
    return (jnp.cos(angle), jnp.sin(angle))


def make_plan(seq_len):
    small_len = int(math.isqrt(2 * seq_len))
    while seq_len % small_len:
        small_len -= 1
    large_len = 2 * seq_len // small_len
    large_cos, large_sin = table_pair(large_len // 2, large_len, large_len)
    small_cos, small_sin = table_pair(small_len, small_len, small_len)
    twist_cos, twist_sin = table_pair(large_len, small_len, small_len * large_len)
    fwd_large = jnp.stack([large_cos, -large_sin], axis=1)
    fwd_small = jnp.stack([jnp.stack([small_cos, -small_sin]), jnp.stack([small_sin, small_cos])])
    inv_small = jnp.stack([jnp.stack([small_cos, small_sin]), jnp.stack([-small_sin, small_cos])])
    inv_large = jnp.stack([large_cos, -large_sin])
    return (small_len, large_len, fwd_large, fwd_small, inv_small, inv_large, twist_cos, twist_sin)


def forward_spec(signal, dft_plan):
    small_len, large_len, fwd_large, fwd_small, inv_small, inv_large, twist_cos, twist_sin = (
        dft_plan
    )
    cube = signal.reshape(signal.shape[0], large_len // 2, small_len)
    section_one = contract("cba,bpk->cpka", cube, fwd_large)
    real_one = section_one[:, 0]
    imag_one = section_one[:, 1]
    section_two = jnp.stack(
        [real_one * twist_cos + imag_one * twist_sin, imag_one * twist_cos - real_one * twist_sin],
        axis=1,
    )
    return contract("cpka,pqaj->cqkj", section_two, fwd_small)


def inverse_half(spec, dft_plan):
    small_len, large_len, fwd_large, fwd_small, inv_small, inv_large, twist_cos, twist_sin = (
        dft_plan
    )
    section_one = contract("cqkj,qpja->cpka", spec, inv_small)
    real_one = section_one[:, 0]
    imag_one = section_one[:, 1]
    section_two = jnp.stack(
        [real_one * twist_cos - imag_one * twist_sin, imag_one * twist_cos + real_one * twist_sin],
        axis=1,
    )
    signal = contract("cpka,pbk->cba", section_two, inv_large)
    return signal.reshape(signal.shape[0], -1) / float(small_len * large_len)


def complex_mul(left, right):
    left_real, left_imag = (left[:, 0], left[:, 1])
    right_real, right_imag = (right[:, 0], right[:, 1])
    return jnp.stack(
        [
            left_real * right_real - left_imag * right_imag,
            left_real * right_imag + left_imag * right_real,
        ],
        axis=1,
    )


def conj_mul(left, right):
    left_real, left_imag = (left[:, 0], left[:, 1])
    right_real, right_imag = (right[:, 0], right[:, 1])
    return jnp.stack(
        [
            left_real * right_real + left_imag * right_imag,
            left_real * right_imag - left_imag * right_real,
        ],
        axis=1,
    )


def conv_forward(prod_chan, filter_spec, dft_plan):
    prod_spec = forward_spec(prod_chan.astype(jnp.float32), dft_plan)
    conv_chan = inverse_half(complex_mul(prod_spec, filter_spec), dft_plan).astype(jnp.bfloat16)
    return (conv_chan, prod_spec)


def conv_backward(grad_chan, filter_spec, prod_spec, dft_plan, grad_scale):
    grad_spec = forward_spec(grad_chan.astype(jnp.float32), dft_plan)
    dconv_chan = inverse_half(conj_mul(filter_spec, grad_spec), dft_plan).astype(jnp.bfloat16)
    dfilter_chan = inverse_half(conj_mul(prod_spec, grad_spec), dft_plan) * grad_scale
    return (dconv_chan, dfilter_chan)


def receive_filter(filter_taps, dft_plan):
    filter_chan = lax.all_to_all(filter_taps.T, "ctx", split_axis=0, concat_axis=1, tiled=True)
    return forward_spec(filter_chan, dft_plan)


def return_filter(dfilter_chan):
    return (
        lax.all_to_all(
            dfilter_chan.astype(jnp.bfloat16), "ctx", split_axis=1, concat_axis=0, tiled=True
        )
        .astype(dfilter_chan.dtype)
        .T
    )


def causal_taps(extended, weights, length, axis):
    rim_rows = len(weights) - 1
    summed = weights[0] * lax.slice_in_dim(extended, rim_rows, rim_rows + length, axis=axis)
    for offset in range(1, len(weights)):
        summed = summed + weights[offset] * lax.slice_in_dim(
            extended, rim_rows - offset, rim_rows - offset + length, axis=axis
        )
    return summed


def reverse_taps(extended, weights, length, axis):
    summed = weights[0] * lax.slice_in_dim(extended, 0, length, axis=axis)
    for offset in range(1, len(weights)):
        summed = summed + weights[offset] * lax.slice_in_dim(
            extended, offset, offset + length, axis=axis
        )
    return summed


def tap_grads(grad_in, extended, tap_count, length, axis):
    rim_rows = tap_count - 1
    rows = [
        jnp.sum(
            grad_in
            * lax.slice_in_dim(extended, rim_rows - offset, rim_rows - offset + length, axis=axis),
            axis=axis,
        )
        for offset in range(tap_count)
    ]
    return jnp.stack(rows, axis=1)


def spread_shards(query_proj, key_proj, value_proj, cotangent, filter_taps, short_weights):
    tokens = query_proj.shape[0]
    tap_count = short_weights.shape[1]
    rim_rows = tap_count - 1
    seq_len = tokens * lax.axis_size("ctx")
    grad_scale = 1.0 / math.sqrt(seq_len)
    dft_plan = make_plan(seq_len)
    stacked = jnp.stack([query_proj, key_proj, value_proj])
    prev_rim = from_behind(stacked[:, tokens - rim_rows :], "ctx", 1)
    extended = jnp.concatenate([prev_rim, stacked], axis=1).astype(jnp.float32)
    weights = [short_weights[:, offset, None, :] for offset in range(tap_count)]
    short_out = causal_taps(extended, weights, tokens, 1)
    product = (short_out[1] * short_out[2]).astype(jnp.bfloat16)
    cot_wide = cotangent.astype(jnp.float32)
    gate_grad = (cot_wide * short_out[0]).astype(jnp.bfloat16)
    filter_spec = receive_filter(filter_taps, dft_plan)
    prod_chan = lax.all_to_all(product.T, "ctx", split_axis=0, concat_axis=1, tiled=True)
    conv_chan, prod_spec = conv_forward(prod_chan, filter_spec, dft_plan)
    conv_tok = lax.all_to_all(conv_chan, "ctx", split_axis=1, concat_axis=0, tiled=True)
    grad_chan = lax.all_to_all(gate_grad.T, "ctx", split_axis=0, concat_axis=1, tiled=True)
    dconv_chan, dfilter_chan = conv_backward(
        grad_chan, filter_spec, prod_spec, dft_plan, grad_scale
    )
    dconv_tok = lax.all_to_all(dconv_chan, "ctx", split_axis=1, concat_axis=0, tiled=True)
    filter_grad = return_filter(dfilter_chan)
    conv_wide = conv_tok.T.astype(jnp.float32)
    dconv_wide = dconv_tok.T.astype(jnp.float32)
    gated = (short_out[0] * conv_wide).astype(jnp.bfloat16)
    token_grads = jnp.stack(
        [cot_wide * conv_wide, dconv_wide * short_out[2], dconv_wide * short_out[1]]
    )
    next_rim = from_behind(token_grads[:, :rim_rows], "ctx", -1)
    grad_ext = jnp.concatenate([token_grads, next_rim], axis=1)
    inputs_grad = reverse_taps(grad_ext, weights, tokens, 1).astype(jnp.bfloat16)
    weight_part = tap_grads(token_grads, extended, tap_count, tokens, 1)
    short_grad = lax.psum(weight_part, "ctx") * grad_scale
    results = (gated, inputs_grad[0], inputs_grad[1], inputs_grad[2])
    return (results[0], results[1], results[2], results[3], filter_grad, short_grad)


def fits(query_proj, short_weights):
    peers = lax.axis_size("ctx")
    tokens, width = query_proj.shape
    tap_count = short_weights.shape[1]
    return (
        width == peers * LANES
        and peers.bit_count() == 1
        and tokens % (PHASES * CHUNK) == 0
        and tap_count == RIM + 1
        and peers * tokens <= 2048
    )


def shards(*arrays):
    return channel_shards(*arrays) if fits(arrays[0], arrays[5]) else spread_shards(*arrays)


def solution(mesh):
    placed = (
        P("ctx", "tp"),
        P("ctx", "tp"),
        P("ctx", "tp"),
        P("ctx", "tp"),
        P("ctx", "tp"),
        P(None, None, "tp"),
    )
    return jax.shard_map(
        shards,
        mesh=mesh,
        in_specs=placed,
        out_specs=(
            P("ctx", "tp"),
            P("ctx", "tp"),
            P("ctx", "tp"),
            P("ctx", "tp"),
            P("ctx", "tp"),
            P(None, None, "tp"),
        ),
        check_vma=False,
    )
```

```python
import functools
import math

import jax
import jax.numpy as jnp
import numpy as np
from jax import lax
from jax.experimental import pallas as pl
from jax.experimental.pallas import tpu as pltpu
from jax.sharding import PartitionSpec as P

F32 = jnp.float32
BF16 = jnp.bfloat16
LANES = 128
PHASES = 4
TILE = 16
PAD = 8
CHUNK = 32
RIM = 2
PIECES = 2
MIB = 1024 * 1024
VMEM_LIMIT = 24 * MIB
PACK_VMEM = 60680 * 1024


def partners(peers, diagonal_first):
    def rank(step):
        links, other_core = (step >> 1).bit_count(), step & 1
        if links == 0:
            return (4, 0, 0)
        if links == 1:
            return (3 if other_core else 1, 0, -step)
        return (0 if diagonal_first else 2, other_core, -step)

    return [0] + sorted(range(1, peers), key=rank)


def exchange(blocks, steps):
    peers = len(blocks)
    got = [blocks[0]]
    for step, block in list(zip(steps, blocks))[1:]:
        got.append(lax.ppermute(block, "ctx", [(i, i ^ step) for i in range(peers)]))
    return got


def in_vmem(count):
    return [pl.BlockSpec(memory_space=pltpu.VMEM)] * count


def lanes_of(place):
    return pl.ds(pl.multiple_of(place * LANES, LANES), LANES)


def pack_kernel(count, steps, *refs):
    sources, packed = refs[:count], refs[count : count + len(steps)]
    held, sems = refs[count + len(steps) : -1], refs[-1]
    tokens = sources[0].shape[0]
    me = lax.axis_index("ctx")
    arriving = [
        pltpu.make_async_copy(source, target, sems.at[at])
        for at, (source, target) in enumerate(zip(sources, held))
    ]
    for copy in arriving:
        copy.start()
    for at, source in enumerate(held):
        arriving[at].wait()
        rows = slice(at * tokens, (at + 1) * tokens)
        for step, target in zip(steps, packed):
            target[rows, :] = source[:, lanes_of(me ^ step)].astype(BF16)


def pack(arrays, steps):
    tokens = arrays[0].shape[0]
    count = len(arrays)
    return pl.pallas_call(
        functools.partial(pack_kernel, count, steps),
        in_specs=[pl.BlockSpec(memory_space=pl.ANY)] * count,
        out_specs=in_vmem(len(steps)),
        out_shape=[jax.ShapeDtypeStruct((count * tokens, LANES), BF16)] * len(steps),
        scratch_shapes=[
            *[pltpu.VMEM(array.shape, array.dtype) for array in arrays],
            pltpu.SemaphoreType.DMA((count,)),
        ],
        compiler_params=pltpu.CompilerParams(vmem_limit_bytes=PACK_VMEM),
        cost_estimate=pl.CostEstimate(flops=0, bytes_accessed=8 * MIB, transcendentals=0),
        name="pack_inputs",
    )(*arrays)


@functools.lru_cache(maxsize=None)
def dft_tables(seq_len):
    size = seq_len // PHASES
    k = np.arange(size, dtype=np.int64)[:, None]
    m = np.arange(size, dtype=np.int64)[None, :]
    forward = []
    for phase in range(PHASES):
        turns = ((4 * k + 1) * (PHASES * m + phase)) % (4 * seq_len)
        angle = 2.0 * np.pi / (4 * seq_len) * turns
        forward.append(np.concatenate([np.cos(angle), -np.sin(angle)], axis=0))
    forward = np.stack(forward)
    backward = np.swapaxes(forward, 1, 2) / seq_len

    def pieces(table):
        high = table.astype(BF16)
        low = (table - high.astype(np.float64)).astype(BF16)
        return np.stack([high, low], axis=1)

    return pieces(forward), pieces(backward)


def forward_mix(parts):
    (r0, i0), (r1, i1), (r2, i2), (r3, i3) = parts
    ar, ai, br, bi = r0 + r2, i0 + i2, r0 - r2, i0 - i2
    cr, ci, dr, di = r1 + r3, i1 + i3, r1 - r3, i1 - i3
    return ((ar + cr, ai + ci), (br + di, bi - dr), (ar - cr, ai - ci), (br - di, bi + dr))


def inverse_mix(parts):
    (r0, i0), (r1, i1), (r2, i2), (r3, i3) = parts
    ar, ai, br, bi = r0 + r2, i0 + i2, r0 - r2, i0 - i2
    cr, ci, dr, di = r1 + r3, i1 + i3, r1 - r3, i1 - i3
    return ((ar + cr, ai + ci), (br - di, bi + dr), (ar - cr, ai - ci), (br + di, bi - dr))


def times(left, right):
    return tuple(
        (lr * rr - li * ri, lr * ri + li * rr) for (lr, li), (rr, ri) in zip(left, right)
    )


def conj_times(left, right):
    return tuple(
        (lr * rr + li * ri, lr * ri - li * rr) for (lr, li), (rr, ri) in zip(left, right)
    )


def transform(tables, signal):
    return jnp.dot(tables[0], signal, preferred_element_type=F32) + jnp.dot(
        tables[1], signal, preferred_element_type=F32
    )


def phases_near(ref, chunk, tap_count):
    start = PAD + chunk * CHUNK * PHASES
    return {
        offset: ref[pl.ds(start + offset, CHUNK, stride=PHASES), :]
        for offset in range(1 - tap_count, PHASES)
    }


def short_conv(near, taps):
    results = []
    for r in range(PHASES):
        summed = taps[0] * near[r]
        for at in range(1, len(taps)):
            summed = summed + taps[at] * near[r - at]
        results.append(summed)
    return results


def add_rows(total, terms):
    for term in terms:
        folded = jnp.sum(term.reshape(CHUNK // 8, 8, LANES), axis=0)
        total = folded if total is None else total + folded
    return total


def clear_ends(ref):
    ref[:PAD, :] = jnp.zeros((PAD, LANES), F32)
    ref[ref.shape[0] - PAD :, :] = jnp.zeros((PAD, LANES), F32)


def stage_kernel(count, *refs):
    sources, targets, sems = refs[:count], refs[count + 1 : 2 * count + 1], refs[2 * count + 1]
    copies = [
        pltpu.make_async_copy(source, target, sems.at[at])
        for at, (source, target) in enumerate(zip(sources, targets))
    ]
    for copy in copies:
        copy.start()
    for copy in copies:
        copy.wait()


def stage(arrays, after):
    count = len(arrays)
    return pl.pallas_call(
        functools.partial(stage_kernel, count),
        in_specs=[pl.BlockSpec(memory_space=pl.ANY)] * (count + 1),
        out_specs=in_vmem(count),
        out_shape=[jax.ShapeDtypeStruct(array.shape, array.dtype) for array in arrays],
        scratch_shapes=[pltpu.SemaphoreType.DMA((count,))],
        compiler_params=pltpu.CompilerParams(vmem_limit_bytes=8 * MIB),
        cost_estimate=pl.CostEstimate(flops=0, bytes_accessed=8 * MIB, transcendentals=0),
        name="stage_tables",
    )(*arrays, after)


def extra_rows(short_weights):
    sums = PIECES * short_weights.shape[0] * short_weights.shape[1]
    return sums, -(-(sums + 6 * RIM) // TILE) * TILE


def channel_kernel(tokens, heard, told, grad_scale, *refs):
    peers = len(heard)
    arrived = refs[:peers]
    weights, forward, backward = refs[peers : peers + 3]
    out = refs[peers + 3 : 2 * peers + 3]
    (
        query,
        key,
        value,
        cot,
        conv,
        conv_grad,
        filter_grad,
        taps,
        key_short,
        value_short,
        signals,
        spectra,
        products,
        extra,
    ) = refs[2 * peers + 3 :]
    size = peers * tokens // PHASES
    tap_count = weights.shape[1]
    me = lax.axis_index("ctx")
    own = lanes_of(me)
    for ref in (query, key, value, cot, conv, conv_grad):
        clear_ends(ref)
    for ref in (key_short, value_short):
        ref[:, size:, :] = jnp.zeros((PHASES, PAD, LANES), F32)
    for step, source in zip(heard, arrived):
        start = (me ^ step) * tokens
        inner = pl.ds(pl.multiple_of(PAD + start, PAD), tokens)
        for at, ref in enumerate((query, key, value, cot)):
            ref[inner, :] = source[at * tokens : (at + 1) * tokens, :].astype(F32)
        taps[pl.ds(pl.multiple_of(start, PAD), tokens), :] = source[4 * tokens :, :].astype(F32)
    chunks = range(size // CHUNK)
    taps_of = [
        [weights[array, tap : tap + 1, own] for tap in range(tap_count)] for array in range(3)
    ]

    def rows_of(chunk):
        return slice(chunk * CHUNK, (chunk + 1) * CHUNK)

    def spectrum(at, real, imag):
        lanes = slice(at * LANES, (at + 1) * LANES)
        return forward_mix(
            [(spectra[r, real, lanes], spectra[r, imag, lanes]) for r in range(PHASES)]
        )

    def keep(at, real, imag, mixed):
        lanes = slice(at * LANES, (at + 1) * LANES)
        for r, pair in enumerate(inverse_mix(mixed)):
            for rows, part in zip((real, imag), pair):
                products[r, rows, lanes] = part.astype(BF16)

    for chunk in chunks:
        rows = rows_of(chunk)
        key_now = short_conv(phases_near(key, chunk, tap_count), taps_of[1])
        value_now = short_conv(phases_near(value, chunk, tap_count), taps_of[2])
        for r in range(PHASES):
            key_short[r, rows, :] = key_now[r]
            value_short[r, rows, :] = value_now[r]
            signals[r, rows, :LANES] = (key_now[r] * value_now[r]).astype(BF16)
            filt = taps[pl.ds(chunk * CHUNK * PHASES + r, CHUNK, stride=PHASES), :]
            signals[r, rows, LANES : 2 * LANES] = filt.astype(BF16)
    for r in range(PHASES):
        spectra[r, :, : 2 * LANES] = transform(forward[r], signals[r, :, : 2 * LANES])
    for chunk in chunks:
        rows = rows_of(chunk)
        query_now = short_conv(phases_near(query, chunk, tap_count), taps_of[0])
        cot_now = phases_near(cot, chunk, 1)
        for r in range(PHASES):
            signals[r, rows, 2 * LANES :] = (cot_now[r] * query_now[r]).astype(BF16)
    for r in range(PHASES):
        spectra[r, :, 2 * LANES :] = transform(forward[r], signals[r, :, 2 * LANES :])
    for step in range(size // TILE):
        real = slice(step * TILE, (step + 1) * TILE)
        imag = slice(size + step * TILE, size + (step + 1) * TILE)
        prod, filt = spectrum(0, real, imag), spectrum(1, real, imag)
        for at, mixed in enumerate((prod, filt)):
            lanes = slice(at * LANES, (at + 1) * LANES)
            for q, pair in enumerate(mixed):
                spectra[q, real, lanes], spectra[q, imag, lanes] = pair
        keep(0, real, imag, times(prod, filt))
    for r in range(PHASES):
        result = transform(backward[r], products[r, :, :LANES])
        conv[pl.ds(PAD + r, size, stride=PHASES), :] = result.astype(BF16).astype(F32)
    for step in range(size // TILE):
        real = slice(step * TILE, (step + 1) * TILE)
        imag = slice(size + step * TILE, size + (step + 1) * TILE)
        grad = spectrum(2, real, imag)
        for at in range(2):
            lanes = slice(at * LANES, (at + 1) * LANES)
            known = [(spectra[q, real, lanes], spectra[q, imag, lanes]) for q in range(PHASES)]
            keep(2 - at, real, imag, conj_times(known, grad))
    for r in range(PHASES):
        result = transform(backward[r], products[r, :, LANES:])
        conv_grad[pl.ds(PAD + r, size, stride=PHASES), :] = (
            result[:, :LANES].astype(BF16).astype(F32)
        )
        filter_grad[pl.ds(r, size, stride=PHASES), :] = result[:, LANES:] * grad_scale

    totals = [[None] * tap_count for _ in range(3)]

    def add_sums(array, signal, chunk, pre):
        near = phases_near(signal, chunk, tap_count)
        for tap in range(tap_count):
            totals[array][tap] = add_rows(
                totals[array][tap], [pre[r] * near[r - tap] for r in range(PHASES)]
            )

    for chunk in chunks:
        cot_now, conv_now = phases_near(cot, chunk, 1), phases_near(conv, chunk, 1)
        add_sums(0, query, chunk, [cot_now[r] * conv_now[r] for r in range(PHASES)])
    for chunk in chunks:
        rows = rows_of(chunk)
        grad_now = phases_near(conv_grad, chunk, 1)
        add_sums(1, key, chunk, [grad_now[r] * value_short[r, rows, :] for r in range(PHASES)])
        add_sums(2, value, chunk, [grad_now[r] * key_short[r, rows, :] for r in range(PHASES)])
    sums = [jnp.sum(total, axis=0, keepdims=True) for row in totals for total in row]
    rest = jnp.concatenate(sums, axis=0) * grad_scale
    extra[...] = jnp.zeros_like(extra)
    for piece in range(PIECES):
        rounded = rest.astype(BF16).astype(F32)
        extra[piece * len(sums) : (piece + 1) * len(sums), :] = rounded
        rest = rest - rounded
    for step, target in zip(told, out):
        start = (me ^ step) * tokens
        inner = pl.ds(pl.multiple_of(PAD + start, PAD), tokens)
        target[:tokens, :] = conv[inner, :].astype(BF16)
        target[tokens : 2 * tokens, :] = conv_grad[inner, :].astype(BF16)
        target[2 * tokens : 3 * tokens, :] = filter_grad[
            pl.ds(pl.multiple_of(start, PAD), tokens), :
        ].astype(BF16)
        before = pl.ds(pl.multiple_of(start, PAD), PAD)
        after = pl.ds(pl.multiple_of(PAD + start + tokens, PAD), PAD)
        at = PIECES * len(sums)
        for ref in (query, key, value):
            extra[at : at + RIM, :] = ref[before, :][PAD - RIM :]
            at += RIM
        row = pl.ds(pl.multiple_of((start + tokens) // PHASES, PAD), PAD)
        extra[at : at + RIM, :] = (cot[after, :] * conv[after, :])[:RIM]
        for short in (value_short, key_short):
            at += RIM
            shorts = jnp.concatenate([short[r, row, :][:1] for r in range(RIM)], axis=0)
            extra[at : at + RIM, :] = conv_grad[after, :][:RIM] * shorts
        target[3 * tokens :, :] = extra[...].astype(BF16)


def channel_step(arrived, heard, told, short_weights, tables, tokens):
    peers = len(arrived)
    seq_len = peers * tokens
    size = seq_len // PHASES
    extra = extra_rows(short_weights)[1]
    padded = pltpu.VMEM((seq_len + 2 * PAD, LANES), F32)
    plain = pltpu.VMEM((seq_len, LANES), F32)
    phases = pltpu.VMEM((PHASES, size + PAD, LANES), F32)
    return pl.pallas_call(
        functools.partial(channel_kernel, tokens, heard, told, 1.0 / math.sqrt(seq_len)),
        in_specs=in_vmem(peers + 3),
        out_specs=in_vmem(peers),
        out_shape=[jax.ShapeDtypeStruct((3 * tokens + extra, LANES), BF16)] * peers,
        scratch_shapes=[
            *[padded] * 6,
            plain,
            plain,
            phases,
            phases,
            pltpu.VMEM((PHASES, size, 3 * LANES), BF16),
            pltpu.VMEM((PHASES, 2 * size, 3 * LANES), F32),
            pltpu.VMEM((PHASES, 2 * size, 3 * LANES), BF16),
            pltpu.VMEM((extra, LANES), F32),
        ],
        compiler_params=pltpu.CompilerParams(vmem_limit_bytes=VMEM_LIMIT),
        name="channel_operator",
    )(*arrived, short_weights, *tables)


def token_kernel(steps, sum_rows, carried, *refs):
    count_in = len(steps)
    arrived = refs[:count_in]
    query, key, value, cot, weights = refs[count_in : count_in + 5]
    results = refs[count_in + 5 + carried : count_in + 11 + carried]
    (gated, query_grad, key_grad, value_grad, filter_grad, short_grad, longer, pre, sems) = refs[
        count_in + 11 + carried :
    ]
    copies = []
    tokens = query.shape[0]
    tap_count = weights.shape[1]
    count = sum_rows // PIECES
    me = lax.axis_index("ctx")
    for slot, (step, source) in enumerate(zip(steps, arrived)):
        lanes = lanes_of(me ^ step)
        extra = source[3 * tokens :, :].astype(F32)

        def rim(at):
            return extra[sum_rows + at * RIM : sum_rows + (at + 1) * RIM]

        def short(array, signal):
            longer[array, PAD - RIM : PAD, :] = rim(array)
            longer[array, PAD :, :] = signal[:, lanes].astype(F32)
            summed = weights[array, 0:1, lanes] * longer[array, PAD:, :]
            for tap in range(1, tap_count):
                summed = (
                    summed
                    + weights[array, tap : tap + 1, lanes]
                    * longer[array, PAD - tap : PAD - tap + tokens, :]
                )
            return summed

        def taps_back(array, grad, target):
            pre[array, :tokens, :] = grad
            pre[array, tokens : tokens + RIM, :] = rim(3 + array)
            summed = weights[array, 0:1, lanes] * grad
            for tap in range(1, tap_count):
                summed = (
                    summed
                    + weights[array, tap : tap + 1, lanes] * pre[array, tap : tap + tokens, :]
                )
            target[slot] = summed.astype(BF16)

        conv = source[:tokens, :].astype(F32)
        conv_grad = source[tokens : 2 * tokens, :].astype(F32)
        gated[slot] = (short(0, query) * conv).astype(BF16)
        taps_back(0, cot[:, lanes].astype(F32) * conv, query_grad)
        taps_back(1, conv_grad * short(2, value), key_grad)
        taps_back(2, conv_grad * short(1, key), value_grad)
        filter_grad[slot] = source[2 * tokens : 3 * tokens, :].astype(F32)
        whole = extra[:count]
        for piece in range(1, PIECES):
            whole = whole + extra[piece * count : (piece + 1) * count]
        for row in range(count):
            which, tap = divmod(row, tap_count)
            short_grad[slot, which, tap : tap + 1, :] = whole[row : row + 1]
        held = (gated, query_grad, key_grad, value_grad, filter_grad, short_grad)
        for at, (source, target) in enumerate(zip(held, results)):
            place = target.at[:, :, lanes] if at == 5 else target.at[:, lanes]
            copies.append(pltpu.make_async_copy(source.at[slot], place, sems.at[slot, at]))
            copies[-1].start()
    for copy in copies:
        copy.wait()


def token_step(arrived, steps, query, key, value, cot, short_weights, begun=()):
    tokens, width = query.shape
    count = len(arrived)
    wide = jax.ShapeDtypeStruct((tokens, width), BF16)
    anywhere = pl.BlockSpec(memory_space=pl.ANY)
    return pl.pallas_call(
        functools.partial(token_kernel, steps, extra_rows(short_weights)[0], len(begun)),
        in_specs=in_vmem(count + 5) + [anywhere] * len(begun),
        out_specs=[anywhere] * 6,
        out_shape=[wide] * 4
        + [
            jax.ShapeDtypeStruct((tokens, width), F32),
            jax.ShapeDtypeStruct(short_weights.shape, F32),
        ],
        scratch_shapes=[
            *[pltpu.VMEM((count, tokens, LANES), BF16)] * 4,
            pltpu.VMEM((count, tokens, LANES), F32),
            pltpu.VMEM((count, *short_weights.shape[:2], LANES), F32),
            pltpu.VMEM((3, tokens + PAD, LANES), F32),
            pltpu.VMEM((3, tokens + PAD, LANES), F32),
            pltpu.SemaphoreType.DMA((count, 6)),
        ],
        input_output_aliases={count + 5 + at: at for at in range(len(begun))},
        compiler_params=pltpu.CompilerParams(vmem_limit_bytes=VMEM_LIMIT),
        cost_estimate=pl.CostEstimate(flops=0, bytes_accessed=4 * MIB, transcendentals=0),
        name="token_outputs",
    )(*arrived, query, key, value, cot, short_weights, *begun)


def channel_shards(query_proj, key_proj, value_proj, cotangent, filter_taps, short_weights):
    peers = lax.axis_size("ctx")
    tokens = query_proj.shape[0]
    tables = [jnp.asarray(table) for table in dft_tables(peers * tokens)]
    going, coming = partners(peers, False), partners(peers, True)
    sent = pack((query_proj, key_proj, value_proj, cotangent, filter_taps), going)
    arrived = exchange(sent, going)
    staged = stage((sent[0], short_weights, *tables), arrived[1])
    arrived[0] = staged[0]
    results = channel_step(arrived, going, coming, staged[1], staged[2:], tokens)
    back = exchange(results, coming)
    local = (query_proj, key_proj, value_proj, cotangent, short_weights)
    half = peers // 2
    begun = token_step(back[:half], coming[:half], *local)
    return tuple(token_step(back[half:], coming[half:], *local, begun))


def from_behind(array, axis, by):
    peers = lax.axis_size(axis)
    pairs = [(i, i + by) for i in range(peers) if 0 <= i + by < peers]
    return lax.ppermute(array, axis, pairs)


def contract(form, left, right):
    return jnp.einsum(
        form, left, right, precision=lax.Precision.HIGHEST, preferred_element_type=jnp.float32
    )


def table_pair(rows, cols, period):
    row_ids = lax.broadcasted_iota(jnp.int32, (rows, cols), 0)
    col_ids = lax.broadcasted_iota(jnp.int32, (rows, cols), 1)
    angle = 2.0 * math.pi / period * (row_ids * col_ids % period).astype(jnp.float32)
    return (jnp.cos(angle), jnp.sin(angle))


def make_plan(seq_len):
    small_len = int(math.isqrt(2 * seq_len))
    while seq_len % small_len:
        small_len -= 1
    large_len = 2 * seq_len // small_len
    large_cos, large_sin = table_pair(large_len // 2, large_len, large_len)
    small_cos, small_sin = table_pair(small_len, small_len, small_len)
    twist_cos, twist_sin = table_pair(large_len, small_len, small_len * large_len)
    fwd_large = jnp.stack([large_cos, -large_sin], axis=1)
    fwd_small = jnp.stack([jnp.stack([small_cos, -small_sin]), jnp.stack([small_sin, small_cos])])
    inv_small = jnp.stack([jnp.stack([small_cos, small_sin]), jnp.stack([-small_sin, small_cos])])
    inv_large = jnp.stack([large_cos, -large_sin])
    return (small_len, large_len, fwd_large, fwd_small, inv_small, inv_large, twist_cos, twist_sin)


def forward_spec(signal, dft_plan):
    small_len, large_len, fwd_large, fwd_small, inv_small, inv_large, twist_cos, twist_sin = (
        dft_plan
    )
    cube = signal.reshape(signal.shape[0], large_len // 2, small_len)
    section_one = contract("cba,bpk->cpka", cube, fwd_large)
    real_one = section_one[:, 0]
    imag_one = section_one[:, 1]
    section_two = jnp.stack(
        [real_one * twist_cos + imag_one * twist_sin, imag_one * twist_cos - real_one * twist_sin],
        axis=1,
    )
    return contract("cpka,pqaj->cqkj", section_two, fwd_small)


def inverse_half(spec, dft_plan):
    small_len, large_len, fwd_large, fwd_small, inv_small, inv_large, twist_cos, twist_sin = (
        dft_plan
    )
    section_one = contract("cqkj,qpja->cpka", spec, inv_small)
    real_one = section_one[:, 0]
    imag_one = section_one[:, 1]
    section_two = jnp.stack(
        [real_one * twist_cos - imag_one * twist_sin, imag_one * twist_cos + real_one * twist_sin],
        axis=1,
    )
    signal = contract("cpka,pbk->cba", section_two, inv_large)
    return signal.reshape(signal.shape[0], -1) / float(small_len * large_len)


def complex_mul(left, right):
    left_real, left_imag = (left[:, 0], left[:, 1])
    right_real, right_imag = (right[:, 0], right[:, 1])
    return jnp.stack(
        [
            left_real * right_real - left_imag * right_imag,
            left_real * right_imag + left_imag * right_real,
        ],
        axis=1,
    )


def conj_mul(left, right):
    left_real, left_imag = (left[:, 0], left[:, 1])
    right_real, right_imag = (right[:, 0], right[:, 1])
    return jnp.stack(
        [
            left_real * right_real + left_imag * right_imag,
            left_real * right_imag - left_imag * right_real,
        ],
        axis=1,
    )


def conv_forward(prod_chan, filter_spec, dft_plan):
    prod_spec = forward_spec(prod_chan.astype(jnp.float32), dft_plan)
    conv_chan = inverse_half(complex_mul(prod_spec, filter_spec), dft_plan).astype(jnp.bfloat16)
    return (conv_chan, prod_spec)


def conv_backward(grad_chan, filter_spec, prod_spec, dft_plan, grad_scale):
    grad_spec = forward_spec(grad_chan.astype(jnp.float32), dft_plan)
    dconv_chan = inverse_half(conj_mul(filter_spec, grad_spec), dft_plan).astype(jnp.bfloat16)
    dfilter_chan = inverse_half(conj_mul(prod_spec, grad_spec), dft_plan) * grad_scale
    return (dconv_chan, dfilter_chan)


def receive_filter(filter_taps, dft_plan):
    filter_chan = lax.all_to_all(filter_taps.T, "ctx", split_axis=0, concat_axis=1, tiled=True)
    return forward_spec(filter_chan, dft_plan)


def return_filter(dfilter_chan):
    return (
        lax.all_to_all(
            dfilter_chan.astype(jnp.bfloat16), "ctx", split_axis=1, concat_axis=0, tiled=True
        )
        .astype(dfilter_chan.dtype)
        .T
    )


def causal_taps(extended, weights, length, axis):
    rim_rows = len(weights) - 1
    summed = weights[0] * lax.slice_in_dim(extended, rim_rows, rim_rows + length, axis=axis)
    for offset in range(1, len(weights)):
        summed = summed + weights[offset] * lax.slice_in_dim(
            extended, rim_rows - offset, rim_rows - offset + length, axis=axis
        )
    return summed


def reverse_taps(extended, weights, length, axis):
    summed = weights[0] * lax.slice_in_dim(extended, 0, length, axis=axis)
    for offset in range(1, len(weights)):
        summed = summed + weights[offset] * lax.slice_in_dim(
            extended, offset, offset + length, axis=axis
        )
    return summed


def tap_grads(grad_in, extended, tap_count, length, axis):
    rim_rows = tap_count - 1
    rows = [
        jnp.sum(
            grad_in
            * lax.slice_in_dim(extended, rim_rows - offset, rim_rows - offset + length, axis=axis),
            axis=axis,
        )
        for offset in range(tap_count)
    ]
    return jnp.stack(rows, axis=1)


def spread_shards(query_proj, key_proj, value_proj, cotangent, filter_taps, short_weights):
    tokens = query_proj.shape[0]
    tap_count = short_weights.shape[1]
    rim_rows = tap_count - 1
    seq_len = tokens * lax.axis_size("ctx")
    grad_scale = 1.0 / math.sqrt(seq_len)
    dft_plan = make_plan(seq_len)
    stacked = jnp.stack([query_proj, key_proj, value_proj])
    prev_rim = from_behind(stacked[:, tokens - rim_rows :], "ctx", 1)
    extended = jnp.concatenate([prev_rim, stacked], axis=1).astype(jnp.float32)
    weights = [short_weights[:, offset, None, :] for offset in range(tap_count)]
    short_out = causal_taps(extended, weights, tokens, 1)
    product = (short_out[1] * short_out[2]).astype(jnp.bfloat16)
    cot_wide = cotangent.astype(jnp.float32)
    gate_grad = (cot_wide * short_out[0]).astype(jnp.bfloat16)
    filter_spec = receive_filter(filter_taps, dft_plan)
    prod_chan = lax.all_to_all(product.T, "ctx", split_axis=0, concat_axis=1, tiled=True)
    conv_chan, prod_spec = conv_forward(prod_chan, filter_spec, dft_plan)
    conv_tok = lax.all_to_all(conv_chan, "ctx", split_axis=1, concat_axis=0, tiled=True)
    grad_chan = lax.all_to_all(gate_grad.T, "ctx", split_axis=0, concat_axis=1, tiled=True)
    dconv_chan, dfilter_chan = conv_backward(
        grad_chan, filter_spec, prod_spec, dft_plan, grad_scale
    )
    dconv_tok = lax.all_to_all(dconv_chan, "ctx", split_axis=1, concat_axis=0, tiled=True)
    filter_grad = return_filter(dfilter_chan)
    conv_wide = conv_tok.T.astype(jnp.float32)
    dconv_wide = dconv_tok.T.astype(jnp.float32)
    gated = (short_out[0] * conv_wide).astype(jnp.bfloat16)
    token_grads = jnp.stack(
        [cot_wide * conv_wide, dconv_wide * short_out[2], dconv_wide * short_out[1]]
    )
    next_rim = from_behind(token_grads[:, :rim_rows], "ctx", -1)
    grad_ext = jnp.concatenate([token_grads, next_rim], axis=1)
    inputs_grad = reverse_taps(grad_ext, weights, tokens, 1).astype(jnp.bfloat16)
    weight_part = tap_grads(token_grads, extended, tap_count, tokens, 1)
    short_grad = lax.psum(weight_part, "ctx") * grad_scale
    results = (gated, inputs_grad[0], inputs_grad[1], inputs_grad[2])
    return (results[0], results[1], results[2], results[3], filter_grad, short_grad)


def fits(query_proj, short_weights):
    peers = lax.axis_size("ctx")
    tokens, width = query_proj.shape
    tap_count = short_weights.shape[1]
    return (
        width == peers * LANES
        and peers.bit_count() == 1
        and tokens % (PHASES * CHUNK) == 0
        and tap_count == RIM + 1
        and peers * tokens <= 2048
    )


def shards(*arrays):
    return channel_shards(*arrays) if fits(arrays[0], arrays[5]) else spread_shards(*arrays)


def solution(mesh):
    placed = (
        P("ctx", "tp"),
        P("ctx", "tp"),
        P("ctx", "tp"),
        P("ctx", "tp"),
        P("ctx", "tp"),
        P(None, None, "tp"),
    )
    return jax.shard_map(
        shards,
        mesh=mesh,
        in_specs=placed,
        out_specs=(
            P("ctx", "tp"),
            P("ctx", "tp"),
            P("ctx", "tp"),
            P("ctx", "tp"),
            P("ctx", "tp"),
            P(None, None, "tp"),
        ),
        check_vma=False,
    )
```

```python
import functools
import math

import jax
import jax.numpy as jnp
import numpy as np
from jax import lax
from jax.experimental import pallas as pl
from jax.experimental.pallas import tpu as pltpu
from jax.sharding import PartitionSpec as P

F32 = jnp.float32
BF16 = jnp.bfloat16
LANES = 128
PHASES = 4
TILE = 16
PAD = 8
CHUNK = 32
RIM = 2
PIECES = 2
MIB = 1024 * 1024
VMEM_LIMIT = 24 * MIB
PACK_VMEM = 53862 * 1024


def partners(peers, diagonal_first):
    def rank(step):
        links, other_core = (step >> 1).bit_count(), step & 1
        if links == 0:
            return (4, 0, 0)
        if links == 1:
            return (3 if other_core else 1, 0, -step)
        return (0 if diagonal_first else 2, other_core, -step)

    return [0] + sorted(range(1, peers), key=rank)


def exchange(blocks, steps):
    peers = len(blocks)
    got = [blocks[0]]
    for step, block in list(zip(steps, blocks))[1:]:
        got.append(lax.ppermute(block, "ctx", [(i, i ^ step) for i in range(peers)]))
    return got


def in_vmem(count):
    return [pl.BlockSpec(memory_space=pltpu.VMEM)] * count


def lanes_of(place):
    return pl.ds(pl.multiple_of(place * LANES, LANES), LANES)


def pack_kernel(count, steps, *refs):
    sources, packed = refs[:count], refs[count : count + len(steps)]
    held, sems = refs[count + len(steps) : -1], refs[-1]
    tokens = sources[0].shape[0]
    me = lax.axis_index("ctx")
    arriving = [
        pltpu.make_async_copy(source, target, sems.at[at])
        for at, (source, target) in enumerate(zip(sources, held))
    ]
    for copy in arriving:
        copy.start()
    for at, source in enumerate(held):
        arriving[at].wait()
        rows = slice(at * tokens, (at + 1) * tokens)
        for step, target in zip(steps, packed):
            target[rows, :] = source[:, lanes_of(me ^ step)].astype(BF16)


def pack(arrays, steps):
    tokens = arrays[0].shape[0]
    count = len(arrays)
    return pl.pallas_call(
        functools.partial(pack_kernel, count, steps),
        in_specs=[pl.BlockSpec(memory_space=pl.ANY)] * count,
        out_specs=in_vmem(len(steps)),
        out_shape=[jax.ShapeDtypeStruct((count * tokens, LANES), BF16)] * len(steps),
        scratch_shapes=[
            *[pltpu.VMEM(array.shape, array.dtype) for array in arrays],
            pltpu.SemaphoreType.DMA((count,)),
        ],
        compiler_params=pltpu.CompilerParams(vmem_limit_bytes=PACK_VMEM),
        cost_estimate=pl.CostEstimate(flops=0, bytes_accessed=8 * MIB, transcendentals=0),
        name="pack_inputs",
    )(*arrays)


@functools.lru_cache(maxsize=None)
def dft_tables(seq_len):
    size = seq_len // PHASES
    k = np.arange(size, dtype=np.int64)[:, None]
    m = np.arange(size, dtype=np.int64)[None, :]
    forward = []
    for phase in range(PHASES):
        turns = ((4 * k + 1) * (PHASES * m + phase)) % (4 * seq_len)
        angle = 2.0 * np.pi / (4 * seq_len) * turns
        forward.append(np.concatenate([np.cos(angle), -np.sin(angle)], axis=0))
    forward = np.stack(forward)
    backward = np.swapaxes(forward, 1, 2) / seq_len

    def pieces(table):
        high = table.astype(BF16)
        low = (table - high.astype(np.float64)).astype(BF16)
        return np.stack([high, low], axis=1)

    return pieces(forward), pieces(backward)


def forward_mix(parts):
    (r0, i0), (r1, i1), (r2, i2), (r3, i3) = parts
    ar, ai, br, bi = r0 + r2, i0 + i2, r0 - r2, i0 - i2
    cr, ci, dr, di = r1 + r3, i1 + i3, r1 - r3, i1 - i3
    return ((ar + cr, ai + ci), (br + di, bi - dr), (ar - cr, ai - ci), (br - di, bi + dr))


def inverse_mix(parts):
    (r0, i0), (r1, i1), (r2, i2), (r3, i3) = parts
    ar, ai, br, bi = r0 + r2, i0 + i2, r0 - r2, i0 - i2
    cr, ci, dr, di = r1 + r3, i1 + i3, r1 - r3, i1 - i3
    return ((ar + cr, ai + ci), (br - di, bi + dr), (ar - cr, ai - ci), (br + di, bi - dr))


def times(left, right):
    return tuple(
        (lr * rr - li * ri, lr * ri + li * rr) for (lr, li), (rr, ri) in zip(left, right)
    )


def conj_times(left, right):
    return tuple(
        (lr * rr + li * ri, lr * ri - li * rr) for (lr, li), (rr, ri) in zip(left, right)
    )


def transform(tables, signal):
    return jnp.dot(tables[0], signal, preferred_element_type=F32) + jnp.dot(
        tables[1], signal, preferred_element_type=F32
    )


def phases_near(ref, chunk, tap_count):
    start = PAD + chunk * CHUNK * PHASES
    return {
        offset: ref[pl.ds(start + offset, CHUNK, stride=PHASES), :]
        for offset in range(1 - tap_count, PHASES)
    }


def short_conv(near, taps):
    results = []
    for r in range(PHASES):
        summed = taps[0] * near[r]
        for at in range(1, len(taps)):
            summed = summed + taps[at] * near[r - at]
        results.append(summed)
    return results


def add_rows(total, terms):
    for term in terms:
        folded = jnp.sum(term.reshape(CHUNK // 8, 8, LANES), axis=0)
        total = folded if total is None else total + folded
    return total


def clear_ends(ref):
    ref[:PAD, :] = jnp.zeros((PAD, LANES), F32)
    ref[ref.shape[0] - PAD :, :] = jnp.zeros((PAD, LANES), F32)


def stage_kernel(count, *refs):
    sources, targets, sems = refs[:count], refs[count + 1 : 2 * count + 1], refs[2 * count + 1]
    copies = [
        pltpu.make_async_copy(source, target, sems.at[at])
        for at, (source, target) in enumerate(zip(sources, targets))
    ]
    for copy in copies:
        copy.start()
    for copy in copies:
        copy.wait()


def stage(arrays, after):
    count = len(arrays)
    return pl.pallas_call(
        functools.partial(stage_kernel, count),
        in_specs=[pl.BlockSpec(memory_space=pl.ANY)] * (count + 1),
        out_specs=in_vmem(count),
        out_shape=[jax.ShapeDtypeStruct(array.shape, array.dtype) for array in arrays],
        scratch_shapes=[pltpu.SemaphoreType.DMA((count,))],
        compiler_params=pltpu.CompilerParams(vmem_limit_bytes=8 * MIB),
        cost_estimate=pl.CostEstimate(flops=0, bytes_accessed=8 * MIB, transcendentals=0),
        name="stage_tables",
    )(*arrays, after)


def extra_rows(short_weights):
    sums = PIECES * short_weights.shape[0] * short_weights.shape[1]
    return sums, -(-(sums + 6 * RIM) // TILE) * TILE


def channel_kernel(tokens, heard, told, grad_scale, *refs):
    peers = len(heard)
    arrived = refs[:peers]
    weights, forward, backward = refs[peers : peers + 3]
    out = refs[peers + 3 : 2 * peers + 3]
    (
        query,
        key,
        value,
        cot,
        conv,
        conv_grad,
        filter_grad,
        taps,
        key_short,
        value_short,
        signals,
        spectra,
        products,
        extra,
    ) = refs[2 * peers + 3 :]
    size = peers * tokens // PHASES
    tap_count = weights.shape[1]
    me = lax.axis_index("ctx")
    own = lanes_of(me)
    for ref in (query, key, value, cot, conv, conv_grad):
        clear_ends(ref)
    for ref in (key_short, value_short):
        ref[:, size:, :] = jnp.zeros((PHASES, PAD, LANES), F32)
    for step, source in zip(heard, arrived):
        start = (me ^ step) * tokens
        inner = pl.ds(pl.multiple_of(PAD + start, PAD), tokens)
        for at, ref in enumerate((query, key, value, cot)):
            ref[inner, :] = source[at * tokens : (at + 1) * tokens, :].astype(F32)
        taps[pl.ds(pl.multiple_of(start, PAD), tokens), :] = source[4 * tokens :, :].astype(F32)
    chunks = range(size // CHUNK)
    taps_of = [
        [weights[array, tap : tap + 1, own] for tap in range(tap_count)] for array in range(3)
    ]

    def rows_of(chunk):
        return slice(chunk * CHUNK, (chunk + 1) * CHUNK)

    def spectrum(at, real, imag):
        lanes = slice(at * LANES, (at + 1) * LANES)
        return forward_mix(
            [(spectra[r, real, lanes], spectra[r, imag, lanes]) for r in range(PHASES)]
        )

    def keep(at, real, imag, mixed):
        lanes = slice(at * LANES, (at + 1) * LANES)
        for r, pair in enumerate(inverse_mix(mixed)):
            for rows, part in zip((real, imag), pair):
                products[r, rows, lanes] = part.astype(BF16)

    for chunk in chunks:
        rows = rows_of(chunk)
        key_now = short_conv(phases_near(key, chunk, tap_count), taps_of[1])
        value_now = short_conv(phases_near(value, chunk, tap_count), taps_of[2])
        for r in range(PHASES):
            key_short[r, rows, :] = key_now[r]
            value_short[r, rows, :] = value_now[r]
            signals[r, rows, :LANES] = (key_now[r] * value_now[r]).astype(BF16)
            filt = taps[pl.ds(chunk * CHUNK * PHASES + r, CHUNK, stride=PHASES), :]
            signals[r, rows, LANES : 2 * LANES] = filt.astype(BF16)
    for r in range(PHASES):
        spectra[r, :, : 2 * LANES] = transform(forward[r], signals[r, :, : 2 * LANES])
    for chunk in chunks:
        rows = rows_of(chunk)
        query_now = short_conv(phases_near(query, chunk, tap_count), taps_of[0])
        cot_now = phases_near(cot, chunk, 1)
        for r in range(PHASES):
            signals[r, rows, 2 * LANES :] = (cot_now[r] * query_now[r]).astype(BF16)
    for r in range(PHASES):
        spectra[r, :, 2 * LANES :] = transform(forward[r], signals[r, :, 2 * LANES :])
    for step in range(size // TILE):
        real = slice(step * TILE, (step + 1) * TILE)
        imag = slice(size + step * TILE, size + (step + 1) * TILE)
        prod, filt = spectrum(0, real, imag), spectrum(1, real, imag)
        for at, mixed in enumerate((prod, filt)):
            lanes = slice(at * LANES, (at + 1) * LANES)
            for q, pair in enumerate(mixed):
                spectra[q, real, lanes], spectra[q, imag, lanes] = pair
        keep(0, real, imag, times(prod, filt))
    for r in range(PHASES):
        result = transform(backward[r], products[r, :, :LANES])
        conv[pl.ds(PAD + r, size, stride=PHASES), :] = result.astype(BF16).astype(F32)
    for step in range(size // TILE):
        real = slice(step * TILE, (step + 1) * TILE)
        imag = slice(size + step * TILE, size + (step + 1) * TILE)
        grad = spectrum(2, real, imag)
        for at in range(2):
            lanes = slice(at * LANES, (at + 1) * LANES)
            known = [(spectra[q, real, lanes], spectra[q, imag, lanes]) for q in range(PHASES)]
            keep(2 - at, real, imag, conj_times(known, grad))
    for r in range(PHASES):
        result = transform(backward[r], products[r, :, LANES:])
        conv_grad[pl.ds(PAD + r, size, stride=PHASES), :] = (
            result[:, :LANES].astype(BF16).astype(F32)
        )
        filter_grad[pl.ds(r, size, stride=PHASES), :] = result[:, LANES:] * grad_scale

    totals = [[None] * tap_count for _ in range(3)]

    def add_sums(array, signal, chunk, pre):
        near = phases_near(signal, chunk, tap_count)
        for tap in range(tap_count):
            totals[array][tap] = add_rows(
                totals[array][tap], [pre[r] * near[r - tap] for r in range(PHASES)]
            )

    for chunk in chunks:
        cot_now, conv_now = phases_near(cot, chunk, 1), phases_near(conv, chunk, 1)
        add_sums(0, query, chunk, [cot_now[r] * conv_now[r] for r in range(PHASES)])
    for chunk in chunks:
        rows = rows_of(chunk)
        grad_now = phases_near(conv_grad, chunk, 1)
        add_sums(1, key, chunk, [grad_now[r] * value_short[r, rows, :] for r in range(PHASES)])
        add_sums(2, value, chunk, [grad_now[r] * key_short[r, rows, :] for r in range(PHASES)])
    sums = [jnp.sum(total, axis=0, keepdims=True) for row in totals for total in row]
    rest = jnp.concatenate(sums, axis=0) * grad_scale
    extra[...] = jnp.zeros_like(extra)
    for piece in range(PIECES):
        rounded = rest.astype(BF16).astype(F32)
        extra[piece * len(sums) : (piece + 1) * len(sums), :] = rounded
        rest = rest - rounded
    for step, target in zip(told, out):
        start = (me ^ step) * tokens
        inner = pl.ds(pl.multiple_of(PAD + start, PAD), tokens)
        target[:tokens, :] = conv[inner, :].astype(BF16)
        target[tokens : 2 * tokens, :] = conv_grad[inner, :].astype(BF16)
        target[2 * tokens : 3 * tokens, :] = filter_grad[
            pl.ds(pl.multiple_of(start, PAD), tokens), :
        ].astype(BF16)
        before = pl.ds(pl.multiple_of(start, PAD), PAD)
        after = pl.ds(pl.multiple_of(PAD + start + tokens, PAD), PAD)
        at = PIECES * len(sums)
        for ref in (query, key, value):
            extra[at : at + RIM, :] = ref[before, :][PAD - RIM :]
            at += RIM
        row = pl.ds(pl.multiple_of((start + tokens) // PHASES, PAD), PAD)
        extra[at : at + RIM, :] = (cot[after, :] * conv[after, :])[:RIM]
        for short in (value_short, key_short):
            at += RIM
            shorts = jnp.concatenate([short[r, row, :][:1] for r in range(RIM)], axis=0)
            extra[at : at + RIM, :] = conv_grad[after, :][:RIM] * shorts
        target[3 * tokens :, :] = extra[...].astype(BF16)


def channel_step(arrived, heard, told, short_weights, tables, tokens):
    peers = len(arrived)
    seq_len = peers * tokens
    size = seq_len // PHASES
    extra = extra_rows(short_weights)[1]
    padded = pltpu.VMEM((seq_len + 2 * PAD, LANES), F32)
    plain = pltpu.VMEM((seq_len, LANES), F32)
    phases = pltpu.VMEM((PHASES, size + PAD, LANES), F32)
    return pl.pallas_call(
        functools.partial(channel_kernel, tokens, heard, told, 1.0 / math.sqrt(seq_len)),
        in_specs=in_vmem(peers + 3),
        out_specs=in_vmem(peers),
        out_shape=[jax.ShapeDtypeStruct((3 * tokens + extra, LANES), BF16)] * peers,
        scratch_shapes=[
            *[padded] * 6,
            plain,
            plain,
            phases,
            phases,
            pltpu.VMEM((PHASES, size, 3 * LANES), BF16),
            pltpu.VMEM((PHASES, 2 * size, 3 * LANES), F32),
            pltpu.VMEM((PHASES, 2 * size, 3 * LANES), BF16),
            pltpu.VMEM((extra, LANES), F32),
        ],
        compiler_params=pltpu.CompilerParams(vmem_limit_bytes=VMEM_LIMIT),
        name="channel_operator",
    )(*arrived, short_weights, *tables)


def token_kernel(steps, sum_rows, carried, *refs):
    count_in = len(steps)
    arrived = refs[:count_in]
    query, key, value, cot, weights = refs[count_in : count_in + 5]
    results = refs[count_in + 5 + carried : count_in + 11 + carried]
    (gated, query_grad, key_grad, value_grad, filter_grad, short_grad, longer, pre, sems) = refs[
        count_in + 11 + carried :
    ]
    copies = []
    tokens = query.shape[0]
    tap_count = weights.shape[1]
    count = sum_rows // PIECES
    me = lax.axis_index("ctx")
    for slot, (step, source) in enumerate(zip(steps, arrived)):
        lanes = lanes_of(me ^ step)
        extra = source[3 * tokens :, :].astype(F32)

        def rim(at):
            return extra[sum_rows + at * RIM : sum_rows + (at + 1) * RIM]

        def short(array, signal):
            longer[array, PAD - RIM : PAD, :] = rim(array)
            longer[array, PAD :, :] = signal[:, lanes].astype(F32)
            summed = weights[array, 0:1, lanes] * longer[array, PAD:, :]
            for tap in range(1, tap_count):
                summed = (
                    summed
                    + weights[array, tap : tap + 1, lanes]
                    * longer[array, PAD - tap : PAD - tap + tokens, :]
                )
            return summed

        def taps_back(array, grad, target):
            pre[array, :tokens, :] = grad
            pre[array, tokens : tokens + RIM, :] = rim(3 + array)
            summed = weights[array, 0:1, lanes] * grad
            for tap in range(1, tap_count):
                summed = (
                    summed
                    + weights[array, tap : tap + 1, lanes] * pre[array, tap : tap + tokens, :]
                )
            target[slot] = summed.astype(BF16)

        conv = source[:tokens, :].astype(F32)
        conv_grad = source[tokens : 2 * tokens, :].astype(F32)
        gated[slot] = (short(0, query) * conv).astype(BF16)
        taps_back(0, cot[:, lanes].astype(F32) * conv, query_grad)
        taps_back(1, conv_grad * short(2, value), key_grad)
        taps_back(2, conv_grad * short(1, key), value_grad)
        filter_grad[slot] = source[2 * tokens : 3 * tokens, :].astype(F32)
        whole = extra[:count]
        for piece in range(1, PIECES):
            whole = whole + extra[piece * count : (piece + 1) * count]
        for row in range(count):
            which, tap = divmod(row, tap_count)
            short_grad[slot, which, tap : tap + 1, :] = whole[row : row + 1]
        held = (gated, query_grad, key_grad, value_grad, filter_grad, short_grad)
        for at, (source, target) in enumerate(zip(held, results)):
            place = target.at[:, :, lanes] if at == 5 else target.at[:, lanes]
            copies.append(pltpu.make_async_copy(source.at[slot], place, sems.at[slot, at]))
            copies[-1].start()
    for copy in copies:
        copy.wait()


def token_step(arrived, steps, query, key, value, cot, short_weights, begun=()):
    tokens, width = query.shape
    count = len(arrived)
    wide = jax.ShapeDtypeStruct((tokens, width), BF16)
    anywhere = pl.BlockSpec(memory_space=pl.ANY)
    return pl.pallas_call(
        functools.partial(token_kernel, steps, extra_rows(short_weights)[0], len(begun)),
        in_specs=in_vmem(count + 5) + [anywhere] * len(begun),
        out_specs=[anywhere] * 6,
        out_shape=[wide] * 4
        + [
            jax.ShapeDtypeStruct((tokens, width), F32),
            jax.ShapeDtypeStruct(short_weights.shape, F32),
        ],
        scratch_shapes=[
            *[pltpu.VMEM((count, tokens, LANES), BF16)] * 4,
            pltpu.VMEM((count, tokens, LANES), F32),
            pltpu.VMEM((count, *short_weights.shape[:2], LANES), F32),
            pltpu.VMEM((3, tokens + PAD, LANES), F32),
            pltpu.VMEM((3, tokens + PAD, LANES), F32),
            pltpu.SemaphoreType.DMA((count, 6)),
        ],
        input_output_aliases={count + 5 + at: at for at in range(len(begun))},
        compiler_params=pltpu.CompilerParams(vmem_limit_bytes=VMEM_LIMIT),
        cost_estimate=pl.CostEstimate(flops=0, bytes_accessed=4 * MIB, transcendentals=0),
        name="token_outputs",
    )(*arrived, query, key, value, cot, short_weights, *begun)


def channel_shards(query_proj, key_proj, value_proj, cotangent, filter_taps, short_weights):
    peers = lax.axis_size("ctx")
    tokens = query_proj.shape[0]
    tables = [jnp.asarray(table) for table in dft_tables(peers * tokens)]
    going, coming = partners(peers, False), partners(peers, True)
    sent = pack((query_proj, key_proj, value_proj, cotangent, filter_taps), going)
    arrived = exchange(sent, going)
    staged = stage((sent[0], short_weights, *tables), arrived[1])
    arrived[0] = staged[0]
    results = channel_step(arrived, going, coming, staged[1], staged[2:], tokens)
    back = exchange(results, coming)
    local = (query_proj, key_proj, value_proj, cotangent, short_weights)
    early = 1 + sum((step >> 1).bit_count() > 1 for step in coming)
    begun = token_step(back[:early], coming[:early], *local)
    return tuple(token_step(back[early:], coming[early:], *local, begun))


def from_behind(array, axis, by):
    peers = lax.axis_size(axis)
    pairs = [(i, i + by) for i in range(peers) if 0 <= i + by < peers]
    return lax.ppermute(array, axis, pairs)


def contract(form, left, right):
    return jnp.einsum(
        form, left, right, precision=lax.Precision.HIGHEST, preferred_element_type=jnp.float32
    )


def table_pair(rows, cols, period):
    row_ids = lax.broadcasted_iota(jnp.int32, (rows, cols), 0)
    col_ids = lax.broadcasted_iota(jnp.int32, (rows, cols), 1)
    angle = 2.0 * math.pi / period * (row_ids * col_ids % period).astype(jnp.float32)
    return (jnp.cos(angle), jnp.sin(angle))


def make_plan(seq_len):
    small_len = int(math.isqrt(2 * seq_len))
    while seq_len % small_len:
        small_len -= 1
    large_len = 2 * seq_len // small_len
    large_cos, large_sin = table_pair(large_len // 2, large_len, large_len)
    small_cos, small_sin = table_pair(small_len, small_len, small_len)
    twist_cos, twist_sin = table_pair(large_len, small_len, small_len * large_len)
    fwd_large = jnp.stack([large_cos, -large_sin], axis=1)
    fwd_small = jnp.stack([jnp.stack([small_cos, -small_sin]), jnp.stack([small_sin, small_cos])])
    inv_small = jnp.stack([jnp.stack([small_cos, small_sin]), jnp.stack([-small_sin, small_cos])])
    inv_large = jnp.stack([large_cos, -large_sin])
    return (small_len, large_len, fwd_large, fwd_small, inv_small, inv_large, twist_cos, twist_sin)


def forward_spec(signal, dft_plan):
    small_len, large_len, fwd_large, fwd_small, inv_small, inv_large, twist_cos, twist_sin = (
        dft_plan
    )
    cube = signal.reshape(signal.shape[0], large_len // 2, small_len)
    section_one = contract("cba,bpk->cpka", cube, fwd_large)
    real_one = section_one[:, 0]
    imag_one = section_one[:, 1]
    section_two = jnp.stack(
        [real_one * twist_cos + imag_one * twist_sin, imag_one * twist_cos - real_one * twist_sin],
        axis=1,
    )
    return contract("cpka,pqaj->cqkj", section_two, fwd_small)


def inverse_half(spec, dft_plan):
    small_len, large_len, fwd_large, fwd_small, inv_small, inv_large, twist_cos, twist_sin = (
        dft_plan
    )
    section_one = contract("cqkj,qpja->cpka", spec, inv_small)
    real_one = section_one[:, 0]
    imag_one = section_one[:, 1]
    section_two = jnp.stack(
        [real_one * twist_cos - imag_one * twist_sin, imag_one * twist_cos + real_one * twist_sin],
        axis=1,
    )
    signal = contract("cpka,pbk->cba", section_two, inv_large)
    return signal.reshape(signal.shape[0], -1) / float(small_len * large_len)


def complex_mul(left, right):
    left_real, left_imag = (left[:, 0], left[:, 1])
    right_real, right_imag = (right[:, 0], right[:, 1])
    return jnp.stack(
        [
            left_real * right_real - left_imag * right_imag,
            left_real * right_imag + left_imag * right_real,
        ],
        axis=1,
    )


def conj_mul(left, right):
    left_real, left_imag = (left[:, 0], left[:, 1])
    right_real, right_imag = (right[:, 0], right[:, 1])
    return jnp.stack(
        [
            left_real * right_real + left_imag * right_imag,
            left_real * right_imag - left_imag * right_real,
        ],
        axis=1,
    )


def conv_forward(prod_chan, filter_spec, dft_plan):
    prod_spec = forward_spec(prod_chan.astype(jnp.float32), dft_plan)
    conv_chan = inverse_half(complex_mul(prod_spec, filter_spec), dft_plan).astype(jnp.bfloat16)
    return (conv_chan, prod_spec)


def conv_backward(grad_chan, filter_spec, prod_spec, dft_plan, grad_scale):
    grad_spec = forward_spec(grad_chan.astype(jnp.float32), dft_plan)
    dconv_chan = inverse_half(conj_mul(filter_spec, grad_spec), dft_plan).astype(jnp.bfloat16)
    dfilter_chan = inverse_half(conj_mul(prod_spec, grad_spec), dft_plan) * grad_scale
    return (dconv_chan, dfilter_chan)


def receive_filter(filter_taps, dft_plan):
    filter_chan = lax.all_to_all(filter_taps.T, "ctx", split_axis=0, concat_axis=1, tiled=True)
    return forward_spec(filter_chan, dft_plan)


def return_filter(dfilter_chan):
    return (
        lax.all_to_all(
            dfilter_chan.astype(jnp.bfloat16), "ctx", split_axis=1, concat_axis=0, tiled=True
        )
        .astype(dfilter_chan.dtype)
        .T
    )


def causal_taps(extended, weights, length, axis):
    rim_rows = len(weights) - 1
    summed = weights[0] * lax.slice_in_dim(extended, rim_rows, rim_rows + length, axis=axis)
    for offset in range(1, len(weights)):
        summed = summed + weights[offset] * lax.slice_in_dim(
            extended, rim_rows - offset, rim_rows - offset + length, axis=axis
        )
    return summed


def reverse_taps(extended, weights, length, axis):
    summed = weights[0] * lax.slice_in_dim(extended, 0, length, axis=axis)
    for offset in range(1, len(weights)):
        summed = summed + weights[offset] * lax.slice_in_dim(
            extended, offset, offset + length, axis=axis
        )
    return summed


def tap_grads(grad_in, extended, tap_count, length, axis):
    rim_rows = tap_count - 1
    rows = [
        jnp.sum(
            grad_in
            * lax.slice_in_dim(extended, rim_rows - offset, rim_rows - offset + length, axis=axis),
            axis=axis,
        )
        for offset in range(tap_count)
    ]
    return jnp.stack(rows, axis=1)


def spread_shards(query_proj, key_proj, value_proj, cotangent, filter_taps, short_weights):
    tokens = query_proj.shape[0]
    tap_count = short_weights.shape[1]
    rim_rows = tap_count - 1
    seq_len = tokens * lax.axis_size("ctx")
    grad_scale = 1.0 / math.sqrt(seq_len)
    dft_plan = make_plan(seq_len)
    stacked = jnp.stack([query_proj, key_proj, value_proj])
    prev_rim = from_behind(stacked[:, tokens - rim_rows :], "ctx", 1)
    extended = jnp.concatenate([prev_rim, stacked], axis=1).astype(jnp.float32)
    weights = [short_weights[:, offset, None, :] for offset in range(tap_count)]
    short_out = causal_taps(extended, weights, tokens, 1)
    product = (short_out[1] * short_out[2]).astype(jnp.bfloat16)
    cot_wide = cotangent.astype(jnp.float32)
    gate_grad = (cot_wide * short_out[0]).astype(jnp.bfloat16)
    filter_spec = receive_filter(filter_taps, dft_plan)
    prod_chan = lax.all_to_all(product.T, "ctx", split_axis=0, concat_axis=1, tiled=True)
    conv_chan, prod_spec = conv_forward(prod_chan, filter_spec, dft_plan)
    conv_tok = lax.all_to_all(conv_chan, "ctx", split_axis=1, concat_axis=0, tiled=True)
    grad_chan = lax.all_to_all(gate_grad.T, "ctx", split_axis=0, concat_axis=1, tiled=True)
    dconv_chan, dfilter_chan = conv_backward(
        grad_chan, filter_spec, prod_spec, dft_plan, grad_scale
    )
    dconv_tok = lax.all_to_all(dconv_chan, "ctx", split_axis=1, concat_axis=0, tiled=True)
    filter_grad = return_filter(dfilter_chan)
    conv_wide = conv_tok.T.astype(jnp.float32)
    dconv_wide = dconv_tok.T.astype(jnp.float32)
    gated = (short_out[0] * conv_wide).astype(jnp.bfloat16)
    token_grads = jnp.stack(
        [cot_wide * conv_wide, dconv_wide * short_out[2], dconv_wide * short_out[1]]
    )
    next_rim = from_behind(token_grads[:, :rim_rows], "ctx", -1)
    grad_ext = jnp.concatenate([token_grads, next_rim], axis=1)
    inputs_grad = reverse_taps(grad_ext, weights, tokens, 1).astype(jnp.bfloat16)
    weight_part = tap_grads(token_grads, extended, tap_count, tokens, 1)
    short_grad = lax.psum(weight_part, "ctx") * grad_scale
    results = (gated, inputs_grad[0], inputs_grad[1], inputs_grad[2])
    return (results[0], results[1], results[2], results[3], filter_grad, short_grad)


def fits(query_proj, short_weights):
    peers = lax.axis_size("ctx")
    tokens, width = query_proj.shape
    tap_count = short_weights.shape[1]
    return (
        width == peers * LANES
        and peers.bit_count() == 1
        and tokens % (PHASES * CHUNK) == 0
        and tap_count == RIM + 1
        and peers * tokens <= 2048
    )


def shards(*arrays):
    return channel_shards(*arrays) if fits(arrays[0], arrays[5]) else spread_shards(*arrays)


def solution(mesh):
    placed = (
        P("ctx", "tp"),
        P("ctx", "tp"),
        P("ctx", "tp"),
        P("ctx", "tp"),
        P("ctx", "tp"),
        P(None, None, "tp"),
    )
    return jax.shard_map(
        shards,
        mesh=mesh,
        in_specs=placed,
        out_specs=(
            P("ctx", "tp"),
            P("ctx", "tp"),
            P("ctx", "tp"),
            P("ctx", "tp"),
            P("ctx", "tp"),
            P(None, None, "tp"),
        ),
        check_vma=False,
    )
```

```python
import functools
import math

import jax
import jax.numpy as jnp
import numpy as np
from jax import lax
from jax.experimental import pallas as pl
from jax.experimental.pallas import tpu as pltpu
from jax.sharding import PartitionSpec as P

F32 = jnp.float32
BF16 = jnp.bfloat16
LANES = 128
PHASES = 4
TILE = 16
PAD = 8
CHUNK = 32
RIM = 2
PIECES = 2
MIB = 1024 * 1024
VMEM_LIMIT = 24 * MIB
PACK_VMEM = 53862 * 1024


def partners(peers, diagonal_first):
    def rank(step):
        links, other_core = (step >> 1).bit_count(), step & 1
        if links == 1:
            return (3 if other_core else 1 + diagonal_first, 0, -step)
        if links == 0:
            return (1 if diagonal_first else 4, 0, 0)
        return (0 if diagonal_first else 2, other_core, -step)

    return [0] + sorted(range(1, peers), key=rank)


def exchange(blocks, steps):
    peers = len(blocks)
    got = [blocks[0]]
    for step, block in list(zip(steps, blocks))[1:]:
        got.append(lax.ppermute(block, "ctx", [(i, i ^ step) for i in range(peers)]))
    return got


def in_vmem(count):
    return [pl.BlockSpec(memory_space=pltpu.VMEM)] * count


def lanes_of(place):
    return pl.ds(pl.multiple_of(place * LANES, LANES), LANES)


def pack_kernel(count, steps, *refs):
    sources, packed = refs[:count], refs[count : count + len(steps)]
    held, sems = refs[count + len(steps) : -1], refs[-1]
    tokens = sources[0].shape[0]
    me = lax.axis_index("ctx")
    arriving = [
        pltpu.make_async_copy(source, target, sems.at[at])
        for at, (source, target) in enumerate(zip(sources, held))
    ]
    for copy in arriving:
        copy.start()
    for at, source in enumerate(held):
        arriving[at].wait()
        rows = slice(at * tokens, (at + 1) * tokens)
        for step, target in zip(steps, packed):
            target[rows, :] = source[:, lanes_of(me ^ step)].astype(BF16)


def pack(arrays, steps):
    tokens = arrays[0].shape[0]
    count = len(arrays)
    return pl.pallas_call(
        functools.partial(pack_kernel, count, steps),
        in_specs=[pl.BlockSpec(memory_space=pl.ANY)] * count,
        out_specs=in_vmem(len(steps)),
        out_shape=[jax.ShapeDtypeStruct((count * tokens, LANES), BF16)] * len(steps),
        scratch_shapes=[
            *[pltpu.VMEM(array.shape, array.dtype) for array in arrays],
            pltpu.SemaphoreType.DMA((count,)),
        ],
        compiler_params=pltpu.CompilerParams(vmem_limit_bytes=PACK_VMEM),
        cost_estimate=pl.CostEstimate(flops=0, bytes_accessed=8 * MIB, transcendentals=0),
        name="pack_inputs",
    )(*arrays)


@functools.lru_cache(maxsize=None)
def dft_tables(seq_len):
    size = seq_len // PHASES
    k = np.arange(size, dtype=np.int64)[:, None]
    m = np.arange(size, dtype=np.int64)[None, :]
    forward = []
    for phase in range(PHASES):
        turns = ((4 * k + 1) * (PHASES * m + phase)) % (4 * seq_len)
        angle = 2.0 * np.pi / (4 * seq_len) * turns
        forward.append(np.concatenate([np.cos(angle), -np.sin(angle)], axis=0))
    forward = np.stack(forward)
    backward = np.swapaxes(forward, 1, 2) / seq_len

    def pieces(table):
        high = table.astype(BF16)
        low = (table - high.astype(np.float64)).astype(BF16)
        return np.stack([high, low], axis=1)

    return pieces(forward), backward.astype(BF16)


def forward_mix(parts):
    (r0, i0), (r1, i1), (r2, i2), (r3, i3) = parts
    ar, ai, br, bi = r0 + r2, i0 + i2, r0 - r2, i0 - i2
    cr, ci, dr, di = r1 + r3, i1 + i3, r1 - r3, i1 - i3
    return ((ar + cr, ai + ci), (br + di, bi - dr), (ar - cr, ai - ci), (br - di, bi + dr))


def inverse_mix(parts):
    (r0, i0), (r1, i1), (r2, i2), (r3, i3) = parts
    ar, ai, br, bi = r0 + r2, i0 + i2, r0 - r2, i0 - i2
    cr, ci, dr, di = r1 + r3, i1 + i3, r1 - r3, i1 - i3
    return ((ar + cr, ai + ci), (br - di, bi + dr), (ar - cr, ai - ci), (br + di, bi - dr))


def times(left, right):
    return tuple(
        (lr * rr - li * ri, lr * ri + li * rr) for (lr, li), (rr, ri) in zip(left, right)
    )


def conj_times(left, right):
    return tuple(
        (lr * rr + li * ri, lr * ri - li * rr) for (lr, li), (rr, ri) in zip(left, right)
    )


def transform(tables, signal):
    return jnp.dot(tables[0], signal, preferred_element_type=F32) + jnp.dot(
        tables[1], signal, preferred_element_type=F32
    )


def phases_near(ref, chunk, tap_count):
    start = PAD + chunk * CHUNK * PHASES
    return {
        offset: ref[pl.ds(start + offset, CHUNK, stride=PHASES), :]
        for offset in range(1 - tap_count, PHASES)
    }


def short_conv(near, taps):
    results = []
    for r in range(PHASES):
        summed = taps[0] * near[r]
        for at in range(1, len(taps)):
            summed = summed + taps[at] * near[r - at]
        results.append(summed)
    return results


def add_rows(total, terms):
    for term in terms:
        folded = jnp.sum(term.reshape(CHUNK // 8, 8, LANES), axis=0)
        total = folded if total is None else total + folded
    return total


def clear_ends(ref):
    ref[:PAD, :] = jnp.zeros((PAD, LANES), F32)
    ref[ref.shape[0] - PAD :, :] = jnp.zeros((PAD, LANES), F32)


def stage_kernel(count, *refs):
    sources, targets, sems = refs[:count], refs[count + 1 : 2 * count + 1], refs[2 * count + 1]
    copies = [
        pltpu.make_async_copy(source, target, sems.at[at])
        for at, (source, target) in enumerate(zip(sources, targets))
    ]
    for copy in copies:
        copy.start()
    for copy in copies:
        copy.wait()


def stage(arrays, after):
    count = len(arrays)
    return pl.pallas_call(
        functools.partial(stage_kernel, count),
        in_specs=[pl.BlockSpec(memory_space=pl.ANY)] * (count + 1),
        out_specs=in_vmem(count),
        out_shape=[jax.ShapeDtypeStruct(array.shape, array.dtype) for array in arrays],
        scratch_shapes=[pltpu.SemaphoreType.DMA((count,))],
        compiler_params=pltpu.CompilerParams(vmem_limit_bytes=8 * MIB),
        cost_estimate=pl.CostEstimate(flops=0, bytes_accessed=8 * MIB, transcendentals=0),
        name="stage_tables",
    )(*arrays, after)


def extra_rows(short_weights):
    sums = PIECES * short_weights.shape[0] * short_weights.shape[1]
    return sums, -(-(sums + 6 * RIM) // TILE) * TILE


def channel_kernel(tokens, heard, told, grad_scale, *refs):
    peers = len(heard)
    arrived = refs[:peers]
    weights, forward, backward = refs[peers : peers + 3]
    out = refs[peers + 3 : 2 * peers + 3]
    (
        query,
        key,
        value,
        cot,
        conv,
        conv_grad,
        filter_grad,
        taps,
        key_short,
        value_short,
        signals,
        spectra,
        products,
        extra,
    ) = refs[2 * peers + 3 :]
    size = peers * tokens // PHASES
    tap_count = weights.shape[1]
    me = lax.axis_index("ctx")
    own = lanes_of(me)
    for ref in (query, key, value, cot, conv, conv_grad):
        clear_ends(ref)
    for ref in (key_short, value_short):
        ref[:, size:, :] = jnp.zeros((PHASES, PAD, LANES), F32)
    for step, source in zip(heard, arrived):
        start = (me ^ step) * tokens
        inner = pl.ds(pl.multiple_of(PAD + start, PAD), tokens)
        for at, ref in enumerate((query, key, value, cot)):
            ref[inner, :] = source[at * tokens : (at + 1) * tokens, :].astype(F32)
        taps[pl.ds(pl.multiple_of(start, PAD), tokens), :] = source[4 * tokens :, :].astype(F32)
    chunks = range(size // CHUNK)
    taps_of = [
        [weights[array, tap : tap + 1, own] for tap in range(tap_count)] for array in range(3)
    ]

    def rows_of(chunk):
        return slice(chunk * CHUNK, (chunk + 1) * CHUNK)

    def spectrum(at, real, imag):
        lanes = slice(at * LANES, (at + 1) * LANES)
        return forward_mix(
            [(spectra[r, real, lanes], spectra[r, imag, lanes]) for r in range(PHASES)]
        )

    def keep(at, real, imag, mixed):
        lanes = slice(at * LANES, (at + 1) * LANES)
        for r, pair in enumerate(inverse_mix(mixed)):
            for rows, part in zip((real, imag), pair):
                products[r, rows, lanes] = part.astype(BF16)

    for chunk in chunks:
        rows = rows_of(chunk)
        key_now = short_conv(phases_near(key, chunk, tap_count), taps_of[1])
        value_now = short_conv(phases_near(value, chunk, tap_count), taps_of[2])
        for r in range(PHASES):
            key_short[r, rows, :] = key_now[r]
            value_short[r, rows, :] = value_now[r]
            signals[r, rows, :LANES] = (key_now[r] * value_now[r]).astype(BF16)
            filt = taps[pl.ds(chunk * CHUNK * PHASES + r, CHUNK, stride=PHASES), :]
            signals[r, rows, LANES : 2 * LANES] = filt.astype(BF16)
    for r in range(PHASES):
        spectra[r, :, : 2 * LANES] = transform(forward[r], signals[r, :, : 2 * LANES])
    for chunk in chunks:
        rows = rows_of(chunk)
        query_now = short_conv(phases_near(query, chunk, tap_count), taps_of[0])
        cot_now = phases_near(cot, chunk, 1)
        for r in range(PHASES):
            signals[r, rows, 2 * LANES :] = (cot_now[r] * query_now[r]).astype(BF16)
    for r in range(PHASES):
        spectra[r, :, 2 * LANES :] = transform(forward[r], signals[r, :, 2 * LANES :])
    for step in range(size // TILE):
        real = slice(step * TILE, (step + 1) * TILE)
        imag = slice(size + step * TILE, size + (step + 1) * TILE)
        prod, filt = spectrum(0, real, imag), spectrum(1, real, imag)
        for at, mixed in enumerate((prod, filt)):
            lanes = slice(at * LANES, (at + 1) * LANES)
            for q, pair in enumerate(mixed):
                spectra[q, real, lanes], spectra[q, imag, lanes] = pair
        keep(0, real, imag, times(prod, filt))
    for r in range(PHASES):
        result = jnp.dot(backward[r], products[r, :, :LANES], preferred_element_type=F32)
        conv[pl.ds(PAD + r, size, stride=PHASES), :] = result.astype(BF16).astype(F32)
    for step in range(size // TILE):
        real = slice(step * TILE, (step + 1) * TILE)
        imag = slice(size + step * TILE, size + (step + 1) * TILE)
        grad = spectrum(2, real, imag)
        for at in range(2):
            lanes = slice(at * LANES, (at + 1) * LANES)
            known = [(spectra[q, real, lanes], spectra[q, imag, lanes]) for q in range(PHASES)]
            keep(2 - at, real, imag, conj_times(known, grad))
    for r in range(PHASES):
        result = jnp.dot(backward[r], products[r, :, LANES:], preferred_element_type=F32)
        conv_grad[pl.ds(PAD + r, size, stride=PHASES), :] = (
            result[:, :LANES].astype(BF16).astype(F32)
        )
        filter_grad[pl.ds(r, size, stride=PHASES), :] = result[:, LANES:] * grad_scale

    totals = [[None] * tap_count for _ in range(3)]

    def add_sums(array, signal, chunk, pre):
        near = phases_near(signal, chunk, tap_count)
        for tap in range(tap_count):
            totals[array][tap] = add_rows(
                totals[array][tap], [pre[r] * near[r - tap] for r in range(PHASES)]
            )

    for chunk in chunks:
        cot_now, conv_now = phases_near(cot, chunk, 1), phases_near(conv, chunk, 1)
        add_sums(0, query, chunk, [cot_now[r] * conv_now[r] for r in range(PHASES)])
    for chunk in chunks:
        rows = rows_of(chunk)
        grad_now = phases_near(conv_grad, chunk, 1)
        add_sums(1, key, chunk, [grad_now[r] * value_short[r, rows, :] for r in range(PHASES)])
        add_sums(2, value, chunk, [grad_now[r] * key_short[r, rows, :] for r in range(PHASES)])
    sums = [jnp.sum(total, axis=0, keepdims=True) for row in totals for total in row]
    rest = jnp.concatenate(sums, axis=0) * grad_scale
    extra[...] = jnp.zeros_like(extra)
    for piece in range(PIECES):
        rounded = rest.astype(BF16).astype(F32)
        extra[piece * len(sums) : (piece + 1) * len(sums), :] = rounded
        rest = rest - rounded
    for step, target in zip(told, out):
        start = (me ^ step) * tokens
        inner = pl.ds(pl.multiple_of(PAD + start, PAD), tokens)
        target[:tokens, :] = conv[inner, :].astype(BF16)
        target[tokens : 2 * tokens, :] = conv_grad[inner, :].astype(BF16)
        target[2 * tokens : 3 * tokens, :] = filter_grad[
            pl.ds(pl.multiple_of(start, PAD), tokens), :
        ].astype(BF16)
        before = pl.ds(pl.multiple_of(start, PAD), PAD)
        after = pl.ds(pl.multiple_of(PAD + start + tokens, PAD), PAD)
        at = PIECES * len(sums)
        for ref in (query, key, value):
            extra[at : at + RIM, :] = ref[before, :][PAD - RIM :]
            at += RIM
        row = pl.ds(pl.multiple_of((start + tokens) // PHASES, PAD), PAD)
        extra[at : at + RIM, :] = (cot[after, :] * conv[after, :])[:RIM]
        for short in (value_short, key_short):
            at += RIM
            shorts = jnp.concatenate([short[r, row, :][:1] for r in range(RIM)], axis=0)
            extra[at : at + RIM, :] = conv_grad[after, :][:RIM] * shorts
        target[3 * tokens :, :] = extra[...].astype(BF16)


def channel_step(arrived, heard, told, short_weights, tables, tokens):
    peers = len(arrived)
    seq_len = peers * tokens
    size = seq_len // PHASES
    extra = extra_rows(short_weights)[1]
    padded = pltpu.VMEM((seq_len + 2 * PAD, LANES), F32)
    plain = pltpu.VMEM((seq_len, LANES), F32)
    phases = pltpu.VMEM((PHASES, size + PAD, LANES), F32)
    return pl.pallas_call(
        functools.partial(channel_kernel, tokens, heard, told, 1.0 / math.sqrt(seq_len)),
        in_specs=in_vmem(peers + 3),
        out_specs=in_vmem(peers),
        out_shape=[jax.ShapeDtypeStruct((3 * tokens + extra, LANES), BF16)] * peers,
        scratch_shapes=[
            *[padded] * 6,
            plain,
            plain,
            phases,
            phases,
            pltpu.VMEM((PHASES, size, 3 * LANES), BF16),
            pltpu.VMEM((PHASES, 2 * size, 3 * LANES), F32),
            pltpu.VMEM((PHASES, 2 * size, 3 * LANES), BF16),
            pltpu.VMEM((extra, LANES), F32),
        ],
        compiler_params=pltpu.CompilerParams(vmem_limit_bytes=VMEM_LIMIT),
        name="channel_operator",
    )(*arrived, short_weights, *tables)


def token_kernel(steps, sum_rows, carried, *refs):
    count_in = len(steps)
    arrived = refs[:count_in]
    query, key, value, cot, weights = refs[count_in : count_in + 5]
    results = refs[count_in + 5 + carried : count_in + 11 + carried]
    (gated, query_grad, key_grad, value_grad, filter_grad, short_grad, longer, pre, sems) = refs[
        count_in + 11 + carried :
    ]
    copies = []
    tokens = query.shape[0]
    tap_count = weights.shape[1]
    count = sum_rows // PIECES
    me = lax.axis_index("ctx")
    for slot, (step, source) in enumerate(zip(steps, arrived)):
        lanes = lanes_of(me ^ step)
        extra = source[3 * tokens :, :].astype(F32)

        def rim(at):
            return extra[sum_rows + at * RIM : sum_rows + (at + 1) * RIM]

        def short(array, signal):
            longer[array, PAD - RIM : PAD, :] = rim(array)
            longer[array, PAD :, :] = signal[:, lanes].astype(F32)
            summed = weights[array, 0:1, lanes] * longer[array, PAD:, :]
            for tap in range(1, tap_count):
                summed = (
                    summed
                    + weights[array, tap : tap + 1, lanes]
                    * longer[array, PAD - tap : PAD - tap + tokens, :]
                )
            return summed

        def taps_back(array, grad, target):
            pre[array, :tokens, :] = grad
            pre[array, tokens : tokens + RIM, :] = rim(3 + array)
            summed = weights[array, 0:1, lanes] * grad
            for tap in range(1, tap_count):
                summed = (
                    summed
                    + weights[array, tap : tap + 1, lanes] * pre[array, tap : tap + tokens, :]
                )
            target[slot] = summed.astype(BF16)

        conv = source[:tokens, :].astype(F32)
        conv_grad = source[tokens : 2 * tokens, :].astype(F32)
        gated[slot] = (short(0, query) * conv).astype(BF16)
        taps_back(0, cot[:, lanes].astype(F32) * conv, query_grad)
        taps_back(1, conv_grad * short(2, value), key_grad)
        taps_back(2, conv_grad * short(1, key), value_grad)
        filter_grad[slot] = source[2 * tokens : 3 * tokens, :].astype(F32)
        whole = extra[:count]
        for piece in range(1, PIECES):
            whole = whole + extra[piece * count : (piece + 1) * count]
        for row in range(count):
            which, tap = divmod(row, tap_count)
            short_grad[slot, which, tap : tap + 1, :] = whole[row : row + 1]
        held = (gated, query_grad, key_grad, value_grad, filter_grad, short_grad)
        for at, (source, target) in enumerate(zip(held, results)):
            place = target.at[:, :, lanes] if at == 5 else target.at[:, lanes]
            copies.append(pltpu.make_async_copy(source.at[slot], place, sems.at[slot, at]))
            copies[-1].start()
    for copy in copies:
        copy.wait()


def token_step(arrived, steps, query, key, value, cot, short_weights, begun=()):
    tokens, width = query.shape
    count = len(arrived)
    wide = jax.ShapeDtypeStruct((tokens, width), BF16)
    anywhere = pl.BlockSpec(memory_space=pl.ANY)
    return pl.pallas_call(
        functools.partial(token_kernel, steps, extra_rows(short_weights)[0], len(begun)),
        in_specs=in_vmem(count + 5) + [anywhere] * len(begun),
        out_specs=[anywhere] * 6,
        out_shape=[wide] * 4
        + [
            jax.ShapeDtypeStruct((tokens, width), F32),
            jax.ShapeDtypeStruct(short_weights.shape, F32),
        ],
        scratch_shapes=[
            *[pltpu.VMEM((count, tokens, LANES), BF16)] * 4,
            pltpu.VMEM((count, tokens, LANES), F32),
            pltpu.VMEM((count, *short_weights.shape[:2], LANES), F32),
            pltpu.VMEM((3, tokens + PAD, LANES), F32),
            pltpu.VMEM((3, tokens + PAD, LANES), F32),
            pltpu.SemaphoreType.DMA((count, 6)),
        ],
        input_output_aliases={count + 5 + at: at for at in range(len(begun))},
        compiler_params=pltpu.CompilerParams(vmem_limit_bytes=VMEM_LIMIT),
        cost_estimate=pl.CostEstimate(flops=0, bytes_accessed=4 * MIB, transcendentals=0),
        name="token_outputs",
    )(*arrived, query, key, value, cot, short_weights, *begun)


def channel_shards(query_proj, key_proj, value_proj, cotangent, filter_taps, short_weights):
    peers = lax.axis_size("ctx")
    tokens = query_proj.shape[0]
    tables = [jnp.asarray(table) for table in dft_tables(peers * tokens)]
    going, coming = partners(peers, False), partners(peers, True)
    sent = pack((query_proj, key_proj, value_proj, cotangent, filter_taps), going)
    arrived = exchange(sent, going)
    staged = stage((sent[0], short_weights, *tables), arrived[1])
    arrived[0] = staged[0]
    results = channel_step(arrived, going, coming, staged[1], staged[2:], tokens)
    back = exchange(results, coming)
    local = (query_proj, key_proj, value_proj, cotangent, short_weights)
    ends = [at for at in (4, 6) if at < peers] + [peers]
    begun, start = (), 0
    for end in ends:
        begun = token_step(back[start:end], coming[start:end], *local, begun)
        start = end
    return tuple(begun)


def from_behind(array, axis, by):
    peers = lax.axis_size(axis)
    pairs = [(i, i + by) for i in range(peers) if 0 <= i + by < peers]
    return lax.ppermute(array, axis, pairs)


def contract(form, left, right):
    return jnp.einsum(
        form, left, right, precision=lax.Precision.HIGHEST, preferred_element_type=jnp.float32
    )


def table_pair(rows, cols, period):
    row_ids = lax.broadcasted_iota(jnp.int32, (rows, cols), 0)
    col_ids = lax.broadcasted_iota(jnp.int32, (rows, cols), 1)
    angle = 2.0 * math.pi / period * (row_ids * col_ids % period).astype(jnp.float32)
    return (jnp.cos(angle), jnp.sin(angle))


def make_plan(seq_len):
    small_len = int(math.isqrt(2 * seq_len))
    while seq_len % small_len:
        small_len -= 1
    large_len = 2 * seq_len // small_len
    large_cos, large_sin = table_pair(large_len // 2, large_len, large_len)
    small_cos, small_sin = table_pair(small_len, small_len, small_len)
    twist_cos, twist_sin = table_pair(large_len, small_len, small_len * large_len)
    fwd_large = jnp.stack([large_cos, -large_sin], axis=1)
    fwd_small = jnp.stack([jnp.stack([small_cos, -small_sin]), jnp.stack([small_sin, small_cos])])
    inv_small = jnp.stack([jnp.stack([small_cos, small_sin]), jnp.stack([-small_sin, small_cos])])
    inv_large = jnp.stack([large_cos, -large_sin])
    return (small_len, large_len, fwd_large, fwd_small, inv_small, inv_large, twist_cos, twist_sin)


def forward_spec(signal, dft_plan):
    small_len, large_len, fwd_large, fwd_small, inv_small, inv_large, twist_cos, twist_sin = (
        dft_plan
    )
    cube = signal.reshape(signal.shape[0], large_len // 2, small_len)
    section_one = contract("cba,bpk->cpka", cube, fwd_large)
    real_one = section_one[:, 0]
    imag_one = section_one[:, 1]
    section_two = jnp.stack(
        [real_one * twist_cos + imag_one * twist_sin, imag_one * twist_cos - real_one * twist_sin],
        axis=1,
    )
    return contract("cpka,pqaj->cqkj", section_two, fwd_small)


def inverse_half(spec, dft_plan):
    small_len, large_len, fwd_large, fwd_small, inv_small, inv_large, twist_cos, twist_sin = (
        dft_plan
    )
    section_one = contract("cqkj,qpja->cpka", spec, inv_small)
    real_one = section_one[:, 0]
    imag_one = section_one[:, 1]
    section_two = jnp.stack(
        [real_one * twist_cos - imag_one * twist_sin, imag_one * twist_cos + real_one * twist_sin],
        axis=1,
    )
    signal = contract("cpka,pbk->cba", section_two, inv_large)
    return signal.reshape(signal.shape[0], -1) / float(small_len * large_len)


def complex_mul(left, right):
    left_real, left_imag = (left[:, 0], left[:, 1])
    right_real, right_imag = (right[:, 0], right[:, 1])
    return jnp.stack(
        [
            left_real * right_real - left_imag * right_imag,
            left_real * right_imag + left_imag * right_real,
        ],
        axis=1,
    )


def conj_mul(left, right):
    left_real, left_imag = (left[:, 0], left[:, 1])
    right_real, right_imag = (right[:, 0], right[:, 1])
    return jnp.stack(
        [
            left_real * right_real + left_imag * right_imag,
            left_real * right_imag - left_imag * right_real,
        ],
        axis=1,
    )


def conv_forward(prod_chan, filter_spec, dft_plan):
    prod_spec = forward_spec(prod_chan.astype(jnp.float32), dft_plan)
    conv_chan = inverse_half(complex_mul(prod_spec, filter_spec), dft_plan).astype(jnp.bfloat16)
    return (conv_chan, prod_spec)


def conv_backward(grad_chan, filter_spec, prod_spec, dft_plan, grad_scale):
    grad_spec = forward_spec(grad_chan.astype(jnp.float32), dft_plan)
    dconv_chan = inverse_half(conj_mul(filter_spec, grad_spec), dft_plan).astype(jnp.bfloat16)
    dfilter_chan = inverse_half(conj_mul(prod_spec, grad_spec), dft_plan) * grad_scale
    return (dconv_chan, dfilter_chan)


def receive_filter(filter_taps, dft_plan):
    filter_chan = lax.all_to_all(filter_taps.T, "ctx", split_axis=0, concat_axis=1, tiled=True)
    return forward_spec(filter_chan, dft_plan)


def return_filter(dfilter_chan):
    return (
        lax.all_to_all(
            dfilter_chan.astype(jnp.bfloat16), "ctx", split_axis=1, concat_axis=0, tiled=True
        )
        .astype(dfilter_chan.dtype)
        .T
    )


def causal_taps(extended, weights, length, axis):
    rim_rows = len(weights) - 1
    summed = weights[0] * lax.slice_in_dim(extended, rim_rows, rim_rows + length, axis=axis)
    for offset in range(1, len(weights)):
        summed = summed + weights[offset] * lax.slice_in_dim(
            extended, rim_rows - offset, rim_rows - offset + length, axis=axis
        )
    return summed


def reverse_taps(extended, weights, length, axis):
    summed = weights[0] * lax.slice_in_dim(extended, 0, length, axis=axis)
    for offset in range(1, len(weights)):
        summed = summed + weights[offset] * lax.slice_in_dim(
            extended, offset, offset + length, axis=axis
        )
    return summed


def tap_grads(grad_in, extended, tap_count, length, axis):
    rim_rows = tap_count - 1
    rows = [
        jnp.sum(
            grad_in
            * lax.slice_in_dim(extended, rim_rows - offset, rim_rows - offset + length, axis=axis),
            axis=axis,
        )
        for offset in range(tap_count)
    ]
    return jnp.stack(rows, axis=1)


def spread_shards(query_proj, key_proj, value_proj, cotangent, filter_taps, short_weights):
    tokens = query_proj.shape[0]
    tap_count = short_weights.shape[1]
    rim_rows = tap_count - 1
    seq_len = tokens * lax.axis_size("ctx")
    grad_scale = 1.0 / math.sqrt(seq_len)
    dft_plan = make_plan(seq_len)
    stacked = jnp.stack([query_proj, key_proj, value_proj])
    prev_rim = from_behind(stacked[:, tokens - rim_rows :], "ctx", 1)
    extended = jnp.concatenate([prev_rim, stacked], axis=1).astype(jnp.float32)
    weights = [short_weights[:, offset, None, :] for offset in range(tap_count)]
    short_out = causal_taps(extended, weights, tokens, 1)
    product = (short_out[1] * short_out[2]).astype(jnp.bfloat16)
    cot_wide = cotangent.astype(jnp.float32)
    gate_grad = (cot_wide * short_out[0]).astype(jnp.bfloat16)
    filter_spec = receive_filter(filter_taps, dft_plan)
    prod_chan = lax.all_to_all(product.T, "ctx", split_axis=0, concat_axis=1, tiled=True)
    conv_chan, prod_spec = conv_forward(prod_chan, filter_spec, dft_plan)
    conv_tok = lax.all_to_all(conv_chan, "ctx", split_axis=1, concat_axis=0, tiled=True)
    grad_chan = lax.all_to_all(gate_grad.T, "ctx", split_axis=0, concat_axis=1, tiled=True)
    dconv_chan, dfilter_chan = conv_backward(
        grad_chan, filter_spec, prod_spec, dft_plan, grad_scale
    )
    dconv_tok = lax.all_to_all(dconv_chan, "ctx", split_axis=1, concat_axis=0, tiled=True)
    filter_grad = return_filter(dfilter_chan)
    conv_wide = conv_tok.T.astype(jnp.float32)
    dconv_wide = dconv_tok.T.astype(jnp.float32)
    gated = (short_out[0] * conv_wide).astype(jnp.bfloat16)
    token_grads = jnp.stack(
        [cot_wide * conv_wide, dconv_wide * short_out[2], dconv_wide * short_out[1]]
    )
    next_rim = from_behind(token_grads[:, :rim_rows], "ctx", -1)
    grad_ext = jnp.concatenate([token_grads, next_rim], axis=1)
    inputs_grad = reverse_taps(grad_ext, weights, tokens, 1).astype(jnp.bfloat16)
    weight_part = tap_grads(token_grads, extended, tap_count, tokens, 1)
    short_grad = lax.psum(weight_part, "ctx") * grad_scale
    results = (gated, inputs_grad[0], inputs_grad[1], inputs_grad[2])
    return (results[0], results[1], results[2], results[3], filter_grad, short_grad)


def fits(query_proj, short_weights):
    peers = lax.axis_size("ctx")
    tokens, width = query_proj.shape
    tap_count = short_weights.shape[1]
    return (
        width == peers * LANES
        and peers.bit_count() == 1
        and tokens % (PHASES * CHUNK) == 0
        and tap_count == RIM + 1
        and peers * tokens <= 2048
    )


def shards(*arrays):
    return channel_shards(*arrays) if fits(arrays[0], arrays[5]) else spread_shards(*arrays)


def solution(mesh):
    placed = (
        P("ctx", "tp"),
        P("ctx", "tp"),
        P("ctx", "tp"),
        P("ctx", "tp"),
        P("ctx", "tp"),
        P(None, None, "tp"),
    )
    return jax.shard_map(
        shards,
        mesh=mesh,
        in_specs=placed,
        out_specs=(
            P("ctx", "tp"),
            P("ctx", "tp"),
            P("ctx", "tp"),
            P("ctx", "tp"),
            P("ctx", "tp"),
            P(None, None, "tp"),
        ),
        check_vma=False,
    )
```

```python
import functools
import math

import jax
import jax.numpy as jnp
import numpy as np
from jax import lax
from jax.experimental import pallas as pl
from jax.experimental.pallas import tpu as pltpu
from jax.sharding import PartitionSpec as P

F32 = jnp.float32
BF16 = jnp.bfloat16
LANES = 128
PHASES = 4
TILE = 16
PAD = 8
CHUNK = 32
RIM = 2
PIECES = 2
MIB = 1024 * 1024
VMEM_LIMIT = 24 * MIB
PACK_VMEM = 53862 * 1024


def partners(peers, diagonal_first):
    def rank(step):
        links, other_core = (step >> 1).bit_count(), step & 1
        if links == 0:
            return (1 if diagonal_first else 5, 0)
        if links == 1:
            return (4 if other_core else 3, -step)
        return (2 * other_core if diagonal_first else 3.5, other_core)

    return [0] + sorted(range(1, peers), key=rank)


def exchange(blocks, steps):
    peers = len(blocks)
    got = [blocks[0]]
    for step, block in list(zip(steps, blocks))[1:]:
        got.append(lax.ppermute(block, "ctx", [(i, i ^ step) for i in range(peers)]))
    return got


def in_vmem(count):
    return [pl.BlockSpec(memory_space=pltpu.VMEM)] * count


def lanes_of(place):
    return pl.ds(pl.multiple_of(place * LANES, LANES), LANES)


def pack_kernel(count, steps, *refs):
    sources, packed = refs[:count], refs[count : count + len(steps)]
    held, sems = refs[count + len(steps) : -1], refs[-1]
    tokens = sources[0].shape[0]
    me = lax.axis_index("ctx")
    arriving = [
        pltpu.make_async_copy(source, target, sems.at[at])
        for at, (source, target) in enumerate(zip(sources, held))
    ]
    for copy in arriving:
        copy.start()
    for at, source in enumerate(held):
        arriving[at].wait()
        rows = slice(at * tokens, (at + 1) * tokens)
        for step, target in zip(steps, packed):
            target[rows, :] = source[:, lanes_of(me ^ step)].astype(BF16)


def pack(arrays, steps):
    tokens = arrays[0].shape[0]
    count = len(arrays)
    return pl.pallas_call(
        functools.partial(pack_kernel, count, steps),
        in_specs=[pl.BlockSpec(memory_space=pl.ANY)] * count,
        out_specs=in_vmem(len(steps)),
        out_shape=[jax.ShapeDtypeStruct((count * tokens, LANES), BF16)] * len(steps),
        scratch_shapes=[
            *[pltpu.VMEM(array.shape, array.dtype) for array in arrays],
            pltpu.SemaphoreType.DMA((count,)),
        ],
        compiler_params=pltpu.CompilerParams(vmem_limit_bytes=PACK_VMEM),
        cost_estimate=pl.CostEstimate(flops=0, bytes_accessed=8 * MIB, transcendentals=0),
        name="pack_inputs",
    )(*arrays)


@functools.lru_cache(maxsize=None)
def dft_tables(seq_len):
    size = seq_len // PHASES
    k = np.arange(size, dtype=np.int64)[:, None]
    m = np.arange(size, dtype=np.int64)[None, :]
    forward = []
    for phase in range(PHASES):
        turns = ((4 * k + 1) * (PHASES * m + phase)) % (4 * seq_len)
        angle = 2.0 * np.pi / (4 * seq_len) * turns
        forward.append(np.concatenate([np.cos(angle), -np.sin(angle)], axis=0))
    forward = np.stack(forward)
    backward = np.swapaxes(forward, 1, 2) / seq_len

    return forward.astype(BF16), backward.astype(BF16)


def forward_mix(parts):
    (r0, i0), (r1, i1), (r2, i2), (r3, i3) = parts
    ar, ai, br, bi = r0 + r2, i0 + i2, r0 - r2, i0 - i2
    cr, ci, dr, di = r1 + r3, i1 + i3, r1 - r3, i1 - i3
    return ((ar + cr, ai + ci), (br + di, bi - dr), (ar - cr, ai - ci), (br - di, bi + dr))


def inverse_mix(parts):
    (r0, i0), (r1, i1), (r2, i2), (r3, i3) = parts
    ar, ai, br, bi = r0 + r2, i0 + i2, r0 - r2, i0 - i2
    cr, ci, dr, di = r1 + r3, i1 + i3, r1 - r3, i1 - i3
    return ((ar + cr, ai + ci), (br - di, bi + dr), (ar - cr, ai - ci), (br + di, bi - dr))


def times(left, right):
    return tuple(
        (lr * rr - li * ri, lr * ri + li * rr) for (lr, li), (rr, ri) in zip(left, right)
    )


def conj_times(left, right):
    return tuple(
        (lr * rr + li * ri, lr * ri - li * rr) for (lr, li), (rr, ri) in zip(left, right)
    )


def transform(table, signal):
    return jnp.dot(table, signal, preferred_element_type=F32)


def phases_near(ref, chunk, tap_count):
    start = PAD + chunk * CHUNK * PHASES
    return {
        offset: ref[pl.ds(start + offset, CHUNK, stride=PHASES), :]
        for offset in range(1 - tap_count, PHASES)
    }


def short_conv(near, taps):
    results = []
    for r in range(PHASES):
        summed = taps[0] * near[r]
        for at in range(1, len(taps)):
            summed = summed + taps[at] * near[r - at]
        results.append(summed)
    return results


def add_rows(total, terms):
    for term in terms:
        folded = jnp.sum(term.reshape(CHUNK // 8, 8, LANES), axis=0)
        total = folded if total is None else total + folded
    return total


def clear_ends(ref):
    ref[:PAD, :] = jnp.zeros((PAD, LANES), F32)
    ref[ref.shape[0] - PAD :, :] = jnp.zeros((PAD, LANES), F32)


def stage_kernel(count, *refs):
    sources, targets, sems = refs[:count], refs[count + 1 : 2 * count + 1], refs[2 * count + 1]
    copies = [
        pltpu.make_async_copy(source, target, sems.at[at])
        for at, (source, target) in enumerate(zip(sources, targets))
    ]
    for copy in copies:
        copy.start()
    for copy in copies:
        copy.wait()


def stage(arrays, after):
    count = len(arrays)
    return pl.pallas_call(
        functools.partial(stage_kernel, count),
        in_specs=[pl.BlockSpec(memory_space=pl.ANY)] * (count + 1),
        out_specs=in_vmem(count),
        out_shape=[jax.ShapeDtypeStruct(array.shape, array.dtype) for array in arrays],
        scratch_shapes=[pltpu.SemaphoreType.DMA((count,))],
        compiler_params=pltpu.CompilerParams(vmem_limit_bytes=8 * MIB),
        cost_estimate=pl.CostEstimate(flops=0, bytes_accessed=8 * MIB, transcendentals=0),
        name="stage_tables",
    )(*arrays, after)


def extra_rows(short_weights):
    sums = PIECES * short_weights.shape[0] * short_weights.shape[1]
    return sums, -(-(sums + 6 * RIM) // TILE) * TILE


def channel_kernel(tokens, heard, told, grad_scale, *refs):
    peers = len(heard)
    arrived = refs[:peers]
    weights, forward, backward = refs[peers : peers + 3]
    out = refs[peers + 3 : 2 * peers + 3]
    (
        query,
        key,
        value,
        cot,
        conv,
        conv_grad,
        filter_grad,
        taps,
        key_short,
        value_short,
        signals,
        spectra,
        products,
        extra,
    ) = refs[2 * peers + 3 :]
    size = peers * tokens // PHASES
    tap_count = weights.shape[1]
    me = lax.axis_index("ctx")
    own = lanes_of(me)
    for ref in (query, key, value, cot, conv, conv_grad):
        clear_ends(ref)
    for ref in (key_short, value_short):
        ref[:, size:, :] = jnp.zeros((PHASES, PAD, LANES), F32)
    for step, source in zip(heard, arrived):
        start = (me ^ step) * tokens
        inner = pl.ds(pl.multiple_of(PAD + start, PAD), tokens)
        for at, ref in enumerate((query, key, value, cot)):
            ref[inner, :] = source[at * tokens : (at + 1) * tokens, :].astype(F32)
        taps[pl.ds(pl.multiple_of(start, PAD), tokens), :] = source[4 * tokens :, :].astype(F32)
    chunks = range(size // CHUNK)
    taps_of = [
        [weights[array, tap : tap + 1, own] for tap in range(tap_count)] for array in range(3)
    ]

    def rows_of(chunk):
        return slice(chunk * CHUNK, (chunk + 1) * CHUNK)

    def spectrum(at, real, imag):
        lanes = slice(at * LANES, (at + 1) * LANES)
        return forward_mix(
            [(spectra[r, real, lanes], spectra[r, imag, lanes]) for r in range(PHASES)]
        )

    def keep(at, real, imag, mixed):
        lanes = slice(at * LANES, (at + 1) * LANES)
        for r, pair in enumerate(inverse_mix(mixed)):
            for rows, part in zip((real, imag), pair):
                products[r, rows, lanes] = part.astype(BF16)

    for chunk in chunks:
        rows = rows_of(chunk)
        key_now = short_conv(phases_near(key, chunk, tap_count), taps_of[1])
        value_now = short_conv(phases_near(value, chunk, tap_count), taps_of[2])
        for r in range(PHASES):
            key_short[r, rows, :] = key_now[r]
            value_short[r, rows, :] = value_now[r]
            signals[r, rows, :LANES] = (key_now[r] * value_now[r]).astype(BF16)
            filt = taps[pl.ds(chunk * CHUNK * PHASES + r, CHUNK, stride=PHASES), :]
            signals[r, rows, LANES : 2 * LANES] = filt.astype(BF16)
    for r in range(PHASES):
        spectra[r, :, : 2 * LANES] = transform(forward[r], signals[r, :, : 2 * LANES])
    for chunk in chunks:
        rows = rows_of(chunk)
        query_now = short_conv(phases_near(query, chunk, tap_count), taps_of[0])
        cot_now = phases_near(cot, chunk, 1)
        for r in range(PHASES):
            signals[r, rows, 2 * LANES :] = (cot_now[r] * query_now[r]).astype(BF16)
    for r in range(PHASES):
        spectra[r, :, 2 * LANES :] = transform(forward[r], signals[r, :, 2 * LANES :])
    for step in range(size // TILE):
        real = slice(step * TILE, (step + 1) * TILE)
        imag = slice(size + step * TILE, size + (step + 1) * TILE)
        prod, filt = spectrum(0, real, imag), spectrum(1, real, imag)
        for at, mixed in enumerate((prod, filt)):
            lanes = slice(at * LANES, (at + 1) * LANES)
            for q, pair in enumerate(mixed):
                spectra[q, real, lanes], spectra[q, imag, lanes] = pair
        keep(0, real, imag, times(prod, filt))
    for r in range(PHASES):
        result = transform(backward[r], products[r, :, :LANES])
        conv[pl.ds(PAD + r, size, stride=PHASES), :] = result.astype(BF16).astype(F32)
    for step in range(size // TILE):
        real = slice(step * TILE, (step + 1) * TILE)
        imag = slice(size + step * TILE, size + (step + 1) * TILE)
        grad = spectrum(2, real, imag)
        for at in range(2):
            lanes = slice(at * LANES, (at + 1) * LANES)
            known = [(spectra[q, real, lanes], spectra[q, imag, lanes]) for q in range(PHASES)]
            keep(2 - at, real, imag, conj_times(known, grad))
    for r in range(PHASES):
        result = transform(backward[r], products[r, :, LANES:])
        conv_grad[pl.ds(PAD + r, size, stride=PHASES), :] = (
            result[:, :LANES].astype(BF16).astype(F32)
        )
        filter_grad[pl.ds(r, size, stride=PHASES), :] = result[:, LANES:] * grad_scale

    totals = [[None] * tap_count for _ in range(3)]

    def add_sums(array, signal, chunk, pre):
        near = phases_near(signal, chunk, tap_count)
        for tap in range(tap_count):
            totals[array][tap] = add_rows(
                totals[array][tap], [pre[r] * near[r - tap] for r in range(PHASES)]
            )

    for chunk in chunks:
        cot_now, conv_now = phases_near(cot, chunk, 1), phases_near(conv, chunk, 1)
        add_sums(0, query, chunk, [cot_now[r] * conv_now[r] for r in range(PHASES)])
    for chunk in chunks:
        rows = rows_of(chunk)
        grad_now = phases_near(conv_grad, chunk, 1)
        add_sums(1, key, chunk, [grad_now[r] * value_short[r, rows, :] for r in range(PHASES)])
        add_sums(2, value, chunk, [grad_now[r] * key_short[r, rows, :] for r in range(PHASES)])
    sums = [jnp.sum(total, axis=0, keepdims=True) for row in totals for total in row]
    rest = jnp.concatenate(sums, axis=0) * grad_scale
    extra[...] = jnp.zeros_like(extra)
    for piece in range(PIECES):
        rounded = rest.astype(BF16).astype(F32)
        extra[piece * len(sums) : (piece + 1) * len(sums), :] = rounded
        rest = rest - rounded
    for step, target in zip(told, out):
        start = (me ^ step) * tokens
        inner = pl.ds(pl.multiple_of(PAD + start, PAD), tokens)
        target[:tokens, :] = conv[inner, :].astype(BF16)
        target[tokens : 2 * tokens, :] = conv_grad[inner, :].astype(BF16)
        target[2 * tokens : 3 * tokens, :] = filter_grad[
            pl.ds(pl.multiple_of(start, PAD), tokens), :
        ].astype(BF16)
        before = pl.ds(pl.multiple_of(start, PAD), PAD)
        after = pl.ds(pl.multiple_of(PAD + start + tokens, PAD), PAD)
        at = PIECES * len(sums)
        for ref in (query, key, value):
            extra[at : at + RIM, :] = ref[before, :][PAD - RIM :]
            at += RIM
        row = pl.ds(pl.multiple_of((start + tokens) // PHASES, PAD), PAD)
        extra[at : at + RIM, :] = (cot[after, :] * conv[after, :])[:RIM]
        for short in (value_short, key_short):
            at += RIM
            shorts = jnp.concatenate([short[r, row, :][:1] for r in range(RIM)], axis=0)
            extra[at : at + RIM, :] = conv_grad[after, :][:RIM] * shorts
        target[3 * tokens :, :] = extra[...].astype(BF16)


def channel_step(arrived, heard, told, short_weights, tables, tokens):
    peers = len(arrived)
    seq_len = peers * tokens
    size = seq_len // PHASES
    extra = extra_rows(short_weights)[1]
    padded = pltpu.VMEM((seq_len + 2 * PAD, LANES), F32)
    plain = pltpu.VMEM((seq_len, LANES), F32)
    phases = pltpu.VMEM((PHASES, size + PAD, LANES), F32)
    return pl.pallas_call(
        functools.partial(channel_kernel, tokens, heard, told, 1.0 / math.sqrt(seq_len)),
        in_specs=in_vmem(peers + 3),
        out_specs=in_vmem(peers),
        out_shape=[jax.ShapeDtypeStruct((3 * tokens + extra, LANES), BF16)] * peers,
        scratch_shapes=[
            *[padded] * 6,
            plain,
            plain,
            phases,
            phases,
            pltpu.VMEM((PHASES, size, 3 * LANES), BF16),
            pltpu.VMEM((PHASES, 2 * size, 3 * LANES), F32),
            pltpu.VMEM((PHASES, 2 * size, 3 * LANES), BF16),
            pltpu.VMEM((extra, LANES), F32),
        ],
        compiler_params=pltpu.CompilerParams(vmem_limit_bytes=VMEM_LIMIT),
        name="channel_operator",
    )(*arrived, short_weights, *tables)


def token_kernel(steps, sum_rows, carried, *refs):
    count_in = len(steps)
    arrived = refs[:count_in]
    query, key, value, cot, weights = refs[count_in : count_in + 5]
    results = refs[count_in + 5 + carried : count_in + 11 + carried]
    (gated, query_grad, key_grad, value_grad, filter_grad, short_grad, longer, pre, sems) = refs[
        count_in + 11 + carried :
    ]
    copies = []
    tokens = query.shape[0]
    tap_count = weights.shape[1]
    count = sum_rows // PIECES
    me = lax.axis_index("ctx")
    for slot, (step, source) in enumerate(zip(steps, arrived)):
        lanes = lanes_of(me ^ step)
        extra = source[3 * tokens :, :].astype(F32)

        def rim(at):
            return extra[sum_rows + at * RIM : sum_rows + (at + 1) * RIM]

        def short(array, signal):
            longer[array, PAD - RIM : PAD, :] = rim(array)
            longer[array, PAD :, :] = signal[:, lanes].astype(F32)
            summed = weights[array, 0:1, lanes] * longer[array, PAD:, :]
            for tap in range(1, tap_count):
                summed = (
                    summed
                    + weights[array, tap : tap + 1, lanes]
                    * longer[array, PAD - tap : PAD - tap + tokens, :]
                )
            return summed

        def taps_back(array, grad, target):
            pre[array, :tokens, :] = grad
            pre[array, tokens : tokens + RIM, :] = rim(3 + array)
            summed = weights[array, 0:1, lanes] * grad
            for tap in range(1, tap_count):
                summed = (
                    summed
                    + weights[array, tap : tap + 1, lanes] * pre[array, tap : tap + tokens, :]
                )
            target[slot] = summed.astype(BF16)

        conv = source[:tokens, :].astype(F32)
        conv_grad = source[tokens : 2 * tokens, :].astype(F32)
        gated[slot] = (short(0, query) * conv).astype(BF16)
        taps_back(0, cot[:, lanes].astype(F32) * conv, query_grad)
        taps_back(1, conv_grad * short(2, value), key_grad)
        taps_back(2, conv_grad * short(1, key), value_grad)
        filter_grad[slot] = source[2 * tokens : 3 * tokens, :].astype(F32)
        whole = extra[:count]
        for piece in range(1, PIECES):
            whole = whole + extra[piece * count : (piece + 1) * count]
        for row in range(count):
            which, tap = divmod(row, tap_count)
            short_grad[slot, which, tap : tap + 1, :] = whole[row : row + 1]
        held = (gated, query_grad, key_grad, value_grad, filter_grad, short_grad)
        for at, (source, target) in enumerate(zip(held, results)):
            place = target.at[:, :, lanes] if at == 5 else target.at[:, lanes]
            copies.append(pltpu.make_async_copy(source.at[slot], place, sems.at[slot, at]))
            copies[-1].start()
    for copy in copies:
        copy.wait()


def token_step(arrived, steps, query, key, value, cot, short_weights, begun=()):
    tokens, width = query.shape
    count = len(arrived)
    wide = jax.ShapeDtypeStruct((tokens, width), BF16)
    anywhere = pl.BlockSpec(memory_space=pl.ANY)
    return pl.pallas_call(
        functools.partial(token_kernel, steps, extra_rows(short_weights)[0], len(begun)),
        in_specs=in_vmem(count + 5) + [anywhere] * len(begun),
        out_specs=[anywhere] * 6,
        out_shape=[wide] * 4
        + [
            jax.ShapeDtypeStruct((tokens, width), F32),
            jax.ShapeDtypeStruct(short_weights.shape, F32),
        ],
        scratch_shapes=[
            *[pltpu.VMEM((count, tokens, LANES), BF16)] * 4,
            pltpu.VMEM((count, tokens, LANES), F32),
            pltpu.VMEM((count, *short_weights.shape[:2], LANES), F32),
            pltpu.VMEM((3, tokens + PAD, LANES), F32),
            pltpu.VMEM((3, tokens + PAD, LANES), F32),
            pltpu.SemaphoreType.DMA((count, 6)),
        ],
        input_output_aliases={count + 5 + at: at for at in range(len(begun))},
        compiler_params=pltpu.CompilerParams(vmem_limit_bytes=VMEM_LIMIT),
        cost_estimate=pl.CostEstimate(flops=0, bytes_accessed=4 * MIB, transcendentals=0),
        name="token_outputs",
    )(*arrived, query, key, value, cot, short_weights, *begun)


def channel_shards(query_proj, key_proj, value_proj, cotangent, filter_taps, short_weights):
    peers = lax.axis_size("ctx")
    tokens = query_proj.shape[0]
    tables = [jnp.asarray(table) for table in dft_tables(peers * tokens)]
    going, coming = partners(peers, False), partners(peers, True)
    sent = pack((query_proj, key_proj, value_proj, cotangent, filter_taps), going)
    arrived = exchange(sent, going)
    staged = stage((sent[0], short_weights, *tables), arrived[1])
    arrived[0] = staged[0]
    results = channel_step(arrived, going, coming, staged[1], staged[2:], tokens)
    back = exchange(results, coming)
    local = (query_proj, key_proj, value_proj, cotangent, short_weights)
    ends = [at for at in (4, 6) if at < peers] + [peers]
    begun, start = (), 0
    for end in ends:
        begun = token_step(back[start:end], coming[start:end], *local, begun)
        start = end
    return tuple(begun)


def from_behind(array, axis, by):
    peers = lax.axis_size(axis)
    pairs = [(i, i + by) for i in range(peers) if 0 <= i + by < peers]
    return lax.ppermute(array, axis, pairs)


def contract(form, left, right):
    return jnp.einsum(
        form, left, right, precision=lax.Precision.HIGHEST, preferred_element_type=jnp.float32
    )


def table_pair(rows, cols, period):
    row_ids = lax.broadcasted_iota(jnp.int32, (rows, cols), 0)
    col_ids = lax.broadcasted_iota(jnp.int32, (rows, cols), 1)
    angle = 2.0 * math.pi / period * (row_ids * col_ids % period).astype(jnp.float32)
    return (jnp.cos(angle), jnp.sin(angle))


def make_plan(seq_len):
    small_len = int(math.isqrt(2 * seq_len))
    while seq_len % small_len:
        small_len -= 1
    large_len = 2 * seq_len // small_len
    large_cos, large_sin = table_pair(large_len // 2, large_len, large_len)
    small_cos, small_sin = table_pair(small_len, small_len, small_len)
    twist_cos, twist_sin = table_pair(large_len, small_len, small_len * large_len)
    fwd_large = jnp.stack([large_cos, -large_sin], axis=1)
    fwd_small = jnp.stack([jnp.stack([small_cos, -small_sin]), jnp.stack([small_sin, small_cos])])
    inv_small = jnp.stack([jnp.stack([small_cos, small_sin]), jnp.stack([-small_sin, small_cos])])
    inv_large = jnp.stack([large_cos, -large_sin])
    return (small_len, large_len, fwd_large, fwd_small, inv_small, inv_large, twist_cos, twist_sin)


def forward_spec(signal, dft_plan):
    small_len, large_len, fwd_large, fwd_small, inv_small, inv_large, twist_cos, twist_sin = (
        dft_plan
    )
    cube = signal.reshape(signal.shape[0], large_len // 2, small_len)
    section_one = contract("cba,bpk->cpka", cube, fwd_large)
    real_one = section_one[:, 0]
    imag_one = section_one[:, 1]
    section_two = jnp.stack(
        [real_one * twist_cos + imag_one * twist_sin, imag_one * twist_cos - real_one * twist_sin],
        axis=1,
    )
    return contract("cpka,pqaj->cqkj", section_two, fwd_small)


def inverse_half(spec, dft_plan):
    small_len, large_len, fwd_large, fwd_small, inv_small, inv_large, twist_cos, twist_sin = (
        dft_plan
    )
    section_one = contract("cqkj,qpja->cpka", spec, inv_small)
    real_one = section_one[:, 0]
    imag_one = section_one[:, 1]
    section_two = jnp.stack(
        [real_one * twist_cos - imag_one * twist_sin, imag_one * twist_cos + real_one * twist_sin],
        axis=1,
    )
    signal = contract("cpka,pbk->cba", section_two, inv_large)
    return signal.reshape(signal.shape[0], -1) / float(small_len * large_len)


def complex_mul(left, right):
    left_real, left_imag = (left[:, 0], left[:, 1])
    right_real, right_imag = (right[:, 0], right[:, 1])
    return jnp.stack(
        [
            left_real * right_real - left_imag * right_imag,
            left_real * right_imag + left_imag * right_real,
        ],
        axis=1,
    )


def conj_mul(left, right):
    left_real, left_imag = (left[:, 0], left[:, 1])
    right_real, right_imag = (right[:, 0], right[:, 1])
    return jnp.stack(
        [
            left_real * right_real + left_imag * right_imag,
            left_real * right_imag - left_imag * right_real,
        ],
        axis=1,
    )


def conv_forward(prod_chan, filter_spec, dft_plan):
    prod_spec = forward_spec(prod_chan.astype(jnp.float32), dft_plan)
    conv_chan = inverse_half(complex_mul(prod_spec, filter_spec), dft_plan).astype(jnp.bfloat16)
    return (conv_chan, prod_spec)


def conv_backward(grad_chan, filter_spec, prod_spec, dft_plan, grad_scale):
    grad_spec = forward_spec(grad_chan.astype(jnp.float32), dft_plan)
    dconv_chan = inverse_half(conj_mul(filter_spec, grad_spec), dft_plan).astype(jnp.bfloat16)
    dfilter_chan = inverse_half(conj_mul(prod_spec, grad_spec), dft_plan) * grad_scale
    return (dconv_chan, dfilter_chan)


def receive_filter(filter_taps, dft_plan):
    filter_chan = lax.all_to_all(filter_taps.T, "ctx", split_axis=0, concat_axis=1, tiled=True)
    return forward_spec(filter_chan, dft_plan)


def return_filter(dfilter_chan):
    return (
        lax.all_to_all(
            dfilter_chan.astype(jnp.bfloat16), "ctx", split_axis=1, concat_axis=0, tiled=True
        )
        .astype(dfilter_chan.dtype)
        .T
    )


def causal_taps(extended, weights, length, axis):
    rim_rows = len(weights) - 1
    summed = weights[0] * lax.slice_in_dim(extended, rim_rows, rim_rows + length, axis=axis)
    for offset in range(1, len(weights)):
        summed = summed + weights[offset] * lax.slice_in_dim(
            extended, rim_rows - offset, rim_rows - offset + length, axis=axis
        )
    return summed


def reverse_taps(extended, weights, length, axis):
    summed = weights[0] * lax.slice_in_dim(extended, 0, length, axis=axis)
    for offset in range(1, len(weights)):
        summed = summed + weights[offset] * lax.slice_in_dim(
            extended, offset, offset + length, axis=axis
        )
    return summed


def tap_grads(grad_in, extended, tap_count, length, axis):
    rim_rows = tap_count - 1
    rows = [
        jnp.sum(
            grad_in
            * lax.slice_in_dim(extended, rim_rows - offset, rim_rows - offset + length, axis=axis),
            axis=axis,
        )
        for offset in range(tap_count)
    ]
    return jnp.stack(rows, axis=1)


def spread_shards(query_proj, key_proj, value_proj, cotangent, filter_taps, short_weights):
    tokens = query_proj.shape[0]
    tap_count = short_weights.shape[1]
    rim_rows = tap_count - 1
    seq_len = tokens * lax.axis_size("ctx")
    grad_scale = 1.0 / math.sqrt(seq_len)
    dft_plan = make_plan(seq_len)
    stacked = jnp.stack([query_proj, key_proj, value_proj])
    prev_rim = from_behind(stacked[:, tokens - rim_rows :], "ctx", 1)
    extended = jnp.concatenate([prev_rim, stacked], axis=1).astype(jnp.float32)
    weights = [short_weights[:, offset, None, :] for offset in range(tap_count)]
    short_out = causal_taps(extended, weights, tokens, 1)
    product = (short_out[1] * short_out[2]).astype(jnp.bfloat16)
    cot_wide = cotangent.astype(jnp.float32)
    gate_grad = (cot_wide * short_out[0]).astype(jnp.bfloat16)
    filter_spec = receive_filter(filter_taps, dft_plan)
    prod_chan = lax.all_to_all(product.T, "ctx", split_axis=0, concat_axis=1, tiled=True)
    conv_chan, prod_spec = conv_forward(prod_chan, filter_spec, dft_plan)
    conv_tok = lax.all_to_all(conv_chan, "ctx", split_axis=1, concat_axis=0, tiled=True)
    grad_chan = lax.all_to_all(gate_grad.T, "ctx", split_axis=0, concat_axis=1, tiled=True)
    dconv_chan, dfilter_chan = conv_backward(
        grad_chan, filter_spec, prod_spec, dft_plan, grad_scale
    )
    dconv_tok = lax.all_to_all(dconv_chan, "ctx", split_axis=1, concat_axis=0, tiled=True)
    filter_grad = return_filter(dfilter_chan)
    conv_wide = conv_tok.T.astype(jnp.float32)
    dconv_wide = dconv_tok.T.astype(jnp.float32)
    gated = (short_out[0] * conv_wide).astype(jnp.bfloat16)
    token_grads = jnp.stack(
        [cot_wide * conv_wide, dconv_wide * short_out[2], dconv_wide * short_out[1]]
    )
    next_rim = from_behind(token_grads[:, :rim_rows], "ctx", -1)
    grad_ext = jnp.concatenate([token_grads, next_rim], axis=1)
    inputs_grad = reverse_taps(grad_ext, weights, tokens, 1).astype(jnp.bfloat16)
    weight_part = tap_grads(token_grads, extended, tap_count, tokens, 1)
    short_grad = lax.psum(weight_part, "ctx") * grad_scale
    results = (gated, inputs_grad[0], inputs_grad[1], inputs_grad[2])
    return (results[0], results[1], results[2], results[3], filter_grad, short_grad)


def fits(query_proj, short_weights):
    peers = lax.axis_size("ctx")
    tokens, width = query_proj.shape
    tap_count = short_weights.shape[1]
    return (
        width == peers * LANES
        and peers.bit_count() == 1
        and tokens % (PHASES * CHUNK) == 0
        and tap_count == RIM + 1
        and peers * tokens <= 2048
    )


def shards(*arrays):
    return channel_shards(*arrays) if fits(arrays[0], arrays[5]) else spread_shards(*arrays)


def solution(mesh):
    placed = (
        P("ctx", "tp"),
        P("ctx", "tp"),
        P("ctx", "tp"),
        P("ctx", "tp"),
        P("ctx", "tp"),
        P(None, None, "tp"),
    )
    return jax.shard_map(
        shards,
        mesh=mesh,
        in_specs=placed,
        out_specs=(
            P("ctx", "tp"),
            P("ctx", "tp"),
            P("ctx", "tp"),
            P("ctx", "tp"),
            P("ctx", "tp"),
            P(None, None, "tp"),
        ),
        check_vma=False,
    )
```

```python
import functools
import math

import jax
import jax.numpy as jnp
import numpy as np
from jax import lax
from jax.experimental import pallas as pl
from jax.experimental.pallas import tpu as pltpu
from jax.sharding import PartitionSpec as P

F32 = jnp.float32
BF16 = jnp.bfloat16
LANES = 128
PHASES = 4
TILE = 16
PAD = 8
CHUNK = 32
PARTS = 4
RIM = 2
PIECES = 2
MIB = 1024 * 1024
VMEM_LIMIT = 24 * MIB
PACK_VMEM = 53862 * 1024


def partners(peers, diagonal_first):
    def rank(step):
        links, other_core = (step >> 1).bit_count(), step & 1
        if links == 0:
            return (1 if diagonal_first else 5, 0)
        if links == 1:
            return (4 if other_core else 3, -step)
        return (2 * other_core if diagonal_first else 3.5, other_core)

    return [0] + sorted(range(1, peers), key=rank)


def exchange(blocks, steps):
    peers = len(blocks)
    got = [blocks[0]]
    for step, block in list(zip(steps, blocks))[1:]:
        got.append(lax.ppermute(block, "ctx", [(i, i ^ step) for i in range(peers)]))
    return got


def in_vmem(count):
    return [pl.BlockSpec(memory_space=pltpu.VMEM)] * count


def lanes_of(place):
    return pl.ds(pl.multiple_of(place * LANES, LANES), LANES)


def pack_kernel(count, steps, *refs):
    sources, packed = refs[:count], refs[count : count + len(steps)]
    held, sems = refs[count + len(steps) : -1], refs[-1]
    tokens = sources[0].shape[0]
    me = lax.axis_index("ctx")
    part = tokens // PARTS
    arriving = [
        [
            pltpu.make_async_copy(
                source.at[pl.ds(piece * part, part), :],
                target.at[pl.ds(piece * part, part), :],
                sems.at[at, piece],
            )
            for piece in range(PARTS)
        ]
        for at, (source, target) in enumerate(zip(sources, held))
    ]
    for copies in arriving:
        for copy in copies:
            copy.start()
    for at, source in enumerate(held):
        for copy in arriving[at]:
            copy.wait()
        rows = slice(at * tokens, (at + 1) * tokens)
        for step, target in zip(steps, packed):
            target[rows, :] = source[:, lanes_of(me ^ step)].astype(BF16)


def pack(arrays, steps):
    tokens = arrays[0].shape[0]
    count = len(arrays)
    return pl.pallas_call(
        functools.partial(pack_kernel, count, steps),
        in_specs=[pl.BlockSpec(memory_space=pl.ANY)] * count,
        out_specs=in_vmem(len(steps)),
        out_shape=[jax.ShapeDtypeStruct((count * tokens, LANES), BF16)] * len(steps),
        scratch_shapes=[
            *[pltpu.VMEM(array.shape, array.dtype) for array in arrays],
            pltpu.SemaphoreType.DMA((count, PARTS)),
        ],
        compiler_params=pltpu.CompilerParams(vmem_limit_bytes=PACK_VMEM),
        cost_estimate=pl.CostEstimate(flops=0, bytes_accessed=8 * MIB, transcendentals=0),
        name="pack_inputs",
    )(*arrays)


@functools.lru_cache(maxsize=None)
def dft_tables(seq_len):
    size = seq_len // PHASES
    k = np.arange(size, dtype=np.int64)[:, None]
    m = np.arange(size, dtype=np.int64)[None, :]
    forward = []
    for phase in range(PHASES):
        turns = ((4 * k + 1) * (PHASES * m + phase)) % (4 * seq_len)
        angle = 2.0 * np.pi / (4 * seq_len) * turns
        forward.append(np.concatenate([np.cos(angle), -np.sin(angle)], axis=0))
    forward = np.stack(forward)
    backward = np.swapaxes(forward, 1, 2) / seq_len

    return forward.astype(BF16), backward.astype(BF16)


def forward_mix(parts):
    (r0, i0), (r1, i1), (r2, i2), (r3, i3) = parts
    ar, ai, br, bi = r0 + r2, i0 + i2, r0 - r2, i0 - i2
    cr, ci, dr, di = r1 + r3, i1 + i3, r1 - r3, i1 - i3
    return ((ar + cr, ai + ci), (br + di, bi - dr), (ar - cr, ai - ci), (br - di, bi + dr))


def inverse_mix(parts):
    (r0, i0), (r1, i1), (r2, i2), (r3, i3) = parts
    ar, ai, br, bi = r0 + r2, i0 + i2, r0 - r2, i0 - i2
    cr, ci, dr, di = r1 + r3, i1 + i3, r1 - r3, i1 - i3
    return ((ar + cr, ai + ci), (br - di, bi + dr), (ar - cr, ai - ci), (br + di, bi - dr))


def times(left, right):
    return tuple(
        (lr * rr - li * ri, lr * ri + li * rr) for (lr, li), (rr, ri) in zip(left, right)
    )


def conj_times(left, right):
    return tuple(
        (lr * rr + li * ri, lr * ri - li * rr) for (lr, li), (rr, ri) in zip(left, right)
    )


def transform(table, signal):
    return jnp.dot(table, signal, preferred_element_type=F32)


def phases_near(ref, chunk, tap_count):
    start = PAD + chunk * CHUNK * PHASES
    return {
        offset: ref[pl.ds(start + offset, CHUNK, stride=PHASES), :]
        for offset in range(1 - tap_count, PHASES)
    }


def short_conv(near, taps):
    results = []
    for r in range(PHASES):
        summed = taps[0] * near[r]
        for at in range(1, len(taps)):
            summed = summed + taps[at] * near[r - at]
        results.append(summed)
    return results


def add_rows(total, terms):
    for term in terms:
        folded = jnp.sum(term.reshape(CHUNK // 8, 8, LANES), axis=0)
        total = folded if total is None else total + folded
    return total


def clear_ends(ref):
    ref[:PAD, :] = jnp.zeros((PAD, LANES), F32)
    ref[ref.shape[0] - PAD :, :] = jnp.zeros((PAD, LANES), F32)


def stage_kernel(count, *refs):
    sources, targets, sems = refs[:count], refs[count + 1 : 2 * count + 1], refs[2 * count + 1]
    copies = [
        pltpu.make_async_copy(source, target, sems.at[at])
        for at, (source, target) in enumerate(zip(sources, targets))
    ]
    for copy in copies:
        copy.start()
    for copy in copies:
        copy.wait()


def stage(arrays, after):
    count = len(arrays)
    return pl.pallas_call(
        functools.partial(stage_kernel, count),
        in_specs=[pl.BlockSpec(memory_space=pl.ANY)] * (count + 1),
        out_specs=in_vmem(count),
        out_shape=[jax.ShapeDtypeStruct(array.shape, array.dtype) for array in arrays],
        scratch_shapes=[pltpu.SemaphoreType.DMA((count,))],
        compiler_params=pltpu.CompilerParams(vmem_limit_bytes=8 * MIB),
        cost_estimate=pl.CostEstimate(flops=0, bytes_accessed=8 * MIB, transcendentals=0),
        name="stage_tables",
    )(*arrays, after)


def extra_rows(short_weights):
    sums = PIECES * short_weights.shape[0] * short_weights.shape[1]
    return sums, -(-(sums + 6 * RIM) // TILE) * TILE


def channel_kernel(tokens, heard, told, grad_scale, *refs):
    peers = len(heard)
    arrived = refs[:peers]
    weights, forward, backward = refs[peers : peers + 3]
    out = refs[peers + 3 : 2 * peers + 3]
    (
        query,
        key,
        value,
        cot,
        conv,
        conv_grad,
        filter_grad,
        taps,
        key_short,
        value_short,
        signals,
        spectra,
        products,
        extra,
    ) = refs[2 * peers + 3 :]
    size = peers * tokens // PHASES
    tap_count = weights.shape[1]
    me = lax.axis_index("ctx")
    own = lanes_of(me)
    for ref in (query, key, value, cot, conv, conv_grad):
        clear_ends(ref)
    for ref in (key_short, value_short):
        ref[:, size:, :] = jnp.zeros((PHASES, PAD, LANES), F32)
    for step, source in zip(heard, arrived):
        start = (me ^ step) * tokens
        inner = pl.ds(pl.multiple_of(PAD + start, PAD), tokens)
        for at, ref in enumerate((query, key, value, cot)):
            ref[inner, :] = source[at * tokens : (at + 1) * tokens, :].astype(F32)
        taps[pl.ds(pl.multiple_of(start, PAD), tokens), :] = source[4 * tokens :, :].astype(F32)
    chunks = range(size // CHUNK)
    taps_of = [
        [weights[array, tap : tap + 1, own] for tap in range(tap_count)] for array in range(3)
    ]

    def rows_of(chunk):
        return slice(chunk * CHUNK, (chunk + 1) * CHUNK)

    def spectrum(at, real, imag):
        lanes = slice(at * LANES, (at + 1) * LANES)
        return forward_mix(
            [(spectra[r, real, lanes], spectra[r, imag, lanes]) for r in range(PHASES)]
        )

    def keep(at, real, imag, mixed):
        lanes = slice(at * LANES, (at + 1) * LANES)
        for r, pair in enumerate(inverse_mix(mixed)):
            for rows, part in zip((real, imag), pair):
                products[r, rows, lanes] = part.astype(BF16)

    for chunk in chunks:
        rows = rows_of(chunk)
        key_now = short_conv(phases_near(key, chunk, tap_count), taps_of[1])
        value_now = short_conv(phases_near(value, chunk, tap_count), taps_of[2])
        for r in range(PHASES):
            key_short[r, rows, :] = key_now[r]
            value_short[r, rows, :] = value_now[r]
            signals[r, rows, :LANES] = (key_now[r] * value_now[r]).astype(BF16)
            filt = taps[pl.ds(chunk * CHUNK * PHASES + r, CHUNK, stride=PHASES), :]
            signals[r, rows, LANES : 2 * LANES] = filt.astype(BF16)
    for r in range(PHASES):
        spectra[r, :, : 2 * LANES] = transform(forward[r], signals[r, :, : 2 * LANES])
    for chunk in chunks:
        rows = rows_of(chunk)
        query_now = short_conv(phases_near(query, chunk, tap_count), taps_of[0])
        cot_now = phases_near(cot, chunk, 1)
        for r in range(PHASES):
            signals[r, rows, 2 * LANES :] = (cot_now[r] * query_now[r]).astype(BF16)
    for r in range(PHASES):
        spectra[r, :, 2 * LANES :] = transform(forward[r], signals[r, :, 2 * LANES :])
    for step in range(size // TILE):
        real = slice(step * TILE, (step + 1) * TILE)
        imag = slice(size + step * TILE, size + (step + 1) * TILE)
        prod, filt, grad = (spectrum(at, real, imag) for at in range(3))
        keep(0, real, imag, times(prod, filt))
        keep(1, real, imag, conj_times(filt, grad))
        keep(2, real, imag, conj_times(prod, grad))
    for r in range(PHASES):
        result = transform(backward[r], products[r])
        for at, ref in enumerate((conv, conv_grad)):
            ref[pl.ds(PAD + r, size, stride=PHASES), :] = (
                result[:, at * LANES : (at + 1) * LANES].astype(BF16).astype(F32)
            )
        filter_grad[pl.ds(r, size, stride=PHASES), :] = result[:, 2 * LANES :] * grad_scale

    totals = [[None] * tap_count for _ in range(3)]

    def add_sums(array, signal, chunk, pre):
        near = phases_near(signal, chunk, tap_count)
        for tap in range(tap_count):
            totals[array][tap] = add_rows(
                totals[array][tap], [pre[r] * near[r - tap] for r in range(PHASES)]
            )

    for chunk in chunks:
        cot_now, conv_now = phases_near(cot, chunk, 1), phases_near(conv, chunk, 1)
        add_sums(0, query, chunk, [cot_now[r] * conv_now[r] for r in range(PHASES)])
    for chunk in chunks:
        rows = rows_of(chunk)
        grad_now = phases_near(conv_grad, chunk, 1)
        add_sums(1, key, chunk, [grad_now[r] * value_short[r, rows, :] for r in range(PHASES)])
        add_sums(2, value, chunk, [grad_now[r] * key_short[r, rows, :] for r in range(PHASES)])
    sums = [jnp.sum(total, axis=0, keepdims=True) for row in totals for total in row]
    rest = jnp.concatenate(sums, axis=0) * grad_scale
    extra[...] = jnp.zeros_like(extra)
    for piece in range(PIECES):
        rounded = rest.astype(BF16).astype(F32)
        extra[piece * len(sums) : (piece + 1) * len(sums), :] = rounded
        rest = rest - rounded
    for step, target in zip(told, out):
        start = (me ^ step) * tokens
        inner = pl.ds(pl.multiple_of(PAD + start, PAD), tokens)
        target[:tokens, :] = conv[inner, :].astype(BF16)
        target[tokens : 2 * tokens, :] = conv_grad[inner, :].astype(BF16)
        target[2 * tokens : 3 * tokens, :] = filter_grad[
            pl.ds(pl.multiple_of(start, PAD), tokens), :
        ].astype(BF16)
        before = pl.ds(pl.multiple_of(start, PAD), PAD)
        after = pl.ds(pl.multiple_of(PAD + start + tokens, PAD), PAD)
        at = PIECES * len(sums)
        for ref in (query, key, value):
            extra[at : at + RIM, :] = ref[before, :][PAD - RIM :]
            at += RIM
        row = pl.ds(pl.multiple_of((start + tokens) // PHASES, PAD), PAD)
        extra[at : at + RIM, :] = (cot[after, :] * conv[after, :])[:RIM]
        for short in (value_short, key_short):
            at += RIM
            shorts = jnp.concatenate([short[r, row, :][:1] for r in range(RIM)], axis=0)
            extra[at : at + RIM, :] = conv_grad[after, :][:RIM] * shorts
        target[3 * tokens :, :] = extra[...].astype(BF16)


def channel_step(arrived, heard, told, short_weights, tables, tokens):
    peers = len(arrived)
    seq_len = peers * tokens
    size = seq_len // PHASES
    extra = extra_rows(short_weights)[1]
    padded = pltpu.VMEM((seq_len + 2 * PAD, LANES), F32)
    plain = pltpu.VMEM((seq_len, LANES), F32)
    phases = pltpu.VMEM((PHASES, size + PAD, LANES), F32)
    return pl.pallas_call(
        functools.partial(channel_kernel, tokens, heard, told, 1.0 / math.sqrt(seq_len)),
        in_specs=in_vmem(peers + 3),
        out_specs=in_vmem(peers),
        out_shape=[jax.ShapeDtypeStruct((3 * tokens + extra, LANES), BF16)] * peers,
        scratch_shapes=[
            *[padded] * 6,
            plain,
            plain,
            phases,
            phases,
            pltpu.VMEM((PHASES, size, 3 * LANES), BF16),
            pltpu.VMEM((PHASES, 2 * size, 3 * LANES), F32),
            pltpu.VMEM((PHASES, 2 * size, 3 * LANES), BF16),
            pltpu.VMEM((extra, LANES), F32),
        ],
        compiler_params=pltpu.CompilerParams(vmem_limit_bytes=VMEM_LIMIT),
        name="channel_operator",
    )(*arrived, short_weights, *tables)


def token_kernel(steps, sum_rows, carried, *refs):
    count_in = len(steps)
    arrived = refs[:count_in]
    query, key, value, cot, weights = refs[count_in : count_in + 5]
    results = refs[count_in + 5 + carried : count_in + 11 + carried]
    (gated, query_grad, key_grad, value_grad, filter_grad, short_grad, longer, pre, sems) = refs[
        count_in + 11 + carried :
    ]
    copies = []
    tokens = query.shape[0]
    tap_count = weights.shape[1]
    count = sum_rows // PIECES
    me = lax.axis_index("ctx")
    for slot, (step, source) in enumerate(zip(steps, arrived)):
        lanes = lanes_of(me ^ step)
        extra = source[3 * tokens :, :].astype(F32)

        def rim(at):
            return extra[sum_rows + at * RIM : sum_rows + (at + 1) * RIM]

        def short(array, signal):
            longer[array, PAD - RIM : PAD, :] = rim(array)
            longer[array, PAD :, :] = signal[:, lanes].astype(F32)
            summed = weights[array, 0:1, lanes] * longer[array, PAD:, :]
            for tap in range(1, tap_count):
                summed = (
                    summed
                    + weights[array, tap : tap + 1, lanes]
                    * longer[array, PAD - tap : PAD - tap + tokens, :]
                )
            return summed

        def taps_back(array, grad, target):
            pre[array, :tokens, :] = grad
            pre[array, tokens : tokens + RIM, :] = rim(3 + array)
            summed = weights[array, 0:1, lanes] * grad
            for tap in range(1, tap_count):
                summed = (
                    summed
                    + weights[array, tap : tap + 1, lanes] * pre[array, tap : tap + tokens, :]
                )
            target[slot] = summed.astype(BF16)

        conv = source[:tokens, :].astype(F32)
        conv_grad = source[tokens : 2 * tokens, :].astype(F32)
        gated[slot] = (short(0, query) * conv).astype(BF16)
        taps_back(0, cot[:, lanes].astype(F32) * conv, query_grad)
        taps_back(1, conv_grad * short(2, value), key_grad)
        taps_back(2, conv_grad * short(1, key), value_grad)
        filter_grad[slot] = source[2 * tokens : 3 * tokens, :].astype(F32)
        whole = extra[:count]
        for piece in range(1, PIECES):
            whole = whole + extra[piece * count : (piece + 1) * count]
        for row in range(count):
            which, tap = divmod(row, tap_count)
            short_grad[slot, which, tap : tap + 1, :] = whole[row : row + 1]
        held = (gated, query_grad, key_grad, value_grad, filter_grad, short_grad)
        for at, (source, target) in enumerate(zip(held, results)):
            place = target.at[:, :, lanes] if at == 5 else target.at[:, lanes]
            copies.append(pltpu.make_async_copy(source.at[slot], place, sems.at[slot, at]))
            copies[-1].start()
    for copy in copies:
        copy.wait()


def token_step(arrived, steps, query, key, value, cot, short_weights, begun=()):
    tokens, width = query.shape
    count = len(arrived)
    wide = jax.ShapeDtypeStruct((tokens, width), BF16)
    anywhere = pl.BlockSpec(memory_space=pl.ANY)
    return pl.pallas_call(
        functools.partial(token_kernel, steps, extra_rows(short_weights)[0], len(begun)),
        in_specs=in_vmem(count + 5) + [anywhere] * len(begun),
        out_specs=[anywhere] * 6,
        out_shape=[wide] * 4
        + [
            jax.ShapeDtypeStruct((tokens, width), F32),
            jax.ShapeDtypeStruct(short_weights.shape, F32),
        ],
        scratch_shapes=[
            *[pltpu.VMEM((count, tokens, LANES), BF16)] * 4,
            pltpu.VMEM((count, tokens, LANES), F32),
            pltpu.VMEM((count, *short_weights.shape[:2], LANES), F32),
            pltpu.VMEM((3, tokens + PAD, LANES), F32),
            pltpu.VMEM((3, tokens + PAD, LANES), F32),
            pltpu.SemaphoreType.DMA((count, 6)),
        ],
        input_output_aliases={count + 5 + at: at for at in range(len(begun))},
        compiler_params=pltpu.CompilerParams(vmem_limit_bytes=VMEM_LIMIT),
        cost_estimate=pl.CostEstimate(flops=0, bytes_accessed=4 * MIB, transcendentals=0),
        name="token_outputs",
    )(*arrived, query, key, value, cot, short_weights, *begun)


def channel_shards(query_proj, key_proj, value_proj, cotangent, filter_taps, short_weights):
    peers = lax.axis_size("ctx")
    tokens = query_proj.shape[0]
    tables = [jnp.asarray(table) for table in dft_tables(peers * tokens)]
    going, coming = partners(peers, False), partners(peers, True)
    sent = pack((query_proj, key_proj, value_proj, cotangent, filter_taps), going)
    arrived = exchange(sent, going)
    staged = stage((sent[0], short_weights, *tables), arrived[1])
    arrived[0] = staged[0]
    results = channel_step(arrived, going, coming, staged[1], staged[2:], tokens)
    back = exchange(results, coming)
    local = (query_proj, key_proj, value_proj, cotangent, short_weights)
    ends = [at for at in (4, 6) if at < peers] + [peers]
    begun, start = (), 0
    for end in ends:
        begun = token_step(back[start:end], coming[start:end], *local, begun)
        start = end
    return tuple(begun)


def from_behind(array, axis, by):
    peers = lax.axis_size(axis)
    pairs = [(i, i + by) for i in range(peers) if 0 <= i + by < peers]
    return lax.ppermute(array, axis, pairs)


def contract(form, left, right):
    return jnp.einsum(
        form, left, right, precision=lax.Precision.HIGHEST, preferred_element_type=jnp.float32
    )


def table_pair(rows, cols, period):
    row_ids = lax.broadcasted_iota(jnp.int32, (rows, cols), 0)
    col_ids = lax.broadcasted_iota(jnp.int32, (rows, cols), 1)
    angle = 2.0 * math.pi / period * (row_ids * col_ids % period).astype(jnp.float32)
    return (jnp.cos(angle), jnp.sin(angle))


def make_plan(seq_len):
    small_len = int(math.isqrt(2 * seq_len))
    while seq_len % small_len:
        small_len -= 1
    large_len = 2 * seq_len // small_len
    large_cos, large_sin = table_pair(large_len // 2, large_len, large_len)
    small_cos, small_sin = table_pair(small_len, small_len, small_len)
    twist_cos, twist_sin = table_pair(large_len, small_len, small_len * large_len)
    fwd_large = jnp.stack([large_cos, -large_sin], axis=1)
    fwd_small = jnp.stack([jnp.stack([small_cos, -small_sin]), jnp.stack([small_sin, small_cos])])
    inv_small = jnp.stack([jnp.stack([small_cos, small_sin]), jnp.stack([-small_sin, small_cos])])
    inv_large = jnp.stack([large_cos, -large_sin])
    return (small_len, large_len, fwd_large, fwd_small, inv_small, inv_large, twist_cos, twist_sin)


def forward_spec(signal, dft_plan):
    small_len, large_len, fwd_large, fwd_small, inv_small, inv_large, twist_cos, twist_sin = (
        dft_plan
    )
    cube = signal.reshape(signal.shape[0], large_len // 2, small_len)
    section_one = contract("cba,bpk->cpka", cube, fwd_large)
    real_one = section_one[:, 0]
    imag_one = section_one[:, 1]
    section_two = jnp.stack(
        [real_one * twist_cos + imag_one * twist_sin, imag_one * twist_cos - real_one * twist_sin],
        axis=1,
    )
    return contract("cpka,pqaj->cqkj", section_two, fwd_small)


def inverse_half(spec, dft_plan):
    small_len, large_len, fwd_large, fwd_small, inv_small, inv_large, twist_cos, twist_sin = (
        dft_plan
    )
    section_one = contract("cqkj,qpja->cpka", spec, inv_small)
    real_one = section_one[:, 0]
    imag_one = section_one[:, 1]
    section_two = jnp.stack(
        [real_one * twist_cos - imag_one * twist_sin, imag_one * twist_cos + real_one * twist_sin],
        axis=1,
    )
    signal = contract("cpka,pbk->cba", section_two, inv_large)
    return signal.reshape(signal.shape[0], -1) / float(small_len * large_len)


def complex_mul(left, right):
    left_real, left_imag = (left[:, 0], left[:, 1])
    right_real, right_imag = (right[:, 0], right[:, 1])
    return jnp.stack(
        [
            left_real * right_real - left_imag * right_imag,
            left_real * right_imag + left_imag * right_real,
        ],
        axis=1,
    )


def conj_mul(left, right):
    left_real, left_imag = (left[:, 0], left[:, 1])
    right_real, right_imag = (right[:, 0], right[:, 1])
    return jnp.stack(
        [
            left_real * right_real + left_imag * right_imag,
            left_real * right_imag - left_imag * right_real,
        ],
        axis=1,
    )


def conv_forward(prod_chan, filter_spec, dft_plan):
    prod_spec = forward_spec(prod_chan.astype(jnp.float32), dft_plan)
    conv_chan = inverse_half(complex_mul(prod_spec, filter_spec), dft_plan).astype(jnp.bfloat16)
    return (conv_chan, prod_spec)


def conv_backward(grad_chan, filter_spec, prod_spec, dft_plan, grad_scale):
    grad_spec = forward_spec(grad_chan.astype(jnp.float32), dft_plan)
    dconv_chan = inverse_half(conj_mul(filter_spec, grad_spec), dft_plan).astype(jnp.bfloat16)
    dfilter_chan = inverse_half(conj_mul(prod_spec, grad_spec), dft_plan) * grad_scale
    return (dconv_chan, dfilter_chan)


def receive_filter(filter_taps, dft_plan):
    filter_chan = lax.all_to_all(filter_taps.T, "ctx", split_axis=0, concat_axis=1, tiled=True)
    return forward_spec(filter_chan, dft_plan)


def return_filter(dfilter_chan):
    return (
        lax.all_to_all(
            dfilter_chan.astype(jnp.bfloat16), "ctx", split_axis=1, concat_axis=0, tiled=True
        )
        .astype(dfilter_chan.dtype)
        .T
    )


def causal_taps(extended, weights, length, axis):
    rim_rows = len(weights) - 1
    summed = weights[0] * lax.slice_in_dim(extended, rim_rows, rim_rows + length, axis=axis)
    for offset in range(1, len(weights)):
        summed = summed + weights[offset] * lax.slice_in_dim(
            extended, rim_rows - offset, rim_rows - offset + length, axis=axis
        )
    return summed


def reverse_taps(extended, weights, length, axis):
    summed = weights[0] * lax.slice_in_dim(extended, 0, length, axis=axis)
    for offset in range(1, len(weights)):
        summed = summed + weights[offset] * lax.slice_in_dim(
            extended, offset, offset + length, axis=axis
        )
    return summed


def tap_grads(grad_in, extended, tap_count, length, axis):
    rim_rows = tap_count - 1
    rows = [
        jnp.sum(
            grad_in
            * lax.slice_in_dim(extended, rim_rows - offset, rim_rows - offset + length, axis=axis),
            axis=axis,
        )
        for offset in range(tap_count)
    ]
    return jnp.stack(rows, axis=1)


def spread_shards(query_proj, key_proj, value_proj, cotangent, filter_taps, short_weights):
    tokens = query_proj.shape[0]
    tap_count = short_weights.shape[1]
    rim_rows = tap_count - 1
    seq_len = tokens * lax.axis_size("ctx")
    grad_scale = 1.0 / math.sqrt(seq_len)
    dft_plan = make_plan(seq_len)
    stacked = jnp.stack([query_proj, key_proj, value_proj])
    prev_rim = from_behind(stacked[:, tokens - rim_rows :], "ctx", 1)
    extended = jnp.concatenate([prev_rim, stacked], axis=1).astype(jnp.float32)
    weights = [short_weights[:, offset, None, :] for offset in range(tap_count)]
    short_out = causal_taps(extended, weights, tokens, 1)
    product = (short_out[1] * short_out[2]).astype(jnp.bfloat16)
    cot_wide = cotangent.astype(jnp.float32)
    gate_grad = (cot_wide * short_out[0]).astype(jnp.bfloat16)
    filter_spec = receive_filter(filter_taps, dft_plan)
    prod_chan = lax.all_to_all(product.T, "ctx", split_axis=0, concat_axis=1, tiled=True)
    conv_chan, prod_spec = conv_forward(prod_chan, filter_spec, dft_plan)
    conv_tok = lax.all_to_all(conv_chan, "ctx", split_axis=1, concat_axis=0, tiled=True)
    grad_chan = lax.all_to_all(gate_grad.T, "ctx", split_axis=0, concat_axis=1, tiled=True)
    dconv_chan, dfilter_chan = conv_backward(
        grad_chan, filter_spec, prod_spec, dft_plan, grad_scale
    )
    dconv_tok = lax.all_to_all(dconv_chan, "ctx", split_axis=1, concat_axis=0, tiled=True)
    filter_grad = return_filter(dfilter_chan)
    conv_wide = conv_tok.T.astype(jnp.float32)
    dconv_wide = dconv_tok.T.astype(jnp.float32)
    gated = (short_out[0] * conv_wide).astype(jnp.bfloat16)
    token_grads = jnp.stack(
        [cot_wide * conv_wide, dconv_wide * short_out[2], dconv_wide * short_out[1]]
    )
    next_rim = from_behind(token_grads[:, :rim_rows], "ctx", -1)
    grad_ext = jnp.concatenate([token_grads, next_rim], axis=1)
    inputs_grad = reverse_taps(grad_ext, weights, tokens, 1).astype(jnp.bfloat16)
    weight_part = tap_grads(token_grads, extended, tap_count, tokens, 1)
    short_grad = lax.psum(weight_part, "ctx") * grad_scale
    results = (gated, inputs_grad[0], inputs_grad[1], inputs_grad[2])
    return (results[0], results[1], results[2], results[3], filter_grad, short_grad)


def fits(query_proj, short_weights):
    peers = lax.axis_size("ctx")
    tokens, width = query_proj.shape
    tap_count = short_weights.shape[1]
    return (
        width == peers * LANES
        and peers.bit_count() == 1
        and tokens % (PHASES * CHUNK) == 0
        and tap_count == RIM + 1
        and peers * tokens <= 2048
    )


def shards(*arrays):
    return channel_shards(*arrays) if fits(arrays[0], arrays[5]) else spread_shards(*arrays)


def solution(mesh):
    placed = (
        P("ctx", "tp"),
        P("ctx", "tp"),
        P("ctx", "tp"),
        P("ctx", "tp"),
        P("ctx", "tp"),
        P(None, None, "tp"),
    )
    return jax.shard_map(
        shards,
        mesh=mesh,
        in_specs=placed,
        out_specs=(
            P("ctx", "tp"),
            P("ctx", "tp"),
            P("ctx", "tp"),
            P("ctx", "tp"),
            P("ctx", "tp"),
            P(None, None, "tp"),
        ),
        check_vma=False,
    )
```

```python
import functools
import math

import jax
import jax.numpy as jnp
import numpy as np
from jax import lax
from jax.experimental import pallas as pl
from jax.experimental.pallas import tpu as pltpu
from jax.sharding import PartitionSpec as P

F32 = jnp.float32
BF16 = jnp.bfloat16
LANES = 128
PHASES = 4
TILE = 16
PAD = 8
CHUNK = 16
RIM = 2
PIECES = 2
MIB = 1024 * 1024
VMEM_LIMIT = 24 * MIB
PACK_VMEM = 53862 * 1024


def partners(peers, diagonal_first):
    def rank(step):
        links, other_core = (step >> 1).bit_count(), step & 1
        if links == 0:
            return (1 if diagonal_first else 5, 0)
        if links == 1:
            return (4 if other_core else 3, -step)
        return (2 * other_core if diagonal_first else 3.5, other_core)

    return [0] + sorted(range(1, peers), key=rank)


def exchange(blocks, steps):
    peers = len(blocks)
    got = [blocks[0]]
    for step, block in list(zip(steps, blocks))[1:]:
        got.append(lax.ppermute(block, "ctx", [(i, i ^ step) for i in range(peers)]))
    return got


def in_vmem(count):
    return [pl.BlockSpec(memory_space=pltpu.VMEM)] * count


def lanes_of(place):
    return pl.ds(pl.multiple_of(place * LANES, LANES), LANES)


def pack_kernel(count, steps, *refs):
    sources, packed = refs[:count], refs[count : count + len(steps)]
    held, sems = refs[count + len(steps) : -1], refs[-1]
    tokens = sources[0].shape[0]
    me = lax.axis_index("ctx")
    arriving = [
        pltpu.make_async_copy(source, target, sems.at[at])
        for at, (source, target) in enumerate(zip(sources, held))
    ]
    for copy in reversed(arriving):
        copy.start()
    for at, source in enumerate(held):
        arriving[at].wait()
        rows = slice(at * tokens, (at + 1) * tokens)
        for step, target in zip(steps, packed):
            target[rows, :] = source[:, lanes_of(me ^ step)].astype(BF16)


def pack(arrays, steps):
    tokens = arrays[0].shape[0]
    count = len(arrays)
    return pl.pallas_call(
        functools.partial(pack_kernel, count, steps),
        in_specs=[pl.BlockSpec(memory_space=pl.ANY)] * count,
        out_specs=in_vmem(len(steps)),
        out_shape=[jax.ShapeDtypeStruct((count * tokens, LANES), BF16)] * len(steps),
        scratch_shapes=[
            *[pltpu.VMEM(array.shape, array.dtype) for array in arrays],
            pltpu.SemaphoreType.DMA((count,)),
        ],
        compiler_params=pltpu.CompilerParams(vmem_limit_bytes=PACK_VMEM),
        cost_estimate=pl.CostEstimate(flops=0, bytes_accessed=8 * MIB, transcendentals=0),
        name="pack_inputs",
    )(*arrays)


@functools.lru_cache(maxsize=None)
def dft_tables(seq_len):
    size = seq_len // PHASES
    k = np.arange(size, dtype=np.int64)[:, None]
    m = np.arange(size, dtype=np.int64)[None, :]
    forward = []
    for phase in range(PHASES):
        turns = ((4 * k + 1) * (PHASES * m + phase)) % (4 * seq_len)
        angle = 2.0 * np.pi / (4 * seq_len) * turns
        forward.append(np.concatenate([np.cos(angle), -np.sin(angle)], axis=0))
    forward = np.stack(forward)
    backward = np.swapaxes(forward, 1, 2) / seq_len

    return forward.astype(BF16), backward.astype(BF16)


def forward_mix(parts):
    (r0, i0), (r1, i1), (r2, i2), (r3, i3) = parts
    ar, ai, br, bi = r0 + r2, i0 + i2, r0 - r2, i0 - i2
    cr, ci, dr, di = r1 + r3, i1 + i3, r1 - r3, i1 - i3
    return ((ar + cr, ai + ci), (br + di, bi - dr), (ar - cr, ai - ci), (br - di, bi + dr))


def inverse_mix(parts):
    (r0, i0), (r1, i1), (r2, i2), (r3, i3) = parts
    ar, ai, br, bi = r0 + r2, i0 + i2, r0 - r2, i0 - i2
    cr, ci, dr, di = r1 + r3, i1 + i3, r1 - r3, i1 - i3
    return ((ar + cr, ai + ci), (br - di, bi + dr), (ar - cr, ai - ci), (br + di, bi - dr))


def times(left, right):
    return tuple(
        (lr * rr - li * ri, lr * ri + li * rr) for (lr, li), (rr, ri) in zip(left, right)
    )


def conj_times(left, right):
    return tuple(
        (lr * rr + li * ri, lr * ri - li * rr) for (lr, li), (rr, ri) in zip(left, right)
    )


def transform(table, signal):
    return jnp.dot(table, signal, preferred_element_type=F32)


def phases_near(ref, chunk, tap_count):
    start = PAD + chunk * CHUNK * PHASES
    return {
        offset: ref[pl.ds(start + offset, CHUNK, stride=PHASES), :]
        for offset in range(1 - tap_count, PHASES)
    }


def short_conv(near, taps):
    results = []
    for r in range(PHASES):
        summed = taps[0] * near[r]
        for at in range(1, len(taps)):
            summed = summed + taps[at] * near[r - at]
        results.append(summed)
    return results


def add_rows(total, terms):
    for term in terms:
        folded = jnp.sum(term.reshape(CHUNK // 8, 8, LANES), axis=0)
        total = folded if total is None else total + folded
    return total


def clear_ends(ref):
    ref[:PAD, :] = jnp.zeros((PAD, LANES), F32)
    ref[ref.shape[0] - PAD :, :] = jnp.zeros((PAD, LANES), F32)


def stage_kernel(count, *refs):
    sources, targets, sems = refs[:count], refs[count + 1 : 2 * count + 1], refs[2 * count + 1]
    copies = [
        pltpu.make_async_copy(source, target, sems.at[at])
        for at, (source, target) in enumerate(zip(sources, targets))
    ]
    for copy in copies:
        copy.start()
    for copy in copies:
        copy.wait()


def stage(arrays, after):
    count = len(arrays)
    return pl.pallas_call(
        functools.partial(stage_kernel, count),
        in_specs=[pl.BlockSpec(memory_space=pl.ANY)] * (count + 1),
        out_specs=in_vmem(count),
        out_shape=[jax.ShapeDtypeStruct(array.shape, array.dtype) for array in arrays],
        scratch_shapes=[pltpu.SemaphoreType.DMA((count,))],
        compiler_params=pltpu.CompilerParams(vmem_limit_bytes=8 * MIB),
        cost_estimate=pl.CostEstimate(flops=0, bytes_accessed=8 * MIB, transcendentals=0),
        name="stage_tables",
    )(*arrays, after)


def extra_rows(short_weights):
    sums = PIECES * short_weights.shape[0] * short_weights.shape[1]
    return sums, -(-(sums + 6 * RIM) // TILE) * TILE


def channel_kernel(tokens, heard, told, grad_scale, *refs):
    peers = len(heard)
    arrived = refs[:peers]
    weights, forward, backward = refs[peers : peers + 3]
    out = refs[peers + 3 : 2 * peers + 3]
    (
        query,
        key,
        value,
        cot,
        conv,
        conv_grad,
        filter_grad,
        taps,
        key_short,
        value_short,
        signals,
        spectra,
        products,
        extra,
    ) = refs[2 * peers + 3 :]
    size = peers * tokens // PHASES
    tap_count = weights.shape[1]
    me = lax.axis_index("ctx")
    own = lanes_of(me)
    for ref in (query, key, value, cot, conv, conv_grad):
        clear_ends(ref)
    for ref in (key_short, value_short):
        ref[:, size:, :] = jnp.zeros((PHASES, PAD, LANES), F32)
    for step, source in zip(heard, arrived):
        start = (me ^ step) * tokens
        inner = pl.ds(pl.multiple_of(PAD + start, PAD), tokens)
        for at, ref in enumerate((query, key, value, cot)):
            ref[inner, :] = source[at * tokens : (at + 1) * tokens, :].astype(F32)
        taps[pl.ds(pl.multiple_of(start, PAD), tokens), :] = source[4 * tokens :, :].astype(F32)
    chunks = range(size // CHUNK)
    taps_of = [
        [weights[array, tap : tap + 1, own] for tap in range(tap_count)] for array in range(3)
    ]

    def rows_of(chunk):
        return slice(chunk * CHUNK, (chunk + 1) * CHUNK)

    def spectrum(at, real, imag):
        lanes = slice(at * LANES, (at + 1) * LANES)
        return forward_mix(
            [(spectra[r, real, lanes], spectra[r, imag, lanes]) for r in range(PHASES)]
        )

    def keep(at, real, imag, mixed):
        lanes = slice(at * LANES, (at + 1) * LANES)
        for r, pair in enumerate(inverse_mix(mixed)):
            for rows, part in zip((real, imag), pair):
                products[r, rows, lanes] = part.astype(BF16)

    for chunk in chunks:
        rows = rows_of(chunk)
        key_now = short_conv(phases_near(key, chunk, tap_count), taps_of[1])
        value_now = short_conv(phases_near(value, chunk, tap_count), taps_of[2])
        for r in range(PHASES):
            key_short[r, rows, :] = key_now[r]
            value_short[r, rows, :] = value_now[r]
            signals[r, rows, :LANES] = (key_now[r] * value_now[r]).astype(BF16)
            filt = taps[pl.ds(chunk * CHUNK * PHASES + r, CHUNK, stride=PHASES), :]
            signals[r, rows, LANES : 2 * LANES] = filt.astype(BF16)
    for r in range(PHASES):
        spectra[r, :, : 2 * LANES] = transform(forward[r], signals[r, :, : 2 * LANES])
    for chunk in chunks:
        rows = rows_of(chunk)
        query_now = short_conv(phases_near(query, chunk, tap_count), taps_of[0])
        cot_now = phases_near(cot, chunk, 1)
        for r in range(PHASES):
            signals[r, rows, 2 * LANES :] = (cot_now[r] * query_now[r]).astype(BF16)
    for r in range(PHASES):
        spectra[r, :, 2 * LANES :] = transform(forward[r], signals[r, :, 2 * LANES :])
    for step in range(size // TILE):
        real = slice(step * TILE, (step + 1) * TILE)
        imag = slice(size + step * TILE, size + (step + 1) * TILE)
        prod, filt = spectrum(0, real, imag), spectrum(1, real, imag)
        for at, mixed in enumerate((prod, filt)):
            lanes = slice(at * LANES, (at + 1) * LANES)
            for q, pair in enumerate(mixed):
                spectra[q, real, lanes], spectra[q, imag, lanes] = pair
        keep(0, real, imag, times(prod, filt))
    for r in range(PHASES):
        result = transform(backward[r], products[r, :, :LANES])
        conv[pl.ds(PAD + r, size, stride=PHASES), :] = result.astype(BF16).astype(F32)
    for step in range(size // TILE):
        real = slice(step * TILE, (step + 1) * TILE)
        imag = slice(size + step * TILE, size + (step + 1) * TILE)
        grad = spectrum(2, real, imag)
        for at in range(2):
            lanes = slice(at * LANES, (at + 1) * LANES)
            known = [(spectra[q, real, lanes], spectra[q, imag, lanes]) for q in range(PHASES)]
            keep(2 - at, real, imag, conj_times(known, grad))
    for r in range(PHASES):
        result = transform(backward[r], products[r, :, LANES:])
        conv_grad[pl.ds(PAD + r, size, stride=PHASES), :] = (
            result[:, :LANES].astype(BF16).astype(F32)
        )
        filter_grad[pl.ds(r, size, stride=PHASES), :] = result[:, LANES:] * grad_scale

    totals = [[None] * tap_count for _ in range(3)]

    def add_sums(array, signal, chunk, pre):
        near = phases_near(signal, chunk, tap_count)
        for tap in range(tap_count):
            totals[array][tap] = add_rows(
                totals[array][tap], [pre[r] * near[r - tap] for r in range(PHASES)]
            )

    for chunk in chunks:
        cot_now, conv_now = phases_near(cot, chunk, 1), phases_near(conv, chunk, 1)
        add_sums(0, query, chunk, [cot_now[r] * conv_now[r] for r in range(PHASES)])
    for chunk in chunks:
        rows = rows_of(chunk)
        grad_now = phases_near(conv_grad, chunk, 1)
        add_sums(1, key, chunk, [grad_now[r] * value_short[r, rows, :] for r in range(PHASES)])
        add_sums(2, value, chunk, [grad_now[r] * key_short[r, rows, :] for r in range(PHASES)])
    sums = [jnp.sum(total, axis=0, keepdims=True) for row in totals for total in row]
    rest = jnp.concatenate(sums, axis=0) * grad_scale
    extra[...] = jnp.zeros_like(extra)
    for piece in range(PIECES):
        rounded = rest.astype(BF16).astype(F32)
        extra[piece * len(sums) : (piece + 1) * len(sums), :] = rounded
        rest = rest - rounded
    for step, target in zip(told, out):
        start = (me ^ step) * tokens
        inner = pl.ds(pl.multiple_of(PAD + start, PAD), tokens)
        target[:tokens, :] = conv[inner, :].astype(BF16)
        target[tokens : 2 * tokens, :] = conv_grad[inner, :].astype(BF16)
        target[2 * tokens : 3 * tokens, :] = filter_grad[
            pl.ds(pl.multiple_of(start, PAD), tokens), :
        ].astype(BF16)
        before = pl.ds(pl.multiple_of(start, PAD), PAD)
        after = pl.ds(pl.multiple_of(PAD + start + tokens, PAD), PAD)
        at = PIECES * len(sums)
        for ref in (query, key, value):
            extra[at : at + RIM, :] = ref[before, :][PAD - RIM :]
            at += RIM
        row = pl.ds(pl.multiple_of((start + tokens) // PHASES, PAD), PAD)
        extra[at : at + RIM, :] = (cot[after, :] * conv[after, :])[:RIM]
        for short in (value_short, key_short):
            at += RIM
            shorts = jnp.concatenate([short[r, row, :][:1] for r in range(RIM)], axis=0)
            extra[at : at + RIM, :] = conv_grad[after, :][:RIM] * shorts
        target[3 * tokens :, :] = extra[...].astype(BF16)


def channel_step(arrived, heard, told, short_weights, tables, tokens):
    peers = len(arrived)
    seq_len = peers * tokens
    size = seq_len // PHASES
    extra = extra_rows(short_weights)[1]
    padded = pltpu.VMEM((seq_len + 2 * PAD, LANES), F32)
    plain = pltpu.VMEM((seq_len, LANES), F32)
    phases = pltpu.VMEM((PHASES, size + PAD, LANES), F32)
    return pl.pallas_call(
        functools.partial(channel_kernel, tokens, heard, told, 1.0 / math.sqrt(seq_len)),
        in_specs=in_vmem(peers + 3),
        out_specs=in_vmem(peers),
        out_shape=[jax.ShapeDtypeStruct((3 * tokens + extra, LANES), BF16)] * peers,
        scratch_shapes=[
            *[padded] * 6,
            plain,
            plain,
            phases,
            phases,
            pltpu.VMEM((PHASES, size, 3 * LANES), BF16),
            pltpu.VMEM((PHASES, 2 * size, 3 * LANES), F32),
            pltpu.VMEM((PHASES, 2 * size, 3 * LANES), BF16),
            pltpu.VMEM((extra, LANES), F32),
        ],
        compiler_params=pltpu.CompilerParams(vmem_limit_bytes=VMEM_LIMIT),
        name="channel_operator",
    )(*arrived, short_weights, *tables)


def token_kernel(steps, sum_rows, carried, *refs):
    count_in = len(steps)
    arrived = refs[:count_in]
    query, key, value, cot, weights = refs[count_in : count_in + 5]
    results = refs[count_in + 5 + carried : count_in + 11 + carried]
    (gated, query_grad, key_grad, value_grad, filter_grad, short_grad, longer, pre, sems) = refs[
        count_in + 11 + carried :
    ]
    copies = []
    tokens = query.shape[0]
    tap_count = weights.shape[1]
    count = sum_rows // PIECES
    me = lax.axis_index("ctx")
    for slot, (step, source) in enumerate(zip(steps, arrived)):
        lanes = lanes_of(me ^ step)
        extra = source[3 * tokens :, :].astype(F32)

        def rim(at):
            return extra[sum_rows + at * RIM : sum_rows + (at + 1) * RIM]

        def short(array, signal):
            longer[array, PAD - RIM : PAD, :] = rim(array)
            longer[array, PAD :, :] = signal[:, lanes].astype(F32)
            summed = weights[array, 0:1, lanes] * longer[array, PAD:, :]
            for tap in range(1, tap_count):
                summed = (
                    summed
                    + weights[array, tap : tap + 1, lanes]
                    * longer[array, PAD - tap : PAD - tap + tokens, :]
                )
            return summed

        def taps_back(array, grad, target):
            pre[array, :tokens, :] = grad
            pre[array, tokens : tokens + RIM, :] = rim(3 + array)
            summed = weights[array, 0:1, lanes] * grad
            for tap in range(1, tap_count):
                summed = (
                    summed
                    + weights[array, tap : tap + 1, lanes] * pre[array, tap : tap + tokens, :]
                )
            target[slot] = summed.astype(BF16)

        conv = source[:tokens, :].astype(F32)
        conv_grad = source[tokens : 2 * tokens, :].astype(F32)
        gated[slot] = (short(0, query) * conv).astype(BF16)
        taps_back(0, cot[:, lanes].astype(F32) * conv, query_grad)
        taps_back(1, conv_grad * short(2, value), key_grad)
        taps_back(2, conv_grad * short(1, key), value_grad)
        filter_grad[slot] = source[2 * tokens : 3 * tokens, :].astype(F32)
        whole = extra[:count]
        for piece in range(1, PIECES):
            whole = whole + extra[piece * count : (piece + 1) * count]
        for row in range(count):
            which, tap = divmod(row, tap_count)
            short_grad[slot, which, tap : tap + 1, :] = whole[row : row + 1]
        held = (gated, query_grad, key_grad, value_grad, filter_grad, short_grad)
        for at, (source, target) in enumerate(zip(held, results)):
            place = target.at[:, :, lanes] if at == 5 else target.at[:, lanes]
            copies.append(pltpu.make_async_copy(source.at[slot], place, sems.at[slot, at]))
            copies[-1].start()
    for copy in copies:
        copy.wait()


def token_step(arrived, steps, query, key, value, cot, short_weights, begun=()):
    tokens, width = query.shape
    count = len(arrived)
    wide = jax.ShapeDtypeStruct((tokens, width), BF16)
    anywhere = pl.BlockSpec(memory_space=pl.ANY)
    return pl.pallas_call(
        functools.partial(token_kernel, steps, extra_rows(short_weights)[0], len(begun)),
        in_specs=in_vmem(count + 5) + [anywhere] * len(begun),
        out_specs=[anywhere] * 6,
        out_shape=[wide] * 4
        + [
            jax.ShapeDtypeStruct((tokens, width), F32),
            jax.ShapeDtypeStruct(short_weights.shape, F32),
        ],
        scratch_shapes=[
            *[pltpu.VMEM((count, tokens, LANES), BF16)] * 4,
            pltpu.VMEM((count, tokens, LANES), F32),
            pltpu.VMEM((count, *short_weights.shape[:2], LANES), F32),
            pltpu.VMEM((3, tokens + PAD, LANES), F32),
            pltpu.VMEM((3, tokens + PAD, LANES), F32),
            pltpu.SemaphoreType.DMA((count, 6)),
        ],
        input_output_aliases={count + 5 + at: at for at in range(len(begun))},
        compiler_params=pltpu.CompilerParams(vmem_limit_bytes=VMEM_LIMIT),
        cost_estimate=pl.CostEstimate(flops=0, bytes_accessed=4 * MIB, transcendentals=0),
        name="token_outputs",
    )(*arrived, query, key, value, cot, short_weights, *begun)


def channel_shards(query_proj, key_proj, value_proj, cotangent, filter_taps, short_weights):
    peers = lax.axis_size("ctx")
    tokens = query_proj.shape[0]
    tables = [jnp.asarray(table) for table in dft_tables(peers * tokens)]
    going, coming = partners(peers, False), partners(peers, True)
    sent = pack((query_proj, key_proj, value_proj, cotangent, filter_taps), going)
    arrived = exchange(sent, going)
    staged = stage((sent[0], short_weights, *tables), arrived[1])
    arrived[0] = staged[0]
    results = channel_step(arrived, going, coming, staged[1], staged[2:], tokens)
    back = exchange(results, coming)
    local = (query_proj, key_proj, value_proj, cotangent, short_weights)
    ends = [at for at in (4, 6) if at < peers] + [peers]
    begun, start = (), 0
    for end in ends:
        begun = token_step(back[start:end], coming[start:end], *local, begun)
        start = end
    return tuple(begun)


def from_behind(array, axis, by):
    peers = lax.axis_size(axis)
    pairs = [(i, i + by) for i in range(peers) if 0 <= i + by < peers]
    return lax.ppermute(array, axis, pairs)


def contract(form, left, right):
    return jnp.einsum(
        form, left, right, precision=lax.Precision.HIGHEST, preferred_element_type=jnp.float32
    )


def table_pair(rows, cols, period):
    row_ids = lax.broadcasted_iota(jnp.int32, (rows, cols), 0)
    col_ids = lax.broadcasted_iota(jnp.int32, (rows, cols), 1)
    angle = 2.0 * math.pi / period * (row_ids * col_ids % period).astype(jnp.float32)
    return (jnp.cos(angle), jnp.sin(angle))


def make_plan(seq_len):
    small_len = int(math.isqrt(2 * seq_len))
    while seq_len % small_len:
        small_len -= 1
    large_len = 2 * seq_len // small_len
    large_cos, large_sin = table_pair(large_len // 2, large_len, large_len)
    small_cos, small_sin = table_pair(small_len, small_len, small_len)
    twist_cos, twist_sin = table_pair(large_len, small_len, small_len * large_len)
    fwd_large = jnp.stack([large_cos, -large_sin], axis=1)
    fwd_small = jnp.stack([jnp.stack([small_cos, -small_sin]), jnp.stack([small_sin, small_cos])])
    inv_small = jnp.stack([jnp.stack([small_cos, small_sin]), jnp.stack([-small_sin, small_cos])])
    inv_large = jnp.stack([large_cos, -large_sin])
    return (small_len, large_len, fwd_large, fwd_small, inv_small, inv_large, twist_cos, twist_sin)


def forward_spec(signal, dft_plan):
    small_len, large_len, fwd_large, fwd_small, inv_small, inv_large, twist_cos, twist_sin = (
        dft_plan
    )
    cube = signal.reshape(signal.shape[0], large_len // 2, small_len)
    section_one = contract("cba,bpk->cpka", cube, fwd_large)
    real_one = section_one[:, 0]
    imag_one = section_one[:, 1]
    section_two = jnp.stack(
        [real_one * twist_cos + imag_one * twist_sin, imag_one * twist_cos - real_one * twist_sin],
        axis=1,
    )
    return contract("cpka,pqaj->cqkj", section_two, fwd_small)


def inverse_half(spec, dft_plan):
    small_len, large_len, fwd_large, fwd_small, inv_small, inv_large, twist_cos, twist_sin = (
        dft_plan
    )
    section_one = contract("cqkj,qpja->cpka", spec, inv_small)
    real_one = section_one[:, 0]
    imag_one = section_one[:, 1]
    section_two = jnp.stack(
        [real_one * twist_cos - imag_one * twist_sin, imag_one * twist_cos + real_one * twist_sin],
        axis=1,
    )
    signal = contract("cpka,pbk->cba", section_two, inv_large)
    return signal.reshape(signal.shape[0], -1) / float(small_len * large_len)


def complex_mul(left, right):
    left_real, left_imag = (left[:, 0], left[:, 1])
    right_real, right_imag = (right[:, 0], right[:, 1])
    return jnp.stack(
        [
            left_real * right_real - left_imag * right_imag,
            left_real * right_imag + left_imag * right_real,
        ],
        axis=1,
    )


def conj_mul(left, right):
    left_real, left_imag = (left[:, 0], left[:, 1])
    right_real, right_imag = (right[:, 0], right[:, 1])
    return jnp.stack(
        [
            left_real * right_real + left_imag * right_imag,
            left_real * right_imag - left_imag * right_real,
        ],
        axis=1,
    )


def conv_forward(prod_chan, filter_spec, dft_plan):
    prod_spec = forward_spec(prod_chan.astype(jnp.float32), dft_plan)
    conv_chan = inverse_half(complex_mul(prod_spec, filter_spec), dft_plan).astype(jnp.bfloat16)
    return (conv_chan, prod_spec)


def conv_backward(grad_chan, filter_spec, prod_spec, dft_plan, grad_scale):
    grad_spec = forward_spec(grad_chan.astype(jnp.float32), dft_plan)
    dconv_chan = inverse_half(conj_mul(filter_spec, grad_spec), dft_plan).astype(jnp.bfloat16)
    dfilter_chan = inverse_half(conj_mul(prod_spec, grad_spec), dft_plan) * grad_scale
    return (dconv_chan, dfilter_chan)


def receive_filter(filter_taps, dft_plan):
    filter_chan = lax.all_to_all(filter_taps.T, "ctx", split_axis=0, concat_axis=1, tiled=True)
    return forward_spec(filter_chan, dft_plan)


def return_filter(dfilter_chan):
    return (
        lax.all_to_all(
            dfilter_chan.astype(jnp.bfloat16), "ctx", split_axis=1, concat_axis=0, tiled=True
        )
        .astype(dfilter_chan.dtype)
        .T
    )


def causal_taps(extended, weights, length, axis):
    rim_rows = len(weights) - 1
    summed = weights[0] * lax.slice_in_dim(extended, rim_rows, rim_rows + length, axis=axis)
    for offset in range(1, len(weights)):
        summed = summed + weights[offset] * lax.slice_in_dim(
            extended, rim_rows - offset, rim_rows - offset + length, axis=axis
        )
    return summed


def reverse_taps(extended, weights, length, axis):
    summed = weights[0] * lax.slice_in_dim(extended, 0, length, axis=axis)
    for offset in range(1, len(weights)):
        summed = summed + weights[offset] * lax.slice_in_dim(
            extended, offset, offset + length, axis=axis
        )
    return summed


def tap_grads(grad_in, extended, tap_count, length, axis):
    rim_rows = tap_count - 1
    rows = [
        jnp.sum(
            grad_in
            * lax.slice_in_dim(extended, rim_rows - offset, rim_rows - offset + length, axis=axis),
            axis=axis,
        )
        for offset in range(tap_count)
    ]
    return jnp.stack(rows, axis=1)


def spread_shards(query_proj, key_proj, value_proj, cotangent, filter_taps, short_weights):
    tokens = query_proj.shape[0]
    tap_count = short_weights.shape[1]
    rim_rows = tap_count - 1
    seq_len = tokens * lax.axis_size("ctx")
    grad_scale = 1.0 / math.sqrt(seq_len)
    dft_plan = make_plan(seq_len)
    stacked = jnp.stack([query_proj, key_proj, value_proj])
    prev_rim = from_behind(stacked[:, tokens - rim_rows :], "ctx", 1)
    extended = jnp.concatenate([prev_rim, stacked], axis=1).astype(jnp.float32)
    weights = [short_weights[:, offset, None, :] for offset in range(tap_count)]
    short_out = causal_taps(extended, weights, tokens, 1)
    product = (short_out[1] * short_out[2]).astype(jnp.bfloat16)
    cot_wide = cotangent.astype(jnp.float32)
    gate_grad = (cot_wide * short_out[0]).astype(jnp.bfloat16)
    filter_spec = receive_filter(filter_taps, dft_plan)
    prod_chan = lax.all_to_all(product.T, "ctx", split_axis=0, concat_axis=1, tiled=True)
    conv_chan, prod_spec = conv_forward(prod_chan, filter_spec, dft_plan)
    conv_tok = lax.all_to_all(conv_chan, "ctx", split_axis=1, concat_axis=0, tiled=True)
    grad_chan = lax.all_to_all(gate_grad.T, "ctx", split_axis=0, concat_axis=1, tiled=True)
    dconv_chan, dfilter_chan = conv_backward(
        grad_chan, filter_spec, prod_spec, dft_plan, grad_scale
    )
    dconv_tok = lax.all_to_all(dconv_chan, "ctx", split_axis=1, concat_axis=0, tiled=True)
    filter_grad = return_filter(dfilter_chan)
    conv_wide = conv_tok.T.astype(jnp.float32)
    dconv_wide = dconv_tok.T.astype(jnp.float32)
    gated = (short_out[0] * conv_wide).astype(jnp.bfloat16)
    token_grads = jnp.stack(
        [cot_wide * conv_wide, dconv_wide * short_out[2], dconv_wide * short_out[1]]
    )
    next_rim = from_behind(token_grads[:, :rim_rows], "ctx", -1)
    grad_ext = jnp.concatenate([token_grads, next_rim], axis=1)
    inputs_grad = reverse_taps(grad_ext, weights, tokens, 1).astype(jnp.bfloat16)
    weight_part = tap_grads(token_grads, extended, tap_count, tokens, 1)
    short_grad = lax.psum(weight_part, "ctx") * grad_scale
    results = (gated, inputs_grad[0], inputs_grad[1], inputs_grad[2])
    return (results[0], results[1], results[2], results[3], filter_grad, short_grad)


def fits(query_proj, short_weights):
    peers = lax.axis_size("ctx")
    tokens, width = query_proj.shape
    tap_count = short_weights.shape[1]
    return (
        width == peers * LANES
        and peers.bit_count() == 1
        and tokens % (PHASES * CHUNK) == 0
        and tap_count == RIM + 1
        and peers * tokens <= 2048
    )


def shards(*arrays):
    return channel_shards(*arrays) if fits(arrays[0], arrays[5]) else spread_shards(*arrays)


def solution(mesh):
    placed = (
        P("ctx", "tp"),
        P("ctx", "tp"),
        P("ctx", "tp"),
        P("ctx", "tp"),
        P("ctx", "tp"),
        P(None, None, "tp"),
    )
    return jax.shard_map(
        shards,
        mesh=mesh,
        in_specs=placed,
        out_specs=(
            P("ctx", "tp"),
            P("ctx", "tp"),
            P("ctx", "tp"),
            P("ctx", "tp"),
            P("ctx", "tp"),
            P(None, None, "tp"),
        ),
        check_vma=False,
    )
```

```python
import functools
import math

import jax
import jax.numpy as jnp
import numpy as np
from jax import lax
from jax.experimental import pallas as pl
from jax.experimental.pallas import tpu as pltpu
from jax.sharding import PartitionSpec as P

F32 = jnp.float32
BF16 = jnp.bfloat16
LANES = 128
PHASES = 4
TILE = 16
PAD = 8
CHUNK = 16
RIM = 2
PIECES = 2
MIB = 1024 * 1024
VMEM_LIMIT = 24 * MIB
PACK_VMEM = 53862 * 1024


def partners(peers, diagonal_first):
    def rank(step):
        links, other_core = (step >> 1).bit_count(), step & 1
        if links == 0:
            return (1 if diagonal_first else 5, 0)
        if links == 1:
            return (4 if other_core else 3, -step)
        return (2 * other_core if diagonal_first else 3.5, other_core)

    return [0] + sorted(range(1, peers), key=rank)


def exchange(blocks, steps):
    peers = len(blocks)
    got = [blocks[0]]
    for step, block in list(zip(steps, blocks))[1:]:
        got.append(lax.ppermute(block, "ctx", [(i, i ^ step) for i in range(peers)]))
    return got


def in_vmem(count):
    return [pl.BlockSpec(memory_space=pltpu.VMEM)] * count


def lanes_of(place):
    return pl.ds(pl.multiple_of(place * LANES, LANES), LANES)


def pack_kernel(count, steps, *refs):
    sources, packed = refs[:count], refs[count : count + len(steps)]
    held, sems = refs[count + len(steps) : -1], refs[-1]
    tokens = sources[0].shape[0]
    me = lax.axis_index("ctx")
    arriving = [
        pltpu.make_async_copy(source, target, sems.at[at])
        for at, (source, target) in enumerate(zip(sources, held))
    ]
    for copy in arriving:
        copy.start()
    for at, source in enumerate(held):
        arriving[at].wait()
        rows = slice(at * tokens, (at + 1) * tokens)
        for step, target in zip(steps, packed):
            target[rows, :] = source[:, lanes_of(me ^ step)].astype(BF16)


def pack(arrays, steps):
    tokens = arrays[0].shape[0]
    count = len(arrays)
    return pl.pallas_call(
        functools.partial(pack_kernel, count, steps),
        in_specs=[pl.BlockSpec(memory_space=pl.ANY)] * count,
        out_specs=in_vmem(len(steps)),
        out_shape=[jax.ShapeDtypeStruct((count * tokens, LANES), BF16)] * len(steps),
        scratch_shapes=[
            *[pltpu.VMEM(array.shape, array.dtype) for array in arrays],
            pltpu.SemaphoreType.DMA((count,)),
        ],
        compiler_params=pltpu.CompilerParams(vmem_limit_bytes=PACK_VMEM),
        cost_estimate=pl.CostEstimate(flops=0, bytes_accessed=8 * MIB, transcendentals=0),
        name="pack_inputs",
    )(*arrays)


@functools.lru_cache(maxsize=None)
def dft_tables(seq_len):
    size = seq_len // PHASES
    k = np.arange(size, dtype=np.int64)[:, None]
    m = np.arange(size, dtype=np.int64)[None, :]
    forward = []
    for phase in range(PHASES):
        turns = ((4 * k + 1) * (PHASES * m + phase)) % (4 * seq_len)
        angle = 2.0 * np.pi / (4 * seq_len) * turns
        forward.append(np.concatenate([np.cos(angle), -np.sin(angle)], axis=0))
    forward = np.stack(forward)
    backward = np.swapaxes(forward, 1, 2) / seq_len

    return forward.astype(BF16), backward.astype(BF16)


def forward_mix(parts):
    (r0, i0), (r1, i1), (r2, i2), (r3, i3) = parts
    ar, ai, br, bi = r0 + r2, i0 + i2, r0 - r2, i0 - i2
    cr, ci, dr, di = r1 + r3, i1 + i3, r1 - r3, i1 - i3
    return ((ar + cr, ai + ci), (br + di, bi - dr), (ar - cr, ai - ci), (br - di, bi + dr))


def inverse_mix(parts):
    (r0, i0), (r1, i1), (r2, i2), (r3, i3) = parts
    ar, ai, br, bi = r0 + r2, i0 + i2, r0 - r2, i0 - i2
    cr, ci, dr, di = r1 + r3, i1 + i3, r1 - r3, i1 - i3
    return ((ar + cr, ai + ci), (br - di, bi + dr), (ar - cr, ai - ci), (br + di, bi - dr))


def times(left, right):
    return tuple(
        (lr * rr - li * ri, lr * ri + li * rr) for (lr, li), (rr, ri) in zip(left, right)
    )


def conj_times(left, right):
    return tuple(
        (lr * rr + li * ri, lr * ri - li * rr) for (lr, li), (rr, ri) in zip(left, right)
    )


def transform(table, signal):
    return jnp.dot(table, signal, preferred_element_type=F32)


def phases_near(ref, chunk, tap_count):
    start = PAD + chunk * CHUNK * PHASES
    return {
        offset: ref[pl.ds(start + offset, CHUNK, stride=PHASES), :]
        for offset in range(1 - tap_count, PHASES)
    }


def short_conv(near, taps):
    results = []
    for r in range(PHASES):
        summed = taps[0] * near[r]
        for at in range(1, len(taps)):
            summed = summed + taps[at] * near[r - at]
        results.append(summed)
    return results


def add_rows(total, terms):
    for term in terms:
        folded = jnp.sum(term.reshape(CHUNK // 8, 8, LANES), axis=0)
        total = folded if total is None else total + folded
    return total


def clear_ends(ref):
    ref[:PAD, :] = jnp.zeros((PAD, LANES), F32)
    ref[ref.shape[0] - PAD :, :] = jnp.zeros((PAD, LANES), F32)


def stage_kernel(count, *refs):
    sources, targets, sems = refs[:count], refs[count + 1 : 2 * count + 1], refs[2 * count + 1]
    copies = [
        pltpu.make_async_copy(source, target, sems.at[at])
        for at, (source, target) in enumerate(zip(sources, targets))
    ]
    for copy in copies:
        copy.start()
    for copy in copies:
        copy.wait()


def stage(arrays, after):
    count = len(arrays)
    return pl.pallas_call(
        functools.partial(stage_kernel, count),
        in_specs=[pl.BlockSpec(memory_space=pl.ANY)] * (count + 1),
        out_specs=in_vmem(count),
        out_shape=[jax.ShapeDtypeStruct(array.shape, array.dtype) for array in arrays],
        scratch_shapes=[pltpu.SemaphoreType.DMA((count,))],
        compiler_params=pltpu.CompilerParams(vmem_limit_bytes=8 * MIB),
        cost_estimate=pl.CostEstimate(flops=0, bytes_accessed=8 * MIB, transcendentals=0),
        name="stage_tables",
    )(*arrays, after)


def extra_rows(short_weights):
    sums = PIECES * short_weights.shape[0] * short_weights.shape[1]
    return sums, -(-(sums + 6 * RIM) // TILE) * TILE


def channel_kernel(tokens, heard, told, grad_scale, *refs):
    peers = len(heard)
    arrived = refs[:peers]
    weights, forward, backward = refs[peers : peers + 3]
    out = refs[peers + 3 : 2 * peers + 3]
    (
        query,
        key,
        value,
        cot,
        conv,
        conv_grad,
        filter_grad,
        filt,
        key_short,
        value_short,
        signals,
        spectra,
        products,
        extra,
    ) = refs[2 * peers + 3 :]
    size = peers * tokens // PHASES
    per = tokens // PHASES
    tap_count = weights.shape[1]
    me = lax.axis_index("ctx")
    own = lanes_of(me)
    for ref in (query, key, value, cot):
        clear_ends(ref)
    for ref in (key_short, value_short, conv, conv_grad):
        ref[:, size:, :] = jnp.zeros((PHASES, PAD, LANES), F32)
    for step, source in zip(heard, arrived):
        start = (me ^ step) * tokens
        inner = pl.ds(pl.multiple_of(PAD + start, PAD), tokens)
        for at, ref in enumerate((query, key, value, cot)):
            ref[inner, :] = source[at * tokens : (at + 1) * tokens, :].astype(F32)
        filt[pl.ds(pl.multiple_of(start, PAD), tokens), :] = source[4 * tokens :, :].astype(F32)
    chunks = range(size // CHUNK)
    taps_of = [
        [weights[array, tap : tap + 1, own] for tap in range(tap_count)] for array in range(3)
    ]

    def rows_of(chunk):
        return slice(chunk * CHUNK, (chunk + 1) * CHUNK)

    def spectrum(at, real, imag):
        lanes = slice(at * LANES, (at + 1) * LANES)
        return forward_mix(
            [(spectra[r, real, lanes], spectra[r, imag, lanes]) for r in range(PHASES)]
        )

    def keep(at, real, imag, mixed):
        lanes = slice(at * LANES, (at + 1) * LANES)
        for r, pair in enumerate(inverse_mix(mixed)):
            for rows, part in zip((real, imag), pair):
                products[r, rows, lanes] = part.astype(BF16)

    for chunk in chunks:
        rows = rows_of(chunk)
        key_now = short_conv(phases_near(key, chunk, tap_count), taps_of[1])
        value_now = short_conv(phases_near(value, chunk, tap_count), taps_of[2])
        for r in range(PHASES):
            key_short[r, rows, :] = key_now[r]
            value_short[r, rows, :] = value_now[r]
            signals[r, rows, :LANES] = (key_now[r] * value_now[r]).astype(BF16)
            filt_now = filt[pl.ds(chunk * CHUNK * PHASES + r, CHUNK, stride=PHASES), :]
            signals[r, rows, LANES : 2 * LANES] = filt_now.astype(BF16)
    for r in range(PHASES):
        spectra[r, :, : 2 * LANES] = transform(forward[r], signals[r, :, : 2 * LANES])
    for chunk in chunks:
        rows = rows_of(chunk)
        query_now = short_conv(phases_near(query, chunk, tap_count), taps_of[0])
        cot_now = phases_near(cot, chunk, 1)
        for r in range(PHASES):
            signals[r, rows, 2 * LANES :] = (cot_now[r] * query_now[r]).astype(BF16)
    for r in range(PHASES):
        spectra[r, :, 2 * LANES :] = transform(forward[r], signals[r, :, 2 * LANES :])
    for step in range(size // TILE):
        real = slice(step * TILE, (step + 1) * TILE)
        imag = slice(size + step * TILE, size + (step + 1) * TILE)
        prod, filt = spectrum(0, real, imag), spectrum(1, real, imag)
        for at, mixed in enumerate((prod, filt)):
            lanes = slice(at * LANES, (at + 1) * LANES)
            for q, pair in enumerate(mixed):
                spectra[q, real, lanes], spectra[q, imag, lanes] = pair
        keep(0, real, imag, times(prod, filt))
    for r in range(PHASES):
        result = transform(backward[r], products[r, :, :LANES])
        conv[r, :size, :] = result.astype(BF16).astype(F32)
    for step in range(size // TILE):
        real = slice(step * TILE, (step + 1) * TILE)
        imag = slice(size + step * TILE, size + (step + 1) * TILE)
        grad = spectrum(2, real, imag)
        for at in range(2):
            lanes = slice(at * LANES, (at + 1) * LANES)
            known = [(spectra[q, real, lanes], spectra[q, imag, lanes]) for q in range(PHASES)]
            keep(2 - at, real, imag, conj_times(known, grad))
    for r in range(PHASES):
        result = transform(backward[r], products[r, :, LANES:])
        conv_grad[r, :size, :] = result[:, :LANES].astype(BF16).astype(F32)
        filter_grad[r] = (result[:, LANES:] * grad_scale).astype(BF16)

    totals = [[None] * tap_count for _ in range(3)]

    def add_sums(array, signal, chunk, pre):
        near = phases_near(signal, chunk, tap_count)
        for tap in range(tap_count):
            totals[array][tap] = add_rows(
                totals[array][tap], [pre[r] * near[r - tap] for r in range(PHASES)]
            )

    for chunk in chunks:
        rows = rows_of(chunk)
        cot_now = phases_near(cot, chunk, 1)
        add_sums(0, query, chunk, [cot_now[r] * conv[r, rows, :] for r in range(PHASES)])
    for chunk in chunks:
        rows = rows_of(chunk)
        grad_now = [conv_grad[r, rows, :] for r in range(PHASES)]
        add_sums(1, key, chunk, [grad_now[r] * value_short[r, rows, :] for r in range(PHASES)])
        add_sums(2, value, chunk, [grad_now[r] * key_short[r, rows, :] for r in range(PHASES)])
    sums = [jnp.sum(total, axis=0, keepdims=True) for row in totals for total in row]
    rest = jnp.concatenate(sums, axis=0) * grad_scale
    extra[...] = jnp.zeros_like(extra)
    for piece in range(PIECES):
        rounded = rest.astype(BF16).astype(F32)
        extra[piece * len(sums) : (piece + 1) * len(sums), :] = rounded
        rest = rest - rounded
    for step, target in zip(told, out):
        start = (me ^ step) * tokens
        rows = pl.ds(pl.multiple_of((me ^ step) * per, per), per)
        for at, ref in enumerate((conv, conv_grad, filter_grad)):
            for r in range(PHASES):
                begin = at * tokens + r * per
                target[begin : begin + per, :] = ref[r, rows, :].astype(BF16)
        before = pl.ds(pl.multiple_of(start, PAD), PAD)
        after = pl.ds(pl.multiple_of(PAD + start + tokens, PAD), PAD)
        at = PIECES * len(sums)
        for ref in (query, key, value):
            extra[at : at + RIM, :] = ref[before, :][PAD - RIM :]
            at += RIM
        row = pl.ds(pl.multiple_of((me ^ step) * per + per, per), PAD)

        def first(ref):
            return jnp.concatenate([ref[r, row, :][:1] for r in range(RIM)], axis=0)

        grad_first = first(conv_grad)
        pre = (
            cot[after, :][:RIM] * first(conv),
            grad_first * first(value_short),
            grad_first * first(key_short),
        )
        for value_at in pre:
            extra[at : at + RIM, :] = value_at
            at += RIM
        target[3 * tokens :, :] = extra[...].astype(BF16)


def channel_step(arrived, heard, told, short_weights, tables, tokens):
    peers = len(arrived)
    seq_len = peers * tokens
    size = seq_len // PHASES
    extra = extra_rows(short_weights)[1]
    padded = pltpu.VMEM((seq_len + 2 * PAD, LANES), F32)
    phases = pltpu.VMEM((PHASES, size + PAD, LANES), F32)
    return pl.pallas_call(
        functools.partial(channel_kernel, tokens, heard, told, 1.0 / math.sqrt(seq_len)),
        in_specs=in_vmem(peers + 3),
        out_specs=in_vmem(peers),
        out_shape=[jax.ShapeDtypeStruct((3 * tokens + extra, LANES), BF16)] * peers,
        scratch_shapes=[
            *[padded] * 4,
            phases,
            phases,
            pltpu.VMEM((PHASES, size, LANES), BF16),
            pltpu.VMEM((seq_len, LANES), F32),
            phases,
            phases,
            pltpu.VMEM((PHASES, size, 3 * LANES), BF16),
            pltpu.VMEM((PHASES, 2 * size, 3 * LANES), F32),
            pltpu.VMEM((PHASES, 2 * size, 3 * LANES), BF16),
            pltpu.VMEM((extra, LANES), F32),
        ],
        compiler_params=pltpu.CompilerParams(vmem_limit_bytes=VMEM_LIMIT),
        name="channel_operator",
    )(*arrived, short_weights, *tables)


def token_kernel(steps, sum_rows, carried, *refs):
    count_in = len(steps)
    arrived = refs[:count_in]
    query, key, value, cot, weights = refs[count_in : count_in + 5]
    results = refs[count_in + 5 + carried : count_in + 11 + carried]
    gated, query_grad, key_grad, value_grad, filter_grad, short_grad, *scratch = refs[
        count_in + 11 + carried :
    ]
    longer, pre, ordered, sems = scratch
    copies = []
    tokens = query.shape[0]
    per = tokens // PHASES
    tap_count = weights.shape[1]
    count = sum_rows // PIECES
    me = lax.axis_index("ctx")
    for slot, (step, source) in enumerate(zip(steps, arrived)):
        lanes = lanes_of(me ^ step)
        extra = source[3 * tokens :, :].astype(F32)

        def rim(at):
            return extra[sum_rows + at * RIM : sum_rows + (at + 1) * RIM]

        def short(array, signal):
            longer[array, PAD - RIM : PAD, :] = rim(array)
            longer[array, PAD :, :] = signal[:, lanes].astype(F32)
            summed = weights[array, 0:1, lanes] * longer[array, PAD:, :]
            for tap in range(1, tap_count):
                summed = (
                    summed
                    + weights[array, tap : tap + 1, lanes]
                    * longer[array, PAD - tap : PAD - tap + tokens, :]
                )
            return summed

        def taps_back(array, grad, target):
            pre[array, :tokens, :] = grad
            pre[array, tokens : tokens + RIM, :] = rim(3 + array)
            summed = weights[array, 0:1, lanes] * grad
            for tap in range(1, tap_count):
                summed = (
                    summed
                    + weights[array, tap : tap + 1, lanes] * pre[array, tap : tap + tokens, :]
                )
            target[slot] = summed.astype(BF16)

        for at in range(3):
            for r in range(PHASES):
                begin = at * tokens + r * per
                part = source[begin : begin + per, :].astype(F32)
                if at < 2:
                    ordered[at, pl.ds(r, per, stride=PHASES), :] = part
                else:
                    filter_grad[slot, pl.ds(r, per, stride=PHASES), :] = part
        conv, conv_grad = ordered[0], ordered[1]
        gated[slot] = (short(0, query) * conv).astype(BF16)
        taps_back(0, cot[:, lanes].astype(F32) * conv, query_grad)
        taps_back(1, conv_grad * short(2, value), key_grad)
        taps_back(2, conv_grad * short(1, key), value_grad)
        whole = extra[:count]
        for piece in range(1, PIECES):
            whole = whole + extra[piece * count : (piece + 1) * count]
        for row in range(count):
            which, tap = divmod(row, tap_count)
            short_grad[slot, which, tap : tap + 1, :] = whole[row : row + 1]
        held = (gated, query_grad, key_grad, value_grad, filter_grad, short_grad)
        for at, (source, target) in enumerate(zip(held, results)):
            place = target.at[:, :, lanes] if at == 5 else target.at[:, lanes]
            copies.append(pltpu.make_async_copy(source.at[slot], place, sems.at[slot, at]))
            copies[-1].start()
    for copy in copies:
        copy.wait()


def token_step(arrived, steps, query, key, value, cot, short_weights, begun=()):
    tokens, width = query.shape
    count = len(arrived)
    wide = jax.ShapeDtypeStruct((tokens, width), BF16)
    anywhere = pl.BlockSpec(memory_space=pl.ANY)
    return pl.pallas_call(
        functools.partial(token_kernel, steps, extra_rows(short_weights)[0], len(begun)),
        in_specs=in_vmem(count + 5) + [anywhere] * len(begun),
        out_specs=[anywhere] * 6,
        out_shape=[wide] * 4
        + [
            jax.ShapeDtypeStruct((tokens, width), F32),
            jax.ShapeDtypeStruct(short_weights.shape, F32),
        ],
        scratch_shapes=[
            *[pltpu.VMEM((count, tokens, LANES), BF16)] * 4,
            pltpu.VMEM((count, tokens, LANES), F32),
            pltpu.VMEM((count, *short_weights.shape[:2], LANES), F32),
            pltpu.VMEM((3, tokens + PAD, LANES), F32),
            pltpu.VMEM((3, tokens + PAD, LANES), F32),
            pltpu.VMEM((2, tokens, LANES), F32),
            pltpu.SemaphoreType.DMA((count, 6)),
        ],
        input_output_aliases={count + 5 + at: at for at in range(len(begun))},
        compiler_params=pltpu.CompilerParams(vmem_limit_bytes=VMEM_LIMIT),
        cost_estimate=pl.CostEstimate(flops=0, bytes_accessed=4 * MIB, transcendentals=0),
        name="token_outputs",
    )(*arrived, query, key, value, cot, short_weights, *begun)


def channel_shards(query_proj, key_proj, value_proj, cotangent, filter_taps, short_weights):
    peers = lax.axis_size("ctx")
    tokens = query_proj.shape[0]
    tables = [jnp.asarray(table) for table in dft_tables(peers * tokens)]
    going, coming = partners(peers, False), partners(peers, True)
    sent = pack((query_proj, key_proj, value_proj, cotangent, filter_taps), going)
    arrived = exchange(sent, going)
    staged = stage((sent[0], short_weights, *tables), arrived[1])
    arrived[0] = staged[0]
    results = channel_step(arrived, going, coming, staged[1], staged[2:], tokens)
    back = exchange(results, coming)
    local = (query_proj, key_proj, value_proj, cotangent, short_weights)
    ends = [at for at in (4, 6) if at < peers] + [peers]
    begun, start = (), 0
    for end in ends:
        begun = token_step(back[start:end], coming[start:end], *local, begun)
        start = end
    return tuple(begun)


def from_behind(array, axis, by):
    peers = lax.axis_size(axis)
    pairs = [(i, i + by) for i in range(peers) if 0 <= i + by < peers]
    return lax.ppermute(array, axis, pairs)


def contract(form, left, right):
    return jnp.einsum(
        form, left, right, precision=lax.Precision.HIGHEST, preferred_element_type=jnp.float32
    )


def table_pair(rows, cols, period):
    row_ids = lax.broadcasted_iota(jnp.int32, (rows, cols), 0)
    col_ids = lax.broadcasted_iota(jnp.int32, (rows, cols), 1)
    angle = 2.0 * math.pi / period * (row_ids * col_ids % period).astype(jnp.float32)
    return (jnp.cos(angle), jnp.sin(angle))


def make_plan(seq_len):
    small_len = int(math.isqrt(2 * seq_len))
    while seq_len % small_len:
        small_len -= 1
    large_len = 2 * seq_len // small_len
    large_cos, large_sin = table_pair(large_len // 2, large_len, large_len)
    small_cos, small_sin = table_pair(small_len, small_len, small_len)
    twist_cos, twist_sin = table_pair(large_len, small_len, small_len * large_len)
    fwd_large = jnp.stack([large_cos, -large_sin], axis=1)
    fwd_small = jnp.stack([jnp.stack([small_cos, -small_sin]), jnp.stack([small_sin, small_cos])])
    inv_small = jnp.stack([jnp.stack([small_cos, small_sin]), jnp.stack([-small_sin, small_cos])])
    inv_large = jnp.stack([large_cos, -large_sin])
    return (small_len, large_len, fwd_large, fwd_small, inv_small, inv_large, twist_cos, twist_sin)


def forward_spec(signal, dft_plan):
    small_len, large_len, fwd_large, fwd_small, inv_small, inv_large, twist_cos, twist_sin = (
        dft_plan
    )
    cube = signal.reshape(signal.shape[0], large_len // 2, small_len)
    section_one = contract("cba,bpk->cpka", cube, fwd_large)
    real_one = section_one[:, 0]
    imag_one = section_one[:, 1]
    section_two = jnp.stack(
        [real_one * twist_cos + imag_one * twist_sin, imag_one * twist_cos - real_one * twist_sin],
        axis=1,
    )
    return contract("cpka,pqaj->cqkj", section_two, fwd_small)


def inverse_half(spec, dft_plan):
    small_len, large_len, fwd_large, fwd_small, inv_small, inv_large, twist_cos, twist_sin = (
        dft_plan
    )
    section_one = contract("cqkj,qpja->cpka", spec, inv_small)
    real_one = section_one[:, 0]
    imag_one = section_one[:, 1]
    section_two = jnp.stack(
        [real_one * twist_cos - imag_one * twist_sin, imag_one * twist_cos + real_one * twist_sin],
        axis=1,
    )
    signal = contract("cpka,pbk->cba", section_two, inv_large)
    return signal.reshape(signal.shape[0], -1) / float(small_len * large_len)


def complex_mul(left, right):
    left_real, left_imag = (left[:, 0], left[:, 1])
    right_real, right_imag = (right[:, 0], right[:, 1])
    return jnp.stack(
        [
            left_real * right_real - left_imag * right_imag,
            left_real * right_imag + left_imag * right_real,
        ],
        axis=1,
    )


def conj_mul(left, right):
    left_real, left_imag = (left[:, 0], left[:, 1])
    right_real, right_imag = (right[:, 0], right[:, 1])
    return jnp.stack(
        [
            left_real * right_real + left_imag * right_imag,
            left_real * right_imag - left_imag * right_real,
        ],
        axis=1,
    )


def conv_forward(prod_chan, filter_spec, dft_plan):
    prod_spec = forward_spec(prod_chan.astype(jnp.float32), dft_plan)
    conv_chan = inverse_half(complex_mul(prod_spec, filter_spec), dft_plan).astype(jnp.bfloat16)
    return (conv_chan, prod_spec)


def conv_backward(grad_chan, filter_spec, prod_spec, dft_plan, grad_scale):
    grad_spec = forward_spec(grad_chan.astype(jnp.float32), dft_plan)
    dconv_chan = inverse_half(conj_mul(filter_spec, grad_spec), dft_plan).astype(jnp.bfloat16)
    dfilter_chan = inverse_half(conj_mul(prod_spec, grad_spec), dft_plan) * grad_scale
    return (dconv_chan, dfilter_chan)


def receive_filter(filter_taps, dft_plan):
    filter_chan = lax.all_to_all(filter_taps.T, "ctx", split_axis=0, concat_axis=1, tiled=True)
    return forward_spec(filter_chan, dft_plan)


def return_filter(dfilter_chan):
    return (
        lax.all_to_all(
            dfilter_chan.astype(jnp.bfloat16), "ctx", split_axis=1, concat_axis=0, tiled=True
        )
        .astype(dfilter_chan.dtype)
        .T
    )


def causal_taps(extended, weights, length, axis):
    rim_rows = len(weights) - 1
    summed = weights[0] * lax.slice_in_dim(extended, rim_rows, rim_rows + length, axis=axis)
    for offset in range(1, len(weights)):
        summed = summed + weights[offset] * lax.slice_in_dim(
            extended, rim_rows - offset, rim_rows - offset + length, axis=axis
        )
    return summed


def reverse_taps(extended, weights, length, axis):
    summed = weights[0] * lax.slice_in_dim(extended, 0, length, axis=axis)
    for offset in range(1, len(weights)):
        summed = summed + weights[offset] * lax.slice_in_dim(
            extended, offset, offset + length, axis=axis
        )
    return summed


def tap_grads(grad_in, extended, tap_count, length, axis):
    rim_rows = tap_count - 1
    rows = [
        jnp.sum(
            grad_in
            * lax.slice_in_dim(extended, rim_rows - offset, rim_rows - offset + length, axis=axis),
            axis=axis,
        )
        for offset in range(tap_count)
    ]
    return jnp.stack(rows, axis=1)


def spread_shards(query_proj, key_proj, value_proj, cotangent, filter_taps, short_weights):
    tokens = query_proj.shape[0]
    tap_count = short_weights.shape[1]
    rim_rows = tap_count - 1
    seq_len = tokens * lax.axis_size("ctx")
    grad_scale = 1.0 / math.sqrt(seq_len)
    dft_plan = make_plan(seq_len)
    stacked = jnp.stack([query_proj, key_proj, value_proj])
    prev_rim = from_behind(stacked[:, tokens - rim_rows :], "ctx", 1)
    extended = jnp.concatenate([prev_rim, stacked], axis=1).astype(jnp.float32)
    weights = [short_weights[:, offset, None, :] for offset in range(tap_count)]
    short_out = causal_taps(extended, weights, tokens, 1)
    product = (short_out[1] * short_out[2]).astype(jnp.bfloat16)
    cot_wide = cotangent.astype(jnp.float32)
    gate_grad = (cot_wide * short_out[0]).astype(jnp.bfloat16)
    filter_spec = receive_filter(filter_taps, dft_plan)
    prod_chan = lax.all_to_all(product.T, "ctx", split_axis=0, concat_axis=1, tiled=True)
    conv_chan, prod_spec = conv_forward(prod_chan, filter_spec, dft_plan)
    conv_tok = lax.all_to_all(conv_chan, "ctx", split_axis=1, concat_axis=0, tiled=True)
    grad_chan = lax.all_to_all(gate_grad.T, "ctx", split_axis=0, concat_axis=1, tiled=True)
    dconv_chan, dfilter_chan = conv_backward(
        grad_chan, filter_spec, prod_spec, dft_plan, grad_scale
    )
    dconv_tok = lax.all_to_all(dconv_chan, "ctx", split_axis=1, concat_axis=0, tiled=True)
    filter_grad = return_filter(dfilter_chan)
    conv_wide = conv_tok.T.astype(jnp.float32)
    dconv_wide = dconv_tok.T.astype(jnp.float32)
    gated = (short_out[0] * conv_wide).astype(jnp.bfloat16)
    token_grads = jnp.stack(
        [cot_wide * conv_wide, dconv_wide * short_out[2], dconv_wide * short_out[1]]
    )
    next_rim = from_behind(token_grads[:, :rim_rows], "ctx", -1)
    grad_ext = jnp.concatenate([token_grads, next_rim], axis=1)
    inputs_grad = reverse_taps(grad_ext, weights, tokens, 1).astype(jnp.bfloat16)
    weight_part = tap_grads(token_grads, extended, tap_count, tokens, 1)
    short_grad = lax.psum(weight_part, "ctx") * grad_scale
    results = (gated, inputs_grad[0], inputs_grad[1], inputs_grad[2])
    return (results[0], results[1], results[2], results[3], filter_grad, short_grad)


def fits(query_proj, short_weights):
    peers = lax.axis_size("ctx")
    tokens, width = query_proj.shape
    tap_count = short_weights.shape[1]
    return (
        width == peers * LANES
        and peers.bit_count() == 1
        and tokens % (PHASES * CHUNK) == 0
        and tap_count == RIM + 1
        and peers * tokens <= 2048
    )


def shards(*arrays):
    return channel_shards(*arrays) if fits(arrays[0], arrays[5]) else spread_shards(*arrays)


def solution(mesh):
    placed = (
        P("ctx", "tp"),
        P("ctx", "tp"),
        P("ctx", "tp"),
        P("ctx", "tp"),
        P("ctx", "tp"),
        P(None, None, "tp"),
    )
    return jax.shard_map(
        shards,
        mesh=mesh,
        in_specs=placed,
        out_specs=(
            P("ctx", "tp"),
            P("ctx", "tp"),
            P("ctx", "tp"),
            P("ctx", "tp"),
            P("ctx", "tp"),
            P(None, None, "tp"),
        ),
        check_vma=False,
    )
```

```python
import functools
import math

import jax
import jax.numpy as jnp
import numpy as np
from jax import lax
from jax.experimental import pallas as pl
from jax.experimental.pallas import tpu as pltpu
from jax.sharding import PartitionSpec as P

F32 = jnp.float32
BF16 = jnp.bfloat16
LANES = 128
PHASES = 4
TILE = 16
PAD = 8
CHUNK = 32
ROWS = 8
RIM = 2
PIECES = 2
MIB = 1024 * 1024
VMEM_LIMIT = 24 * MIB
PACK_VMEM = 53862 * 1024


def partners(peers, diagonal_first):
    def rank(step):
        links, other_core = (step >> 1).bit_count(), step & 1
        if links == 0:
            return (1 if diagonal_first else 5, 0)
        if links == 1:
            return (4 if other_core else 3, -step)
        return (2 * other_core if diagonal_first else 3.5, other_core)

    return [0] + sorted(range(1, peers), key=rank)


def exchange(blocks, steps):
    peers = len(blocks)
    got = [blocks[0]]
    for step, block in list(zip(steps, blocks))[1:]:
        got.append(lax.ppermute(block, "ctx", [(i, i ^ step) for i in range(peers)]))
    return got


def in_vmem(count):
    return [pl.BlockSpec(memory_space=pltpu.VMEM)] * count


def lanes_of(place):
    return pl.ds(pl.multiple_of(place * LANES, LANES), LANES)


def pack_kernel(count, steps, *refs):
    sources, packed = refs[:count], refs[count : count + len(steps)]
    held, sems = refs[count + len(steps) : -1], refs[-1]
    tokens = sources[0].shape[0]
    me = lax.axis_index("ctx")
    arriving = [
        pltpu.make_async_copy(source, target, sems.at[at])
        for at, (source, target) in enumerate(zip(sources, held))
    ]
    for copy in arriving:
        copy.start()
    for at, source in enumerate(held):
        arriving[at].wait()
        rows = slice(at * tokens, (at + 1) * tokens)
        for step, target in zip(steps, packed):
            target[rows, :] = source[:, lanes_of(me ^ step)].astype(BF16)


def pack(arrays, steps):
    tokens = arrays[0].shape[0]
    count = len(arrays)
    return pl.pallas_call(
        functools.partial(pack_kernel, count, steps),
        in_specs=[pl.BlockSpec(memory_space=pl.ANY)] * count,
        out_specs=in_vmem(len(steps)),
        out_shape=[jax.ShapeDtypeStruct((count * tokens, LANES), BF16)] * len(steps),
        scratch_shapes=[
            *[pltpu.VMEM(array.shape, array.dtype) for array in arrays],
            pltpu.SemaphoreType.DMA((count,)),
        ],
        compiler_params=pltpu.CompilerParams(vmem_limit_bytes=PACK_VMEM),
        cost_estimate=pl.CostEstimate(flops=0, bytes_accessed=8 * MIB, transcendentals=0),
        name="pack_inputs",
    )(*arrays)


@functools.lru_cache(maxsize=None)
def dft_tables(seq_len):
    size = seq_len // PHASES
    k = np.arange(size, dtype=np.int64)[:, None]
    m = np.arange(size, dtype=np.int64)[None, :]
    forward = []
    for phase in range(PHASES):
        turns = ((4 * k + 1) * (PHASES * m + phase)) % (4 * seq_len)
        angle = 2.0 * np.pi / (4 * seq_len) * turns
        forward.append(np.concatenate([np.cos(angle), -np.sin(angle)], axis=0))
    forward = np.stack(forward)
    backward = np.swapaxes(forward, 1, 2) / seq_len

    return forward.astype(BF16), backward.astype(BF16)


def forward_mix(parts):
    (r0, i0), (r1, i1), (r2, i2), (r3, i3) = parts
    ar, ai, br, bi = r0 + r2, i0 + i2, r0 - r2, i0 - i2
    cr, ci, dr, di = r1 + r3, i1 + i3, r1 - r3, i1 - i3
    return ((ar + cr, ai + ci), (br + di, bi - dr), (ar - cr, ai - ci), (br - di, bi + dr))


def inverse_mix(parts):
    (r0, i0), (r1, i1), (r2, i2), (r3, i3) = parts
    ar, ai, br, bi = r0 + r2, i0 + i2, r0 - r2, i0 - i2
    cr, ci, dr, di = r1 + r3, i1 + i3, r1 - r3, i1 - i3
    return ((ar + cr, ai + ci), (br - di, bi + dr), (ar - cr, ai - ci), (br + di, bi - dr))


def times(left, right):
    return tuple(
        (lr * rr - li * ri, lr * ri + li * rr) for (lr, li), (rr, ri) in zip(left, right)
    )


def conj_times(left, right):
    return tuple(
        (lr * rr + li * ri, lr * ri - li * rr) for (lr, li), (rr, ri) in zip(left, right)
    )


def transform(table, signal):
    return jnp.dot(table, signal, preferred_element_type=F32)


def phases_near(ref, chunk, tap_count):
    start = PAD + chunk * CHUNK * PHASES
    return {
        offset: ref[pl.ds(start + offset, CHUNK, stride=PHASES), :]
        for offset in range(1 - tap_count, PHASES)
    }


def short_conv(near, taps):
    results = []
    for r in range(PHASES):
        summed = taps[0] * near[r]
        for at in range(1, len(taps)):
            summed = summed + taps[at] * near[r - at]
        results.append(summed)
    return results


def add_rows(total, terms):
    for term in terms:
        folded = jnp.sum(term.reshape(CHUNK // 8, 8, LANES), axis=0)
        total = folded if total is None else total + folded
    return total


def clear_ends(ref):
    ref[:PAD, :] = jnp.zeros((PAD, LANES), F32)
    ref[ref.shape[0] - PAD :, :] = jnp.zeros((PAD, LANES), F32)


def stage_kernel(count, *refs):
    sources, targets, sems = refs[:count], refs[count + 1 : 2 * count + 1], refs[2 * count + 1]
    copies = [
        pltpu.make_async_copy(source, target, sems.at[at])
        for at, (source, target) in enumerate(zip(sources, targets))
    ]
    for copy in copies:
        copy.start()
    for copy in copies:
        copy.wait()


def stage(arrays, after):
    count = len(arrays)
    return pl.pallas_call(
        functools.partial(stage_kernel, count),
        in_specs=[pl.BlockSpec(memory_space=pl.ANY)] * (count + 1),
        out_specs=in_vmem(count),
        out_shape=[jax.ShapeDtypeStruct(array.shape, array.dtype) for array in arrays],
        scratch_shapes=[pltpu.SemaphoreType.DMA((count,))],
        compiler_params=pltpu.CompilerParams(vmem_limit_bytes=8 * MIB),
        cost_estimate=pl.CostEstimate(flops=0, bytes_accessed=8 * MIB, transcendentals=0),
        name="stage_tables",
    )(*arrays, after)


def extra_rows(short_weights):
    sums = PIECES * short_weights.shape[0] * short_weights.shape[1]
    return sums, -(-(sums + 6 * RIM) // TILE) * TILE


def channel_kernel(tokens, heard, told, grad_scale, *refs):
    peers = len(heard)
    arrived = refs[:peers]
    weights, forward, backward = refs[peers : peers + 3]
    out = refs[peers + 3 : 2 * peers + 3]
    (
        query,
        key,
        value,
        cot,
        conv,
        conv_grad,
        filter_grad,
        taps,
        key_short,
        value_short,
        signals,
        spectra,
        products,
        extra,
    ) = refs[2 * peers + 3 :]
    size = peers * tokens // PHASES
    tap_count = weights.shape[1]
    me = lax.axis_index("ctx")
    own = lanes_of(me)
    for ref in (query, key, value, cot, conv, conv_grad):
        clear_ends(ref)
    for ref in (key_short, value_short):
        ref[:, size:, :] = jnp.zeros((PHASES, PAD, LANES), F32)
    for step, source in zip(heard, arrived):
        start = (me ^ step) * tokens
        inner = pl.ds(pl.multiple_of(PAD + start, PAD), tokens)
        for at, ref in enumerate((query, key, value, cot)):
            ref[inner, :] = source[at * tokens : (at + 1) * tokens, :].astype(F32)
        taps[pl.ds(pl.multiple_of(start, PAD), tokens), :] = source[4 * tokens :, :].astype(F32)
    chunks = range(size // CHUNK)
    taps_of = [
        [weights[array, tap : tap + 1, own] for tap in range(tap_count)] for array in range(3)
    ]

    def rows_of(chunk):
        return slice(chunk * CHUNK, (chunk + 1) * CHUNK)

    def spectrum(at, real, imag):
        lanes = slice(at * LANES, (at + 1) * LANES)
        return forward_mix(
            [(spectra[r, real, lanes], spectra[r, imag, lanes]) for r in range(PHASES)]
        )

    def keep(at, real, imag, mixed):
        lanes = slice(at * LANES, (at + 1) * LANES)
        for r, pair in enumerate(inverse_mix(mixed)):
            for rows, part in zip((real, imag), pair):
                products[r, rows, lanes] = part

    for chunk in chunks:
        rows = rows_of(chunk)
        key_now = short_conv(phases_near(key, chunk, tap_count), taps_of[1])
        value_now = short_conv(phases_near(value, chunk, tap_count), taps_of[2])
        for r in range(PHASES):
            key_short[r, rows, :] = key_now[r]
            value_short[r, rows, :] = value_now[r]
            signals[r, rows, :LANES] = (key_now[r] * value_now[r]).astype(BF16)
            filt = taps[pl.ds(chunk * CHUNK * PHASES + r, CHUNK, stride=PHASES), :]
            signals[r, rows, LANES : 2 * LANES] = filt.astype(BF16)
    for r in range(PHASES):
        spectra[r, :, : 2 * LANES] = transform(forward[r], signals[r, :, : 2 * LANES])
    for chunk in chunks:
        rows = rows_of(chunk)
        query_now = short_conv(phases_near(query, chunk, tap_count), taps_of[0])
        cot_now = phases_near(cot, chunk, 1)
        for r in range(PHASES):
            signals[r, rows, 2 * LANES :] = (cot_now[r] * query_now[r]).astype(BF16)
    for r in range(PHASES):
        spectra[r, :, 2 * LANES :] = transform(forward[r], signals[r, :, 2 * LANES :])
    for step in range(size // ROWS):
        real = slice(step * ROWS, (step + 1) * ROWS)
        imag = slice(size + step * ROWS, size + (step + 1) * ROWS)
        prod, filt = spectrum(0, real, imag), spectrum(1, real, imag)
        for at, mixed in enumerate((prod, filt)):
            lanes = slice(at * LANES, (at + 1) * LANES)
            for q, pair in enumerate(mixed):
                spectra[q, real, lanes], spectra[q, imag, lanes] = pair
        keep(0, real, imag, times(prod, filt))
    for r in range(PHASES):
        result = transform(backward[r], products[r, :, :LANES].astype(BF16))
        conv[pl.ds(PAD + r, size, stride=PHASES), :] = result.astype(BF16).astype(F32)
    for step in range(size // ROWS):
        real = slice(step * ROWS, (step + 1) * ROWS)
        imag = slice(size + step * ROWS, size + (step + 1) * ROWS)
        grad = spectrum(2, real, imag)
        for at in range(2):
            lanes = slice(at * LANES, (at + 1) * LANES)
            known = [(spectra[q, real, lanes], spectra[q, imag, lanes]) for q in range(PHASES)]
            keep(2 - at, real, imag, conj_times(known, grad))
    for r in range(PHASES):
        result = transform(backward[r], products[r, :, LANES:].astype(BF16))
        conv_grad[pl.ds(PAD + r, size, stride=PHASES), :] = (
            result[:, :LANES].astype(BF16).astype(F32)
        )
        filter_grad[pl.ds(r, size, stride=PHASES), :] = result[:, LANES:] * grad_scale

    totals = [[None] * tap_count for _ in range(3)]

    def add_sums(array, signal, chunk, pre):
        near = phases_near(signal, chunk, tap_count)
        for tap in range(tap_count):
            totals[array][tap] = add_rows(
                totals[array][tap], [pre[r] * near[r - tap] for r in range(PHASES)]
            )

    for chunk in chunks:
        cot_now, conv_now = phases_near(cot, chunk, 1), phases_near(conv, chunk, 1)
        add_sums(0, query, chunk, [cot_now[r] * conv_now[r] for r in range(PHASES)])
    for chunk in chunks:
        rows = rows_of(chunk)
        grad_now = phases_near(conv_grad, chunk, 1)
        add_sums(1, key, chunk, [grad_now[r] * value_short[r, rows, :] for r in range(PHASES)])
        add_sums(2, value, chunk, [grad_now[r] * key_short[r, rows, :] for r in range(PHASES)])
    sums = [jnp.sum(total, axis=0, keepdims=True) for row in totals for total in row]
    rest = jnp.concatenate(sums, axis=0) * grad_scale
    extra[...] = jnp.zeros_like(extra)
    for piece in range(PIECES):
        rounded = rest.astype(BF16).astype(F32)
        extra[piece * len(sums) : (piece + 1) * len(sums), :] = rounded
        rest = rest - rounded
    for step, target in zip(told, out):
        start = (me ^ step) * tokens
        inner = pl.ds(pl.multiple_of(PAD + start, PAD), tokens)
        target[:tokens, :] = conv[inner, :].astype(BF16)
        target[tokens : 2 * tokens, :] = conv_grad[inner, :].astype(BF16)
        target[2 * tokens : 3 * tokens, :] = filter_grad[
            pl.ds(pl.multiple_of(start, PAD), tokens), :
        ].astype(BF16)
        before = pl.ds(pl.multiple_of(start, PAD), PAD)
        after = pl.ds(pl.multiple_of(PAD + start + tokens, PAD), PAD)
        at = PIECES * len(sums)
        for ref in (query, key, value):
            extra[at : at + RIM, :] = ref[before, :][PAD - RIM :]
            at += RIM
        row = pl.ds(pl.multiple_of((start + tokens) // PHASES, PAD), PAD)
        extra[at : at + RIM, :] = (cot[after, :] * conv[after, :])[:RIM]
        for short in (value_short, key_short):
            at += RIM
            shorts = jnp.concatenate([short[r, row, :][:1] for r in range(RIM)], axis=0)
            extra[at : at + RIM, :] = conv_grad[after, :][:RIM] * shorts
        target[3 * tokens :, :] = extra[...].astype(BF16)


def channel_step(arrived, heard, told, short_weights, tables, tokens):
    peers = len(arrived)
    seq_len = peers * tokens
    size = seq_len // PHASES
    extra = extra_rows(short_weights)[1]
    padded = pltpu.VMEM((seq_len + 2 * PAD, LANES), F32)
    plain = pltpu.VMEM((seq_len, LANES), F32)
    phases = pltpu.VMEM((PHASES, size + PAD, LANES), F32)
    return pl.pallas_call(
        functools.partial(channel_kernel, tokens, heard, told, 1.0 / math.sqrt(seq_len)),
        in_specs=in_vmem(peers + 3),
        out_specs=in_vmem(peers),
        out_shape=[jax.ShapeDtypeStruct((3 * tokens + extra, LANES), BF16)] * peers,
        scratch_shapes=[
            *[padded] * 6,
            plain,
            plain,
            phases,
            phases,
            pltpu.VMEM((PHASES, size, 3 * LANES), BF16),
            pltpu.VMEM((PHASES, 2 * size, 3 * LANES), F32),
            pltpu.VMEM((PHASES, 2 * size, 3 * LANES), F32),
            pltpu.VMEM((extra, LANES), F32),
        ],
        compiler_params=pltpu.CompilerParams(vmem_limit_bytes=VMEM_LIMIT),
        name="channel_operator",
    )(*arrived, short_weights, *tables)


def token_kernel(steps, sum_rows, carried, *refs):
    count_in = len(steps)
    arrived = refs[:count_in]
    query, key, value, cot, weights = refs[count_in : count_in + 5]
    results = refs[count_in + 5 + carried : count_in + 11 + carried]
    (gated, query_grad, key_grad, value_grad, filter_grad, short_grad, longer, pre, sems) = refs[
        count_in + 11 + carried :
    ]
    copies = []
    tokens = query.shape[0]
    tap_count = weights.shape[1]
    count = sum_rows // PIECES
    me = lax.axis_index("ctx")
    for slot, (step, source) in enumerate(zip(steps, arrived)):
        lanes = lanes_of(me ^ step)
        extra = source[3 * tokens :, :].astype(F32)

        def rim(at):
            return extra[sum_rows + at * RIM : sum_rows + (at + 1) * RIM]

        def short(array, signal):
            longer[array, PAD - RIM : PAD, :] = rim(array)
            longer[array, PAD :, :] = signal[:, lanes].astype(F32)
            summed = weights[array, 0:1, lanes] * longer[array, PAD:, :]
            for tap in range(1, tap_count):
                summed = (
                    summed
                    + weights[array, tap : tap + 1, lanes]
                    * longer[array, PAD - tap : PAD - tap + tokens, :]
                )
            return summed

        def taps_back(array, grad, target):
            pre[array, :tokens, :] = grad
            pre[array, tokens : tokens + RIM, :] = rim(3 + array)
            summed = weights[array, 0:1, lanes] * grad
            for tap in range(1, tap_count):
                summed = (
                    summed
                    + weights[array, tap : tap + 1, lanes] * pre[array, tap : tap + tokens, :]
                )
            target[slot] = summed.astype(BF16)

        conv = source[:tokens, :].astype(F32)
        conv_grad = source[tokens : 2 * tokens, :].astype(F32)
        gated[slot] = (short(0, query) * conv).astype(BF16)
        taps_back(0, cot[:, lanes].astype(F32) * conv, query_grad)
        taps_back(1, conv_grad * short(2, value), key_grad)
        taps_back(2, conv_grad * short(1, key), value_grad)
        filter_grad[slot] = source[2 * tokens : 3 * tokens, :].astype(F32)
        whole = extra[:count]
        for piece in range(1, PIECES):
            whole = whole + extra[piece * count : (piece + 1) * count]
        for row in range(count):
            which, tap = divmod(row, tap_count)
            short_grad[slot, which, tap : tap + 1, :] = whole[row : row + 1]
        held = (gated, query_grad, key_grad, value_grad, filter_grad, short_grad)
        for at, (source, target) in enumerate(zip(held, results)):
            place = target.at[:, :, lanes] if at == 5 else target.at[:, lanes]
            copies.append(pltpu.make_async_copy(source.at[slot], place, sems.at[slot, at]))
            copies[-1].start()
    for copy in copies:
        copy.wait()


def token_step(arrived, steps, query, key, value, cot, short_weights, begun=()):
    tokens, width = query.shape
    count = len(arrived)
    wide = jax.ShapeDtypeStruct((tokens, width), BF16)
    anywhere = pl.BlockSpec(memory_space=pl.ANY)
    return pl.pallas_call(
        functools.partial(token_kernel, steps, extra_rows(short_weights)[0], len(begun)),
        in_specs=in_vmem(count + 5) + [anywhere] * len(begun),
        out_specs=[anywhere] * 6,
        out_shape=[wide] * 4
        + [
            jax.ShapeDtypeStruct((tokens, width), F32),
            jax.ShapeDtypeStruct(short_weights.shape, F32),
        ],
        scratch_shapes=[
            *[pltpu.VMEM((count, tokens, LANES), BF16)] * 4,
            pltpu.VMEM((count, tokens, LANES), F32),
            pltpu.VMEM((count, *short_weights.shape[:2], LANES), F32),
            pltpu.VMEM((3, tokens + PAD, LANES), F32),
            pltpu.VMEM((3, tokens + PAD, LANES), F32),
            pltpu.SemaphoreType.DMA((count, 6)),
        ],
        input_output_aliases={count + 5 + at: at for at in range(len(begun))},
        compiler_params=pltpu.CompilerParams(vmem_limit_bytes=VMEM_LIMIT),
        cost_estimate=pl.CostEstimate(flops=0, bytes_accessed=4 * MIB, transcendentals=0),
        name="token_outputs",
    )(*arrived, query, key, value, cot, short_weights, *begun)


def channel_shards(query_proj, key_proj, value_proj, cotangent, filter_taps, short_weights):
    peers = lax.axis_size("ctx")
    tokens = query_proj.shape[0]
    tables = [jnp.asarray(table) for table in dft_tables(peers * tokens)]
    going, coming = partners(peers, False), partners(peers, True)
    sent = pack((query_proj, key_proj, value_proj, cotangent, filter_taps), going)
    arrived = exchange(sent, going)
    staged = stage((sent[0], short_weights, *tables), arrived[1])
    arrived[0] = staged[0]
    results = channel_step(arrived, going, coming, staged[1], staged[2:], tokens)
    back = exchange(results, coming)
    local = (query_proj, key_proj, value_proj, cotangent, short_weights)
    ends = [at for at in (4, 6) if at < peers] + [peers]
    begun, start = (), 0
    for end in ends:
        begun = token_step(back[start:end], coming[start:end], *local, begun)
        start = end
    return tuple(begun)


def from_behind(array, axis, by):
    peers = lax.axis_size(axis)
    pairs = [(i, i + by) for i in range(peers) if 0 <= i + by < peers]
    return lax.ppermute(array, axis, pairs)


def contract(form, left, right):
    return jnp.einsum(
        form, left, right, precision=lax.Precision.HIGHEST, preferred_element_type=jnp.float32
    )


def table_pair(rows, cols, period):
    row_ids = lax.broadcasted_iota(jnp.int32, (rows, cols), 0)
    col_ids = lax.broadcasted_iota(jnp.int32, (rows, cols), 1)
    angle = 2.0 * math.pi / period * (row_ids * col_ids % period).astype(jnp.float32)
    return (jnp.cos(angle), jnp.sin(angle))


def make_plan(seq_len):
    small_len = int(math.isqrt(2 * seq_len))
    while seq_len % small_len:
        small_len -= 1
    large_len = 2 * seq_len // small_len
    large_cos, large_sin = table_pair(large_len // 2, large_len, large_len)
    small_cos, small_sin = table_pair(small_len, small_len, small_len)
    twist_cos, twist_sin = table_pair(large_len, small_len, small_len * large_len)
    fwd_large = jnp.stack([large_cos, -large_sin], axis=1)
    fwd_small = jnp.stack([jnp.stack([small_cos, -small_sin]), jnp.stack([small_sin, small_cos])])
    inv_small = jnp.stack([jnp.stack([small_cos, small_sin]), jnp.stack([-small_sin, small_cos])])
    inv_large = jnp.stack([large_cos, -large_sin])
    return (small_len, large_len, fwd_large, fwd_small, inv_small, inv_large, twist_cos, twist_sin)


def forward_spec(signal, dft_plan):
    small_len, large_len, fwd_large, fwd_small, inv_small, inv_large, twist_cos, twist_sin = (
        dft_plan
    )
    cube = signal.reshape(signal.shape[0], large_len // 2, small_len)
    section_one = contract("cba,bpk->cpka", cube, fwd_large)
    real_one = section_one[:, 0]
    imag_one = section_one[:, 1]
    section_two = jnp.stack(
        [real_one * twist_cos + imag_one * twist_sin, imag_one * twist_cos - real_one * twist_sin],
        axis=1,
    )
    return contract("cpka,pqaj->cqkj", section_two, fwd_small)


def inverse_half(spec, dft_plan):
    small_len, large_len, fwd_large, fwd_small, inv_small, inv_large, twist_cos, twist_sin = (
        dft_plan
    )
    section_one = contract("cqkj,qpja->cpka", spec, inv_small)
    real_one = section_one[:, 0]
    imag_one = section_one[:, 1]
    section_two = jnp.stack(
        [real_one * twist_cos - imag_one * twist_sin, imag_one * twist_cos + real_one * twist_sin],
        axis=1,
    )
    signal = contract("cpka,pbk->cba", section_two, inv_large)
    return signal.reshape(signal.shape[0], -1) / float(small_len * large_len)


def complex_mul(left, right):
    left_real, left_imag = (left[:, 0], left[:, 1])
    right_real, right_imag = (right[:, 0], right[:, 1])
    return jnp.stack(
        [
            left_real * right_real - left_imag * right_imag,
            left_real * right_imag + left_imag * right_real,
        ],
        axis=1,
    )


def conj_mul(left, right):
    left_real, left_imag = (left[:, 0], left[:, 1])
    right_real, right_imag = (right[:, 0], right[:, 1])
    return jnp.stack(
        [
            left_real * right_real + left_imag * right_imag,
            left_real * right_imag - left_imag * right_real,
        ],
        axis=1,
    )


def conv_forward(prod_chan, filter_spec, dft_plan):
    prod_spec = forward_spec(prod_chan.astype(jnp.float32), dft_plan)
    conv_chan = inverse_half(complex_mul(prod_spec, filter_spec), dft_plan).astype(jnp.bfloat16)
    return (conv_chan, prod_spec)


def conv_backward(grad_chan, filter_spec, prod_spec, dft_plan, grad_scale):
    grad_spec = forward_spec(grad_chan.astype(jnp.float32), dft_plan)
    dconv_chan = inverse_half(conj_mul(filter_spec, grad_spec), dft_plan).astype(jnp.bfloat16)
    dfilter_chan = inverse_half(conj_mul(prod_spec, grad_spec), dft_plan) * grad_scale
    return (dconv_chan, dfilter_chan)


def receive_filter(filter_taps, dft_plan):
    filter_chan = lax.all_to_all(filter_taps.T, "ctx", split_axis=0, concat_axis=1, tiled=True)
    return forward_spec(filter_chan, dft_plan)


def return_filter(dfilter_chan):
    return (
        lax.all_to_all(
            dfilter_chan.astype(jnp.bfloat16), "ctx", split_axis=1, concat_axis=0, tiled=True
        )
        .astype(dfilter_chan.dtype)
        .T
    )


def causal_taps(extended, weights, length, axis):
    rim_rows = len(weights) - 1
    summed = weights[0] * lax.slice_in_dim(extended, rim_rows, rim_rows + length, axis=axis)
    for offset in range(1, len(weights)):
        summed = summed + weights[offset] * lax.slice_in_dim(
            extended, rim_rows - offset, rim_rows - offset + length, axis=axis
        )
    return summed


def reverse_taps(extended, weights, length, axis):
    summed = weights[0] * lax.slice_in_dim(extended, 0, length, axis=axis)
    for offset in range(1, len(weights)):
        summed = summed + weights[offset] * lax.slice_in_dim(
            extended, offset, offset + length, axis=axis
        )
    return summed


def tap_grads(grad_in, extended, tap_count, length, axis):
    rim_rows = tap_count - 1
    rows = [
        jnp.sum(
            grad_in
            * lax.slice_in_dim(extended, rim_rows - offset, rim_rows - offset + length, axis=axis),
            axis=axis,
        )
        for offset in range(tap_count)
    ]
    return jnp.stack(rows, axis=1)


def spread_shards(query_proj, key_proj, value_proj, cotangent, filter_taps, short_weights):
    tokens = query_proj.shape[0]
    tap_count = short_weights.shape[1]
    rim_rows = tap_count - 1
    seq_len = tokens * lax.axis_size("ctx")
    grad_scale = 1.0 / math.sqrt(seq_len)
    dft_plan = make_plan(seq_len)
    stacked = jnp.stack([query_proj, key_proj, value_proj])
    prev_rim = from_behind(stacked[:, tokens - rim_rows :], "ctx", 1)
    extended = jnp.concatenate([prev_rim, stacked], axis=1).astype(jnp.float32)
    weights = [short_weights[:, offset, None, :] for offset in range(tap_count)]
    short_out = causal_taps(extended, weights, tokens, 1)
    product = (short_out[1] * short_out[2]).astype(jnp.bfloat16)
    cot_wide = cotangent.astype(jnp.float32)
    gate_grad = (cot_wide * short_out[0]).astype(jnp.bfloat16)
    filter_spec = receive_filter(filter_taps, dft_plan)
    prod_chan = lax.all_to_all(product.T, "ctx", split_axis=0, concat_axis=1, tiled=True)
    conv_chan, prod_spec = conv_forward(prod_chan, filter_spec, dft_plan)
    conv_tok = lax.all_to_all(conv_chan, "ctx", split_axis=1, concat_axis=0, tiled=True)
    grad_chan = lax.all_to_all(gate_grad.T, "ctx", split_axis=0, concat_axis=1, tiled=True)
    dconv_chan, dfilter_chan = conv_backward(
        grad_chan, filter_spec, prod_spec, dft_plan, grad_scale
    )
    dconv_tok = lax.all_to_all(dconv_chan, "ctx", split_axis=1, concat_axis=0, tiled=True)
    filter_grad = return_filter(dfilter_chan)
    conv_wide = conv_tok.T.astype(jnp.float32)
    dconv_wide = dconv_tok.T.astype(jnp.float32)
    gated = (short_out[0] * conv_wide).astype(jnp.bfloat16)
    token_grads = jnp.stack(
        [cot_wide * conv_wide, dconv_wide * short_out[2], dconv_wide * short_out[1]]
    )
    next_rim = from_behind(token_grads[:, :rim_rows], "ctx", -1)
    grad_ext = jnp.concatenate([token_grads, next_rim], axis=1)
    inputs_grad = reverse_taps(grad_ext, weights, tokens, 1).astype(jnp.bfloat16)
    weight_part = tap_grads(token_grads, extended, tap_count, tokens, 1)
    short_grad = lax.psum(weight_part, "ctx") * grad_scale
    results = (gated, inputs_grad[0], inputs_grad[1], inputs_grad[2])
    return (results[0], results[1], results[2], results[3], filter_grad, short_grad)


def fits(query_proj, short_weights):
    peers = lax.axis_size("ctx")
    tokens, width = query_proj.shape
    tap_count = short_weights.shape[1]
    return (
        width == peers * LANES
        and peers.bit_count() == 1
        and tokens % (PHASES * CHUNK) == 0
        and tap_count == RIM + 1
        and peers * tokens <= 2048
    )


def shards(*arrays):
    return channel_shards(*arrays) if fits(arrays[0], arrays[5]) else spread_shards(*arrays)


def solution(mesh):
    placed = (
        P("ctx", "tp"),
        P("ctx", "tp"),
        P("ctx", "tp"),
        P("ctx", "tp"),
        P("ctx", "tp"),
        P(None, None, "tp"),
    )
    return jax.shard_map(
        shards,
        mesh=mesh,
        in_specs=placed,
        out_specs=(
            P("ctx", "tp"),
            P("ctx", "tp"),
            P("ctx", "tp"),
            P("ctx", "tp"),
            P("ctx", "tp"),
            P(None, None, "tp"),
        ),
        check_vma=False,
    )
```

```python
import functools
import math

import jax
import jax.numpy as jnp
import numpy as np
from jax import lax
from jax.experimental import pallas as pl
from jax.experimental.pallas import tpu as pltpu
from jax.sharding import PartitionSpec as P

F32 = jnp.float32
BF16 = jnp.bfloat16
LANES = 128
PHASES = 4
TILE = 16
PAD = 8
CHUNK = 32
ROWS = 8
RIM = 2
PIECES = 2
MIB = 1024 * 1024
VMEM_LIMIT = 24 * MIB
PACK_VMEM = 53862 * 1024


def partners(peers, diagonal_first):
    def rank(step):
        links, other_core = (step >> 1).bit_count(), step & 1
        if links == 0:
            return (1 if diagonal_first else 5, 0)
        if links == 1:
            return (4 if other_core else 3, -step)
        return (2 * other_core if diagonal_first else 3.5, other_core)

    return [0] + sorted(range(1, peers), key=rank)


def exchange(blocks, steps):
    peers = len(blocks)
    got = [blocks[0]]
    for step, block in list(zip(steps, blocks))[1:]:
        got.append(lax.ppermute(block, "ctx", [(i, i ^ step) for i in range(peers)]))
    return got


def in_vmem(count):
    return [pl.BlockSpec(memory_space=pltpu.VMEM)] * count


def lanes_of(place):
    return pl.ds(pl.multiple_of(place * LANES, LANES), LANES)


def pack_kernel(count, steps, *refs):
    sources, packed = refs[:count], refs[count : count + len(steps)]
    held, sems = refs[count + len(steps) : -1], refs[-1]
    tokens = sources[0].shape[0]
    me = lax.axis_index("ctx")
    arriving = [
        pltpu.make_async_copy(source, target, sems.at[at])
        for at, (source, target) in enumerate(zip(sources, held))
    ]
    for copy in arriving:
        copy.start()
    for at, source in enumerate(held):
        arriving[at].wait()
        rows = slice(at * tokens, (at + 1) * tokens)
        for step, target in zip(steps, packed):
            target[rows, :] = source[:, lanes_of(me ^ step)].astype(BF16)


def pack(arrays, steps):
    tokens = arrays[0].shape[0]
    count = len(arrays)
    return pl.pallas_call(
        functools.partial(pack_kernel, count, steps),
        in_specs=[pl.BlockSpec(memory_space=pl.ANY)] * count,
        out_specs=in_vmem(len(steps)),
        out_shape=[jax.ShapeDtypeStruct((count * tokens, LANES), BF16)] * len(steps),
        scratch_shapes=[
            *[pltpu.VMEM(array.shape, array.dtype) for array in arrays],
            pltpu.SemaphoreType.DMA((count,)),
        ],
        compiler_params=pltpu.CompilerParams(vmem_limit_bytes=PACK_VMEM),
        cost_estimate=pl.CostEstimate(flops=0, bytes_accessed=8 * MIB, transcendentals=0),
        name="pack_inputs",
    )(*arrays)


@functools.lru_cache(maxsize=None)
def dft_tables(seq_len):
    size = seq_len // PHASES
    k = np.arange(size, dtype=np.int64)[:, None]
    m = np.arange(size, dtype=np.int64)[None, :]
    forward = []
    for phase in range(PHASES):
        turns = ((4 * k + 1) * (PHASES * m + phase)) % (4 * seq_len)
        angle = 2.0 * np.pi / (4 * seq_len) * turns
        forward.append(np.concatenate([np.cos(angle), -np.sin(angle)], axis=0))
    forward = np.stack(forward)
    backward = np.swapaxes(forward, 1, 2) / seq_len

    return forward.astype(BF16), backward.astype(BF16)


def forward_mix(parts):
    (r0, i0), (r1, i1), (r2, i2), (r3, i3) = parts
    ar, ai, br, bi = r0 + r2, i0 + i2, r0 - r2, i0 - i2
    cr, ci, dr, di = r1 + r3, i1 + i3, r1 - r3, i1 - i3
    return ((ar + cr, ai + ci), (br + di, bi - dr), (ar - cr, ai - ci), (br - di, bi + dr))


def inverse_mix(parts):
    (r0, i0), (r1, i1), (r2, i2), (r3, i3) = parts
    ar, ai, br, bi = r0 + r2, i0 + i2, r0 - r2, i0 - i2
    cr, ci, dr, di = r1 + r3, i1 + i3, r1 - r3, i1 - i3
    return ((ar + cr, ai + ci), (br - di, bi + dr), (ar - cr, ai - ci), (br + di, bi - dr))


def times(left, right):
    return tuple(
        (lr * rr - li * ri, lr * ri + li * rr) for (lr, li), (rr, ri) in zip(left, right)
    )


def conj_times(left, right):
    return tuple(
        (lr * rr + li * ri, lr * ri - li * rr) for (lr, li), (rr, ri) in zip(left, right)
    )


def transform(table, signal):
    return jnp.dot(table, signal, preferred_element_type=F32)


def phases_near(ref, chunk, tap_count):
    start = PAD + chunk * CHUNK * PHASES
    return {
        offset: ref[pl.ds(start + offset, CHUNK, stride=PHASES), :]
        for offset in range(1 - tap_count, PHASES)
    }


def short_conv(near, taps):
    results = []
    for r in range(PHASES):
        summed = taps[0] * near[r]
        for at in range(1, len(taps)):
            summed = summed + taps[at] * near[r - at]
        results.append(summed)
    return results


def add_rows(total, terms):
    for term in terms:
        folded = jnp.sum(term.reshape(CHUNK // 8, 8, LANES), axis=0)
        total = folded if total is None else total + folded
    return total


def clear_ends(ref):
    ref[:PAD, :] = jnp.zeros((PAD, LANES), F32)
    ref[ref.shape[0] - PAD :, :] = jnp.zeros((PAD, LANES), F32)


def stage_kernel(count, *refs):
    sources, targets, sems = refs[:count], refs[count + 1 : 2 * count + 1], refs[2 * count + 1]
    copies = [
        pltpu.make_async_copy(source, target, sems.at[at])
        for at, (source, target) in enumerate(zip(sources, targets))
    ]
    for copy in copies:
        copy.start()
    for copy in copies:
        copy.wait()


def stage(arrays, after):
    count = len(arrays)
    return pl.pallas_call(
        functools.partial(stage_kernel, count),
        in_specs=[pl.BlockSpec(memory_space=pl.ANY)] * (count + 1),
        out_specs=in_vmem(count),
        out_shape=[jax.ShapeDtypeStruct(array.shape, array.dtype) for array in arrays],
        scratch_shapes=[pltpu.SemaphoreType.DMA((count,))],
        compiler_params=pltpu.CompilerParams(vmem_limit_bytes=8 * MIB),
        cost_estimate=pl.CostEstimate(flops=0, bytes_accessed=8 * MIB, transcendentals=0),
        name="stage_tables",
    )(*arrays, after)


def extra_rows(short_weights):
    sums = PIECES * short_weights.shape[0] * short_weights.shape[1]
    return sums, -(-(sums + 6 * RIM) // TILE) * TILE


def channel_kernel(tokens, heard, told, grad_scale, *refs):
    peers = len(heard)
    arrived = refs[:peers]
    weights, forward, backward = refs[peers : peers + 3]
    out = refs[peers + 3 : 2 * peers + 3]
    (
        query,
        key,
        value,
        cot,
        conv,
        conv_grad,
        filter_grad,
        taps,
        key_short,
        value_short,
        signals,
        spectra,
        products,
        extra,
    ) = refs[2 * peers + 3 :]
    size = peers * tokens // PHASES
    tap_count = weights.shape[1]
    me = lax.axis_index("ctx")
    own = lanes_of(me)
    for ref in (query, key, value, cot, conv, conv_grad):
        clear_ends(ref)
    for ref in (key_short, value_short):
        ref[:, size:, :] = jnp.zeros((PHASES, PAD, LANES), F32)
    for step, source in zip(heard, arrived):
        start = (me ^ step) * tokens
        inner = pl.ds(pl.multiple_of(PAD + start, PAD), tokens)
        for at, ref in enumerate((query, key, value, cot)):
            ref[inner, :] = source[at * tokens : (at + 1) * tokens, :].astype(F32)
        taps[pl.ds(pl.multiple_of(start, PAD), tokens), :] = source[4 * tokens :, :].astype(F32)
    chunks = range(size // CHUNK)
    taps_of = [
        [weights[array, tap : tap + 1, own] for tap in range(tap_count)] for array in range(3)
    ]

    def rows_of(chunk):
        return slice(chunk * CHUNK, (chunk + 1) * CHUNK)

    def spectrum(at, real, imag):
        lanes = slice(at * LANES, (at + 1) * LANES)
        return forward_mix(
            [(spectra[r, real, lanes], spectra[r, imag, lanes]) for r in range(PHASES)]
        )

    def keep(at, real, imag, mixed):
        lanes = slice(at * LANES, (at + 1) * LANES)
        for r, pair in enumerate(inverse_mix(mixed)):
            for rows, part in zip((real, imag), pair):
                products[r, rows, lanes] = part

    for chunk in chunks:
        rows = rows_of(chunk)
        key_now = short_conv(phases_near(key, chunk, tap_count), taps_of[1])
        value_now = short_conv(phases_near(value, chunk, tap_count), taps_of[2])
        for r in range(PHASES):
            key_short[r, rows, :] = key_now[r]
            value_short[r, rows, :] = value_now[r]
            signals[r, rows, :LANES] = (key_now[r] * value_now[r]).astype(BF16)
            filt = taps[pl.ds(chunk * CHUNK * PHASES + r, CHUNK, stride=PHASES), :]
            signals[r, rows, LANES : 2 * LANES] = filt.astype(BF16)
    for r in range(PHASES):
        spectra[r, :, : 2 * LANES] = transform(forward[r], signals[r, :, : 2 * LANES])
    for chunk in chunks:
        rows = rows_of(chunk)
        query_now = short_conv(phases_near(query, chunk, tap_count), taps_of[0])
        cot_now = phases_near(cot, chunk, 1)
        for r in range(PHASES):
            signals[r, rows, 2 * LANES :] = (cot_now[r] * query_now[r]).astype(BF16)
    for r in range(PHASES):
        spectra[r, :, 2 * LANES :] = transform(forward[r], signals[r, :, 2 * LANES :])
    for step in range(size // ROWS):
        real = slice(step * ROWS, (step + 1) * ROWS)
        imag = slice(size + step * ROWS, size + (step + 1) * ROWS)
        prod, filt = spectrum(0, real, imag), spectrum(1, real, imag)
        keep(0, real, imag, times(prod, filt))
        grad = spectrum(2, real, imag)
        keep(1, real, imag, conj_times(filt, grad))
        keep(2, real, imag, conj_times(prod, grad))
    for r in range(PHASES):
        result = transform(backward[r], products[r].astype(BF16))
        for at, ref in enumerate((conv, conv_grad)):
            ref[pl.ds(PAD + r, size, stride=PHASES), :] = (
                result[:, at * LANES : (at + 1) * LANES].astype(BF16).astype(F32)
            )
        filter_grad[pl.ds(r, size, stride=PHASES), :] = result[:, 2 * LANES :] * grad_scale

    totals = [[None] * tap_count for _ in range(3)]

    def add_sums(array, signal, chunk, pre):
        near = phases_near(signal, chunk, tap_count)
        for tap in range(tap_count):
            totals[array][tap] = add_rows(
                totals[array][tap], [pre[r] * near[r - tap] for r in range(PHASES)]
            )

    for chunk in chunks:
        cot_now, conv_now = phases_near(cot, chunk, 1), phases_near(conv, chunk, 1)
        add_sums(0, query, chunk, [cot_now[r] * conv_now[r] for r in range(PHASES)])
    for chunk in chunks:
        rows = rows_of(chunk)
        grad_now = phases_near(conv_grad, chunk, 1)
        add_sums(1, key, chunk, [grad_now[r] * value_short[r, rows, :] for r in range(PHASES)])
        add_sums(2, value, chunk, [grad_now[r] * key_short[r, rows, :] for r in range(PHASES)])
    sums = [jnp.sum(total, axis=0, keepdims=True) for row in totals for total in row]
    rest = jnp.concatenate(sums, axis=0) * grad_scale
    extra[...] = jnp.zeros_like(extra)
    for piece in range(PIECES):
        rounded = rest.astype(BF16).astype(F32)
        extra[piece * len(sums) : (piece + 1) * len(sums), :] = rounded
        rest = rest - rounded
    for step, target in zip(told, out):
        start = (me ^ step) * tokens
        inner = pl.ds(pl.multiple_of(PAD + start, PAD), tokens)
        target[:tokens, :] = conv[inner, :].astype(BF16)
        target[tokens : 2 * tokens, :] = conv_grad[inner, :].astype(BF16)
        target[2 * tokens : 3 * tokens, :] = filter_grad[
            pl.ds(pl.multiple_of(start, PAD), tokens), :
        ].astype(BF16)
        before = pl.ds(pl.multiple_of(start, PAD), PAD)
        after = pl.ds(pl.multiple_of(PAD + start + tokens, PAD), PAD)
        at = PIECES * len(sums)
        for ref in (query, key, value):
            extra[at : at + RIM, :] = ref[before, :][PAD - RIM :]
            at += RIM
        row = pl.ds(pl.multiple_of((start + tokens) // PHASES, PAD), PAD)
        extra[at : at + RIM, :] = (cot[after, :] * conv[after, :])[:RIM]
        for short in (value_short, key_short):
            at += RIM
            shorts = jnp.concatenate([short[r, row, :][:1] for r in range(RIM)], axis=0)
            extra[at : at + RIM, :] = conv_grad[after, :][:RIM] * shorts
        target[3 * tokens :, :] = extra[...].astype(BF16)


def channel_step(arrived, heard, told, short_weights, tables, tokens):
    peers = len(arrived)
    seq_len = peers * tokens
    size = seq_len // PHASES
    extra = extra_rows(short_weights)[1]
    padded = pltpu.VMEM((seq_len + 2 * PAD, LANES), F32)
    plain = pltpu.VMEM((seq_len, LANES), F32)
    phases = pltpu.VMEM((PHASES, size + PAD, LANES), F32)
    return pl.pallas_call(
        functools.partial(channel_kernel, tokens, heard, told, 1.0 / math.sqrt(seq_len)),
        in_specs=in_vmem(peers + 3),
        out_specs=in_vmem(peers),
        out_shape=[jax.ShapeDtypeStruct((3 * tokens + extra, LANES), BF16)] * peers,
        scratch_shapes=[
            *[padded] * 6,
            plain,
            plain,
            phases,
            phases,
            pltpu.VMEM((PHASES, size, 3 * LANES), BF16),
            pltpu.VMEM((PHASES, 2 * size, 3 * LANES), F32),
            pltpu.VMEM((PHASES, 2 * size, 3 * LANES), F32),
            pltpu.VMEM((extra, LANES), F32),
        ],
        compiler_params=pltpu.CompilerParams(vmem_limit_bytes=VMEM_LIMIT),
        name="channel_operator",
    )(*arrived, short_weights, *tables)


def token_kernel(steps, sum_rows, carried, *refs):
    count_in = len(steps)
    arrived = refs[:count_in]
    query, key, value, cot, weights = refs[count_in : count_in + 5]
    results = refs[count_in + 5 + carried : count_in + 11 + carried]
    (gated, query_grad, key_grad, value_grad, filter_grad, short_grad, longer, pre, sems) = refs[
        count_in + 11 + carried :
    ]
    copies = []
    tokens = query.shape[0]
    tap_count = weights.shape[1]
    count = sum_rows // PIECES
    me = lax.axis_index("ctx")
    for slot, (step, source) in enumerate(zip(steps, arrived)):
        lanes = lanes_of(me ^ step)
        extra = source[3 * tokens :, :].astype(F32)

        def rim(at):
            return extra[sum_rows + at * RIM : sum_rows + (at + 1) * RIM]

        def short(array, signal):
            longer[array, PAD - RIM : PAD, :] = rim(array)
            longer[array, PAD :, :] = signal[:, lanes].astype(F32)
            summed = weights[array, 0:1, lanes] * longer[array, PAD:, :]
            for tap in range(1, tap_count):
                summed = (
                    summed
                    + weights[array, tap : tap + 1, lanes]
                    * longer[array, PAD - tap : PAD - tap + tokens, :]
                )
            return summed

        def taps_back(array, grad, target):
            pre[array, :tokens, :] = grad
            pre[array, tokens : tokens + RIM, :] = rim(3 + array)
            summed = weights[array, 0:1, lanes] * grad
            for tap in range(1, tap_count):
                summed = (
                    summed
                    + weights[array, tap : tap + 1, lanes] * pre[array, tap : tap + tokens, :]
                )
            target[slot] = summed.astype(BF16)

        conv = source[:tokens, :].astype(F32)
        conv_grad = source[tokens : 2 * tokens, :].astype(F32)
        gated[slot] = (short(0, query) * conv).astype(BF16)
        taps_back(0, cot[:, lanes].astype(F32) * conv, query_grad)
        taps_back(1, conv_grad * short(2, value), key_grad)
        taps_back(2, conv_grad * short(1, key), value_grad)
        filter_grad[slot] = source[2 * tokens : 3 * tokens, :].astype(F32)
        whole = extra[:count]
        for piece in range(1, PIECES):
            whole = whole + extra[piece * count : (piece + 1) * count]
        for row in range(count):
            which, tap = divmod(row, tap_count)
            short_grad[slot, which, tap : tap + 1, :] = whole[row : row + 1]
        held = (gated, query_grad, key_grad, value_grad, filter_grad, short_grad)
        for at, (source, target) in enumerate(zip(held, results)):
            place = target.at[:, :, lanes] if at == 5 else target.at[:, lanes]
            copies.append(pltpu.make_async_copy(source.at[slot], place, sems.at[slot, at]))
            copies[-1].start()
    for copy in copies:
        copy.wait()


def token_step(arrived, steps, query, key, value, cot, short_weights, begun=()):
    tokens, width = query.shape
    count = len(arrived)
    wide = jax.ShapeDtypeStruct((tokens, width), BF16)
    anywhere = pl.BlockSpec(memory_space=pl.ANY)
    return pl.pallas_call(
        functools.partial(token_kernel, steps, extra_rows(short_weights)[0], len(begun)),
        in_specs=in_vmem(count + 5) + [anywhere] * len(begun),
        out_specs=[anywhere] * 6,
        out_shape=[wide] * 4
        + [
            jax.ShapeDtypeStruct((tokens, width), F32),
            jax.ShapeDtypeStruct(short_weights.shape, F32),
        ],
        scratch_shapes=[
            *[pltpu.VMEM((count, tokens, LANES), BF16)] * 4,
            pltpu.VMEM((count, tokens, LANES), F32),
            pltpu.VMEM((count, *short_weights.shape[:2], LANES), F32),
            pltpu.VMEM((3, tokens + PAD, LANES), F32),
            pltpu.VMEM((3, tokens + PAD, LANES), F32),
            pltpu.SemaphoreType.DMA((count, 6)),
        ],
        input_output_aliases={count + 5 + at: at for at in range(len(begun))},
        compiler_params=pltpu.CompilerParams(vmem_limit_bytes=VMEM_LIMIT),
        cost_estimate=pl.CostEstimate(flops=0, bytes_accessed=4 * MIB, transcendentals=0),
        name="token_outputs",
    )(*arrived, query, key, value, cot, short_weights, *begun)


def channel_shards(query_proj, key_proj, value_proj, cotangent, filter_taps, short_weights):
    peers = lax.axis_size("ctx")
    tokens = query_proj.shape[0]
    tables = [jnp.asarray(table) for table in dft_tables(peers * tokens)]
    going, coming = partners(peers, False), partners(peers, True)
    sent = pack((query_proj, key_proj, value_proj, cotangent, filter_taps), going)
    arrived = exchange(sent, going)
    staged = stage((sent[0], short_weights, *tables), arrived[1])
    arrived[0] = staged[0]
    results = channel_step(arrived, going, coming, staged[1], staged[2:], tokens)
    back = exchange(results, coming)
    local = (query_proj, key_proj, value_proj, cotangent, short_weights)
    ends = [at for at in (4, 6) if at < peers] + [peers]
    begun, start = (), 0
    for end in ends:
        begun = token_step(back[start:end], coming[start:end], *local, begun)
        start = end
    return tuple(begun)


def from_behind(array, axis, by):
    peers = lax.axis_size(axis)
    pairs = [(i, i + by) for i in range(peers) if 0 <= i + by < peers]
    return lax.ppermute(array, axis, pairs)


def contract(form, left, right):
    return jnp.einsum(
        form, left, right, precision=lax.Precision.HIGHEST, preferred_element_type=jnp.float32
    )


def table_pair(rows, cols, period):
    row_ids = lax.broadcasted_iota(jnp.int32, (rows, cols), 0)
    col_ids = lax.broadcasted_iota(jnp.int32, (rows, cols), 1)
    angle = 2.0 * math.pi / period * (row_ids * col_ids % period).astype(jnp.float32)
    return (jnp.cos(angle), jnp.sin(angle))


def make_plan(seq_len):
    small_len = int(math.isqrt(2 * seq_len))
    while seq_len % small_len:
        small_len -= 1
    large_len = 2 * seq_len // small_len
    large_cos, large_sin = table_pair(large_len // 2, large_len, large_len)
    small_cos, small_sin = table_pair(small_len, small_len, small_len)
    twist_cos, twist_sin = table_pair(large_len, small_len, small_len * large_len)
    fwd_large = jnp.stack([large_cos, -large_sin], axis=1)
    fwd_small = jnp.stack([jnp.stack([small_cos, -small_sin]), jnp.stack([small_sin, small_cos])])
    inv_small = jnp.stack([jnp.stack([small_cos, small_sin]), jnp.stack([-small_sin, small_cos])])
    inv_large = jnp.stack([large_cos, -large_sin])
    return (small_len, large_len, fwd_large, fwd_small, inv_small, inv_large, twist_cos, twist_sin)


def forward_spec(signal, dft_plan):
    small_len, large_len, fwd_large, fwd_small, inv_small, inv_large, twist_cos, twist_sin = (
        dft_plan
    )
    cube = signal.reshape(signal.shape[0], large_len // 2, small_len)
    section_one = contract("cba,bpk->cpka", cube, fwd_large)
    real_one = section_one[:, 0]
    imag_one = section_one[:, 1]
    section_two = jnp.stack(
        [real_one * twist_cos + imag_one * twist_sin, imag_one * twist_cos - real_one * twist_sin],
        axis=1,
    )
    return contract("cpka,pqaj->cqkj", section_two, fwd_small)


def inverse_half(spec, dft_plan):
    small_len, large_len, fwd_large, fwd_small, inv_small, inv_large, twist_cos, twist_sin = (
        dft_plan
    )
    section_one = contract("cqkj,qpja->cpka", spec, inv_small)
    real_one = section_one[:, 0]
    imag_one = section_one[:, 1]
    section_two = jnp.stack(
        [real_one * twist_cos - imag_one * twist_sin, imag_one * twist_cos + real_one * twist_sin],
        axis=1,
    )
    signal = contract("cpka,pbk->cba", section_two, inv_large)
    return signal.reshape(signal.shape[0], -1) / float(small_len * large_len)


def complex_mul(left, right):
    left_real, left_imag = (left[:, 0], left[:, 1])
    right_real, right_imag = (right[:, 0], right[:, 1])
    return jnp.stack(
        [
            left_real * right_real - left_imag * right_imag,
            left_real * right_imag + left_imag * right_real,
        ],
        axis=1,
    )


def conj_mul(left, right):
    left_real, left_imag = (left[:, 0], left[:, 1])
    right_real, right_imag = (right[:, 0], right[:, 1])
    return jnp.stack(
        [
            left_real * right_real + left_imag * right_imag,
            left_real * right_imag - left_imag * right_real,
        ],
        axis=1,
    )


def conv_forward(prod_chan, filter_spec, dft_plan):
    prod_spec = forward_spec(prod_chan.astype(jnp.float32), dft_plan)
    conv_chan = inverse_half(complex_mul(prod_spec, filter_spec), dft_plan).astype(jnp.bfloat16)
    return (conv_chan, prod_spec)


def conv_backward(grad_chan, filter_spec, prod_spec, dft_plan, grad_scale):
    grad_spec = forward_spec(grad_chan.astype(jnp.float32), dft_plan)
    dconv_chan = inverse_half(conj_mul(filter_spec, grad_spec), dft_plan).astype(jnp.bfloat16)
    dfilter_chan = inverse_half(conj_mul(prod_spec, grad_spec), dft_plan) * grad_scale
    return (dconv_chan, dfilter_chan)


def receive_filter(filter_taps, dft_plan):
    filter_chan = lax.all_to_all(filter_taps.T, "ctx", split_axis=0, concat_axis=1, tiled=True)
    return forward_spec(filter_chan, dft_plan)


def return_filter(dfilter_chan):
    return (
        lax.all_to_all(
            dfilter_chan.astype(jnp.bfloat16), "ctx", split_axis=1, concat_axis=0, tiled=True
        )
        .astype(dfilter_chan.dtype)
        .T
    )


def causal_taps(extended, weights, length, axis):
    rim_rows = len(weights) - 1
    summed = weights[0] * lax.slice_in_dim(extended, rim_rows, rim_rows + length, axis=axis)
    for offset in range(1, len(weights)):
        summed = summed + weights[offset] * lax.slice_in_dim(
            extended, rim_rows - offset, rim_rows - offset + length, axis=axis
        )
    return summed


def reverse_taps(extended, weights, length, axis):
    summed = weights[0] * lax.slice_in_dim(extended, 0, length, axis=axis)
    for offset in range(1, len(weights)):
        summed = summed + weights[offset] * lax.slice_in_dim(
            extended, offset, offset + length, axis=axis
        )
    return summed


def tap_grads(grad_in, extended, tap_count, length, axis):
    rim_rows = tap_count - 1
    rows = [
        jnp.sum(
            grad_in
            * lax.slice_in_dim(extended, rim_rows - offset, rim_rows - offset + length, axis=axis),
            axis=axis,
        )
        for offset in range(tap_count)
    ]
    return jnp.stack(rows, axis=1)


def spread_shards(query_proj, key_proj, value_proj, cotangent, filter_taps, short_weights):
    tokens = query_proj.shape[0]
    tap_count = short_weights.shape[1]
    rim_rows = tap_count - 1
    seq_len = tokens * lax.axis_size("ctx")
    grad_scale = 1.0 / math.sqrt(seq_len)
    dft_plan = make_plan(seq_len)
    stacked = jnp.stack([query_proj, key_proj, value_proj])
    prev_rim = from_behind(stacked[:, tokens - rim_rows :], "ctx", 1)
    extended = jnp.concatenate([prev_rim, stacked], axis=1).astype(jnp.float32)
    weights = [short_weights[:, offset, None, :] for offset in range(tap_count)]
    short_out = causal_taps(extended, weights, tokens, 1)
    product = (short_out[1] * short_out[2]).astype(jnp.bfloat16)
    cot_wide = cotangent.astype(jnp.float32)
    gate_grad = (cot_wide * short_out[0]).astype(jnp.bfloat16)
    filter_spec = receive_filter(filter_taps, dft_plan)
    prod_chan = lax.all_to_all(product.T, "ctx", split_axis=0, concat_axis=1, tiled=True)
    conv_chan, prod_spec = conv_forward(prod_chan, filter_spec, dft_plan)
    conv_tok = lax.all_to_all(conv_chan, "ctx", split_axis=1, concat_axis=0, tiled=True)
    grad_chan = lax.all_to_all(gate_grad.T, "ctx", split_axis=0, concat_axis=1, tiled=True)
    dconv_chan, dfilter_chan = conv_backward(
        grad_chan, filter_spec, prod_spec, dft_plan, grad_scale
    )
    dconv_tok = lax.all_to_all(dconv_chan, "ctx", split_axis=1, concat_axis=0, tiled=True)
    filter_grad = return_filter(dfilter_chan)
    conv_wide = conv_tok.T.astype(jnp.float32)
    dconv_wide = dconv_tok.T.astype(jnp.float32)
    gated = (short_out[0] * conv_wide).astype(jnp.bfloat16)
    token_grads = jnp.stack(
        [cot_wide * conv_wide, dconv_wide * short_out[2], dconv_wide * short_out[1]]
    )
    next_rim = from_behind(token_grads[:, :rim_rows], "ctx", -1)
    grad_ext = jnp.concatenate([token_grads, next_rim], axis=1)
    inputs_grad = reverse_taps(grad_ext, weights, tokens, 1).astype(jnp.bfloat16)
    weight_part = tap_grads(token_grads, extended, tap_count, tokens, 1)
    short_grad = lax.psum(weight_part, "ctx") * grad_scale
    results = (gated, inputs_grad[0], inputs_grad[1], inputs_grad[2])
    return (results[0], results[1], results[2], results[3], filter_grad, short_grad)


def fits(query_proj, short_weights):
    peers = lax.axis_size("ctx")
    tokens, width = query_proj.shape
    tap_count = short_weights.shape[1]
    return (
        width == peers * LANES
        and peers.bit_count() == 1
        and tokens % (PHASES * CHUNK) == 0
        and tap_count == RIM + 1
        and peers * tokens <= 2048
    )


def shards(*arrays):
    return channel_shards(*arrays) if fits(arrays[0], arrays[5]) else spread_shards(*arrays)


def solution(mesh):
    placed = (
        P("ctx", "tp"),
        P("ctx", "tp"),
        P("ctx", "tp"),
        P("ctx", "tp"),
        P("ctx", "tp"),
        P(None, None, "tp"),
    )
    return jax.shard_map(
        shards,
        mesh=mesh,
        in_specs=placed,
        out_specs=(
            P("ctx", "tp"),
            P("ctx", "tp"),
            P("ctx", "tp"),
            P("ctx", "tp"),
            P("ctx", "tp"),
            P(None, None, "tp"),
        ),
        check_vma=False,
    )
```

```python
import functools
import math

import jax
import jax.numpy as jnp
import numpy as np
from jax import lax
from jax.experimental import pallas as pl
from jax.experimental.pallas import tpu as pltpu
from jax.sharding import PartitionSpec as P

F32 = jnp.float32
BF16 = jnp.bfloat16
LANES = 128
PHASES = 4
TILE = 16
PAD = 8
CHUNK = 32
ROWS = 8
RIM = 2
PIECES = 2
MIB = 1024 * 1024
VMEM_LIMIT = 24 * MIB
PACK_VMEM = 53862 * 1024


def partners(peers, diagonal_first):
    def rank(step):
        links, other_core = (step >> 1).bit_count(), step & 1
        if links == 0:
            return (1 if diagonal_first else 5, 0)
        if links == 1:
            return (4 if other_core else 3, -step)
        return (2 * other_core if diagonal_first else 3.5, other_core)

    return [0] + sorted(range(1, peers), key=rank)


def exchange(blocks, steps):
    peers = len(blocks)
    got = [blocks[0]]
    for step, block in list(zip(steps, blocks))[1:]:
        got.append(lax.ppermute(block, "ctx", [(i, i ^ step) for i in range(peers)]))
    return got


def in_vmem(count):
    return [pl.BlockSpec(memory_space=pltpu.VMEM)] * count


def lanes_of(place):
    return pl.ds(pl.multiple_of(place * LANES, LANES), LANES)


def pack_kernel(count, steps, *refs):
    sources, packed = refs[:count], refs[count : count + len(steps)]
    held, sems = refs[count + len(steps) : -1], refs[-1]
    tokens = sources[0].shape[0]
    me = lax.axis_index("ctx")
    arriving = [
        pltpu.make_async_copy(source, target, sems.at[at])
        for at, (source, target) in enumerate(zip(sources, held))
    ]
    for copy in arriving:
        copy.start()
    for at, source in enumerate(held):
        arriving[at].wait()
        rows = slice(at * tokens, (at + 1) * tokens)
        for step, target in zip(steps, packed):
            target[rows, :] = source[:, lanes_of(me ^ step)].astype(BF16)


def pack(arrays, steps):
    tokens = arrays[0].shape[0]
    count = len(arrays)
    return pl.pallas_call(
        functools.partial(pack_kernel, count, steps),
        in_specs=[pl.BlockSpec(memory_space=pl.ANY)] * count,
        out_specs=in_vmem(len(steps)),
        out_shape=[jax.ShapeDtypeStruct((count * tokens, LANES), BF16)] * len(steps),
        scratch_shapes=[
            *[pltpu.VMEM(array.shape, array.dtype) for array in arrays],
            pltpu.SemaphoreType.DMA((count,)),
        ],
        compiler_params=pltpu.CompilerParams(vmem_limit_bytes=PACK_VMEM),
        cost_estimate=pl.CostEstimate(flops=0, bytes_accessed=8 * MIB, transcendentals=0),
        name="pack_inputs",
    )(*arrays)


@functools.lru_cache(maxsize=None)
def dft_tables(seq_len):
    size = seq_len // PHASES
    k = np.arange(size, dtype=np.int64)[:, None]
    m = np.arange(size, dtype=np.int64)[None, :]
    forward = []
    for phase in range(PHASES):
        turns = ((4 * k + 1) * (PHASES * m + phase)) % (4 * seq_len)
        angle = 2.0 * np.pi / (4 * seq_len) * turns
        forward.append(np.concatenate([np.cos(angle), -np.sin(angle)], axis=0))
    forward = np.stack(forward)
    backward = np.swapaxes(forward, 1, 2) / seq_len

    return forward.astype(BF16), backward.astype(BF16)


def forward_mix(parts):
    (r0, i0), (r1, i1), (r2, i2), (r3, i3) = parts
    ar, ai, br, bi = r0 + r2, i0 + i2, r0 - r2, i0 - i2
    cr, ci, dr, di = r1 + r3, i1 + i3, r1 - r3, i1 - i3
    return ((ar + cr, ai + ci), (br + di, bi - dr), (ar - cr, ai - ci), (br - di, bi + dr))


def inverse_mix(parts):
    (r0, i0), (r1, i1), (r2, i2), (r3, i3) = parts
    ar, ai, br, bi = r0 + r2, i0 + i2, r0 - r2, i0 - i2
    cr, ci, dr, di = r1 + r3, i1 + i3, r1 - r3, i1 - i3
    return ((ar + cr, ai + ci), (br - di, bi + dr), (ar - cr, ai - ci), (br + di, bi - dr))


def times(left, right):
    return tuple(
        (lr * rr - li * ri, lr * ri + li * rr) for (lr, li), (rr, ri) in zip(left, right)
    )


def conj_times(left, right):
    return tuple(
        (lr * rr + li * ri, lr * ri - li * rr) for (lr, li), (rr, ri) in zip(left, right)
    )


def transform(table, signal):
    return jnp.dot(table, signal, preferred_element_type=F32)


def phases_near(ref, chunk, tap_count):
    start = PAD + chunk * CHUNK * PHASES
    return {
        offset: ref[pl.ds(start + offset, CHUNK, stride=PHASES), :]
        for offset in range(1 - tap_count, PHASES)
    }


def short_conv(near, taps):
    results = []
    for r in range(PHASES):
        summed = taps[0] * near[r]
        for at in range(1, len(taps)):
            summed = summed + taps[at] * near[r - at]
        results.append(summed)
    return results


def add_rows(total, terms):
    for term in terms:
        folded = jnp.sum(term.reshape(CHUNK // 8, 8, LANES), axis=0)
        total = folded if total is None else total + folded
    return total


def clear_ends(ref):
    ref[:PAD, :] = jnp.zeros((PAD, LANES), F32)
    ref[ref.shape[0] - PAD :, :] = jnp.zeros((PAD, LANES), F32)


def stage_kernel(count, *refs):
    sources, targets, sems = refs[:count], refs[count + 1 : 2 * count + 1], refs[2 * count + 1]
    copies = [
        pltpu.make_async_copy(source, target, sems.at[at])
        for at, (source, target) in enumerate(zip(sources, targets))
    ]
    for copy in copies:
        copy.start()
    for copy in copies:
        copy.wait()


def stage(arrays, after):
    count = len(arrays)
    return pl.pallas_call(
        functools.partial(stage_kernel, count),
        in_specs=[pl.BlockSpec(memory_space=pl.ANY)] * (count + 1),
        out_specs=in_vmem(count),
        out_shape=[jax.ShapeDtypeStruct(array.shape, array.dtype) for array in arrays],
        scratch_shapes=[pltpu.SemaphoreType.DMA((count,))],
        compiler_params=pltpu.CompilerParams(vmem_limit_bytes=8 * MIB),
        cost_estimate=pl.CostEstimate(flops=0, bytes_accessed=8 * MIB, transcendentals=0),
        name="stage_tables",
    )(*arrays, after)


def extra_rows(short_weights):
    sums = PIECES * short_weights.shape[0] * short_weights.shape[1]
    return sums, -(-(sums + 6 * RIM) // TILE) * TILE


def channel_kernel(tokens, heard, told, grad_scale, *refs):
    peers = len(heard)
    arrived = refs[:peers]
    weights, forward, backward = refs[peers : peers + 3]
    out = refs[peers + 3 : 2 * peers + 3]
    (
        query,
        key,
        value,
        cot,
        conv,
        conv_grad,
        filter_grad,
        taps,
        key_short,
        value_short,
        signals,
        spectra,
        products,
        extra,
    ) = refs[2 * peers + 3 :]
    size = peers * tokens // PHASES
    tap_count = weights.shape[1]
    me = lax.axis_index("ctx")
    own = lanes_of(me)
    for ref in (query, key, value, cot, conv, conv_grad):
        clear_ends(ref)
    for ref in (key_short, value_short):
        ref[:, size:, :] = jnp.zeros((PHASES, PAD, LANES), F32)
    for step, source in zip(heard, arrived):
        start = (me ^ step) * tokens
        inner = pl.ds(pl.multiple_of(PAD + start, PAD), tokens)
        for at, ref in enumerate((query, key, value, cot)):
            ref[inner, :] = source[at * tokens : (at + 1) * tokens, :].astype(F32)
        taps[pl.ds(pl.multiple_of(start, PAD), tokens), :] = source[4 * tokens :, :].astype(F32)
    chunks = range(size // CHUNK)
    taps_of = [
        [weights[array, tap : tap + 1, own] for tap in range(tap_count)] for array in range(3)
    ]

    def rows_of(chunk):
        return slice(chunk * CHUNK, (chunk + 1) * CHUNK)

    def spectrum(at, real, imag):
        lanes = slice(at * LANES, (at + 1) * LANES)
        return forward_mix(
            [(spectra[r, real, lanes], spectra[r, imag, lanes]) for r in range(PHASES)]
        )

    def mixed_spectrum(at, real, imag):
        lanes = slice(at * LANES, (at + 1) * LANES)
        return [(spectra[q, real, lanes], spectra[q, imag, lanes]) for q in range(PHASES)]

    def keep(at, real, imag, mixed):
        lanes = slice(at * LANES, (at + 1) * LANES)
        for r, pair in enumerate(inverse_mix(mixed)):
            for rows, part in zip((real, imag), pair):
                products[r, rows, lanes] = part

    for chunk in chunks:
        rows = rows_of(chunk)
        key_now = short_conv(phases_near(key, chunk, tap_count), taps_of[1])
        value_now = short_conv(phases_near(value, chunk, tap_count), taps_of[2])
        for r in range(PHASES):
            key_short[r, rows, :] = key_now[r]
            value_short[r, rows, :] = value_now[r]
            signals[r, rows, :LANES] = (key_now[r] * value_now[r]).astype(BF16)
            filt = taps[pl.ds(chunk * CHUNK * PHASES + r, CHUNK, stride=PHASES), :]
            signals[r, rows, LANES : 2 * LANES] = filt.astype(BF16)
    for r in range(PHASES):
        spectra[r, :, : 2 * LANES] = transform(forward[r], signals[r, :, : 2 * LANES])
    for chunk in chunks:
        rows = rows_of(chunk)
        query_now = short_conv(phases_near(query, chunk, tap_count), taps_of[0])
        cot_now = phases_near(cot, chunk, 1)
        for r in range(PHASES):
            signals[r, rows, 2 * LANES :] = (cot_now[r] * query_now[r]).astype(BF16)
    for r in range(PHASES):
        spectra[r, :, 2 * LANES :] = transform(forward[r], signals[r, :, 2 * LANES :])
    for step in range(size // ROWS):
        real = slice(step * ROWS, (step + 1) * ROWS)
        imag = slice(size + step * ROWS, size + (step + 1) * ROWS)
        prod, filt = spectrum(0, real, imag), spectrum(1, real, imag)
        for at, mixed in enumerate((prod, filt)):
            lanes = slice(at * LANES, (at + 1) * LANES)
            for q, pair in enumerate(mixed):
                spectra[q, real, lanes], spectra[q, imag, lanes] = pair
        keep(0, real, imag, times(prod, filt))
    for r in range(PHASES):
        result = transform(backward[r], products[r, :, :LANES].astype(BF16))
        conv[pl.ds(PAD + r, size, stride=PHASES), :] = result.astype(BF16).astype(F32)
    for step in range(size // ROWS):
        real = slice(step * ROWS, (step + 1) * ROWS)
        imag = slice(size + step * ROWS, size + (step + 1) * ROWS)
        grad = spectrum(2, real, imag)
        for q, pair in enumerate(grad):
            spectra[q, real, 2 * LANES :], spectra[q, imag, 2 * LANES :] = pair
        keep(1, real, imag, conj_times(mixed_spectrum(1, real, imag), grad))
    for r in range(PHASES):
        result = transform(backward[r], products[r, :, LANES : 2 * LANES].astype(BF16))
        conv_grad[pl.ds(PAD + r, size, stride=PHASES), :] = result.astype(BF16).astype(F32)
    for step in range(size // ROWS):
        real = slice(step * ROWS, (step + 1) * ROWS)
        imag = slice(size + step * ROWS, size + (step + 1) * ROWS)
        known = (mixed_spectrum(at, real, imag) for at in (0, 2))
        keep(2, real, imag, conj_times(*known))
    for r in range(PHASES):
        result = transform(backward[r], products[r, :, 2 * LANES :].astype(BF16))
        filter_grad[pl.ds(r, size, stride=PHASES), :] = result * grad_scale

    totals = [[None] * tap_count for _ in range(3)]

    def add_sums(array, signal, chunk, pre):
        near = phases_near(signal, chunk, tap_count)
        for tap in range(tap_count):
            totals[array][tap] = add_rows(
                totals[array][tap], [pre[r] * near[r - tap] for r in range(PHASES)]
            )

    for chunk in chunks:
        cot_now, conv_now = phases_near(cot, chunk, 1), phases_near(conv, chunk, 1)
        add_sums(0, query, chunk, [cot_now[r] * conv_now[r] for r in range(PHASES)])
    for chunk in chunks:
        rows = rows_of(chunk)
        grad_now = phases_near(conv_grad, chunk, 1)
        add_sums(1, key, chunk, [grad_now[r] * value_short[r, rows, :] for r in range(PHASES)])
        add_sums(2, value, chunk, [grad_now[r] * key_short[r, rows, :] for r in range(PHASES)])
    sums = [jnp.sum(total, axis=0, keepdims=True) for row in totals for total in row]
    rest = jnp.concatenate(sums, axis=0) * grad_scale
    extra[...] = jnp.zeros_like(extra)
    for piece in range(PIECES):
        rounded = rest.astype(BF16).astype(F32)
        extra[piece * len(sums) : (piece + 1) * len(sums), :] = rounded
        rest = rest - rounded
    for step, target in zip(told, out):
        start = (me ^ step) * tokens
        inner = pl.ds(pl.multiple_of(PAD + start, PAD), tokens)
        target[:tokens, :] = conv[inner, :].astype(BF16)
        target[tokens : 2 * tokens, :] = conv_grad[inner, :].astype(BF16)
        target[2 * tokens : 3 * tokens, :] = filter_grad[
            pl.ds(pl.multiple_of(start, PAD), tokens), :
        ].astype(BF16)
        before = pl.ds(pl.multiple_of(start, PAD), PAD)
        after = pl.ds(pl.multiple_of(PAD + start + tokens, PAD), PAD)
        at = PIECES * len(sums)
        for ref in (query, key, value):
            extra[at : at + RIM, :] = ref[before, :][PAD - RIM :]
            at += RIM
        row = pl.ds(pl.multiple_of((start + tokens) // PHASES, PAD), PAD)
        extra[at : at + RIM, :] = (cot[after, :] * conv[after, :])[:RIM]
        for short in (value_short, key_short):
            at += RIM
            shorts = jnp.concatenate([short[r, row, :][:1] for r in range(RIM)], axis=0)
            extra[at : at + RIM, :] = conv_grad[after, :][:RIM] * shorts
        target[3 * tokens :, :] = extra[...].astype(BF16)


def channel_step(arrived, heard, told, short_weights, tables, tokens):
    peers = len(arrived)
    seq_len = peers * tokens
    size = seq_len // PHASES
    extra = extra_rows(short_weights)[1]
    padded = pltpu.VMEM((seq_len + 2 * PAD, LANES), F32)
    plain = pltpu.VMEM((seq_len, LANES), F32)
    phases = pltpu.VMEM((PHASES, size + PAD, LANES), F32)
    return pl.pallas_call(
        functools.partial(channel_kernel, tokens, heard, told, 1.0 / math.sqrt(seq_len)),
        in_specs=in_vmem(peers + 3),
        out_specs=in_vmem(peers),
        out_shape=[jax.ShapeDtypeStruct((3 * tokens + extra, LANES), BF16)] * peers,
        scratch_shapes=[
            *[padded] * 6,
            plain,
            plain,
            phases,
            phases,
            pltpu.VMEM((PHASES, size, 3 * LANES), BF16),
            pltpu.VMEM((PHASES, 2 * size, 3 * LANES), F32),
            pltpu.VMEM((PHASES, 2 * size, 3 * LANES), F32),
            pltpu.VMEM((extra, LANES), F32),
        ],
        compiler_params=pltpu.CompilerParams(vmem_limit_bytes=VMEM_LIMIT),
        name="channel_operator",
    )(*arrived, short_weights, *tables)


def token_kernel(steps, sum_rows, carried, *refs):
    count_in = len(steps)
    arrived = refs[:count_in]
    query, key, value, cot, weights = refs[count_in : count_in + 5]
    results = refs[count_in + 5 + carried : count_in + 11 + carried]
    (gated, query_grad, key_grad, value_grad, filter_grad, short_grad, longer, pre, sems) = refs[
        count_in + 11 + carried :
    ]
    copies = []
    tokens = query.shape[0]
    tap_count = weights.shape[1]
    count = sum_rows // PIECES
    me = lax.axis_index("ctx")
    for slot, (step, source) in enumerate(zip(steps, arrived)):
        lanes = lanes_of(me ^ step)
        extra = source[3 * tokens :, :].astype(F32)

        def rim(at):
            return extra[sum_rows + at * RIM : sum_rows + (at + 1) * RIM]

        def short(array, signal):
            longer[array, PAD - RIM : PAD, :] = rim(array)
            longer[array, PAD :, :] = signal[:, lanes].astype(F32)
            summed = weights[array, 0:1, lanes] * longer[array, PAD:, :]
            for tap in range(1, tap_count):
                summed = (
                    summed
                    + weights[array, tap : tap + 1, lanes]
                    * longer[array, PAD - tap : PAD - tap + tokens, :]
                )
            return summed

        def taps_back(array, grad, target):
            pre[array, :tokens, :] = grad
            pre[array, tokens : tokens + RIM, :] = rim(3 + array)
            summed = weights[array, 0:1, lanes] * grad
            for tap in range(1, tap_count):
                summed = (
                    summed
                    + weights[array, tap : tap + 1, lanes] * pre[array, tap : tap + tokens, :]
                )
            target[slot] = summed.astype(BF16)

        conv = source[:tokens, :].astype(F32)
        conv_grad = source[tokens : 2 * tokens, :].astype(F32)
        gated[slot] = (short(0, query) * conv).astype(BF16)
        taps_back(0, cot[:, lanes].astype(F32) * conv, query_grad)
        taps_back(1, conv_grad * short(2, value), key_grad)
        taps_back(2, conv_grad * short(1, key), value_grad)
        filter_grad[slot] = source[2 * tokens : 3 * tokens, :].astype(F32)
        whole = extra[:count]
        for piece in range(1, PIECES):
            whole = whole + extra[piece * count : (piece + 1) * count]
        for row in range(count):
            which, tap = divmod(row, tap_count)
            short_grad[slot, which, tap : tap + 1, :] = whole[row : row + 1]
        held = (gated, query_grad, key_grad, value_grad, filter_grad, short_grad)
        for at, (source, target) in enumerate(zip(held, results)):
            place = target.at[:, :, lanes] if at == 5 else target.at[:, lanes]
            copies.append(pltpu.make_async_copy(source.at[slot], place, sems.at[slot, at]))
            copies[-1].start()
    for copy in copies:
        copy.wait()


def token_step(arrived, steps, query, key, value, cot, short_weights, begun=()):
    tokens, width = query.shape
    count = len(arrived)
    wide = jax.ShapeDtypeStruct((tokens, width), BF16)
    anywhere = pl.BlockSpec(memory_space=pl.ANY)
    return pl.pallas_call(
        functools.partial(token_kernel, steps, extra_rows(short_weights)[0], len(begun)),
        in_specs=in_vmem(count + 5) + [anywhere] * len(begun),
        out_specs=[anywhere] * 6,
        out_shape=[wide] * 4
        + [
            jax.ShapeDtypeStruct((tokens, width), F32),
            jax.ShapeDtypeStruct(short_weights.shape, F32),
        ],
        scratch_shapes=[
            *[pltpu.VMEM((count, tokens, LANES), BF16)] * 4,
            pltpu.VMEM((count, tokens, LANES), F32),
            pltpu.VMEM((count, *short_weights.shape[:2], LANES), F32),
            pltpu.VMEM((3, tokens + PAD, LANES), F32),
            pltpu.VMEM((3, tokens + PAD, LANES), F32),
            pltpu.SemaphoreType.DMA((count, 6)),
        ],
        input_output_aliases={count + 5 + at: at for at in range(len(begun))},
        compiler_params=pltpu.CompilerParams(vmem_limit_bytes=VMEM_LIMIT),
        cost_estimate=pl.CostEstimate(flops=0, bytes_accessed=4 * MIB, transcendentals=0),
        name="token_outputs",
    )(*arrived, query, key, value, cot, short_weights, *begun)


def channel_shards(query_proj, key_proj, value_proj, cotangent, filter_taps, short_weights):
    peers = lax.axis_size("ctx")
    tokens = query_proj.shape[0]
    tables = [jnp.asarray(table) for table in dft_tables(peers * tokens)]
    going, coming = partners(peers, False), partners(peers, True)
    sent = pack((query_proj, key_proj, value_proj, cotangent, filter_taps), going)
    arrived = exchange(sent, going)
    staged = stage((sent[0], short_weights, *tables), arrived[1])
    arrived[0] = staged[0]
    results = channel_step(arrived, going, coming, staged[1], staged[2:], tokens)
    back = exchange(results, coming)
    local = (query_proj, key_proj, value_proj, cotangent, short_weights)
    ends = [at for at in (4, 6) if at < peers] + [peers]
    begun, start = (), 0
    for end in ends:
        begun = token_step(back[start:end], coming[start:end], *local, begun)
        start = end
    return tuple(begun)


def from_behind(array, axis, by):
    peers = lax.axis_size(axis)
    pairs = [(i, i + by) for i in range(peers) if 0 <= i + by < peers]
    return lax.ppermute(array, axis, pairs)


def contract(form, left, right):
    return jnp.einsum(
        form, left, right, precision=lax.Precision.HIGHEST, preferred_element_type=jnp.float32
    )


def table_pair(rows, cols, period):
    row_ids = lax.broadcasted_iota(jnp.int32, (rows, cols), 0)
    col_ids = lax.broadcasted_iota(jnp.int32, (rows, cols), 1)
    angle = 2.0 * math.pi / period * (row_ids * col_ids % period).astype(jnp.float32)
    return (jnp.cos(angle), jnp.sin(angle))


def make_plan(seq_len):
    small_len = int(math.isqrt(2 * seq_len))
    while seq_len % small_len:
        small_len -= 1
    large_len = 2 * seq_len // small_len
    large_cos, large_sin = table_pair(large_len // 2, large_len, large_len)
    small_cos, small_sin = table_pair(small_len, small_len, small_len)
    twist_cos, twist_sin = table_pair(large_len, small_len, small_len * large_len)
    fwd_large = jnp.stack([large_cos, -large_sin], axis=1)
    fwd_small = jnp.stack([jnp.stack([small_cos, -small_sin]), jnp.stack([small_sin, small_cos])])
    inv_small = jnp.stack([jnp.stack([small_cos, small_sin]), jnp.stack([-small_sin, small_cos])])
    inv_large = jnp.stack([large_cos, -large_sin])
    return (small_len, large_len, fwd_large, fwd_small, inv_small, inv_large, twist_cos, twist_sin)


def forward_spec(signal, dft_plan):
    small_len, large_len, fwd_large, fwd_small, inv_small, inv_large, twist_cos, twist_sin = (
        dft_plan
    )
    cube = signal.reshape(signal.shape[0], large_len // 2, small_len)
    section_one = contract("cba,bpk->cpka", cube, fwd_large)
    real_one = section_one[:, 0]
    imag_one = section_one[:, 1]
    section_two = jnp.stack(
        [real_one * twist_cos + imag_one * twist_sin, imag_one * twist_cos - real_one * twist_sin],
        axis=1,
    )
    return contract("cpka,pqaj->cqkj", section_two, fwd_small)


def inverse_half(spec, dft_plan):
    small_len, large_len, fwd_large, fwd_small, inv_small, inv_large, twist_cos, twist_sin = (
        dft_plan
    )
    section_one = contract("cqkj,qpja->cpka", spec, inv_small)
    real_one = section_one[:, 0]
    imag_one = section_one[:, 1]
    section_two = jnp.stack(
        [real_one * twist_cos - imag_one * twist_sin, imag_one * twist_cos + real_one * twist_sin],
        axis=1,
    )
    signal = contract("cpka,pbk->cba", section_two, inv_large)
    return signal.reshape(signal.shape[0], -1) / float(small_len * large_len)


def complex_mul(left, right):
    left_real, left_imag = (left[:, 0], left[:, 1])
    right_real, right_imag = (right[:, 0], right[:, 1])
    return jnp.stack(
        [
            left_real * right_real - left_imag * right_imag,
            left_real * right_imag + left_imag * right_real,
        ],
        axis=1,
    )


def conj_mul(left, right):
    left_real, left_imag = (left[:, 0], left[:, 1])
    right_real, right_imag = (right[:, 0], right[:, 1])
    return jnp.stack(
        [
            left_real * right_real + left_imag * right_imag,
            left_real * right_imag - left_imag * right_real,
        ],
        axis=1,
    )


def conv_forward(prod_chan, filter_spec, dft_plan):
    prod_spec = forward_spec(prod_chan.astype(jnp.float32), dft_plan)
    conv_chan = inverse_half(complex_mul(prod_spec, filter_spec), dft_plan).astype(jnp.bfloat16)
    return (conv_chan, prod_spec)


def conv_backward(grad_chan, filter_spec, prod_spec, dft_plan, grad_scale):
    grad_spec = forward_spec(grad_chan.astype(jnp.float32), dft_plan)
    dconv_chan = inverse_half(conj_mul(filter_spec, grad_spec), dft_plan).astype(jnp.bfloat16)
    dfilter_chan = inverse_half(conj_mul(prod_spec, grad_spec), dft_plan) * grad_scale
    return (dconv_chan, dfilter_chan)


def receive_filter(filter_taps, dft_plan):
    filter_chan = lax.all_to_all(filter_taps.T, "ctx", split_axis=0, concat_axis=1, tiled=True)
    return forward_spec(filter_chan, dft_plan)


def return_filter(dfilter_chan):
    return (
        lax.all_to_all(
            dfilter_chan.astype(jnp.bfloat16), "ctx", split_axis=1, concat_axis=0, tiled=True
        )
        .astype(dfilter_chan.dtype)
        .T
    )


def causal_taps(extended, weights, length, axis):
    rim_rows = len(weights) - 1
    summed = weights[0] * lax.slice_in_dim(extended, rim_rows, rim_rows + length, axis=axis)
    for offset in range(1, len(weights)):
        summed = summed + weights[offset] * lax.slice_in_dim(
            extended, rim_rows - offset, rim_rows - offset + length, axis=axis
        )
    return summed


def reverse_taps(extended, weights, length, axis):
    summed = weights[0] * lax.slice_in_dim(extended, 0, length, axis=axis)
    for offset in range(1, len(weights)):
        summed = summed + weights[offset] * lax.slice_in_dim(
            extended, offset, offset + length, axis=axis
        )
    return summed


def tap_grads(grad_in, extended, tap_count, length, axis):
    rim_rows = tap_count - 1
    rows = [
        jnp.sum(
            grad_in
            * lax.slice_in_dim(extended, rim_rows - offset, rim_rows - offset + length, axis=axis),
            axis=axis,
        )
        for offset in range(tap_count)
    ]
    return jnp.stack(rows, axis=1)


def spread_shards(query_proj, key_proj, value_proj, cotangent, filter_taps, short_weights):
    tokens = query_proj.shape[0]
    tap_count = short_weights.shape[1]
    rim_rows = tap_count - 1
    seq_len = tokens * lax.axis_size("ctx")
    grad_scale = 1.0 / math.sqrt(seq_len)
    dft_plan = make_plan(seq_len)
    stacked = jnp.stack([query_proj, key_proj, value_proj])
    prev_rim = from_behind(stacked[:, tokens - rim_rows :], "ctx", 1)
    extended = jnp.concatenate([prev_rim, stacked], axis=1).astype(jnp.float32)
    weights = [short_weights[:, offset, None, :] for offset in range(tap_count)]
    short_out = causal_taps(extended, weights, tokens, 1)
    product = (short_out[1] * short_out[2]).astype(jnp.bfloat16)
    cot_wide = cotangent.astype(jnp.float32)
    gate_grad = (cot_wide * short_out[0]).astype(jnp.bfloat16)
    filter_spec = receive_filter(filter_taps, dft_plan)
    prod_chan = lax.all_to_all(product.T, "ctx", split_axis=0, concat_axis=1, tiled=True)
    conv_chan, prod_spec = conv_forward(prod_chan, filter_spec, dft_plan)
    conv_tok = lax.all_to_all(conv_chan, "ctx", split_axis=1, concat_axis=0, tiled=True)
    grad_chan = lax.all_to_all(gate_grad.T, "ctx", split_axis=0, concat_axis=1, tiled=True)
    dconv_chan, dfilter_chan = conv_backward(
        grad_chan, filter_spec, prod_spec, dft_plan, grad_scale
    )
    dconv_tok = lax.all_to_all(dconv_chan, "ctx", split_axis=1, concat_axis=0, tiled=True)
    filter_grad = return_filter(dfilter_chan)
    conv_wide = conv_tok.T.astype(jnp.float32)
    dconv_wide = dconv_tok.T.astype(jnp.float32)
    gated = (short_out[0] * conv_wide).astype(jnp.bfloat16)
    token_grads = jnp.stack(
        [cot_wide * conv_wide, dconv_wide * short_out[2], dconv_wide * short_out[1]]
    )
    next_rim = from_behind(token_grads[:, :rim_rows], "ctx", -1)
    grad_ext = jnp.concatenate([token_grads, next_rim], axis=1)
    inputs_grad = reverse_taps(grad_ext, weights, tokens, 1).astype(jnp.bfloat16)
    weight_part = tap_grads(token_grads, extended, tap_count, tokens, 1)
    short_grad = lax.psum(weight_part, "ctx") * grad_scale
    results = (gated, inputs_grad[0], inputs_grad[1], inputs_grad[2])
    return (results[0], results[1], results[2], results[3], filter_grad, short_grad)


def fits(query_proj, short_weights):
    peers = lax.axis_size("ctx")
    tokens, width = query_proj.shape
    tap_count = short_weights.shape[1]
    return (
        width == peers * LANES
        and peers.bit_count() == 1
        and tokens % (PHASES * CHUNK) == 0
        and tap_count == RIM + 1
        and peers * tokens <= 2048
    )


def shards(*arrays):
    return channel_shards(*arrays) if fits(arrays[0], arrays[5]) else spread_shards(*arrays)


def solution(mesh):
    placed = (
        P("ctx", "tp"),
        P("ctx", "tp"),
        P("ctx", "tp"),
        P("ctx", "tp"),
        P("ctx", "tp"),
        P(None, None, "tp"),
    )
    return jax.shard_map(
        shards,
        mesh=mesh,
        in_specs=placed,
        out_specs=(
            P("ctx", "tp"),
            P("ctx", "tp"),
            P("ctx", "tp"),
            P("ctx", "tp"),
            P("ctx", "tp"),
            P(None, None, "tp"),
        ),
        check_vma=False,
    )
```

```python
import functools
import math

import jax
import jax.numpy as jnp
import numpy as np
from jax import lax
from jax.experimental import pallas as pl
from jax.experimental.pallas import tpu as pltpu
from jax.sharding import PartitionSpec as P

F32 = jnp.float32
BF16 = jnp.bfloat16
LANES = 128
PHASES = 4
TILE = 16
PAD = 8
CHUNK = 32
ROWS = 8
RIM = 2
PIECES = 2
MIB = 1024 * 1024
VMEM_LIMIT = 24 * MIB
PACK_VMEM = 53862 * 1024


def partners(peers, diagonal_first):
    def rank(step):
        links, other_core = (step >> 1).bit_count(), step & 1
        if links == 0:
            return (1 if diagonal_first else 5, 0)
        if links == 1:
            first = diagonal_first and step == peers // 2
            return (4 if other_core else 3 - 4 * first, -step)
        return (2 * other_core if diagonal_first else 3.5, other_core)

    return [0] + sorted(range(1, peers), key=rank)


def exchange(blocks, steps):
    peers = len(blocks)
    got = [blocks[0]]
    for step, block in list(zip(steps, blocks))[1:]:
        got.append(lax.ppermute(block, "ctx", [(i, i ^ step) for i in range(peers)]))
    return got


def in_vmem(count):
    return [pl.BlockSpec(memory_space=pltpu.VMEM)] * count


def lanes_of(place):
    return pl.ds(pl.multiple_of(place * LANES, LANES), LANES)


def pack_kernel(count, steps, *refs):
    sources, packed = refs[:count], refs[count : count + len(steps)]
    held, sems = refs[count + len(steps) : -1], refs[-1]
    tokens = sources[0].shape[0]
    me = lax.axis_index("ctx")
    arriving = [
        pltpu.make_async_copy(source, target, sems.at[at])
        for at, (source, target) in enumerate(zip(sources, held))
    ]
    for copy in arriving:
        copy.start()
    for at, source in enumerate(held):
        arriving[at].wait()
        rows = slice(at * tokens, (at + 1) * tokens)
        for step, target in zip(steps, packed):
            target[rows, :] = source[:, lanes_of(me ^ step)].astype(BF16)


def pack(arrays, steps):
    tokens = arrays[0].shape[0]
    count = len(arrays)
    return pl.pallas_call(
        functools.partial(pack_kernel, count, steps),
        in_specs=[pl.BlockSpec(memory_space=pl.ANY)] * count,
        out_specs=in_vmem(len(steps)),
        out_shape=[jax.ShapeDtypeStruct((count * tokens, LANES), BF16)] * len(steps),
        scratch_shapes=[
            *[pltpu.VMEM(array.shape, array.dtype) for array in arrays],
            pltpu.SemaphoreType.DMA((count,)),
        ],
        compiler_params=pltpu.CompilerParams(vmem_limit_bytes=PACK_VMEM),
        cost_estimate=pl.CostEstimate(flops=0, bytes_accessed=8 * MIB, transcendentals=0),
        name="pack_inputs",
    )(*arrays)


@functools.lru_cache(maxsize=None)
def dft_tables(seq_len):
    size = seq_len // PHASES
    k = np.arange(size, dtype=np.int64)[:, None]
    m = np.arange(size, dtype=np.int64)[None, :]
    forward = []
    for phase in range(PHASES):
        turns = ((4 * k + 1) * (PHASES * m + phase)) % (4 * seq_len)
        angle = 2.0 * np.pi / (4 * seq_len) * turns
        forward.append(np.concatenate([np.cos(angle), -np.sin(angle)], axis=0))
    forward = np.stack(forward)
    backward = np.swapaxes(forward, 1, 2) / seq_len

    return forward.astype(BF16), backward.astype(BF16)


def forward_mix(parts):
    (r0, i0), (r1, i1), (r2, i2), (r3, i3) = parts
    ar, ai, br, bi = r0 + r2, i0 + i2, r0 - r2, i0 - i2
    cr, ci, dr, di = r1 + r3, i1 + i3, r1 - r3, i1 - i3
    return ((ar + cr, ai + ci), (br + di, bi - dr), (ar - cr, ai - ci), (br - di, bi + dr))


def inverse_mix(parts):
    (r0, i0), (r1, i1), (r2, i2), (r3, i3) = parts
    ar, ai, br, bi = r0 + r2, i0 + i2, r0 - r2, i0 - i2
    cr, ci, dr, di = r1 + r3, i1 + i3, r1 - r3, i1 - i3
    return ((ar + cr, ai + ci), (br - di, bi + dr), (ar - cr, ai - ci), (br + di, bi - dr))


def times(left, right):
    return tuple(
        (lr * rr - li * ri, lr * ri + li * rr) for (lr, li), (rr, ri) in zip(left, right)
    )


def conj_times(left, right):
    return tuple(
        (lr * rr + li * ri, lr * ri - li * rr) for (lr, li), (rr, ri) in zip(left, right)
    )


def transform(table, signal):
    return jnp.dot(table, signal, preferred_element_type=F32)


def phases_near(ref, chunk, tap_count):
    start = PAD + chunk * CHUNK * PHASES
    return {
        offset: ref[pl.ds(start + offset, CHUNK, stride=PHASES), :]
        for offset in range(1 - tap_count, PHASES)
    }


def short_conv(near, taps):
    results = []
    for r in range(PHASES):
        summed = taps[0] * near[r]
        for at in range(1, len(taps)):
            summed = summed + taps[at] * near[r - at]
        results.append(summed)
    return results


def add_rows(total, terms):
    for term in terms:
        folded = jnp.sum(term.reshape(CHUNK // 8, 8, LANES), axis=0)
        total = folded if total is None else total + folded
    return total


def clear_ends(ref):
    ref[:PAD, :] = jnp.zeros((PAD, LANES), F32)
    ref[ref.shape[0] - PAD :, :] = jnp.zeros((PAD, LANES), F32)


def stage_kernel(count, *refs):
    sources, targets, sems = refs[:count], refs[count + 1 : 2 * count + 1], refs[2 * count + 1]
    copies = [
        pltpu.make_async_copy(source, target, sems.at[at])
        for at, (source, target) in enumerate(zip(sources, targets))
    ]
    for copy in copies:
        copy.start()
    for copy in copies:
        copy.wait()


def stage(arrays, after):
    count = len(arrays)
    return pl.pallas_call(
        functools.partial(stage_kernel, count),
        in_specs=[pl.BlockSpec(memory_space=pl.ANY)] * (count + 1),
        out_specs=in_vmem(count),
        out_shape=[jax.ShapeDtypeStruct(array.shape, array.dtype) for array in arrays],
        scratch_shapes=[pltpu.SemaphoreType.DMA((count,))],
        compiler_params=pltpu.CompilerParams(vmem_limit_bytes=8 * MIB),
        cost_estimate=pl.CostEstimate(flops=0, bytes_accessed=8 * MIB, transcendentals=0),
        name="stage_tables",
    )(*arrays, after)


def extra_rows(short_weights):
    sums = PIECES * short_weights.shape[0] * short_weights.shape[1]
    return sums, -(-(sums + 6 * RIM) // TILE) * TILE


def channel_kernel(tokens, heard, told, grad_scale, *refs):
    peers = len(heard)
    arrived = refs[:peers]
    weights, forward, backward = refs[peers : peers + 3]
    out = refs[peers + 3 : 2 * peers + 3]
    (
        query,
        key,
        value,
        cot,
        conv,
        conv_grad,
        filter_grad,
        taps,
        key_short,
        value_short,
        signals,
        spectra,
        products,
        extra,
    ) = refs[2 * peers + 3 :]
    size = peers * tokens // PHASES
    tap_count = weights.shape[1]
    me = lax.axis_index("ctx")
    own = lanes_of(me)
    for ref in (query, key, value, cot, conv, conv_grad):
        clear_ends(ref)
    for ref in (key_short, value_short):
        ref[:, size:, :] = jnp.zeros((PHASES, PAD, LANES), F32)
    for step, source in zip(heard, arrived):
        start = (me ^ step) * tokens
        inner = pl.ds(pl.multiple_of(PAD + start, PAD), tokens)
        for at, ref in enumerate((query, key, value, cot)):
            ref[inner, :] = source[at * tokens : (at + 1) * tokens, :].astype(F32)
        taps[pl.ds(pl.multiple_of(start, PAD), tokens), :] = source[4 * tokens :, :].astype(F32)
    chunks = range(size // CHUNK)
    taps_of = [
        [weights[array, tap : tap + 1, own] for tap in range(tap_count)] for array in range(3)
    ]

    def rows_of(chunk):
        return slice(chunk * CHUNK, (chunk + 1) * CHUNK)

    def spectrum(at, real, imag):
        lanes = slice(at * LANES, (at + 1) * LANES)
        return forward_mix(
            [(spectra[r, real, lanes], spectra[r, imag, lanes]) for r in range(PHASES)]
        )

    def keep(at, real, imag, mixed):
        lanes = slice(at * LANES, (at + 1) * LANES)
        for r, pair in enumerate(inverse_mix(mixed)):
            for rows, part in zip((real, imag), pair):
                products[r, rows, lanes] = part

    for chunk in chunks:
        rows = rows_of(chunk)
        key_now = short_conv(phases_near(key, chunk, tap_count), taps_of[1])
        value_now = short_conv(phases_near(value, chunk, tap_count), taps_of[2])
        for r in range(PHASES):
            key_short[r, rows, :] = key_now[r]
            value_short[r, rows, :] = value_now[r]
            signals[r, rows, :LANES] = (key_now[r] * value_now[r]).astype(BF16)
            filt = taps[pl.ds(chunk * CHUNK * PHASES + r, CHUNK, stride=PHASES), :]
            signals[r, rows, LANES : 2 * LANES] = filt.astype(BF16)
    for r in range(PHASES):
        spectra[r, :, : 2 * LANES] = transform(forward[r], signals[r, :, : 2 * LANES])
    for chunk in chunks:
        rows = rows_of(chunk)
        query_now = short_conv(phases_near(query, chunk, tap_count), taps_of[0])
        cot_now = phases_near(cot, chunk, 1)
        for r in range(PHASES):
            signals[r, rows, 2 * LANES :] = (cot_now[r] * query_now[r]).astype(BF16)
    for r in range(PHASES):
        spectra[r, :, 2 * LANES :] = transform(forward[r], signals[r, :, 2 * LANES :])
    for step in range(size // ROWS):
        real = slice(step * ROWS, (step + 1) * ROWS)
        imag = slice(size + step * ROWS, size + (step + 1) * ROWS)
        prod, filt = spectrum(0, real, imag), spectrum(1, real, imag)
        for at, mixed in enumerate((prod, filt)):
            lanes = slice(at * LANES, (at + 1) * LANES)
            for q, pair in enumerate(mixed):
                spectra[q, real, lanes], spectra[q, imag, lanes] = pair
        keep(0, real, imag, times(prod, filt))
    for r in range(PHASES):
        result = transform(backward[r], products[r, :, :LANES].astype(BF16))
        conv[pl.ds(PAD + r, size, stride=PHASES), :] = result.astype(BF16).astype(F32)
    for step in range(size // ROWS):
        real = slice(step * ROWS, (step + 1) * ROWS)
        imag = slice(size + step * ROWS, size + (step + 1) * ROWS)
        grad = spectrum(2, real, imag)
        for at in range(2):
            lanes = slice(at * LANES, (at + 1) * LANES)
            known = [(spectra[q, real, lanes], spectra[q, imag, lanes]) for q in range(PHASES)]
            keep(2 - at, real, imag, conj_times(known, grad))
    for r in range(PHASES):
        result = transform(backward[r], products[r, :, LANES:].astype(BF16))
        conv_grad[pl.ds(PAD + r, size, stride=PHASES), :] = (
            result[:, :LANES].astype(BF16).astype(F32)
        )
        filter_grad[pl.ds(r, size, stride=PHASES), :] = result[:, LANES:] * grad_scale

    totals = [[None] * tap_count for _ in range(3)]

    def add_sums(array, signal, chunk, pre):
        near = phases_near(signal, chunk, tap_count)
        for tap in range(tap_count):
            totals[array][tap] = add_rows(
                totals[array][tap], [pre[r] * near[r - tap] for r in range(PHASES)]
            )

    for chunk in chunks:
        cot_now, conv_now = phases_near(cot, chunk, 1), phases_near(conv, chunk, 1)
        add_sums(0, query, chunk, [cot_now[r] * conv_now[r] for r in range(PHASES)])
    for chunk in chunks:
        rows = rows_of(chunk)
        grad_now = phases_near(conv_grad, chunk, 1)
        add_sums(1, key, chunk, [grad_now[r] * value_short[r, rows, :] for r in range(PHASES)])
        add_sums(2, value, chunk, [grad_now[r] * key_short[r, rows, :] for r in range(PHASES)])
    sums = [jnp.sum(total, axis=0, keepdims=True) for row in totals for total in row]
    rest = jnp.concatenate(sums, axis=0) * grad_scale
    extra[...] = jnp.zeros_like(extra)
    for piece in range(PIECES):
        rounded = rest.astype(BF16).astype(F32)
        extra[piece * len(sums) : (piece + 1) * len(sums), :] = rounded
        rest = rest - rounded
    for step, target in zip(told, out):
        start = (me ^ step) * tokens
        inner = pl.ds(pl.multiple_of(PAD + start, PAD), tokens)
        target[:tokens, :] = conv[inner, :].astype(BF16)
        target[tokens : 2 * tokens, :] = conv_grad[inner, :].astype(BF16)
        target[2 * tokens : 3 * tokens, :] = filter_grad[
            pl.ds(pl.multiple_of(start, PAD), tokens), :
        ].astype(BF16)
        before = pl.ds(pl.multiple_of(start, PAD), PAD)
        after = pl.ds(pl.multiple_of(PAD + start + tokens, PAD), PAD)
        at = PIECES * len(sums)
        for ref in (query, key, value):
            extra[at : at + RIM, :] = ref[before, :][PAD - RIM :]
            at += RIM
        row = pl.ds(pl.multiple_of((start + tokens) // PHASES, PAD), PAD)
        extra[at : at + RIM, :] = (cot[after, :] * conv[after, :])[:RIM]
        for short in (value_short, key_short):
            at += RIM
            shorts = jnp.concatenate([short[r, row, :][:1] for r in range(RIM)], axis=0)
            extra[at : at + RIM, :] = conv_grad[after, :][:RIM] * shorts
        target[3 * tokens :, :] = extra[...].astype(BF16)


def channel_step(arrived, heard, told, short_weights, tables, tokens):
    peers = len(arrived)
    seq_len = peers * tokens
    size = seq_len // PHASES
    extra = extra_rows(short_weights)[1]
    padded = pltpu.VMEM((seq_len + 2 * PAD, LANES), F32)
    plain = pltpu.VMEM((seq_len, LANES), F32)
    phases = pltpu.VMEM((PHASES, size + PAD, LANES), F32)
    return pl.pallas_call(
        functools.partial(channel_kernel, tokens, heard, told, 1.0 / math.sqrt(seq_len)),
        in_specs=in_vmem(peers + 3),
        out_specs=in_vmem(peers),
        out_shape=[jax.ShapeDtypeStruct((3 * tokens + extra, LANES), BF16)] * peers,
        scratch_shapes=[
            *[padded] * 6,
            plain,
            plain,
            phases,
            phases,
            pltpu.VMEM((PHASES, size, 3 * LANES), BF16),
            pltpu.VMEM((PHASES, 2 * size, 3 * LANES), F32),
            pltpu.VMEM((PHASES, 2 * size, 3 * LANES), F32),
            pltpu.VMEM((extra, LANES), F32),
        ],
        compiler_params=pltpu.CompilerParams(vmem_limit_bytes=VMEM_LIMIT),
        name="channel_operator",
    )(*arrived, short_weights, *tables)


def token_kernel(steps, sum_rows, carried, *refs):
    count_in = len(steps)
    arrived = refs[:count_in]
    query, key, value, cot, weights = refs[count_in : count_in + 5]
    results = refs[count_in + 5 + carried : count_in + 11 + carried]
    (gated, query_grad, key_grad, value_grad, filter_grad, short_grad, longer, pre, sems) = refs[
        count_in + 11 + carried :
    ]
    copies = []
    tokens = query.shape[0]
    tap_count = weights.shape[1]
    count = sum_rows // PIECES
    me = lax.axis_index("ctx")
    for slot, (step, source) in enumerate(zip(steps, arrived)):
        lanes = lanes_of(me ^ step)
        extra = source[3 * tokens :, :].astype(F32)

        def rim(at):
            return extra[sum_rows + at * RIM : sum_rows + (at + 1) * RIM]

        def short(array, signal):
            longer[array, PAD - RIM : PAD, :] = rim(array)
            longer[array, PAD :, :] = signal[:, lanes].astype(F32)
            summed = weights[array, 0:1, lanes] * longer[array, PAD:, :]
            for tap in range(1, tap_count):
                summed = (
                    summed
                    + weights[array, tap : tap + 1, lanes]
                    * longer[array, PAD - tap : PAD - tap + tokens, :]
                )
            return summed

        def taps_back(array, grad, target):
            pre[array, :tokens, :] = grad
            pre[array, tokens : tokens + RIM, :] = rim(3 + array)
            summed = weights[array, 0:1, lanes] * grad
            for tap in range(1, tap_count):
                summed = (
                    summed
                    + weights[array, tap : tap + 1, lanes] * pre[array, tap : tap + tokens, :]
                )
            target[slot] = summed.astype(BF16)

        conv = source[:tokens, :].astype(F32)
        conv_grad = source[tokens : 2 * tokens, :].astype(F32)
        gated[slot] = (short(0, query) * conv).astype(BF16)
        taps_back(0, cot[:, lanes].astype(F32) * conv, query_grad)
        taps_back(1, conv_grad * short(2, value), key_grad)
        taps_back(2, conv_grad * short(1, key), value_grad)
        filter_grad[slot] = source[2 * tokens : 3 * tokens, :].astype(F32)
        whole = extra[:count]
        for piece in range(1, PIECES):
            whole = whole + extra[piece * count : (piece + 1) * count]
        for row in range(count):
            which, tap = divmod(row, tap_count)
            short_grad[slot, which, tap : tap + 1, :] = whole[row : row + 1]
        held = (gated, query_grad, key_grad, value_grad, filter_grad, short_grad)
        for at, (source, target) in enumerate(zip(held, results)):
            place = target.at[:, :, lanes] if at == 5 else target.at[:, lanes]
            copies.append(pltpu.make_async_copy(source.at[slot], place, sems.at[slot, at]))
            copies[-1].start()
    for copy in copies:
        copy.wait()


def token_step(arrived, steps, query, key, value, cot, short_weights, begun=()):
    tokens, width = query.shape
    count = len(arrived)
    wide = jax.ShapeDtypeStruct((tokens, width), BF16)
    anywhere = pl.BlockSpec(memory_space=pl.ANY)
    return pl.pallas_call(
        functools.partial(token_kernel, steps, extra_rows(short_weights)[0], len(begun)),
        in_specs=in_vmem(count + 5) + [anywhere] * len(begun),
        out_specs=[anywhere] * 6,
        out_shape=[wide] * 4
        + [
            jax.ShapeDtypeStruct((tokens, width), F32),
            jax.ShapeDtypeStruct(short_weights.shape, F32),
        ],
        scratch_shapes=[
            *[pltpu.VMEM((count, tokens, LANES), BF16)] * 4,
            pltpu.VMEM((count, tokens, LANES), F32),
            pltpu.VMEM((count, *short_weights.shape[:2], LANES), F32),
            pltpu.VMEM((3, tokens + PAD, LANES), F32),
            pltpu.VMEM((3, tokens + PAD, LANES), F32),
            pltpu.SemaphoreType.DMA((count, 6)),
        ],
        input_output_aliases={count + 5 + at: at for at in range(len(begun))},
        compiler_params=pltpu.CompilerParams(vmem_limit_bytes=VMEM_LIMIT),
        cost_estimate=pl.CostEstimate(flops=0, bytes_accessed=4 * MIB, transcendentals=0),
        name="token_outputs",
    )(*arrived, query, key, value, cot, short_weights, *begun)


def channel_shards(query_proj, key_proj, value_proj, cotangent, filter_taps, short_weights):
    peers = lax.axis_size("ctx")
    tokens = query_proj.shape[0]
    tables = [jnp.asarray(table) for table in dft_tables(peers * tokens)]
    going, coming = partners(peers, False), partners(peers, True)
    sent = pack((query_proj, key_proj, value_proj, cotangent, filter_taps), going)
    arrived = exchange(sent, going)
    staged = stage((sent[0], short_weights, *tables), arrived[1])
    arrived[0] = staged[0]
    results = channel_step(arrived, going, coming, staged[1], staged[2:], tokens)
    back = exchange(results, coming)
    local = (query_proj, key_proj, value_proj, cotangent, short_weights)
    ends = [at for at in (4, 6) if at < peers] + [peers]
    begun, start = (), 0
    for end in ends:
        begun = token_step(back[start:end], coming[start:end], *local, begun)
        start = end
    return tuple(begun)


def from_behind(array, axis, by):
    peers = lax.axis_size(axis)
    pairs = [(i, i + by) for i in range(peers) if 0 <= i + by < peers]
    return lax.ppermute(array, axis, pairs)


def contract(form, left, right):
    return jnp.einsum(
        form, left, right, precision=lax.Precision.HIGHEST, preferred_element_type=jnp.float32
    )


def table_pair(rows, cols, period):
    row_ids = lax.broadcasted_iota(jnp.int32, (rows, cols), 0)
    col_ids = lax.broadcasted_iota(jnp.int32, (rows, cols), 1)
    angle = 2.0 * math.pi / period * (row_ids * col_ids % period).astype(jnp.float32)
    return (jnp.cos(angle), jnp.sin(angle))


def make_plan(seq_len):
    small_len = int(math.isqrt(2 * seq_len))
    while seq_len % small_len:
        small_len -= 1
    large_len = 2 * seq_len // small_len
    large_cos, large_sin = table_pair(large_len // 2, large_len, large_len)
    small_cos, small_sin = table_pair(small_len, small_len, small_len)
    twist_cos, twist_sin = table_pair(large_len, small_len, small_len * large_len)
    fwd_large = jnp.stack([large_cos, -large_sin], axis=1)
    fwd_small = jnp.stack([jnp.stack([small_cos, -small_sin]), jnp.stack([small_sin, small_cos])])
    inv_small = jnp.stack([jnp.stack([small_cos, small_sin]), jnp.stack([-small_sin, small_cos])])
    inv_large = jnp.stack([large_cos, -large_sin])
    return (small_len, large_len, fwd_large, fwd_small, inv_small, inv_large, twist_cos, twist_sin)


def forward_spec(signal, dft_plan):
    small_len, large_len, fwd_large, fwd_small, inv_small, inv_large, twist_cos, twist_sin = (
        dft_plan
    )
    cube = signal.reshape(signal.shape[0], large_len // 2, small_len)
    section_one = contract("cba,bpk->cpka", cube, fwd_large)
    real_one = section_one[:, 0]
    imag_one = section_one[:, 1]
    section_two = jnp.stack(
        [real_one * twist_cos + imag_one * twist_sin, imag_one * twist_cos - real_one * twist_sin],
        axis=1,
    )
    return contract("cpka,pqaj->cqkj", section_two, fwd_small)


def inverse_half(spec, dft_plan):
    small_len, large_len, fwd_large, fwd_small, inv_small, inv_large, twist_cos, twist_sin = (
        dft_plan
    )
    section_one = contract("cqkj,qpja->cpka", spec, inv_small)
    real_one = section_one[:, 0]
    imag_one = section_one[:, 1]
    section_two = jnp.stack(
        [real_one * twist_cos - imag_one * twist_sin, imag_one * twist_cos + real_one * twist_sin],
        axis=1,
    )
    signal = contract("cpka,pbk->cba", section_two, inv_large)
    return signal.reshape(signal.shape[0], -1) / float(small_len * large_len)


def complex_mul(left, right):
    left_real, left_imag = (left[:, 0], left[:, 1])
    right_real, right_imag = (right[:, 0], right[:, 1])
    return jnp.stack(
        [
            left_real * right_real - left_imag * right_imag,
            left_real * right_imag + left_imag * right_real,
        ],
        axis=1,
    )


def conj_mul(left, right):
    left_real, left_imag = (left[:, 0], left[:, 1])
    right_real, right_imag = (right[:, 0], right[:, 1])
    return jnp.stack(
        [
            left_real * right_real + left_imag * right_imag,
            left_real * right_imag - left_imag * right_real,
        ],
        axis=1,
    )


def conv_forward(prod_chan, filter_spec, dft_plan):
    prod_spec = forward_spec(prod_chan.astype(jnp.float32), dft_plan)
    conv_chan = inverse_half(complex_mul(prod_spec, filter_spec), dft_plan).astype(jnp.bfloat16)
    return (conv_chan, prod_spec)


def conv_backward(grad_chan, filter_spec, prod_spec, dft_plan, grad_scale):
    grad_spec = forward_spec(grad_chan.astype(jnp.float32), dft_plan)
    dconv_chan = inverse_half(conj_mul(filter_spec, grad_spec), dft_plan).astype(jnp.bfloat16)
    dfilter_chan = inverse_half(conj_mul(prod_spec, grad_spec), dft_plan) * grad_scale
    return (dconv_chan, dfilter_chan)


def receive_filter(filter_taps, dft_plan):
    filter_chan = lax.all_to_all(filter_taps.T, "ctx", split_axis=0, concat_axis=1, tiled=True)
    return forward_spec(filter_chan, dft_plan)


def return_filter(dfilter_chan):
    return (
        lax.all_to_all(
            dfilter_chan.astype(jnp.bfloat16), "ctx", split_axis=1, concat_axis=0, tiled=True
        )
        .astype(dfilter_chan.dtype)
        .T
    )


def causal_taps(extended, weights, length, axis):
    rim_rows = len(weights) - 1
    summed = weights[0] * lax.slice_in_dim(extended, rim_rows, rim_rows + length, axis=axis)
    for offset in range(1, len(weights)):
        summed = summed + weights[offset] * lax.slice_in_dim(
            extended, rim_rows - offset, rim_rows - offset + length, axis=axis
        )
    return summed


def reverse_taps(extended, weights, length, axis):
    summed = weights[0] * lax.slice_in_dim(extended, 0, length, axis=axis)
    for offset in range(1, len(weights)):
        summed = summed + weights[offset] * lax.slice_in_dim(
            extended, offset, offset + length, axis=axis
        )
    return summed


def tap_grads(grad_in, extended, tap_count, length, axis):
    rim_rows = tap_count - 1
    rows = [
        jnp.sum(
            grad_in
            * lax.slice_in_dim(extended, rim_rows - offset, rim_rows - offset + length, axis=axis),
            axis=axis,
        )
        for offset in range(tap_count)
    ]
    return jnp.stack(rows, axis=1)


def spread_shards(query_proj, key_proj, value_proj, cotangent, filter_taps, short_weights):
    tokens = query_proj.shape[0]
    tap_count = short_weights.shape[1]
    rim_rows = tap_count - 1
    seq_len = tokens * lax.axis_size("ctx")
    grad_scale = 1.0 / math.sqrt(seq_len)
    dft_plan = make_plan(seq_len)
    stacked = jnp.stack([query_proj, key_proj, value_proj])
    prev_rim = from_behind(stacked[:, tokens - rim_rows :], "ctx", 1)
    extended = jnp.concatenate([prev_rim, stacked], axis=1).astype(jnp.float32)
    weights = [short_weights[:, offset, None, :] for offset in range(tap_count)]
    short_out = causal_taps(extended, weights, tokens, 1)
    product = (short_out[1] * short_out[2]).astype(jnp.bfloat16)
    cot_wide = cotangent.astype(jnp.float32)
    gate_grad = (cot_wide * short_out[0]).astype(jnp.bfloat16)
    filter_spec = receive_filter(filter_taps, dft_plan)
    prod_chan = lax.all_to_all(product.T, "ctx", split_axis=0, concat_axis=1, tiled=True)
    conv_chan, prod_spec = conv_forward(prod_chan, filter_spec, dft_plan)
    conv_tok = lax.all_to_all(conv_chan, "ctx", split_axis=1, concat_axis=0, tiled=True)
    grad_chan = lax.all_to_all(gate_grad.T, "ctx", split_axis=0, concat_axis=1, tiled=True)
    dconv_chan, dfilter_chan = conv_backward(
        grad_chan, filter_spec, prod_spec, dft_plan, grad_scale
    )
    dconv_tok = lax.all_to_all(dconv_chan, "ctx", split_axis=1, concat_axis=0, tiled=True)
    filter_grad = return_filter(dfilter_chan)
    conv_wide = conv_tok.T.astype(jnp.float32)
    dconv_wide = dconv_tok.T.astype(jnp.float32)
    gated = (short_out[0] * conv_wide).astype(jnp.bfloat16)
    token_grads = jnp.stack(
        [cot_wide * conv_wide, dconv_wide * short_out[2], dconv_wide * short_out[1]]
    )
    next_rim = from_behind(token_grads[:, :rim_rows], "ctx", -1)
    grad_ext = jnp.concatenate([token_grads, next_rim], axis=1)
    inputs_grad = reverse_taps(grad_ext, weights, tokens, 1).astype(jnp.bfloat16)
    weight_part = tap_grads(token_grads, extended, tap_count, tokens, 1)
    short_grad = lax.psum(weight_part, "ctx") * grad_scale
    results = (gated, inputs_grad[0], inputs_grad[1], inputs_grad[2])
    return (results[0], results[1], results[2], results[3], filter_grad, short_grad)


def fits(query_proj, short_weights):
    peers = lax.axis_size("ctx")
    tokens, width = query_proj.shape
    tap_count = short_weights.shape[1]
    return (
        width == peers * LANES
        and peers.bit_count() == 1
        and tokens % (PHASES * CHUNK) == 0
        and tap_count == RIM + 1
        and peers * tokens <= 2048
    )


def shards(*arrays):
    return channel_shards(*arrays) if fits(arrays[0], arrays[5]) else spread_shards(*arrays)


def solution(mesh):
    placed = (
        P("ctx", "tp"),
        P("ctx", "tp"),
        P("ctx", "tp"),
        P("ctx", "tp"),
        P("ctx", "tp"),
        P(None, None, "tp"),
    )
    return jax.shard_map(
        shards,
        mesh=mesh,
        in_specs=placed,
        out_specs=(
            P("ctx", "tp"),
            P("ctx", "tp"),
            P("ctx", "tp"),
            P("ctx", "tp"),
            P("ctx", "tp"),
            P(None, None, "tp"),
        ),
        check_vma=False,
    )
```

```python
import functools
import math

import jax
import jax.numpy as jnp
import numpy as np
from jax import lax
from jax.experimental import pallas as pl
from jax.experimental.pallas import tpu as pltpu
from jax.sharding import PartitionSpec as P

F32 = jnp.float32
BF16 = jnp.bfloat16
LANES = 128
PHASES = 4
TILE = 16
PAD = 8
CHUNK = 16
ROWS = 8
RIM = 2
PIECES = 2
MIB = 1024 * 1024
VMEM_LIMIT = 24 * MIB
PACK_VMEM = 53862 * 1024


def partners(peers, diagonal_first):
    def rank(step):
        links, other_core = (step >> 1).bit_count(), step & 1
        if links == 0:
            return (1 if diagonal_first else 5, 0)
        if links == 1:
            return (4 if other_core else 3, -step)
        return (2 * other_core if diagonal_first else 3.5, other_core)

    return [0] + sorted(range(1, peers), key=rank)


def exchange(blocks, steps):
    peers = len(blocks)
    got = [blocks[0]]
    for step, block in list(zip(steps, blocks))[1:]:
        got.append(lax.ppermute(block, "ctx", [(i, i ^ step) for i in range(peers)]))
    return got


def in_vmem(count):
    return [pl.BlockSpec(memory_space=pltpu.VMEM)] * count


def lanes_of(place):
    return pl.ds(pl.multiple_of(place * LANES, LANES), LANES)


def pack_kernel(count, steps, *refs):
    sources, packed = refs[:count], refs[count : count + len(steps)]
    held, sems = refs[count + len(steps) : -1], refs[-1]
    tokens = sources[0].shape[0]
    me = lax.axis_index("ctx")
    arriving = [
        pltpu.make_async_copy(source, target, sems.at[at])
        for at, (source, target) in enumerate(zip(sources, held))
    ]
    for copy in arriving:
        copy.start()
    for at, source in enumerate(held):
        arriving[at].wait()
        rows = slice(at * tokens, (at + 1) * tokens)
        for step, target in zip(steps, packed):
            target[rows, :] = source[:, lanes_of(me ^ step)].astype(BF16)


def pack(arrays, steps):
    tokens = arrays[0].shape[0]
    count = len(arrays)
    return pl.pallas_call(
        functools.partial(pack_kernel, count, steps),
        in_specs=[pl.BlockSpec(memory_space=pl.ANY)] * count,
        out_specs=in_vmem(len(steps)),
        out_shape=[jax.ShapeDtypeStruct((count * tokens, LANES), BF16)] * len(steps),
        scratch_shapes=[
            *[pltpu.VMEM(array.shape, array.dtype) for array in arrays],
            pltpu.SemaphoreType.DMA((count,)),
        ],
        compiler_params=pltpu.CompilerParams(vmem_limit_bytes=PACK_VMEM),
        cost_estimate=pl.CostEstimate(flops=0, bytes_accessed=8 * MIB, transcendentals=0),
        name="pack_inputs",
    )(*arrays)


@functools.lru_cache(maxsize=None)
def dft_tables(seq_len):
    size = seq_len // PHASES
    k = np.arange(size, dtype=np.int64)[:, None]
    m = np.arange(size, dtype=np.int64)[None, :]
    forward = []
    for phase in range(PHASES):
        turns = ((4 * k + 1) * (PHASES * m + phase)) % (4 * seq_len)
        angle = 2.0 * np.pi / (4 * seq_len) * turns
        forward.append(np.concatenate([np.cos(angle), -np.sin(angle)], axis=0))
    forward = np.stack(forward)
    backward = np.swapaxes(forward, 1, 2) / seq_len

    return forward.astype(BF16), backward.astype(BF16)


def forward_mix(parts):
    (r0, i0), (r1, i1), (r2, i2), (r3, i3) = parts
    ar, ai, br, bi = r0 + r2, i0 + i2, r0 - r2, i0 - i2
    cr, ci, dr, di = r1 + r3, i1 + i3, r1 - r3, i1 - i3
    return ((ar + cr, ai + ci), (br + di, bi - dr), (ar - cr, ai - ci), (br - di, bi + dr))


def inverse_mix(parts):
    (r0, i0), (r1, i1), (r2, i2), (r3, i3) = parts
    ar, ai, br, bi = r0 + r2, i0 + i2, r0 - r2, i0 - i2
    cr, ci, dr, di = r1 + r3, i1 + i3, r1 - r3, i1 - i3
    return ((ar + cr, ai + ci), (br - di, bi + dr), (ar - cr, ai - ci), (br + di, bi - dr))


def times(left, right):
    return tuple(
        (lr * rr - li * ri, lr * ri + li * rr) for (lr, li), (rr, ri) in zip(left, right)
    )


def conj_times(left, right):
    return tuple(
        (lr * rr + li * ri, lr * ri - li * rr) for (lr, li), (rr, ri) in zip(left, right)
    )


def transform(table, signal):
    return jnp.dot(table, signal, preferred_element_type=F32)


def phases_near(ref, chunk, tap_count):
    start = PAD + chunk * CHUNK * PHASES
    return {
        offset: ref[pl.ds(start + offset, CHUNK, stride=PHASES), :]
        for offset in range(1 - tap_count, PHASES)
    }


def short_conv(near, taps):
    results = []
    for r in range(PHASES):
        summed = taps[0] * near[r]
        for at in range(1, len(taps)):
            summed = summed + taps[at] * near[r - at]
        results.append(summed)
    return results


def add_rows(total, terms):
    for term in terms:
        folded = jnp.sum(term.reshape(CHUNK // 8, 8, LANES), axis=0)
        total = folded if total is None else total + folded
    return total


def clear_ends(ref):
    ref[:PAD, :] = jnp.zeros((PAD, LANES), F32)
    ref[ref.shape[0] - PAD :, :] = jnp.zeros((PAD, LANES), F32)


def stage_kernel(count, *refs):
    sources, targets, sems = refs[:count], refs[count + 1 : 2 * count + 1], refs[2 * count + 1]
    copies = [
        pltpu.make_async_copy(source, target, sems.at[at])
        for at, (source, target) in enumerate(zip(sources, targets))
    ]
    for copy in copies:
        copy.start()
    for copy in copies:
        copy.wait()


def stage(arrays, after):
    count = len(arrays)
    return pl.pallas_call(
        functools.partial(stage_kernel, count),
        in_specs=[pl.BlockSpec(memory_space=pl.ANY)] * (count + 1),
        out_specs=in_vmem(count),
        out_shape=[jax.ShapeDtypeStruct(array.shape, array.dtype) for array in arrays],
        scratch_shapes=[pltpu.SemaphoreType.DMA((count,))],
        compiler_params=pltpu.CompilerParams(vmem_limit_bytes=8 * MIB),
        cost_estimate=pl.CostEstimate(flops=0, bytes_accessed=8 * MIB, transcendentals=0),
        name="stage_tables",
    )(*arrays, after)


def extra_rows(short_weights):
    sums = PIECES * short_weights.shape[0] * short_weights.shape[1]
    return sums, -(-(sums + 6 * RIM) // TILE) * TILE


def channel_kernel(tokens, heard, told, grad_scale, *refs):
    peers = len(heard)
    arrived = refs[:peers]
    weights, forward, backward = refs[peers : peers + 3]
    out = refs[peers + 3 : 2 * peers + 3]
    (
        query,
        key,
        value,
        cot,
        conv,
        conv_grad,
        filter_grad,
        filt,
        key_short,
        value_short,
        signals,
        spectra,
        products,
        extra,
    ) = refs[2 * peers + 3 :]
    size = peers * tokens // PHASES
    per = tokens // PHASES
    tap_count = weights.shape[1]
    me = lax.axis_index("ctx")
    own = lanes_of(me)
    for ref in (query, key, value, cot):
        clear_ends(ref)
    for ref in (key_short, value_short, conv, conv_grad):
        ref[:, size:, :] = jnp.zeros((PHASES, PAD, LANES), F32)
    for step, source in zip(heard, arrived):
        start = (me ^ step) * tokens
        inner = pl.ds(pl.multiple_of(PAD + start, PAD), tokens)
        for at, ref in enumerate((query, key, value, cot)):
            ref[inner, :] = source[at * tokens : (at + 1) * tokens, :].astype(F32)
        filt[pl.ds(pl.multiple_of(start, PAD), tokens), :] = source[4 * tokens :, :].astype(F32)
    chunks = range(size // CHUNK)
    taps_of = [
        [weights[array, tap : tap + 1, own] for tap in range(tap_count)] for array in range(3)
    ]

    def rows_of(chunk):
        return slice(chunk * CHUNK, (chunk + 1) * CHUNK)

    def spectrum(at, real, imag):
        lanes = slice(at * LANES, (at + 1) * LANES)
        return forward_mix(
            [(spectra[r, real, lanes], spectra[r, imag, lanes]) for r in range(PHASES)]
        )

    def keep(at, real, imag, mixed):
        lanes = slice(at * LANES, (at + 1) * LANES)
        for r, pair in enumerate(inverse_mix(mixed)):
            for rows, part in zip((real, imag), pair):
                products[r, rows, lanes] = part

    for chunk in chunks:
        rows = rows_of(chunk)
        key_now = short_conv(phases_near(key, chunk, tap_count), taps_of[1])
        value_now = short_conv(phases_near(value, chunk, tap_count), taps_of[2])
        for r in range(PHASES):
            key_short[r, rows, :] = key_now[r]
            value_short[r, rows, :] = value_now[r]
            signals[r, rows, :LANES] = (key_now[r] * value_now[r]).astype(BF16)
            filt_now = filt[pl.ds(chunk * CHUNK * PHASES + r, CHUNK, stride=PHASES), :]
            signals[r, rows, LANES : 2 * LANES] = filt_now.astype(BF16)
    for r in range(PHASES):
        spectra[r, :, : 2 * LANES] = transform(forward[r], signals[r, :, : 2 * LANES])
    for chunk in chunks:
        rows = rows_of(chunk)
        query_now = short_conv(phases_near(query, chunk, tap_count), taps_of[0])
        cot_now = phases_near(cot, chunk, 1)
        for r in range(PHASES):
            signals[r, rows, 2 * LANES :] = (cot_now[r] * query_now[r]).astype(BF16)
    for r in range(PHASES):
        spectra[r, :, 2 * LANES :] = transform(forward[r], signals[r, :, 2 * LANES :])
    for step in range(size // ROWS):
        real = slice(step * ROWS, (step + 1) * ROWS)
        imag = slice(size + step * ROWS, size + (step + 1) * ROWS)
        prod, filt = spectrum(0, real, imag), spectrum(1, real, imag)
        for at, mixed in enumerate((prod, filt)):
            lanes = slice(at * LANES, (at + 1) * LANES)
            for q, pair in enumerate(mixed):
                spectra[q, real, lanes], spectra[q, imag, lanes] = pair
        keep(0, real, imag, times(prod, filt))
    for r in range(PHASES):
        result = transform(backward[r], products[r, :, :LANES].astype(BF16))
        conv[r, :size, :] = result.astype(BF16).astype(F32)
    for step in range(size // ROWS):
        real = slice(step * ROWS, (step + 1) * ROWS)
        imag = slice(size + step * ROWS, size + (step + 1) * ROWS)
        grad = spectrum(2, real, imag)
        for at in range(2):
            lanes = slice(at * LANES, (at + 1) * LANES)
            known = [(spectra[q, real, lanes], spectra[q, imag, lanes]) for q in range(PHASES)]
            keep(2 - at, real, imag, conj_times(known, grad))
    for r in range(PHASES):
        result = transform(backward[r], products[r, :, LANES:].astype(BF16))
        conv_grad[r, :size, :] = result[:, :LANES].astype(BF16).astype(F32)
        filter_grad[r] = (result[:, LANES:] * grad_scale).astype(BF16)

    totals = [[None] * tap_count for _ in range(3)]

    def add_sums(array, signal, chunk, pre):
        near = phases_near(signal, chunk, tap_count)
        for tap in range(tap_count):
            totals[array][tap] = add_rows(
                totals[array][tap], [pre[r] * near[r - tap] for r in range(PHASES)]
            )

    for chunk in chunks:
        rows = rows_of(chunk)
        cot_now = phases_near(cot, chunk, 1)
        add_sums(0, query, chunk, [cot_now[r] * conv[r, rows, :] for r in range(PHASES)])
    for chunk in chunks:
        rows = rows_of(chunk)
        grad_now = [conv_grad[r, rows, :] for r in range(PHASES)]
        add_sums(1, key, chunk, [grad_now[r] * value_short[r, rows, :] for r in range(PHASES)])
        add_sums(2, value, chunk, [grad_now[r] * key_short[r, rows, :] for r in range(PHASES)])
    sums = [jnp.sum(total, axis=0, keepdims=True) for row in totals for total in row]
    rest = jnp.concatenate(sums, axis=0) * grad_scale
    extra[...] = jnp.zeros_like(extra)
    for piece in range(PIECES):
        rounded = rest.astype(BF16).astype(F32)
        extra[piece * len(sums) : (piece + 1) * len(sums), :] = rounded
        rest = rest - rounded
    for step, target in zip(told, out):
        start = (me ^ step) * tokens
        rows = pl.ds(pl.multiple_of((me ^ step) * per, per), per)
        for at, ref in enumerate((conv, conv_grad, filter_grad)):
            for r in range(PHASES):
                begin = at * tokens + r * per
                target[begin : begin + per, :] = ref[r, rows, :].astype(BF16)
        before = pl.ds(pl.multiple_of(start, PAD), PAD)
        after = pl.ds(pl.multiple_of(PAD + start + tokens, PAD), PAD)
        at = PIECES * len(sums)
        for ref in (query, key, value):
            extra[at : at + RIM, :] = ref[before, :][PAD - RIM :]
            at += RIM
        row = pl.ds(pl.multiple_of((me ^ step) * per + per, per), PAD)

        def first(ref):
            return jnp.concatenate([ref[r, row, :][:1] for r in range(RIM)], axis=0)

        grad_first = first(conv_grad)
        pre = (
            cot[after, :][:RIM] * first(conv),
            grad_first * first(value_short),
            grad_first * first(key_short),
        )
        for value_at in pre:
            extra[at : at + RIM, :] = value_at
            at += RIM
        target[3 * tokens :, :] = extra[...].astype(BF16)


def channel_step(arrived, heard, told, short_weights, tables, tokens):
    peers = len(arrived)
    seq_len = peers * tokens
    size = seq_len // PHASES
    extra = extra_rows(short_weights)[1]
    padded = pltpu.VMEM((seq_len + 2 * PAD, LANES), F32)
    phases = pltpu.VMEM((PHASES, size + PAD, LANES), F32)
    return pl.pallas_call(
        functools.partial(channel_kernel, tokens, heard, told, 1.0 / math.sqrt(seq_len)),
        in_specs=in_vmem(peers + 3),
        out_specs=in_vmem(peers),
        out_shape=[jax.ShapeDtypeStruct((3 * tokens + extra, LANES), BF16)] * peers,
        scratch_shapes=[
            *[padded] * 4,
            phases,
            phases,
            pltpu.VMEM((PHASES, size, LANES), BF16),
            pltpu.VMEM((seq_len, LANES), F32),
            phases,
            phases,
            pltpu.VMEM((PHASES, size, 3 * LANES), BF16),
            pltpu.VMEM((PHASES, 2 * size, 3 * LANES), F32),
            pltpu.VMEM((PHASES, 2 * size, 3 * LANES), F32),
            pltpu.VMEM((extra, LANES), F32),
        ],
        compiler_params=pltpu.CompilerParams(vmem_limit_bytes=VMEM_LIMIT),
        name="channel_operator",
    )(*arrived, short_weights, *tables)


def token_kernel(steps, sum_rows, carried, *refs):
    count_in = len(steps)
    arrived = refs[:count_in]
    query, key, value, cot, weights = refs[count_in : count_in + 5]
    results = refs[count_in + 5 + carried : count_in + 11 + carried]
    gated, query_grad, key_grad, value_grad, filter_grad, short_grad, *scratch = refs[
        count_in + 11 + carried :
    ]
    longer, pre, ordered, sems = scratch
    copies = []
    tokens = query.shape[0]
    per = tokens // PHASES
    tap_count = weights.shape[1]
    count = sum_rows // PIECES
    me = lax.axis_index("ctx")
    for slot, (step, source) in enumerate(zip(steps, arrived)):
        lanes = lanes_of(me ^ step)
        extra = source[3 * tokens :, :].astype(F32)

        def rim(at):
            return extra[sum_rows + at * RIM : sum_rows + (at + 1) * RIM]

        def short(array, signal):
            longer[array, PAD - RIM : PAD, :] = rim(array)
            longer[array, PAD :, :] = signal[:, lanes].astype(F32)
            summed = weights[array, 0:1, lanes] * longer[array, PAD:, :]
            for tap in range(1, tap_count):
                summed = (
                    summed
                    + weights[array, tap : tap + 1, lanes]
                    * longer[array, PAD - tap : PAD - tap + tokens, :]
                )
            return summed

        def taps_back(array, grad, target):
            pre[array, :tokens, :] = grad
            pre[array, tokens : tokens + RIM, :] = rim(3 + array)
            summed = weights[array, 0:1, lanes] * grad
            for tap in range(1, tap_count):
                summed = (
                    summed
                    + weights[array, tap : tap + 1, lanes] * pre[array, tap : tap + tokens, :]
                )
            target[slot] = summed.astype(BF16)

        for at in range(3):
            for r in range(PHASES):
                begin = at * tokens + r * per
                part = source[begin : begin + per, :].astype(F32)
                if at < 2:
                    ordered[at, pl.ds(r, per, stride=PHASES), :] = part
                else:
                    filter_grad[slot, pl.ds(r, per, stride=PHASES), :] = part
        conv, conv_grad = ordered[0], ordered[1]
        gated[slot] = (short(0, query) * conv).astype(BF16)
        taps_back(0, cot[:, lanes].astype(F32) * conv, query_grad)
        taps_back(1, conv_grad * short(2, value), key_grad)
        taps_back(2, conv_grad * short(1, key), value_grad)
        whole = extra[:count]
        for piece in range(1, PIECES):
            whole = whole + extra[piece * count : (piece + 1) * count]
        for row in range(count):
            which, tap = divmod(row, tap_count)
            short_grad[slot, which, tap : tap + 1, :] = whole[row : row + 1]
        held = (gated, query_grad, key_grad, value_grad, filter_grad, short_grad)
        for at, (source, target) in enumerate(zip(held, results)):
            place = target.at[:, :, lanes] if at == 5 else target.at[:, lanes]
            copies.append(pltpu.make_async_copy(source.at[slot], place, sems.at[slot, at]))
            copies[-1].start()
    for copy in copies:
        copy.wait()


def token_step(arrived, steps, query, key, value, cot, short_weights, begun=()):
    tokens, width = query.shape
    count = len(arrived)
    wide = jax.ShapeDtypeStruct((tokens, width), BF16)
    anywhere = pl.BlockSpec(memory_space=pl.ANY)
    return pl.pallas_call(
        functools.partial(token_kernel, steps, extra_rows(short_weights)[0], len(begun)),
        in_specs=in_vmem(count + 5) + [anywhere] * len(begun),
        out_specs=[anywhere] * 6,
        out_shape=[wide] * 4
        + [
            jax.ShapeDtypeStruct((tokens, width), F32),
            jax.ShapeDtypeStruct(short_weights.shape, F32),
        ],
        scratch_shapes=[
            *[pltpu.VMEM((count, tokens, LANES), BF16)] * 4,
            pltpu.VMEM((count, tokens, LANES), F32),
            pltpu.VMEM((count, *short_weights.shape[:2], LANES), F32),
            pltpu.VMEM((3, tokens + PAD, LANES), F32),
            pltpu.VMEM((3, tokens + PAD, LANES), F32),
            pltpu.VMEM((2, tokens, LANES), F32),
            pltpu.SemaphoreType.DMA((count, 6)),
        ],
        input_output_aliases={count + 5 + at: at for at in range(len(begun))},
        compiler_params=pltpu.CompilerParams(vmem_limit_bytes=VMEM_LIMIT),
        cost_estimate=pl.CostEstimate(flops=0, bytes_accessed=4 * MIB, transcendentals=0),
        name="token_outputs",
    )(*arrived, query, key, value, cot, short_weights, *begun)


def channel_shards(query_proj, key_proj, value_proj, cotangent, filter_taps, short_weights):
    peers = lax.axis_size("ctx")
    tokens = query_proj.shape[0]
    tables = [jnp.asarray(table) for table in dft_tables(peers * tokens)]
    going, coming = partners(peers, False), partners(peers, True)
    sent = pack((query_proj, key_proj, value_proj, cotangent, filter_taps), going)
    arrived = exchange(sent, going)
    staged = stage((sent[0], short_weights, *tables), arrived[1])
    arrived[0] = staged[0]
    results = channel_step(arrived, going, coming, staged[1], staged[2:], tokens)
    back = exchange(results, coming)
    local = (query_proj, key_proj, value_proj, cotangent, short_weights)
    ends = [at for at in (4, 6) if at < peers] + [peers]
    begun, start = (), 0
    for end in ends:
        begun = token_step(back[start:end], coming[start:end], *local, begun)
        start = end
    return tuple(begun)


def from_behind(array, axis, by):
    peers = lax.axis_size(axis)
    pairs = [(i, i + by) for i in range(peers) if 0 <= i + by < peers]
    return lax.ppermute(array, axis, pairs)


def contract(form, left, right):
    return jnp.einsum(
        form, left, right, precision=lax.Precision.HIGHEST, preferred_element_type=jnp.float32
    )


def table_pair(rows, cols, period):
    row_ids = lax.broadcasted_iota(jnp.int32, (rows, cols), 0)
    col_ids = lax.broadcasted_iota(jnp.int32, (rows, cols), 1)
    angle = 2.0 * math.pi / period * (row_ids * col_ids % period).astype(jnp.float32)
    return (jnp.cos(angle), jnp.sin(angle))


def make_plan(seq_len):
    small_len = int(math.isqrt(2 * seq_len))
    while seq_len % small_len:
        small_len -= 1
    large_len = 2 * seq_len // small_len
    large_cos, large_sin = table_pair(large_len // 2, large_len, large_len)
    small_cos, small_sin = table_pair(small_len, small_len, small_len)
    twist_cos, twist_sin = table_pair(large_len, small_len, small_len * large_len)
    fwd_large = jnp.stack([large_cos, -large_sin], axis=1)
    fwd_small = jnp.stack([jnp.stack([small_cos, -small_sin]), jnp.stack([small_sin, small_cos])])
    inv_small = jnp.stack([jnp.stack([small_cos, small_sin]), jnp.stack([-small_sin, small_cos])])
    inv_large = jnp.stack([large_cos, -large_sin])
    return (small_len, large_len, fwd_large, fwd_small, inv_small, inv_large, twist_cos, twist_sin)


def forward_spec(signal, dft_plan):
    small_len, large_len, fwd_large, fwd_small, inv_small, inv_large, twist_cos, twist_sin = (
        dft_plan
    )
    cube = signal.reshape(signal.shape[0], large_len // 2, small_len)
    section_one = contract("cba,bpk->cpka", cube, fwd_large)
    real_one = section_one[:, 0]
    imag_one = section_one[:, 1]
    section_two = jnp.stack(
        [real_one * twist_cos + imag_one * twist_sin, imag_one * twist_cos - real_one * twist_sin],
        axis=1,
    )
    return contract("cpka,pqaj->cqkj", section_two, fwd_small)


def inverse_half(spec, dft_plan):
    small_len, large_len, fwd_large, fwd_small, inv_small, inv_large, twist_cos, twist_sin = (
        dft_plan
    )
    section_one = contract("cqkj,qpja->cpka", spec, inv_small)
    real_one = section_one[:, 0]
    imag_one = section_one[:, 1]
    section_two = jnp.stack(
        [real_one * twist_cos - imag_one * twist_sin, imag_one * twist_cos + real_one * twist_sin],
        axis=1,
    )
    signal = contract("cpka,pbk->cba", section_two, inv_large)
    return signal.reshape(signal.shape[0], -1) / float(small_len * large_len)


def complex_mul(left, right):
    left_real, left_imag = (left[:, 0], left[:, 1])
    right_real, right_imag = (right[:, 0], right[:, 1])
    return jnp.stack(
        [
            left_real * right_real - left_imag * right_imag,
            left_real * right_imag + left_imag * right_real,
        ],
        axis=1,
    )


def conj_mul(left, right):
    left_real, left_imag = (left[:, 0], left[:, 1])
    right_real, right_imag = (right[:, 0], right[:, 1])
    return jnp.stack(
        [
            left_real * right_real + left_imag * right_imag,
            left_real * right_imag - left_imag * right_real,
        ],
        axis=1,
    )


def conv_forward(prod_chan, filter_spec, dft_plan):
    prod_spec = forward_spec(prod_chan.astype(jnp.float32), dft_plan)
    conv_chan = inverse_half(complex_mul(prod_spec, filter_spec), dft_plan).astype(jnp.bfloat16)
    return (conv_chan, prod_spec)


def conv_backward(grad_chan, filter_spec, prod_spec, dft_plan, grad_scale):
    grad_spec = forward_spec(grad_chan.astype(jnp.float32), dft_plan)
    dconv_chan = inverse_half(conj_mul(filter_spec, grad_spec), dft_plan).astype(jnp.bfloat16)
    dfilter_chan = inverse_half(conj_mul(prod_spec, grad_spec), dft_plan) * grad_scale
    return (dconv_chan, dfilter_chan)


def receive_filter(filter_taps, dft_plan):
    filter_chan = lax.all_to_all(filter_taps.T, "ctx", split_axis=0, concat_axis=1, tiled=True)
    return forward_spec(filter_chan, dft_plan)


def return_filter(dfilter_chan):
    return (
        lax.all_to_all(
            dfilter_chan.astype(jnp.bfloat16), "ctx", split_axis=1, concat_axis=0, tiled=True
        )
        .astype(dfilter_chan.dtype)
        .T
    )


def causal_taps(extended, weights, length, axis):
    rim_rows = len(weights) - 1
    summed = weights[0] * lax.slice_in_dim(extended, rim_rows, rim_rows + length, axis=axis)
    for offset in range(1, len(weights)):
        summed = summed + weights[offset] * lax.slice_in_dim(
            extended, rim_rows - offset, rim_rows - offset + length, axis=axis
        )
    return summed


def reverse_taps(extended, weights, length, axis):
    summed = weights[0] * lax.slice_in_dim(extended, 0, length, axis=axis)
    for offset in range(1, len(weights)):
        summed = summed + weights[offset] * lax.slice_in_dim(
            extended, offset, offset + length, axis=axis
        )
    return summed


def tap_grads(grad_in, extended, tap_count, length, axis):
    rim_rows = tap_count - 1
    rows = [
        jnp.sum(
            grad_in
            * lax.slice_in_dim(extended, rim_rows - offset, rim_rows - offset + length, axis=axis),
            axis=axis,
        )
        for offset in range(tap_count)
    ]
    return jnp.stack(rows, axis=1)


def spread_shards(query_proj, key_proj, value_proj, cotangent, filter_taps, short_weights):
    tokens = query_proj.shape[0]
    tap_count = short_weights.shape[1]
    rim_rows = tap_count - 1
    seq_len = tokens * lax.axis_size("ctx")
    grad_scale = 1.0 / math.sqrt(seq_len)
    dft_plan = make_plan(seq_len)
    stacked = jnp.stack([query_proj, key_proj, value_proj])
    prev_rim = from_behind(stacked[:, tokens - rim_rows :], "ctx", 1)
    extended = jnp.concatenate([prev_rim, stacked], axis=1).astype(jnp.float32)
    weights = [short_weights[:, offset, None, :] for offset in range(tap_count)]
    short_out = causal_taps(extended, weights, tokens, 1)
    product = (short_out[1] * short_out[2]).astype(jnp.bfloat16)
    cot_wide = cotangent.astype(jnp.float32)
    gate_grad = (cot_wide * short_out[0]).astype(jnp.bfloat16)
    filter_spec = receive_filter(filter_taps, dft_plan)
    prod_chan = lax.all_to_all(product.T, "ctx", split_axis=0, concat_axis=1, tiled=True)
    conv_chan, prod_spec = conv_forward(prod_chan, filter_spec, dft_plan)
    conv_tok = lax.all_to_all(conv_chan, "ctx", split_axis=1, concat_axis=0, tiled=True)
    grad_chan = lax.all_to_all(gate_grad.T, "ctx", split_axis=0, concat_axis=1, tiled=True)
    dconv_chan, dfilter_chan = conv_backward(
        grad_chan, filter_spec, prod_spec, dft_plan, grad_scale
    )
    dconv_tok = lax.all_to_all(dconv_chan, "ctx", split_axis=1, concat_axis=0, tiled=True)
    filter_grad = return_filter(dfilter_chan)
    conv_wide = conv_tok.T.astype(jnp.float32)
    dconv_wide = dconv_tok.T.astype(jnp.float32)
    gated = (short_out[0] * conv_wide).astype(jnp.bfloat16)
    token_grads = jnp.stack(
        [cot_wide * conv_wide, dconv_wide * short_out[2], dconv_wide * short_out[1]]
    )
    next_rim = from_behind(token_grads[:, :rim_rows], "ctx", -1)
    grad_ext = jnp.concatenate([token_grads, next_rim], axis=1)
    inputs_grad = reverse_taps(grad_ext, weights, tokens, 1).astype(jnp.bfloat16)
    weight_part = tap_grads(token_grads, extended, tap_count, tokens, 1)
    short_grad = lax.psum(weight_part, "ctx") * grad_scale
    results = (gated, inputs_grad[0], inputs_grad[1], inputs_grad[2])
    return (results[0], results[1], results[2], results[3], filter_grad, short_grad)


def fits(query_proj, short_weights):
    peers = lax.axis_size("ctx")
    tokens, width = query_proj.shape
    tap_count = short_weights.shape[1]
    return (
        width == peers * LANES
        and peers.bit_count() == 1
        and tokens % (PHASES * CHUNK) == 0
        and tap_count == RIM + 1
        and peers * tokens <= 2048
    )


def shards(*arrays):
    return channel_shards(*arrays) if fits(arrays[0], arrays[5]) else spread_shards(*arrays)


def solution(mesh):
    placed = (
        P("ctx", "tp"),
        P("ctx", "tp"),
        P("ctx", "tp"),
        P("ctx", "tp"),
        P("ctx", "tp"),
        P(None, None, "tp"),
    )
    return jax.shard_map(
        shards,
        mesh=mesh,
        in_specs=placed,
        out_specs=(
            P("ctx", "tp"),
            P("ctx", "tp"),
            P("ctx", "tp"),
            P("ctx", "tp"),
            P("ctx", "tp"),
            P(None, None, "tp"),
        ),
        check_vma=False,
    )
```

```python
import functools
import math

import jax
import jax.numpy as jnp
import numpy as np
from jax import lax
from jax.experimental import pallas as pl
from jax.experimental.pallas import tpu as pltpu
from jax.sharding import PartitionSpec as P

F32 = jnp.float32
BF16 = jnp.bfloat16
LANES = 128
PHASES = 4
TILE = 16
PAD = 8
CHUNK = 32
ROWS = 8
RIM = 2
PIECES = 2
MIB = 1024 * 1024
VMEM_LIMIT = 24 * MIB
PACK_VMEM = 53862 * 1024


def partners(peers, diagonal_first):
    def rank(step):
        links, other_core = (step >> 1).bit_count(), step & 1
        if links == 0:
            return (1 if diagonal_first else 5, 0)
        if links == 1:
            return (4 if other_core else 3, -step)
        return (2 * other_core if diagonal_first else 3.5, other_core)

    return [0] + sorted(range(1, peers), key=rank)


def exchange(blocks, steps):
    peers = len(blocks)
    got = [blocks[0]]
    for step, block in list(zip(steps, blocks))[1:]:
        got.append(lax.ppermute(block, "ctx", [(i, i ^ step) for i in range(peers)]))
    return got


def in_vmem(count):
    return [pl.BlockSpec(memory_space=pltpu.VMEM)] * count


def lanes_of(place):
    return pl.ds(pl.multiple_of(place * LANES, LANES), LANES)


def pack_kernel(count, steps, *refs):
    sources, packed = refs[:count], refs[count : count + len(steps)]
    held, sems = refs[count + len(steps) : -1], refs[-1]
    tokens = sources[0].shape[0]
    me = lax.axis_index("ctx")
    arriving = [
        pltpu.make_async_copy(source, target, sems.at[at])
        for at, (source, target) in enumerate(zip(sources, held))
    ]
    order = [count - 1, *range(count - 1)]
    for at in order:
        arriving[at].start()
    for at in order:
        source = held[at]
        arriving[at].wait()
        rows = slice(at * tokens, (at + 1) * tokens)
        for step, target in zip(steps, packed):
            target[rows, :] = source[:, lanes_of(me ^ step)].astype(BF16)


def pack(arrays, steps):
    tokens = arrays[0].shape[0]
    count = len(arrays)
    return pl.pallas_call(
        functools.partial(pack_kernel, count, steps),
        in_specs=[pl.BlockSpec(memory_space=pl.ANY)] * count,
        out_specs=in_vmem(len(steps)),
        out_shape=[jax.ShapeDtypeStruct((count * tokens, LANES), BF16)] * len(steps),
        scratch_shapes=[
            *[pltpu.VMEM(array.shape, array.dtype) for array in arrays],
            pltpu.SemaphoreType.DMA((count,)),
        ],
        compiler_params=pltpu.CompilerParams(vmem_limit_bytes=PACK_VMEM),
        cost_estimate=pl.CostEstimate(flops=0, bytes_accessed=8 * MIB, transcendentals=0),
        name="pack_inputs",
    )(*arrays)


@functools.lru_cache(maxsize=None)
def dft_tables(seq_len):
    size = seq_len // PHASES
    k = np.arange(size, dtype=np.int64)[:, None]
    m = np.arange(size, dtype=np.int64)[None, :]
    forward = []
    for phase in range(PHASES):
        turns = ((4 * k + 1) * (PHASES * m + phase)) % (4 * seq_len)
        angle = 2.0 * np.pi / (4 * seq_len) * turns
        forward.append(np.concatenate([np.cos(angle), -np.sin(angle)], axis=0))
    forward = np.stack(forward)
    backward = np.swapaxes(forward, 1, 2) / seq_len

    return forward.astype(BF16), backward.astype(BF16)


def forward_mix(parts):
    (r0, i0), (r1, i1), (r2, i2), (r3, i3) = parts
    ar, ai, br, bi = r0 + r2, i0 + i2, r0 - r2, i0 - i2
    cr, ci, dr, di = r1 + r3, i1 + i3, r1 - r3, i1 - i3
    return ((ar + cr, ai + ci), (br + di, bi - dr), (ar - cr, ai - ci), (br - di, bi + dr))


def inverse_mix(parts):
    (r0, i0), (r1, i1), (r2, i2), (r3, i3) = parts
    ar, ai, br, bi = r0 + r2, i0 + i2, r0 - r2, i0 - i2
    cr, ci, dr, di = r1 + r3, i1 + i3, r1 - r3, i1 - i3
    return ((ar + cr, ai + ci), (br - di, bi + dr), (ar - cr, ai - ci), (br + di, bi - dr))


def times(left, right):
    return tuple(
        (lr * rr - li * ri, lr * ri + li * rr) for (lr, li), (rr, ri) in zip(left, right)
    )


def conj_times(left, right):
    return tuple(
        (lr * rr + li * ri, lr * ri - li * rr) for (lr, li), (rr, ri) in zip(left, right)
    )


def transform(table, signal):
    return jnp.dot(table, signal, preferred_element_type=F32)


def phases_near(ref, chunk, tap_count):
    start = PAD + chunk * CHUNK * PHASES
    return {
        offset: ref[pl.ds(start + offset, CHUNK, stride=PHASES), :]
        for offset in range(1 - tap_count, PHASES)
    }


def short_conv(near, taps):
    results = []
    for r in range(PHASES):
        summed = taps[0] * near[r]
        for at in range(1, len(taps)):
            summed = summed + taps[at] * near[r - at]
        results.append(summed)
    return results


def add_rows(total, terms):
    for term in terms:
        folded = jnp.sum(term.reshape(CHUNK // 8, 8, LANES), axis=0)
        total = folded if total is None else total + folded
    return total


def clear_ends(ref):
    ref[:PAD, :] = jnp.zeros((PAD, LANES), F32)
    ref[ref.shape[0] - PAD :, :] = jnp.zeros((PAD, LANES), F32)


def stage_kernel(count, *refs):
    sources, targets, sems = refs[:count], refs[count + 1 : 2 * count + 1], refs[2 * count + 1]
    copies = [
        pltpu.make_async_copy(source, target, sems.at[at])
        for at, (source, target) in enumerate(zip(sources, targets))
    ]
    for copy in copies:
        copy.start()
    for copy in copies:
        copy.wait()


def stage(arrays, after):
    count = len(arrays)
    return pl.pallas_call(
        functools.partial(stage_kernel, count),
        in_specs=[pl.BlockSpec(memory_space=pl.ANY)] * (count + 1),
        out_specs=in_vmem(count),
        out_shape=[jax.ShapeDtypeStruct(array.shape, array.dtype) for array in arrays],
        scratch_shapes=[pltpu.SemaphoreType.DMA((count,))],
        compiler_params=pltpu.CompilerParams(vmem_limit_bytes=8 * MIB),
        cost_estimate=pl.CostEstimate(flops=0, bytes_accessed=8 * MIB, transcendentals=0),
        name="stage_tables",
    )(*arrays, after)


def extra_rows(short_weights):
    sums = PIECES * short_weights.shape[0] * short_weights.shape[1]
    return sums, -(-(sums + 6 * RIM) // TILE) * TILE


def channel_kernel(tokens, heard, told, grad_scale, *refs):
    peers = len(heard)
    arrived = refs[:peers]
    weights, forward, backward = refs[peers : peers + 3]
    out = refs[peers + 3 : 2 * peers + 3]
    (
        query,
        key,
        value,
        cot,
        conv,
        conv_grad,
        filter_grad,
        taps,
        key_short,
        value_short,
        signals,
        spectra,
        products,
        extra,
    ) = refs[2 * peers + 3 :]
    size = peers * tokens // PHASES
    tap_count = weights.shape[1]
    me = lax.axis_index("ctx")
    own = lanes_of(me)
    for ref in (query, key, value, cot, conv, conv_grad):
        clear_ends(ref)
    for ref in (key_short, value_short):
        ref[:, size:, :] = jnp.zeros((PHASES, PAD, LANES), F32)
    for step, source in zip(heard, arrived):
        start = (me ^ step) * tokens
        inner = pl.ds(pl.multiple_of(PAD + start, PAD), tokens)
        for at, ref in enumerate((query, key, value, cot)):
            ref[inner, :] = source[at * tokens : (at + 1) * tokens, :].astype(F32)
        taps[pl.ds(pl.multiple_of(start, PAD), tokens), :] = source[4 * tokens :, :].astype(F32)
    chunks = range(size // CHUNK)
    taps_of = [
        [weights[array, tap : tap + 1, own] for tap in range(tap_count)] for array in range(3)
    ]

    def rows_of(chunk):
        return slice(chunk * CHUNK, (chunk + 1) * CHUNK)

    def spectrum(at, real, imag):
        lanes = slice(at * LANES, (at + 1) * LANES)
        return forward_mix(
            [(spectra[r, real, lanes], spectra[r, imag, lanes]) for r in range(PHASES)]
        )

    def keep(at, real, imag, mixed):
        lanes = slice(at * LANES, (at + 1) * LANES)
        for r, pair in enumerate(inverse_mix(mixed)):
            for rows, part in zip((real, imag), pair):
                products[r, rows, lanes] = part

    for chunk in chunks:
        rows = rows_of(chunk)
        key_now = short_conv(phases_near(key, chunk, tap_count), taps_of[1])
        value_now = short_conv(phases_near(value, chunk, tap_count), taps_of[2])
        for r in range(PHASES):
            key_short[r, rows, :] = key_now[r]
            value_short[r, rows, :] = value_now[r]
            signals[r, rows, :LANES] = (key_now[r] * value_now[r]).astype(BF16)
            filt = taps[pl.ds(chunk * CHUNK * PHASES + r, CHUNK, stride=PHASES), :]
            signals[r, rows, LANES : 2 * LANES] = filt.astype(BF16)
    for r in range(PHASES):
        spectra[r, :, : 2 * LANES] = transform(forward[r], signals[r, :, : 2 * LANES])
    for chunk in chunks:
        rows = rows_of(chunk)
        query_now = short_conv(phases_near(query, chunk, tap_count), taps_of[0])
        cot_now = phases_near(cot, chunk, 1)
        for r in range(PHASES):
            signals[r, rows, 2 * LANES :] = (cot_now[r] * query_now[r]).astype(BF16)
    for r in range(PHASES):
        spectra[r, :, 2 * LANES :] = transform(forward[r], signals[r, :, 2 * LANES :])
    for step in range(size // ROWS):
        real = slice(step * ROWS, (step + 1) * ROWS)
        imag = slice(size + step * ROWS, size + (step + 1) * ROWS)
        prod, filt = spectrum(0, real, imag), spectrum(1, real, imag)
        for at, mixed in enumerate((prod, filt)):
            lanes = slice(at * LANES, (at + 1) * LANES)
            for q, pair in enumerate(mixed):
                spectra[q, real, lanes], spectra[q, imag, lanes] = pair
        keep(0, real, imag, times(prod, filt))
    for r in range(PHASES):
        result = transform(backward[r], products[r, :, :LANES].astype(BF16))
        conv[pl.ds(PAD + r, size, stride=PHASES), :] = result.astype(BF16).astype(F32)
    for step in range(size // ROWS):
        real = slice(step * ROWS, (step + 1) * ROWS)
        imag = slice(size + step * ROWS, size + (step + 1) * ROWS)
        grad = spectrum(2, real, imag)
        for at in range(2):
            lanes = slice(at * LANES, (at + 1) * LANES)
            known = [(spectra[q, real, lanes], spectra[q, imag, lanes]) for q in range(PHASES)]
            keep(2 - at, real, imag, conj_times(known, grad))
    for r in range(PHASES):
        result = transform(backward[r], products[r, :, LANES:].astype(BF16))
        conv_grad[pl.ds(PAD + r, size, stride=PHASES), :] = (
            result[:, :LANES].astype(BF16).astype(F32)
        )
        filter_grad[pl.ds(r, size, stride=PHASES), :] = result[:, LANES:] * grad_scale

    totals = [[None] * tap_count for _ in range(3)]

    def add_sums(array, signal, chunk, pre):
        near = phases_near(signal, chunk, tap_count)
        for tap in range(tap_count):
            totals[array][tap] = add_rows(
                totals[array][tap], [pre[r] * near[r - tap] for r in range(PHASES)]
            )

    for chunk in chunks:
        cot_now, conv_now = phases_near(cot, chunk, 1), phases_near(conv, chunk, 1)
        add_sums(0, query, chunk, [cot_now[r] * conv_now[r] for r in range(PHASES)])
    for chunk in chunks:
        rows = rows_of(chunk)
        grad_now = phases_near(conv_grad, chunk, 1)
        add_sums(1, key, chunk, [grad_now[r] * value_short[r, rows, :] for r in range(PHASES)])
        add_sums(2, value, chunk, [grad_now[r] * key_short[r, rows, :] for r in range(PHASES)])
    sums = [jnp.sum(total, axis=0, keepdims=True) for row in totals for total in row]
    rest = jnp.concatenate(sums, axis=0) * grad_scale
    extra[...] = jnp.zeros_like(extra)
    for piece in range(PIECES):
        rounded = rest.astype(BF16).astype(F32)
        extra[piece * len(sums) : (piece + 1) * len(sums), :] = rounded
        rest = rest - rounded
    for step, target in zip(told, out):
        start = (me ^ step) * tokens
        inner = pl.ds(pl.multiple_of(PAD + start, PAD), tokens)
        target[:tokens, :] = conv[inner, :].astype(BF16)
        target[tokens : 2 * tokens, :] = conv_grad[inner, :].astype(BF16)
        target[2 * tokens : 3 * tokens, :] = filter_grad[
            pl.ds(pl.multiple_of(start, PAD), tokens), :
        ].astype(BF16)
        before = pl.ds(pl.multiple_of(start, PAD), PAD)
        after = pl.ds(pl.multiple_of(PAD + start + tokens, PAD), PAD)
        at = PIECES * len(sums)
        for ref in (query, key, value):
            extra[at : at + RIM, :] = ref[before, :][PAD - RIM :]
            at += RIM
        row = pl.ds(pl.multiple_of((start + tokens) // PHASES, PAD), PAD)
        extra[at : at + RIM, :] = (cot[after, :] * conv[after, :])[:RIM]
        for short in (value_short, key_short):
            at += RIM
            shorts = jnp.concatenate([short[r, row, :][:1] for r in range(RIM)], axis=0)
            extra[at : at + RIM, :] = conv_grad[after, :][:RIM] * shorts
        target[3 * tokens :, :] = extra[...].astype(BF16)


def channel_step(arrived, heard, told, short_weights, tables, tokens):
    peers = len(arrived)
    seq_len = peers * tokens
    size = seq_len // PHASES
    extra = extra_rows(short_weights)[1]
    padded = pltpu.VMEM((seq_len + 2 * PAD, LANES), F32)
    plain = pltpu.VMEM((seq_len, LANES), F32)
    phases = pltpu.VMEM((PHASES, size + PAD, LANES), F32)
    return pl.pallas_call(
        functools.partial(channel_kernel, tokens, heard, told, 1.0 / math.sqrt(seq_len)),
        in_specs=in_vmem(peers + 3),
        out_specs=in_vmem(peers),
        out_shape=[jax.ShapeDtypeStruct((3 * tokens + extra, LANES), BF16)] * peers,
        scratch_shapes=[
            *[padded] * 6,
            plain,
            plain,
            phases,
            phases,
            pltpu.VMEM((PHASES, size, 3 * LANES), BF16),
            pltpu.VMEM((PHASES, 2 * size, 3 * LANES), F32),
            pltpu.VMEM((PHASES, 2 * size, 3 * LANES), F32),
            pltpu.VMEM((extra, LANES), F32),
        ],
        compiler_params=pltpu.CompilerParams(vmem_limit_bytes=VMEM_LIMIT),
        name="channel_operator",
    )(*arrived, short_weights, *tables)


def token_kernel(steps, sum_rows, carried, *refs):
    count_in = len(steps)
    arrived = refs[:count_in]
    query, key, value, cot, weights = refs[count_in : count_in + 5]
    results = refs[count_in + 5 + carried : count_in + 11 + carried]
    (gated, query_grad, key_grad, value_grad, filter_grad, short_grad, longer, pre, sems) = refs[
        count_in + 11 + carried :
    ]
    copies = []
    tokens = query.shape[0]
    tap_count = weights.shape[1]
    count = sum_rows // PIECES
    me = lax.axis_index("ctx")
    for slot, (step, source) in enumerate(zip(steps, arrived)):
        lanes = lanes_of(me ^ step)
        extra = source[3 * tokens :, :].astype(F32)

        def rim(at):
            return extra[sum_rows + at * RIM : sum_rows + (at + 1) * RIM]

        def short(array, signal):
            longer[array, PAD - RIM : PAD, :] = rim(array)
            longer[array, PAD :, :] = signal[:, lanes].astype(F32)
            summed = weights[array, 0:1, lanes] * longer[array, PAD:, :]
            for tap in range(1, tap_count):
                summed = (
                    summed
                    + weights[array, tap : tap + 1, lanes]
                    * longer[array, PAD - tap : PAD - tap + tokens, :]
                )
            return summed

        def taps_back(array, grad, target):
            pre[array, :tokens, :] = grad
            pre[array, tokens : tokens + RIM, :] = rim(3 + array)
            summed = weights[array, 0:1, lanes] * grad
            for tap in range(1, tap_count):
                summed = (
                    summed
                    + weights[array, tap : tap + 1, lanes] * pre[array, tap : tap + tokens, :]
                )
            target[slot] = summed.astype(BF16)

        conv = source[:tokens, :].astype(F32)
        conv_grad = source[tokens : 2 * tokens, :].astype(F32)
        gated[slot] = (short(0, query) * conv).astype(BF16)
        taps_back(0, cot[:, lanes].astype(F32) * conv, query_grad)
        taps_back(1, conv_grad * short(2, value), key_grad)
        taps_back(2, conv_grad * short(1, key), value_grad)
        filter_grad[slot] = source[2 * tokens : 3 * tokens, :].astype(F32)
        whole = extra[:count]
        for piece in range(1, PIECES):
            whole = whole + extra[piece * count : (piece + 1) * count]
        for row in range(count):
            which, tap = divmod(row, tap_count)
            short_grad[slot, which, tap : tap + 1, :] = whole[row : row + 1]
        held = (gated, query_grad, key_grad, value_grad, filter_grad, short_grad)
        for at, (source, target) in enumerate(zip(held, results)):
            place = target.at[:, :, lanes] if at == 5 else target.at[:, lanes]
            copies.append(pltpu.make_async_copy(source.at[slot], place, sems.at[slot, at]))
            copies[-1].start()
    for copy in copies:
        copy.wait()


def token_step(arrived, steps, query, key, value, cot, short_weights, begun=()):
    tokens, width = query.shape
    count = len(arrived)
    wide = jax.ShapeDtypeStruct((tokens, width), BF16)
    anywhere = pl.BlockSpec(memory_space=pl.ANY)
    return pl.pallas_call(
        functools.partial(token_kernel, steps, extra_rows(short_weights)[0], len(begun)),
        in_specs=in_vmem(count + 5) + [anywhere] * len(begun),
        out_specs=[anywhere] * 6,
        out_shape=[wide] * 4
        + [
            jax.ShapeDtypeStruct((tokens, width), F32),
            jax.ShapeDtypeStruct(short_weights.shape, F32),
        ],
        scratch_shapes=[
            *[pltpu.VMEM((count, tokens, LANES), BF16)] * 4,
            pltpu.VMEM((count, tokens, LANES), F32),
            pltpu.VMEM((count, *short_weights.shape[:2], LANES), F32),
            pltpu.VMEM((3, tokens + PAD, LANES), F32),
            pltpu.VMEM((3, tokens + PAD, LANES), F32),
            pltpu.SemaphoreType.DMA((count, 6)),
        ],
        input_output_aliases={count + 5 + at: at for at in range(len(begun))},
        compiler_params=pltpu.CompilerParams(vmem_limit_bytes=VMEM_LIMIT),
        cost_estimate=pl.CostEstimate(flops=0, bytes_accessed=4 * MIB, transcendentals=0),
        name="token_outputs",
    )(*arrived, query, key, value, cot, short_weights, *begun)


def channel_shards(query_proj, key_proj, value_proj, cotangent, filter_taps, short_weights):
    peers = lax.axis_size("ctx")
    tokens = query_proj.shape[0]
    tables = [jnp.asarray(table) for table in dft_tables(peers * tokens)]
    going, coming = partners(peers, False), partners(peers, True)
    sent = pack((query_proj, key_proj, value_proj, cotangent, filter_taps), going)
    arrived = exchange(sent, going)
    staged = stage((sent[0], short_weights, *tables), arrived[1])
    arrived[0] = staged[0]
    results = channel_step(arrived, going, coming, staged[1], staged[2:], tokens)
    back = exchange(results, coming)
    local = (query_proj, key_proj, value_proj, cotangent, short_weights)
    ends = [at for at in (4, 6) if at < peers] + [peers]
    begun, start = (), 0
    for end in ends:
        begun = token_step(back[start:end], coming[start:end], *local, begun)
        start = end
    return tuple(begun)


def from_behind(array, axis, by):
    peers = lax.axis_size(axis)
    pairs = [(i, i + by) for i in range(peers) if 0 <= i + by < peers]
    return lax.ppermute(array, axis, pairs)


def contract(form, left, right):
    return jnp.einsum(
        form, left, right, precision=lax.Precision.HIGHEST, preferred_element_type=jnp.float32
    )


def table_pair(rows, cols, period):
    row_ids = lax.broadcasted_iota(jnp.int32, (rows, cols), 0)
    col_ids = lax.broadcasted_iota(jnp.int32, (rows, cols), 1)
    angle = 2.0 * math.pi / period * (row_ids * col_ids % period).astype(jnp.float32)
    return (jnp.cos(angle), jnp.sin(angle))


def make_plan(seq_len):
    small_len = int(math.isqrt(2 * seq_len))
    while seq_len % small_len:
        small_len -= 1
    large_len = 2 * seq_len // small_len
    large_cos, large_sin = table_pair(large_len // 2, large_len, large_len)
    small_cos, small_sin = table_pair(small_len, small_len, small_len)
    twist_cos, twist_sin = table_pair(large_len, small_len, small_len * large_len)
    fwd_large = jnp.stack([large_cos, -large_sin], axis=1)
    fwd_small = jnp.stack([jnp.stack([small_cos, -small_sin]), jnp.stack([small_sin, small_cos])])
    inv_small = jnp.stack([jnp.stack([small_cos, small_sin]), jnp.stack([-small_sin, small_cos])])
    inv_large = jnp.stack([large_cos, -large_sin])
    return (small_len, large_len, fwd_large, fwd_small, inv_small, inv_large, twist_cos, twist_sin)


def forward_spec(signal, dft_plan):
    small_len, large_len, fwd_large, fwd_small, inv_small, inv_large, twist_cos, twist_sin = (
        dft_plan
    )
    cube = signal.reshape(signal.shape[0], large_len // 2, small_len)
    section_one = contract("cba,bpk->cpka", cube, fwd_large)
    real_one = section_one[:, 0]
    imag_one = section_one[:, 1]
    section_two = jnp.stack(
        [real_one * twist_cos + imag_one * twist_sin, imag_one * twist_cos - real_one * twist_sin],
        axis=1,
    )
    return contract("cpka,pqaj->cqkj", section_two, fwd_small)


def inverse_half(spec, dft_plan):
    small_len, large_len, fwd_large, fwd_small, inv_small, inv_large, twist_cos, twist_sin = (
        dft_plan
    )
    section_one = contract("cqkj,qpja->cpka", spec, inv_small)
    real_one = section_one[:, 0]
    imag_one = section_one[:, 1]
    section_two = jnp.stack(
        [real_one * twist_cos - imag_one * twist_sin, imag_one * twist_cos + real_one * twist_sin],
        axis=1,
    )
    signal = contract("cpka,pbk->cba", section_two, inv_large)
    return signal.reshape(signal.shape[0], -1) / float(small_len * large_len)


def complex_mul(left, right):
    left_real, left_imag = (left[:, 0], left[:, 1])
    right_real, right_imag = (right[:, 0], right[:, 1])
    return jnp.stack(
        [
            left_real * right_real - left_imag * right_imag,
            left_real * right_imag + left_imag * right_real,
        ],
        axis=1,
    )


def conj_mul(left, right):
    left_real, left_imag = (left[:, 0], left[:, 1])
    right_real, right_imag = (right[:, 0], right[:, 1])
    return jnp.stack(
        [
            left_real * right_real + left_imag * right_imag,
            left_real * right_imag - left_imag * right_real,
        ],
        axis=1,
    )


def conv_forward(prod_chan, filter_spec, dft_plan):
    prod_spec = forward_spec(prod_chan.astype(jnp.float32), dft_plan)
    conv_chan = inverse_half(complex_mul(prod_spec, filter_spec), dft_plan).astype(jnp.bfloat16)
    return (conv_chan, prod_spec)


def conv_backward(grad_chan, filter_spec, prod_spec, dft_plan, grad_scale):
    grad_spec = forward_spec(grad_chan.astype(jnp.float32), dft_plan)
    dconv_chan = inverse_half(conj_mul(filter_spec, grad_spec), dft_plan).astype(jnp.bfloat16)
    dfilter_chan = inverse_half(conj_mul(prod_spec, grad_spec), dft_plan) * grad_scale
    return (dconv_chan, dfilter_chan)


def receive_filter(filter_taps, dft_plan):
    filter_chan = lax.all_to_all(filter_taps.T, "ctx", split_axis=0, concat_axis=1, tiled=True)
    return forward_spec(filter_chan, dft_plan)


def return_filter(dfilter_chan):
    return (
        lax.all_to_all(
            dfilter_chan.astype(jnp.bfloat16), "ctx", split_axis=1, concat_axis=0, tiled=True
        )
        .astype(dfilter_chan.dtype)
        .T
    )


def causal_taps(extended, weights, length, axis):
    rim_rows = len(weights) - 1
    summed = weights[0] * lax.slice_in_dim(extended, rim_rows, rim_rows + length, axis=axis)
    for offset in range(1, len(weights)):
        summed = summed + weights[offset] * lax.slice_in_dim(
            extended, rim_rows - offset, rim_rows - offset + length, axis=axis
        )
    return summed


def reverse_taps(extended, weights, length, axis):
    summed = weights[0] * lax.slice_in_dim(extended, 0, length, axis=axis)
    for offset in range(1, len(weights)):
        summed = summed + weights[offset] * lax.slice_in_dim(
            extended, offset, offset + length, axis=axis
        )
    return summed


def tap_grads(grad_in, extended, tap_count, length, axis):
    rim_rows = tap_count - 1
    rows = [
        jnp.sum(
            grad_in
            * lax.slice_in_dim(extended, rim_rows - offset, rim_rows - offset + length, axis=axis),
            axis=axis,
        )
        for offset in range(tap_count)
    ]
    return jnp.stack(rows, axis=1)


def spread_shards(query_proj, key_proj, value_proj, cotangent, filter_taps, short_weights):
    tokens = query_proj.shape[0]
    tap_count = short_weights.shape[1]
    rim_rows = tap_count - 1
    seq_len = tokens * lax.axis_size("ctx")
    grad_scale = 1.0 / math.sqrt(seq_len)
    dft_plan = make_plan(seq_len)
    stacked = jnp.stack([query_proj, key_proj, value_proj])
    prev_rim = from_behind(stacked[:, tokens - rim_rows :], "ctx", 1)
    extended = jnp.concatenate([prev_rim, stacked], axis=1).astype(jnp.float32)
    weights = [short_weights[:, offset, None, :] for offset in range(tap_count)]
    short_out = causal_taps(extended, weights, tokens, 1)
    product = (short_out[1] * short_out[2]).astype(jnp.bfloat16)
    cot_wide = cotangent.astype(jnp.float32)
    gate_grad = (cot_wide * short_out[0]).astype(jnp.bfloat16)
    filter_spec = receive_filter(filter_taps, dft_plan)
    prod_chan = lax.all_to_all(product.T, "ctx", split_axis=0, concat_axis=1, tiled=True)
    conv_chan, prod_spec = conv_forward(prod_chan, filter_spec, dft_plan)
    conv_tok = lax.all_to_all(conv_chan, "ctx", split_axis=1, concat_axis=0, tiled=True)
    grad_chan = lax.all_to_all(gate_grad.T, "ctx", split_axis=0, concat_axis=1, tiled=True)
    dconv_chan, dfilter_chan = conv_backward(
        grad_chan, filter_spec, prod_spec, dft_plan, grad_scale
    )
    dconv_tok = lax.all_to_all(dconv_chan, "ctx", split_axis=1, concat_axis=0, tiled=True)
    filter_grad = return_filter(dfilter_chan)
    conv_wide = conv_tok.T.astype(jnp.float32)
    dconv_wide = dconv_tok.T.astype(jnp.float32)
    gated = (short_out[0] * conv_wide).astype(jnp.bfloat16)
    token_grads = jnp.stack(
        [cot_wide * conv_wide, dconv_wide * short_out[2], dconv_wide * short_out[1]]
    )
    next_rim = from_behind(token_grads[:, :rim_rows], "ctx", -1)
    grad_ext = jnp.concatenate([token_grads, next_rim], axis=1)
    inputs_grad = reverse_taps(grad_ext, weights, tokens, 1).astype(jnp.bfloat16)
    weight_part = tap_grads(token_grads, extended, tap_count, tokens, 1)
    short_grad = lax.psum(weight_part, "ctx") * grad_scale
    results = (gated, inputs_grad[0], inputs_grad[1], inputs_grad[2])
    return (results[0], results[1], results[2], results[3], filter_grad, short_grad)


def fits(query_proj, short_weights):
    peers = lax.axis_size("ctx")
    tokens, width = query_proj.shape
    tap_count = short_weights.shape[1]
    return (
        width == peers * LANES
        and peers.bit_count() == 1
        and tokens % (PHASES * CHUNK) == 0
        and tap_count == RIM + 1
        and peers * tokens <= 2048
    )


def shards(*arrays):
    return channel_shards(*arrays) if fits(arrays[0], arrays[5]) else spread_shards(*arrays)


def solution(mesh):
    placed = (
        P("ctx", "tp"),
        P("ctx", "tp"),
        P("ctx", "tp"),
        P("ctx", "tp"),
        P("ctx", "tp"),
        P(None, None, "tp"),
    )
    return jax.shard_map(
        shards,
        mesh=mesh,
        in_specs=placed,
        out_specs=(
            P("ctx", "tp"),
            P("ctx", "tp"),
            P("ctx", "tp"),
            P("ctx", "tp"),
            P("ctx", "tp"),
            P(None, None, "tp"),
        ),
        check_vma=False,
    )
```
